32 devices in a mesh: seq: 8 (over z, y), blk: 4 (over x, core).
Axes of the slice: x: 2, y: 2, z: 4, core: 2. Of those that a mesh axis runs over, the one named last changes fastest.
Arguments:
- chars: bfloat16 [32, 2048, 512], P('seq', 'blk'), may hold values from -6 to 6
- seg_lengths: int32 [32, 512], P('seq'), may hold values from 1 to 16, as said below
- memory: bfloat16 [32, 512, 512], P('seq', 'blk'), may hold values from -6 to 6
- grad_out: bfloat16 [32, 2048, 512], P('seq', 'blk'), may hold values from -6 to 6
- w_query: bfloat16 [512, 512], replicated, may hold values from -0.25 to 0.25
- w_key: bfloat16 [512, 512], replicated, may hold values from -0.25 to 0.25
- w_value: bfloat16 [512, 512], replicated, may hold values from -0.25 to 0.25
- w_rel: bfloat16 [512, 512], replicated, may hold values from -0.375 to 0.375
- w_out: bfloat16 [512, 512], replicated, may hold values from -1 to 1
- w_up: bfloat16 [512, 2048], replicated, may hold values from -0.25 to 0.25
- w_down: bfloat16 [2048, 512], replicated, may hold values from -0.125 to 0.125
- bias_u: bfloat16 [8, 64], replicated, may hold values from -3 to 3
- bias_v: bfloat16 [8, 64], replicated, may hold values from -3 to 3
- gain_one: bfloat16 [512], replicated, may hold values from 0.5 to 1.5
- shift_one: bfloat16 [512], replicated, may hold values from -2 to 2
- gain_two: bfloat16 [512], replicated, may hold values from 0.5 to 1.5
- shift_two: bfloat16 [512], replicated, may hold values from -2 to 2
- bias_up: bfloat16 [2048], replicated, may hold values from -2 to 2
- bias_down: bfloat16 [512], replicated, may hold values from -2 to 2
Outputs:
- out_chars: bfloat16 [32, 2048, 512], P('seq', 'blk')
- grad_chars: float32 [32, 2048, 512], P('seq', 'blk')
- new_memory: bfloat16 [32, 512, 512], P('seq', 'blk')
- grad_w_query: float32 [512, 512], replicated
- grad_w_key: float32 [512, 512], replicated
- grad_w_value: float32 [512, 512], replicated
- grad_w_rel: float32 [512, 512], replicated
- grad_w_out: float32 [512, 512], replicated
- grad_w_up: float32 [512, 2048], replicated
- grad_w_down: float32 [2048, 512], replicated
- grad_bias_u: float32 [8, 64], replicated
- grad_bias_v: float32 [8, 64], replicated
- grad_gain_one: float32 [512], replicated
- grad_shift_one: float32 [512], replicated
- grad_gain_two: float32 [512], replicated
- grad_shift_two: float32 [512], replicated
- grad_bias_up: float32 [2048], replicated
- grad_bias_down: float32 [512], replicated
The draws below stay inside these ranges and needn't reach their ends.
Inputs may be any that keep to these rules, and one draw needn't show every extreme that they name: `seg_lengths`: each row lists the lengths of the 512 segments of one sequence in order; they sum to 2048 and the longest is 16; the first 384 segments of every sequence are one byte long.
All inputs are finite; a program needn't handle non-finite values.
Results may differ from the reference program's by a relative error of at most 0.015.
Values may be sent and summed in bfloat16 or wider, within the bound.
A program may use at most 192 MiB of HBM per device.

```python
import math
import jax
import jax.numpy as jnp
from jax import lax

D = 512
HEADS = 8
HEAD = 64
FF = 2048
LEN = 2048
NSEG = 512
MOST = 16
SEQS = 32


def lengths_one(key):
    quiet = 3 * NSEG // 4
    loud = NSEG - quiet
    cells = loud * (MOST - 1)
    extra = LEN - NSEG
    cell_seg = jnp.arange(cells, dtype=jnp.int32) // (MOST - 1)
    rank = jax.random.permutation(jax.random.fold_in(key, 1), cells).astype(jnp.int32)
    chosen = jax.random.randint(jax.random.fold_in(key, 2), (), 0, loud).astype(jnp.int32)
    adjusted = jnp.where(cell_seg == chosen, rank - cells, rank)
    order = jnp.argsort(adjusted, stable=True)
    picked = jnp.zeros((cells,), jnp.int32).at[order[:extra]].set(1)
    counts = jax.ops.segment_sum(picked, cell_seg, loud)
    return jnp.concatenate([jnp.ones((quiet,), jnp.int32), 1 + counts.astype(jnp.int32)])


def draw_seg_lengths(key, part):
    key = jax.random.fold_in(key, 7)
    keys = jax.random.split(key, SEQS)
    return jax.vmap(lengths_one)(keys)


def levels(key, dims, cuts, least, high):
    loudness, own = 1.0, jax.random.fold_in(key, 6)
    for dim, parts in cuts:
        steps = jnp.exp(jax.random.uniform(jax.random.fold_in(own, dim), (parts,), jnp.float32, least / len(cuts), high / len(cuts)))
        loudness = loudness * jnp.repeat(steps, dims[dim] // parts).reshape([-1 if axis == dim else 1 for axis in range(len(dims))])
    return loudness


def gaussian(key, shape, deviation, reach, shards=(), kind=jnp.bfloat16):
    array = deviation * jax.random.normal(key, shape, jnp.float32)
    if shards:
        array = array * levels(key, shape, shards, -0.22, 0.18)
    return jnp.clip(array, -reach, reach).astype(kind)


def setup_inputs(seed: int = 0) -> dict:
    key_list = jax.random.split(jax.random.key(seed), 20)
    return {
        "chars": gaussian(key_list[0], (SEQS, LEN, D), 1.0, 6.0, ((0, 8), (1, 4))),
        "seg_lengths": draw_seg_lengths(jax.random.fold_in(key_list[19], 71), 0),
        "memory": gaussian(key_list[2], (SEQS, NSEG, D), 1.0, 6.0, ((0, 8), (1, 4))),
        "grad_out": gaussian(key_list[3], (SEQS, LEN, D), 1.0, 6.0, ((0, 8), (1, 4))),
        "w_query": gaussian(key_list[4], (D, D), D ** -0.5, 0.25),
        "w_key": gaussian(key_list[5], (D, D), D ** -0.5, 0.25),
        "w_value": gaussian(key_list[6], (D, D), D ** -0.5, 0.25),
        "w_rel": gaussian(key_list[7], (D, D), (D // 2) ** -0.5, 0.375),
        "w_out": gaussian(key_list[8], (D, D), (D // 16) ** -0.5, 1.0),
        "w_up": gaussian(key_list[9], (D, FF), D ** -0.5, 0.25),
        "w_down": gaussian(key_list[10], (FF, D), FF ** -0.5, 0.125),
        "bias_u": gaussian(key_list[11], (HEADS, HEAD), 0.5, 3.0),
        "bias_v": gaussian(key_list[12], (HEADS, HEAD), 0.5, 3.0),
        "gain_one": jnp.clip(1.0 + 0.1 * jax.random.normal(key_list[13], (D,), jnp.float32), 0.5, 1.5).astype(jnp.bfloat16),
        "shift_one": gaussian(key_list[14], (D,), 0.3, 2.0),
        "gain_two": jnp.clip(1.0 + 0.1 * jax.random.normal(key_list[15], (D,), jnp.float32), 0.5, 1.5).astype(jnp.bfloat16),
        "shift_two": gaussian(key_list[16], (D,), 0.3, 2.0),
        "bias_up": gaussian(key_list[17], (FF,), 0.3, 2.0),
        "bias_down": gaussian(key_list[18], (D,), 0.3, 2.0),
    }


@jax.custom_vjp
def low(v):
    return lax.optimization_barrier(v.astype(jnp.bfloat16)).astype(jnp.float32)

@jax.custom_vjp
def low_back(v):
    return v

def low_keep(v):
    return (low(v), None)

def low_pass(kept, grad):
    return (grad,)

def back_keep(v):
    return (v, None)

def back_low(kept, grad):
    return (low(grad),)
low.defvjp(low_keep, low_pass)
low_back.defvjp(back_keep, back_low)

def layer_norm(value, gain, shift):
    center = value - lax.optimization_barrier(jnp.mean(value, axis=-1, keepdims=True))
    spread = lax.optimization_barrier(jnp.mean(center * center, axis=-1, keepdims=True))
    return center * lax.rsqrt(spread + 1e-05) * gain + shift

def angle_tables(places, feature_width):
    freqs = jnp.exp(jnp.arange(feature_width // 2, dtype=jnp.float32) * (-2.0 * math.log(10000.0) / feature_width))
    angles = places[:, None] * freqs[None, :]
    return (jnp.sin(angles), jnp.cos(angles))

def smooth_gate(value):
    return jax.nn.gelu(value, approximate=False)

def sequence_forward(params, chars_f, memory_f, lengths_seq):
    w_query, w_key, w_value, w_rel, w_out, w_up, w_down, bias_u, bias_v, gain_one, shift_one, gain_two, shift_two, bias_up, bias_down = params
    highest = lax.Precision.HIGHEST
    feature_width = chars_f.shape[1]
    seg_count = lengths_seq.shape[0]
    head_count, head_dim = bias_u.shape
    half_width = feature_width // 2
    score_scale = head_dim ** (-0.5)
    seg_end = jnp.cumsum(lengths_seq)
    char_places = jnp.arange(chars_f.shape[0], dtype=jnp.int32)
    segment = lax.optimization_barrier(jnp.sum((seg_end[None, :] <= char_places[:, None]).astype(jnp.int32), axis=1))
    pooled = jax.ops.segment_sum(chars_f, segment, seg_count) / lengths_seq[:, None].astype(chars_f.dtype)
    normed = low(layer_norm(pooled, gain_one, shift_one))
    normed_mem = low(layer_norm(memory_f, gain_one, shift_one))
    both_rows = jnp.concatenate([normed_mem, normed], axis=0)
    query_rows = low_back(jnp.dot(normed, w_query, precision=highest))
    key_rows = low_back(low(jnp.dot(both_rows, w_key, precision=highest))).reshape(2 * seg_count, head_count, head_dim)
    value_rows = low_back(low(jnp.dot(both_rows, w_value, precision=highest))).reshape(2 * seg_count, head_count, head_dim)
    query_u = low(query_rows + bias_u.reshape(-1)).reshape(seg_count, head_count, head_dim)
    query_v = low(query_rows + bias_v.reshape(-1)).reshape(seg_count, head_count, head_dim)
    rel_coeff = low_back(jnp.einsum('ihe,fhe->ihf', query_v, w_rel.reshape(feature_width, head_count, head_dim), precision=highest))
    sin_all, cos_all = angle_tables(jnp.arange(2 * seg_count).astype(chars_f.dtype), feature_width)
    sin_query = sin_all[seg_count:][:, None, :]
    cos_query = cos_all[seg_count:][:, None, :]
    coeff_sin = rel_coeff[..., :half_width]
    coeff_cos = rel_coeff[..., half_width:]
    query_pos = low(jnp.concatenate([coeff_sin * sin_query + coeff_cos * cos_query, coeff_cos * sin_query - coeff_sin * cos_query], axis=-1))
    key_pos = low(jnp.concatenate([cos_all, sin_all], axis=-1))
    scores = (jnp.einsum('ihe,jhe->hij', query_u, key_rows, precision=highest) + jnp.einsum('ihf,jf->hij', query_pos, key_pos, precision=highest)) * score_scale
    scores = low_back(scores)
    allowed = jnp.arange(2 * seg_count)[None, :] <= (seg_count + jnp.arange(seg_count))[:, None]
    scores = jnp.where(allowed[None], scores, -1e+30)
    att_probs = low(jax.nn.softmax(scores, axis=-1))
    att_mixed = low_back(low(jnp.einsum('hij,jhe->ihe', att_probs, value_rows, precision=highest).reshape(seg_count, feature_width)))
    residual = pooled + low_back(jnp.dot(att_mixed, w_out, precision=highest))
    normed_two = low(layer_norm(residual, gain_two, shift_two))
    ffn_inner = low_back(jnp.dot(normed_two, w_up, precision=highest) + bias_up)
    hidden = low(smooth_gate(ffn_inner))
    pooled_out = low(residual + low_back(jnp.dot(hidden, w_down, precision=highest) + bias_down))
    return (chars_f + pooled_out[segment], pooled)

def reference(chars, seg_lengths, memory, grad_out, w_query, w_key, w_value, w_rel, w_out, w_up, w_down, bias_u, bias_v, gain_one, shift_one, gain_two, shift_two, bias_up, bias_down):
    weights = tuple((weight.astype(jnp.float32) for weight in (w_query, w_key, w_value, w_rel, w_out, w_up, w_down, bias_u, bias_v, gain_one, shift_one, gain_two, shift_two, bias_up, bias_down)))

    def scan_step(grad_total, per_seq):
        chars_seq, lengths_seq, memory_seq, grad_seq = per_seq
        memory_f = memory_seq.astype(jnp.float32)

        def forward_fn(params, chars_f):
            return sequence_forward(params, chars_f, memory_f, lengths_seq)
        out_seq, pull_back, pooled_seq = jax.vjp(forward_fn, weights, chars_seq.astype(jnp.float32), has_aux=True)
        grad_params, grad_seq_chars = pull_back(grad_seq.astype(jnp.float32))
        grad_total = jax.tree.map(jnp.add, grad_total, grad_params)
        return (grad_total, (out_seq.astype(jnp.bfloat16), grad_seq_chars.astype(jnp.float32), pooled_seq.astype(jnp.bfloat16)))
    start_total = jax.tree.map(jnp.zeros_like, weights)
    grad_total, outputs = lax.scan(scan_step, start_total, (chars, seg_lengths, memory, grad_out))
    out_chars, grad_chars, new_memory = outputs
    return (out_chars, grad_chars, new_memory, grad_total[0], grad_total[1], grad_total[2], grad_total[3], grad_total[4], grad_total[5], grad_total[6], grad_total[7], grad_total[8], grad_total[9], grad_total[10], grad_total[11], grad_total[12], grad_total[13], grad_total[14])
```

```python
import functools
import math
import types

import jax
import jax.numpy as jnp
import numpy as np
from jax import lax
from jax.experimental import pallas as pl
from jax.experimental.pallas import tpu as pltpu
from jax.sharding import PartitionSpec as P

F32, BF16 = jnp.float32, jnp.bfloat16
NT = (((1,), (1,)), ((), ()))


def mm(a, b):
    return jnp.dot(a, b, preferred_element_type=F32)


def mm_nt(a, b):
    return lax.dot_general(a, b, NT, preferred_element_type=F32)


def normalize(value):
    center = value - jnp.mean(value, axis=-1, keepdims=True)
    inv = lax.rsqrt(jnp.mean(center * center, axis=-1, keepdims=True) + 1e-05)
    return center * inv, inv


def norm_back(grad, unit, inv, gain):
    scaled = grad * gain
    along = jnp.mean(scaled * unit, axis=-1, keepdims=True)
    return inv * (scaled - jnp.mean(scaled, axis=-1, keepdims=True) - unit * along)


def gelu_parts(value):
    size = jnp.abs(value) * 0.7071067811865476
    t = 1.0 / (1.0 + 0.3275911 * size)
    bell = jnp.exp(-0.5 * value * value)
    poly = t * (0.254829592 + t * (-0.284496736 + t * (1.421413741 + t * (-1.453152027 + t * 1.061405429))))
    tail = 0.5 * poly * bell
    gate = jnp.where(value < 0, tail, 1.0 - tail)
    return gate, gate + value * bell * 0.3989422804014327


def ramp(shape, dim):
    return lax.broadcasted_iota(jnp.int32, shape, dim)


MESH = pl.DeviceIdType.MESH
HALF = 256
PIECE = 512
UNITS = 13
STEPS = 11
VECTORS = ("bias_u", "bias_v", "gain_one", "shift_one", "gain_two", "shift_two", "bias_up", "bias_down")


class Place:
    def __init__(self):
        self.s = lax.axis_index("seq")
        self.b = lax.axis_index("blk")
        self.z, self.y = self.s // 2, self.s % 2
        self.x, self.c = self.b // 2, self.b % 2
        self.bit = dict(x=self.x, y=self.y, near=self.z % 2, far=self.z // 2)

    def group(self, k):
        return (self.s, (self.b + k) % 4)

    def core(self):
        return (self.s, self.b + 1 - 2 * self.c)

    def across(self):
        return (self.s, self.b + 2 - 4 * self.x)

    def move(self, axis):
        reach = dict(x=(0, 2), y=(1, 0), near=(2, 0), far=(4, 0))[axis]
        turn = 1 - 2 * self.bit[axis]
        return reach[0] * turn, reach[1] * turn

    def step(self, n):
        zero, one = ORDERS[0][n], ORDERS[1][n]
        away = [self.move(zero)[m] * (1 - self.c) + self.move(one)[m] * self.c for m in (0, 1)]
        bit = self.bit[zero] * (1 - self.c) + self.bit[one] * self.c
        return (self.s + away[0], self.b + away[1]), bit

    def pair(self, axis):
        away = self.move(axis)
        return (self.s + away[0], self.b + away[1])


ORDERS = (("y", "x", "near", "far"), ("near", "y", "x", "far"))
AXES = ("x", "y", "near", "far")


def rows_at(start, size):
    return pl.ds(pl.multiple_of(start, 16), size)


def remote(src, dst, send, recv, to):
    return pltpu.make_async_remote_copy(src, dst, send, recv, device_id=to, device_id_type=MESH)


class Sum:
    def __init__(self, place, total, land, out, send, recv, store):
        self.p, self.g, self.land, self.out = place, total, land, out
        self.send, self.recv, self.store = send, recv, store

    def offset(self, k, n):
        start = k * PIECE + self.p.c * 256
        for m in range(n):
            start = start + self.p.step(m)[1] * (128 >> m)
        return start

    def copies(self, step, k, landing=False):
        p, g, land = self.p, self.g, self.land

        def copy(src, dst, to):
            return remote(src, dst, self.send.at[k % 2, step], self.recv.at[k, step], to)

        if step == 0:
            return copy(g.at[rows_at(k * PIECE + (1 - p.c) * 256, 256)], land[0].at[k], p.core())
        if step <= 4:
            to, bit = p.step(step - 1)
            size = 256 >> step
            away = self.offset(k, step - 1) + (1 - bit) * size
            return copy(g.at[rows_at(away, size)], land[step].at[k], to)
        if step <= 8:
            n = 8 - step
            to, bit = p.step(n)
            size = 128 >> n
            side = rows_at((1 - bit if landing else bit) * size, size)
            src = land[3].at[k, rows_at(bit * 16, 16)] if n == 3 else land[n + 1].at[k]
            return copy(src, land[n].at[k, side], to)
        span = k * PIECE + (1 - p.c if landing else p.c) * 256
        return copy(land[0].at[k], self.out.at[rows_at(span, 256)], p.core())

    def own(self, k):
        span = rows_at(k * PIECE + self.p.c * 256, 256)
        return pltpu.make_async_copy(self.land[0].at[k], self.out.at[span], self.store.at[k % 2])

    def step(self, step, k):
        g, land = self.g, self.land
        if step > 0:
            self.copies(step - 1, k).wait_send()
            self.copies(step - 1, k, landing=True).wait_recv()
        if 1 <= step <= 4:
            size = 512 >> step
            span = rows_at(self.offset(k, step - 1), size)
            g[span] = (g[span].astype(F32) + land[step - 1][k].astype(F32)).astype(BF16)
        if step == 5:
            total = g[rows_at(self.offset(k, 4), 16)].astype(F32) + land[4][k].astype(F32)
            land[3][k, rows_at(self.p.step(3)[1] * 16, 16)] = total.astype(BF16)
        if 6 <= step <= 8:
            n = 8 - step
            size = 128 >> n
            land[n][k, rows_at(self.p.step(n)[1] * size, size)] = land[n + 1][k]
        if step < STEPS - 1:
            self.copies(step, k).start()
        if step == STEPS - 2:
            self.own(k).start()
        if step == STEPS - 1:
            self.own(k).wait()

    def tick(self, turn, units=UNITS):
        for step in range(STEPS - 1, -1, -1):
            k = turn - 2 * step
            if isinstance(k, int):
                if 0 <= k < units:
                    self.step(step, k)
            else:
                pl.when((k >= 0) & (k < units))(functools.partial(self.step, step, k))


def lane_mask(par):
    lane = ramp((1, 128), 1)
    return jnp.where((lane >= 64) == bool(par), 1.0, 0.0).astype(BF16)


def flip_matrix():
    return jnp.where(ramp((HALF, HALF), 0) + ramp((HALF, HALF), 1) == HALF - 1, 1.0, 0.0).astype(BF16)


def flip(flip_low, value):
    return jnp.concatenate(
        [mm(flip_low, value[r : r + HALF]) for r in range(0, value.shape[0], HALF)], axis=0
    ).astype(value.dtype)


def pool_matrix(end, length, first_place, places):
    place = (ramp((end.shape[0], places), 1) + first_place).astype(F32)
    return jnp.where((place < end) & (place >= end - length), 1.0, 0.0).astype(BF16)


def query_block(n, seg):
    keys = seg + HALF * (n + 1)
    return slice(n * HALF, (n + 1) * HALF), keys, 2 * seg - keys


def attend_pair(p, n, seg, r):
    lanes = pl.ds(pl.multiple_of(p * 128, 128), 128)
    seen = ramp((HALF, HALF), 1) <= ramp((HALF, HALF), 0)
    lane = ramp((HALF, 128), 1)
    rows, keys, skip = query_block(n, seg)
    key, value, place = r.key[0:keys, lanes], r.value[0:keys, lanes], r.place[skip : 2 * seg, lanes]
    mixed = []
    for par in range(2):
        keep = lane_mask(par)
        near = mm_nt(r.query_u[rows, lanes] * keep, key)
        far = mm_nt(r.query_v[rows, lanes] * keep, place)
        scores = near + pltpu.roll(far, keys - (HALF - 1), 1, stride=1, stride_axis=0)
        scores = jnp.concatenate(
            [scores[:, : keys - HALF], jnp.where(seen, scores[:, keys - HALF :], -1e30)], axis=1
        )
        expo = jnp.exp(scores - jnp.max(scores, axis=1, keepdims=True))
        probs = (expo * (1.0 / jnp.sum(expo, axis=1, keepdims=True))).astype(BF16)
        r.probs[2 * p + par, rows, 0:keys] = probs
        mixed.append(mm(probs, value))
    r.mixed[rows, lanes] = jnp.where(lane >= 64, mixed[1], mixed[0]).astype(BF16)


def attend_back_pair(p, seg, r):
    lanes = pl.ds(pl.multiple_of(p * 128, 128), 128)
    flip_low = flip_matrix()
    scale = 0.125
    lane = ramp((HALF, 128), 1)
    sums = [None] * 6
    bias = []
    for n in range(seg // HALF):
        rows, keys, skip = query_block(n, seg)
        key, value, place = r.key[0:keys, lanes], r.value[0:keys, lanes], r.place[skip : 2 * seg, lanes]
        grad_u, grad_v = [], []
        for par in range(2):
            keep = lane_mask(par)
            feats = pl.ds(pl.multiple_of(p * 128 + par * 64, 64), 64)
            probs = r.probs[2 * p + par, rows, 0:keys]
            turned = mm(flip_low, probs)
            grad_mixed = r.grad_mixed[rows, lanes] * keep
            delta = jnp.sum(grad_mixed.astype(F32) * r.mixed_flip[rows, lanes].astype(F32), axis=1, keepdims=True)
            grad_scores = turned * (mm_nt(grad_mixed, value) - delta)
            near = grad_scores.astype(BF16)
            far = pltpu.roll(grad_scores, 0, 1, stride=1, stride_axis=0).astype(BF16)
            grad_u.append(mm(near, key) * scale)
            grad_v.append(mm(far, place) * scale)
            now = (
                mm(r.query_u_t[feats, rows], near),
                mm(r.grad_mixed_t[feats, rows], probs),
                mm(r.query_v_t[feats, rows], far),
            )
            for m in range(3):
                slot = par * 3 + m
                if n == 0:
                    sums[slot] = now[m]
                else:
                    old, new = sums[slot], now[m]
                    cut = old.shape[1]
                    if m < 2:
                        sums[slot] = jnp.concatenate([new[:, :cut] + old, new[:, cut:]], axis=1)
                    else:
                        sums[slot] = jnp.concatenate([new[:, :-cut], new[:, -cut:] + old], axis=1)
        grad_u = jnp.where(lane >= 64, grad_u[1], grad_u[0])
        grad_v = jnp.where(lane >= 64, grad_v[1], grad_v[0])
        bias.append((jnp.sum(grad_u, axis=0, keepdims=True), jnp.sum(grad_v, axis=0, keepdims=True)))
        r.grad_query[rows, lanes] = mm(flip_low, (grad_u + grad_v).astype(BF16)).astype(BF16)
    r.small[0:1, lanes] = sum(b[0] for b in bias)
    r.small[1:2, lanes] = sum(b[1] for b in bias)
    for par in range(2):
        feats = pl.ds(pl.multiple_of(p * 128 + par * 64, 64), 64)
        for m, out in enumerate((r.grad_key_t, r.grad_value_t, r.grad_place_t)):
            out[feats, :] = sums[par * 3 + m].astype(BF16)


def pair_weights(p, seg, r, base):
    lanes = pl.ds(pl.multiple_of(p * 128, 128), 128)
    grad_query_t = r.grad_query[:, lanes].astype(F32).T.astype(BF16)
    r.total[rows_at(base, 128)] = mm(grad_query_t, r.normed[seg : 2 * seg]).astype(BF16)
    r.total[rows_at(base + 128, 128)] = mm(r.grad_key_t[lanes, :], r.normed[...]).astype(BF16)
    r.total[rows_at(base + 256, 128)] = mm(r.grad_value_t[lanes, :], r.normed[...]).astype(BF16)
    r.total[rows_at(base + 384, 128)] = mm(r.grad_place_t[lanes, :], r.table[...]).astype(BF16)


def project_memory(seg, r):
    unit, unused = normalize(r.memory[...].astype(F32))
    low = (unit * r.vec("gain_one") + r.vec("shift_one")).astype(BF16)
    r.normed[0:seg] = low
    r.key[0:seg] = mm(low, r.w_key[...]).astype(BF16)
    r.value[0:seg] = mm(low, r.w_value[...]).astype(BF16)
    r.place[...] = mm(r.table[...], r.w_rel[...]).astype(BF16)


def project_segments(n, seg, r):
    rows, keys, unused = query_block(n, seg)
    places = slice(keys - HALF, keys)
    unit, unused = normalize(r.pooled[rows])
    low = (unit * r.vec("gain_one") + r.vec("shift_one")).astype(BF16)
    r.normed[places] = low
    query = mm(low, r.w_query[...])
    scale = 0.125
    r.query_u[rows] = (query + r.vec("bias_u")).astype(BF16) * jnp.asarray(scale, BF16)
    r.query_v[rows] = (query + r.vec("bias_v")).astype(BF16) * jnp.asarray(scale, BF16)
    r.key[places] = mm(low, r.w_key[...]).astype(BF16)
    r.value[places] = mm(low, r.w_value[...]).astype(BF16)


def feed_forward_in(n, r):
    rows = slice(n * HALF, (n + 1) * HALF)
    residual = r.pooled[rows] + mm(r.mixed[rows], r.w_out[...])
    r.residual[rows] = residual
    unit, unused = normalize(residual)
    r.normed_two[rows] = (unit * r.vec("gain_two") + r.vec("shift_two")).astype(BF16)

    def tile(m, carry):
        cols = pl.ds(pl.multiple_of(m * 512, 512), 512)
        inner = mm(r.normed_two[rows], r.w_up[:, cols]) + r.bias_up[0:1, cols]
        gate, slope = gelu_parts(inner)
        r.hidden[rows, cols] = (inner * gate).astype(BF16)
        r.slope[rows, cols] = slope.astype(BF16)
        return carry

    lax.fori_loop(0, r.w_up.shape[1] // 512, tile, 0)


def feed_forward_back(n, r):
    cols = pl.ds(pl.multiple_of(n * 512, 512), 512)
    r.total[rows_at(n * 1024, 512)] = mm(r.grad_down_t[...], r.hidden[:, cols]).astype(BF16)
    grad_hidden = mm_nt(r.grad_down[...], r.w_down[cols, :])
    low = (grad_hidden * r.slope[:, cols].astype(F32)).astype(BF16)
    r.grad_inner[:, cols] = low
    r.small[pl.ds(7 + n, 1), :] = jnp.sum(low.astype(F32), axis=0, keepdims=True)
    r.total[rows_at(n * 1024 + 512, 512)] = mm(r.normed_two_t[...], low).astype(BF16)


def middle_back(r, base):
    grad_normed = mm_nt(r.grad_inner[...], r.w_up[...])
    unit, inv = normalize(r.residual[...])
    r.small[4:5, :] = jnp.sum(grad_normed * unit, axis=0, keepdims=True)
    r.small[5:6, :] = jnp.sum(grad_normed, axis=0, keepdims=True)
    grad = r.grad_output[...] + norm_back(grad_normed, unit, inv, r.vec("gain_two"))
    r.grad_residual[...] = grad
    low = grad.astype(BF16)
    mixed = r.mixed[...]
    r.total[rows_at(base, 512)] = mm(mixed.astype(F32).T.astype(BF16), low).astype(BF16)
    grad_mixed = mm_nt(low, r.w_out[...]).astype(BF16)
    r.grad_mixed_t[...] = grad_mixed.astype(F32).T.astype(BF16)
    flip_low = flip_matrix()
    r.grad_mixed[...] = flip(flip_low, grad_mixed)
    r.mixed_flip[...] = flip(flip_low, mixed)
    r.query_u_t[...] = flip(flip_low, r.query_u[...]).astype(F32).T.astype(BF16)
    r.query_v_t[...] = flip(flip_low, r.query_v[...]).astype(F32).T.astype(BF16)


def first_back(seg, r):
    grad_key = r.grad_key_t[...].astype(F32).T.astype(BF16)
    grad_value = r.grad_value_t[...].astype(F32).T.astype(BF16)
    grad_normed = mm_nt(r.grad_query[...], r.w_query[...])
    grad_normed += mm_nt(grad_key[seg:], r.w_key[...])
    grad_normed += mm_nt(grad_value[seg:], r.w_value[...])
    grad_mem = mm_nt(grad_key[:seg], r.w_key[...]) + mm_nt(grad_value[:seg], r.w_value[...])
    unit, inv = normalize(r.pooled[...])
    unit_mem, unused = normalize(r.memory[...].astype(F32))
    r.small[2:3, :] = jnp.sum(grad_normed * unit + grad_mem * unit_mem, axis=0, keepdims=True)
    r.small[3:4, :] = jnp.sum(grad_normed + grad_mem, axis=0, keepdims=True)
    return r.grad_residual[...] + norm_back(grad_normed, unit, inv, r.vec("gain_one"))


QUIET = 384


def sine_table(count, width):
    freqs = np.exp(np.arange(width // 2) * (-2.0 * math.log(10000.0) / width))
    angles = np.arange(count)[::-1, None] * freqs[None, :]
    return np.concatenate([np.sin(angles), np.cos(angles)], axis=1).astype(jnp.bfloat16)


def span_columns(lengths, low):
    seg = lengths.shape[1]
    lens = lengths.astype(F32).astype(BF16)
    row, col = ramp((seg - low, seg), 0) + low, ramp((seg - low, seg), 1)
    upto = jnp.where(col <= row, 1.0, 0.0).astype(BF16)
    same = jnp.where(col == row, 1.0, 0.0).astype(BF16)
    return mm_nt(upto, lens), mm_nt(same, lens)


def column(value, n):
    return jnp.sum(jnp.where(ramp(value.shape, 1) == n, value, 0.0), axis=1, keepdims=True)


WEIGHTS = ("w_query", "w_key", "w_value", "w_rel", "w_out", "w_up", "w_down")


def layer_scratch(seg, width, hidden):
    def low(*shape):
        return pltpu.VMEM(shape, BF16)

    def full(*shape):
        return pltpu.VMEM(shape, F32)

    return dict(
        table=low(2 * seg, width),
        w_query=low(width, width),
        w_key=low(width, width),
        w_value=low(width, width),
        w_rel=low(width, width),
        w_out=low(width, width),
        w_up=low(width, hidden),
        w_down=low(hidden, width),
        memory=low(seg, width),
        pooled=full(seg, width),
        normed=low(2 * seg, width),
        key=low(2 * seg, width),
        value=low(2 * seg, width),
        place=low(2 * seg, width),
        query_u=low(seg, width),
        query_v=low(seg, width),
        mixed=low(seg, width),
        probs=low(8, seg, 2 * seg),
        residual=full(seg, width),
        normed_two=low(seg, width),
        normed_two_t=low(width, seg),
        hidden=low(seg, hidden),
        slope=low(seg, hidden),
        grad_inner=low(seg, hidden),
        grad_output=full(seg, width),
        grad_down=low(seg, width),
        grad_down_t=low(width, seg),
        grad_residual=full(seg, width),
        grad_mixed=low(seg, width),
        low_rows=low(seg, width),
        out_rows=low(seg, width),
        grad_rows=low(seg, width),
        chars_quiet=low(QUIET, width),
        chars_parts=low(7, seg - QUIET, width),
        grads_quiet=low(QUIET, width),
        grads_parts=low(7, seg - QUIET, width),
        total=low(UNITS * PIECE, width),
        land_0=low(UNITS, 256, width),
        land_1=low(UNITS, 128, width),
        land_2=low(UNITS, 64, width),
        land_3=low(UNITS, 32, width),
        land_4=low(UNITS, 16, width),
        bias_up=full(1, hidden),
        vectors=full(16, width),
        small=full(16, width),
        small_sum=full(5, 16, width),
        small_land=full(5, 16, width),
        load_sem=pltpu.SemaphoreType.DMA((len(WEIGHTS) + 1,)),
        stage_sem=pltpu.SemaphoreType.DMA((2, 4)),
        memory_send=pltpu.SemaphoreType.DMA((4,)),
        memory_recv=pltpu.SemaphoreType.DMA((4,)),
        quiet_send=pltpu.SemaphoreType.DMA((2, 4, 2)),
        quiet_recv=pltpu.SemaphoreType.DMA((2, 2)),
        parts_send=pltpu.SemaphoreType.DMA((2, 3)),
        parts_recv=pltpu.SemaphoreType.DMA((2, 3)),
        kept_send=pltpu.SemaphoreType.DMA((4,)),
        kept_recv=pltpu.SemaphoreType.DMA((4,)),
        back_send=pltpu.SemaphoreType.DMA((2, 5)),
        back_recv=pltpu.SemaphoreType.DMA((2, 2, 4)),
        sum_send=pltpu.SemaphoreType.DMA((2, STEPS - 1)),
        sum_recv=pltpu.SemaphoreType.DMA((UNITS, STEPS - 1)),
        small_send=pltpu.SemaphoreType.DMA((5,)),
        small_recv=pltpu.SemaphoreType.DMA((5,)),
        store_sem=pltpu.SemaphoreType.DMA((2,)),
    )


class Rows:
    def __init__(self, r, place, way, source, stage, quiet, parts):
        self.r, self.p, self.way = r, place, way
        self.source, self.stage, self.quiet, self.parts = source, stage, quiet, parts

    def load(self, n):
        cols = pl.ds(pl.multiple_of(n * 512, 512), 512)
        return pltpu.make_async_copy(self.source.at[n], self.stage.at[:, cols], self.r.stage_sem.at[self.way, n])

    def quiet_copy(self, to, part):
        r = self.r
        span = pl.ds(0, HALF) if part == 0 else pl.ds(HALF, QUIET - HALF)
        src, dst = self.source.at[to, span], self.quiet.at[span]
        if to == 0:
            return pltpu.make_async_copy(src, dst, r.quiet_send.at[self.way, 0, part])
        return remote(src, dst, r.quiet_send.at[self.way, to, part], r.quiet_recv.at[self.way, part], (self.p.s, to))

    def start_quiet(self):
        @pl.when(self.p.b == 0)
        def _():
            for part in range(2):
                for to in (2, 3, 1, 0):
                    self.quiet_copy(to, part).start()

    def wait_quiet(self, part):
        @pl.when(self.p.b == 0)
        def _():
            self.quiet_copy(0, part).wait()

        @pl.when(self.p.b != 0)
        def _():
            self.quiet_copy(1, part).wait_recv()

    def parts_copy(self, n):
        src, dst, to = ((3, 1, self.p.core()), (4, 5, self.p.core()), (6, 2, self.p.across()))[n]
        return remote(
            self.parts.at[src],
            self.parts.at[dst],
            self.r.parts_send.at[self.way, n],
            self.r.parts_recv.at[self.way, n],
            to,
        )

    def part(self, to, ends, lens):
        self.load(to).wait()
        cols = pl.ds(pl.multiple_of(to * 512, 512), 512)
        chosen = pool_matrix(column(ends, to), column(lens, to), self.p.b * 512, 512)
        return mm(chosen, self.stage[:, cols])

    def start_parts(self, ends, lens):
        b, sibling, away = self.p.b, self.p.core()[1], self.p.across()[1]
        self.parts[4] = self.part(away + sibling - b, ends, lens).astype(BF16)
        self.parts_copy(1).start()
        self.parts[3] = self.part(sibling, ends, lens).astype(BF16)
        self.parts_copy(0).start()
        own = self.part(away, ends, lens)
        self.parts[0] = self.part(b, ends, lens).astype(BF16)
        self.parts_copy(1).wait_recv()
        self.parts[6] = (own + self.parts[5].astype(F32)).astype(BF16)
        self.parts_copy(2).start()

    def wait_parts(self):
        self.parts_copy(0).wait_recv()
        self.parts_copy(2).wait_recv()
        return sum(self.parts[n].astype(F32) for n in range(3))

    def wait_sent(self):
        for n in range(3):
            self.parts_copy(n).wait_send()

        @pl.when(self.p.b == 0)
        def _():
            for part in range(2):
                for to in (1, 2, 3):
                    self.quiet_copy(to, part).wait_send()

    def back(self, rows, quiet_out, loud_out):
        self.rows, self.quiet_out, self.loud_out = rows, quiet_out, loud_out
        return self

    def loud_rows(self):
        return self.rows.at[pl.ds(QUIET, self.rows.shape[0] - QUIET)]

    def quiet_rows(self):
        return self.rows.at[pl.ds(0, QUIET)]

    def loud_copy(self, n, slot):
        r, p, way = self.r, self.p, self.way
        src = self.loud_out.at[slot] if n == 2 else self.loud_rows()
        to = p.across() if n == 1 else p.core()
        return remote(src, self.loud_out.at[slot], r.back_send.at[way, n], r.back_recv.at[way, 0, slot], to)

    def quiet_back(self, slot):
        r, way = self.r, self.way
        return remote(
            self.quiet_rows(),
            self.quiet_out.at[slot],
            r.back_send.at[way, 3],
            r.back_recv.at[way, 1, slot],
            (self.p.s, 0),
        )

    def own_copies(self):
        r, p, way = self.r, self.p, self.way
        loud = pltpu.make_async_copy(self.loud_rows(), self.loud_out.at[p.b], r.back_send.at[way, 4])
        quiet = pltpu.make_async_copy(self.quiet_rows(), self.quiet_out.at[0], r.back_send.at[way, 3])
        return loud, quiet

    def start_back(self):
        p = self.p
        loud, quiet = self.own_copies()
        self.loud_copy(1, p.b).start()
        self.loud_copy(0, p.b).start()
        pl.when(p.b != 0)(self.quiet_back(p.b).start)
        pl.when(p.b == 0)(quiet.start)
        loud.start()

    def pass_on(self):
        away = self.p.across()[1]
        self.loud_copy(1, away).wait_recv()
        self.loud_copy(2, away).start()

    def wait_back(self):
        p = self.p
        sibling, away = p.core()[1], p.across()[1]
        loud, quiet = self.own_copies()
        for n in (0, 1):
            self.loud_copy(n, p.b).wait_send()
        self.loud_copy(2, away).wait_send()
        loud.wait()
        pl.when(p.b != 0)(self.quiet_back(p.b).wait_send)
        pl.when(p.b == 0)(quiet.wait)
        self.loud_copy(0, sibling).wait_recv()
        self.loud_copy(2, away + sibling - p.b).wait_recv()

        @pl.when(p.b == 0)
        def _():
            for n in (1, 2, 3):
                self.quiet_back(n).wait_recv()


class Small:
    def __init__(self, r, place):
        self.r, self.p = r, place

    def source(self, step):
        return self.r.small if step == 0 else self.r.small_sum.at[step - 1]

    def copy(self, step):
        r, p = self.r, self.p
        to = p.core() if step == 0 else p.pair(AXES[step - 1])
        return remote(self.source(step), r.small_land.at[step], r.small_send.at[step], r.small_recv.at[step], to)

    def start(self, step):
        self.copy(step).start()

    def finish(self, step):
        self.copy(step).wait()
        self.r.small_sum[step] = self.source(step)[...] + self.r.small_land[step]


def layer_kernel(names, chars, lengths, memory, grad_out, *rest):
    count = len(VECTORS) + 1 + len(WEIGHTS)
    vectors, table, weights = rest[: len(VECTORS)], rest[len(VECTORS)], rest[len(VECTORS) + 1 : count]
    kept, out_quiet, out_loud, grad_quiet, grad_loud, total_out, small_out = rest[count : count + 7]
    r = types.SimpleNamespace(**dict(zip(names, rest[count + 7 :])))
    p = Place()
    seg, width = r.pooled.shape
    for n, name in enumerate(("mixed_flip", "query_u_t", "query_v_t", "grad_mixed_t")):
        setattr(r, name, r.slope.at[:, n * width : (n + 1) * width])
    r.grad_key_t, r.grad_value_t = r.hidden.at[:, : 2 * seg], r.hidden.at[:, 2 * seg :]
    r.grad_place_t, r.grad_query = r.grad_inner.at[:, : 2 * seg], r.grad_inner.at[:, 2 * seg : 3 * seg]
    loads = [
        pltpu.make_async_copy(src, dst, r.load_sem.at[n])
        for n, (src, dst) in enumerate(
            zip((*weights, table), [getattr(r, name) for name in WEIGHTS] + [r.table])
        )
    ]
    chars_rows = Rows(r, p, 0, chars, r.hidden, r.chars_quiet, r.chars_parts).back(r.out_rows, out_quiet, out_loud)
    grads_rows = Rows(r, p, 1, grad_out, r.grad_inner, r.grads_quiet, r.grads_parts).back(
        r.grad_rows, grad_quiet, grad_loud
    )
    for n in range(4):
        chars_rows.load(n).start()
    for n in range(4):
        grads_rows.load(n).start()
    for copy in loads:
        copy.start()
    for n, name in enumerate(VECTORS):
        value = vectors[n][...].astype(F32)
        if name == "bias_up":
            r.bias_up[...] = value.reshape(1, -1)
        elif value.ndim == 2:
            r.vectors[n : n + 1, :] = jnp.concatenate([value[h : h + 1, :] for h in range(value.shape[0])], axis=1)
        else:
            r.vectors[n : n + 1, :] = value.reshape(1, -1)
    r.vec = lambda name: r.vectors[VECTORS.index(name) : VECTORS.index(name) + 1, :]

    barrier = pltpu.get_barrier_semaphore()
    others = [p.group(1), p.group(2), p.group(3), p.pair("y"), p.pair("near"), p.pair("far")]
    for other in others:
        pl.semaphore_signal(barrier, inc=1, device_id=other, device_id_type=MESH)
    pl.semaphore_wait(barrier, len(others))

    rows = memory.shape[1]

    def memory_copy(k, slot):
        to = (p.b + k) % 4
        return remote(
            memory.at[to], r.memory.at[rows_at(slot * rows, rows)], r.memory_send.at[k], r.memory_recv.at[slot], p.group(k)
        )

    own_memory = pltpu.make_async_copy(memory.at[p.b], r.memory.at[rows_at(p.b * rows, rows)], r.memory_send.at[0])
    for k in (2, 3, 1):
        memory_copy(k, p.b).start()
    own_memory.start()
    chars_rows.start_quiet()
    ends, lens = span_columns(lengths[...], QUIET)
    chars_rows.start_parts(ends, lens)
    grads_rows.start_quiet()
    for copy in loads:
        copy.wait()
    own_memory.wait()
    for k in (1, 2, 3):
        memory_copy(k, (p.b + k) % 4).wait_recv()
    project_memory(seg, r)
    grads_rows.start_parts(ends, lens)
    own_lens = column(lens, p.b)

    def forward(block):
        def pair(n, carry):
            attend_pair(n, block, seg, r)
            return carry

        project_segments(block, seg, r)
        lax.fori_loop(0, 4, pair, 0)
        feed_forward_in(block, r)

    chars_rows.wait_quiet(0)
    r.pooled[0:HALF] = chars_rows.quiet[0:HALF].astype(F32)
    forward(0)
    chars_rows.wait_quiet(1)
    r.pooled[HALF:QUIET] = chars_rows.quiet[HALF:QUIET].astype(F32)
    r.pooled[QUIET:seg] = chars_rows.wait_parts() / own_lens
    r.low_rows[...] = r.pooled[...].astype(BF16)

    def kept_copy(k, slot):
        to = (p.b + k) % 4
        return remote(
            r.low_rows.at[rows_at(to * rows, rows)], kept.at[slot], r.kept_send.at[k], r.kept_recv.at[slot], p.group(k)
        )

    own_kept = pltpu.make_async_copy(r.low_rows.at[rows_at(p.b * rows, rows)], kept.at[p.b], r.kept_send.at[0])
    for k in (2, 3, 1):
        kept_copy(k, p.b).start()
    own_kept.start()
    forward(1)
    grads_rows.wait_quiet(0)
    grads_rows.wait_quiet(1)
    r.grad_output[0:QUIET] = grads_rows.quiet[...].astype(F32)
    r.grad_output[QUIET:seg] = grads_rows.wait_parts()
    low = r.grad_output[...].astype(BF16)
    r.grad_down[...] = low
    r.grad_down_t[...] = low.astype(F32).T.astype(BF16)
    r.normed_two_t[...] = r.normed_two[...].astype(F32).T.astype(BF16)
    r.small[...] = jnp.zeros(r.small.shape, F32)
    r.small[6:7, :] = jnp.sum(low.astype(F32), axis=0, keepdims=True)

    land = [getattr(r, f"land_{n}") for n in range(5)]
    sums = Sum(p, r.total, land, total_out, r.sum_send, r.sum_recv, r.store_sem)

    def feed_back(n, carry):
        feed_forward_back(n, r)
        sums.tick(2 * n)
        sums.tick(2 * n + 1)
        return carry

    lax.fori_loop(0, 4, feed_back, 0)
    r.out_rows[...] = (r.residual[...] + (mm(r.hidden[...], r.w_down[...]) + r.vec("bias_down"))).astype(BF16)
    chars_rows.start_back()
    middle_back(r, 8 * PIECE)
    sums.tick(8)

    def back(n, carry):
        attend_back_pair(n, seg, r)
        pair_weights(n, seg, r, (9 + n) * PIECE)
        sums.tick(9 + n)
        return carry

    lax.fori_loop(0, 4, back, 0)
    grad_pooled = first_back(seg, r)
    r.grad_rows[0:QUIET] = grad_pooled[:QUIET].astype(BF16)
    r.grad_rows[QUIET:seg] = (grad_pooled[QUIET:] / own_lens).astype(BF16)
    grads_rows.start_back()
    small = Small(r, p)
    small.start(0)
    chars_rows.pass_on()

    def tail(n, carry):
        sums.tick(UNITS + n)
        for step in range(5):

            @pl.when(n == 2 * step + 1)
            def _():
                small.finish(step)
                if step < 4:
                    small.start(step + 1)

        pl.when(n == 12)(grads_rows.pass_on)
        return carry

    lax.fori_loop(0, 2 * (STEPS - 1), tail, 0)
    small_out[...] = r.small_sum[4]
    for k in (1, 2, 3):
        memory_copy(k, p.b).wait_send()
        kept_copy(k, p.b).wait_send()
        kept_copy(k, (p.b + k) % 4).wait_recv()
    own_kept.wait()
    chars_rows.wait_sent()
    grads_rows.wait_sent()
    chars_rows.wait_back()
    grads_rows.wait_back()


def spread_kernel(
    lengths, chars, grad_out, out_quiet, out_loud, grad_quiet, grad_loud, wide, flat, pairs, small,
    out_chars, grad_chars, w_query, w_key, w_value, w_rel, w_out, w_up, w_down, bias_u, bias_v, *vectors,
):
    n = pl.program_id(0)
    b = lax.axis_index("blk")
    places = chars.shape[1]
    seg = lengths.shape[1]
    lens = lengths[...].astype(F32).astype(BF16)
    row, col = ramp((seg - QUIET, seg), 0) + QUIET, ramp((seg - QUIET, seg), 1)
    upto = jnp.where(col <= row, 1.0, 0.0).astype(BF16)
    same = jnp.where(col == row, 1.0, 0.0).astype(BF16)
    pick = ramp((lengths.shape[0], seg - QUIET), 0) == n
    end = jnp.sum(jnp.where(pick, mm_nt(lens, upto), 0.0), axis=0, keepdims=True)
    length = jnp.sum(jnp.where(pick, mm_nt(lens, same), 0.0), axis=0, keepdims=True)
    place = (ramp((places, seg - QUIET), 0) + b * places).astype(F32)
    chosen = jnp.where((place < end) & (place >= end - length), 1.0, 0.0).astype(BF16)
    first = b == 0
    for source, quiet, loud, out in (
        (chars, out_quiet, out_loud, out_chars),
        (grad_out, grad_quiet, grad_loud, grad_chars),
    ):
        spread = mm(chosen, loud[0])
        whole = source[0].astype(F32) + spread
        out[0, QUIET:places] = whole[QUIET:].astype(out.dtype)
        out[0, 0:QUIET] = (whole[:QUIET] + jnp.where(first, quiet[0].astype(F32), 0.0)).astype(out.dtype)
    w_down[...] = wide[0:512].astype(F32).T
    w_up[...] = wide[512:1024].astype(F32)
    w_out[...] = flat[...].astype(F32)
    for m, out in enumerate((w_query, w_key, w_value, w_rel)):
        out[...] = pairs[m * 128 : (m + 1) * 128].astype(F32).T
    for m, out in enumerate((bias_u, bias_v)):
        out[...] = jnp.concatenate([small[m : m + 1, h * 64 : (h + 1) * 64] for h in range(8)], axis=0)
    for m, out in enumerate(vectors[:4]):
        out[...] = small[2 + m : 3 + m, :]
    vectors[4][...] = jnp.concatenate([small[m : m + 1, :] for m in range(7, 11)], axis=1)
    vectors[5][...] = small[6:7, :]


def shards_whole(
    chars, seg_lengths, memory, grad_out, w_query, w_key, w_value, w_rel, w_out, w_up, w_down,
    bias_u, bias_v, gain_one, shift_one, gain_two, shift_two, bias_up, bias_down,
):
    count, places, width = chars.shape
    seg, hidden = seg_lengths.shape[1], w_up.shape[1]
    rows = memory.shape[1]
    table = jnp.asarray(sine_table(2 * seg, width))
    scratch = layer_scratch(seg, width, hidden)
    anywhere, near = pl.BlockSpec(memory_space=pl.ANY), pl.BlockSpec(memory_space=pltpu.VMEM)
    loud = seg - QUIET
    kept, out_quiet, out_loud, grad_quiet, grad_loud, total, small = pl.pallas_call(
        functools.partial(layer_kernel, tuple(scratch)),
        out_shape=[
            jax.ShapeDtypeStruct((count, rows, width), BF16),
            jax.ShapeDtypeStruct((count, QUIET, width), BF16),
            jax.ShapeDtypeStruct((count, loud, width), BF16),
            jax.ShapeDtypeStruct((count, QUIET, width), BF16),
            jax.ShapeDtypeStruct((count, loud, width), BF16),
            jax.ShapeDtypeStruct((UNITS * PIECE, width), BF16),
            jax.ShapeDtypeStruct((16, width), F32),
        ],
        in_specs=[anywhere, near, anywhere, anywhere] + [near] * len(VECTORS) + [anywhere] * 8,
        out_specs=[anywhere] * 6 + [near],
        scratch_shapes=list(scratch.values()),
        compiler_params=pltpu.CompilerParams(
            collective_id=0, has_side_effects=True, vmem_limit_bytes=VMEM_BYTES
        ),
        name="layer",
    )(
        chars, seg_lengths, memory, grad_out,
        bias_u, bias_v, gain_one, shift_one, gain_two, shift_two, bias_up, bias_down, table,
        w_query, w_key, w_value, w_rel, w_out, w_up, w_down,
    )

    def block(shape, index):
        return pl.BlockSpec(shape, index)

    def each(*shape):
        return block((1, *shape), lambda n: (n, 0, 0))

    def whole(*shape):
        return block(shape, lambda n: (0, 0))

    vector = [(1, width)] * 4 + [(1, hidden), (1, width)]
    outs = pl.pallas_call(
        spread_kernel,
        grid=(count,),
        out_shape=[
            jax.ShapeDtypeStruct(chars.shape, BF16),
            jax.ShapeDtypeStruct(chars.shape, F32),
            *[jax.ShapeDtypeStruct((width, width), F32)] * 5,
            jax.ShapeDtypeStruct((width, hidden), F32),
            jax.ShapeDtypeStruct((hidden, width), F32),
            *[jax.ShapeDtypeStruct(bias_u.shape, F32)] * 2,
            *[jax.ShapeDtypeStruct(shape, F32) for shape in vector],
        ],
        in_specs=[
            whole(*seg_lengths.shape),
            each(places, width),
            each(places, width),
            each(QUIET, width),
            each(loud, width),
            each(QUIET, width),
            each(loud, width),
            block((2 * PIECE, width), lambda n: (n, 0)),
            block((128, width), lambda n: (8 * (PIECE // 128) + n, 0)),
            block((PIECE, width), lambda n: (9 + n, 0)),
            whole(16, width),
        ],
        out_specs=[
            each(places, width),
            each(places, width),
            *[block((width, 128), lambda n: (0, n))] * 4,
            block((128, width), lambda n: (n, 0)),
            block((width, 512), lambda n: (0, n)),
            block((512, width), lambda n: (n, 0)),
            *[whole(*bias_u.shape)] * 2,
            *[whole(*shape) for shape in vector],
        ],
        compiler_params=pltpu.CompilerParams(vmem_limit_bytes=VMEM_BYTES),
        name="spread",
    )(seg_lengths, chars, grad_out, out_quiet, out_loud, grad_quiet, grad_loud, total, total, total, small)
    out_chars, grad_chars = outs[:2]
    vectors = [v.reshape(-1) for v in outs[11:]]
    return (out_chars, grad_chars, kept, *outs[2:7], outs[7], outs[8], outs[9], outs[10], *vectors)


VMEM_BYTES = 64 * 2**20 - 2**16


def fits_whole(mesh):
    return dict(mesh.shape) == {"seq": 8, "blk": 4}


def layer_norm(value, gain, shift):
    center = value - jnp.mean(value, axis=-1, keepdims=True)
    spread = jnp.mean(center * center, axis=-1, keepdims=True)
    return center * lax.rsqrt(spread + 1e-05) * gain + shift


def angle_tables(places, feature_width):
    freqs = jnp.exp(
        jnp.arange(feature_width // 2, dtype=jnp.float32)
        * (-2.0 * math.log(10000.0) / feature_width)
    )
    angles = places[:, None] * freqs[None, :]
    return (jnp.sin(angles), jnp.cos(angles))


def smooth_gate(value):
    return jax.nn.gelu(value, approximate=False)


def segment_ids(seg_end, char_places):
    return jnp.sum((seg_end[:, None, :] <= char_places[None, :, None]).astype(jnp.int32), axis=2)


def shards(
    chars,
    seg_lengths,
    memory,
    grad_out,
    w_query,
    w_key,
    w_value,
    w_rel,
    w_out,
    w_up,
    w_down,
    bias_u,
    bias_v,
    gain_one,
    shift_one,
    gain_two,
    shift_two,
    bias_up,
    bias_down,
):
    blk_index = lax.axis_index("blk")
    seq_local, char_rows, feature_width = chars.shape
    seg_rows = memory.shape[1]
    seg_count = seg_lengths.shape[1]
    head_count, head_dim = bias_u.shape
    half_width = feature_width // 2
    score_scale = head_dim ** (-0.5)
    seg_start = blk_index * seg_rows
    gain_one_f = gain_one.astype(jnp.float32)
    shift_one_f = shift_one.astype(jnp.float32)
    gain_two_f = gain_two.astype(jnp.float32)
    shift_two_f = shift_two.astype(jnp.float32)
    seg_end = jnp.cumsum(seg_lengths, axis=1)
    char_places = blk_index * char_rows + jnp.arange(char_rows, dtype=jnp.int32)
    segment = segment_ids(seg_end, char_places)
    own_lengths = lax.dynamic_slice_in_dim(seg_lengths, seg_start, seg_rows, 1).astype(jnp.float32)
    chars_f = chars.astype(jnp.float32)
    grad_f = grad_out.astype(jnp.float32)

    def full_table(values, ids):
        return jax.ops.segment_sum(values, ids, num_segments=seg_count)

    part_sums = jax.vmap(full_table)(chars_f, segment)
    pooled_sum = lax.psum_scatter(part_sums, "blk", scatter_dimension=1, tiled=True)
    pooled = pooled_sum / own_lengths[:, :, None]
    normed = layer_norm(pooled, gain_one_f, shift_one_f)
    normed_low = normed.astype(jnp.bfloat16)
    memory_f = memory.astype(jnp.float32)
    mem_low = layer_norm(memory_f, gain_one_f, shift_one_f).astype(jnp.bfloat16)
    query_rows = jnp.einsum("sid,de->sie", normed_low, w_query, preferred_element_type=jnp.float32)
    key_local = jnp.stack(
        [
            jnp.einsum("sid,de->sie", mem_low, w_key, preferred_element_type=jnp.float32),
            jnp.einsum("sid,de->sie", normed_low, w_key, preferred_element_type=jnp.float32),
        ],
        axis=1,
    ).astype(jnp.bfloat16)
    value_local = jnp.stack(
        [
            jnp.einsum("sid,de->sie", mem_low, w_value, preferred_element_type=jnp.float32),
            jnp.einsum("sid,de->sie", normed_low, w_value, preferred_element_type=jnp.float32),
        ],
        axis=1,
    ).astype(jnp.bfloat16)
    key_all, value_all = (
        lax.all_gather(key_local, "blk", axis=2, tiled=True),
        lax.all_gather(value_local, "blk", axis=2, tiled=True),
    )
    key_heads = key_all.reshape(seq_local, 2 * seg_count, head_count, head_dim)
    value_heads = value_all.reshape(seq_local, 2 * seg_count, head_count, head_dim)
    query_u = (
        (query_rows + bias_u.astype(jnp.float32).reshape(-1))
        .astype(jnp.bfloat16)
        .reshape(seq_local, seg_rows, head_count, head_dim)
    )
    query_v = (
        (query_rows + bias_v.astype(jnp.float32).reshape(-1))
        .astype(jnp.bfloat16)
        .reshape(seq_local, seg_rows, head_count, head_dim)
    )
    w_rel_heads = w_rel.reshape(feature_width, head_count, head_dim)
    rel_coeff = jnp.einsum(
        "sihe,fhe->sihf", query_v, w_rel_heads, preferred_element_type=jnp.float32
    )
    sin_all, cos_all = angle_tables(jnp.arange(2 * seg_count).astype(jnp.float32), feature_width)
    key_pos = jnp.concatenate([cos_all, sin_all], axis=-1).astype(jnp.bfloat16)
    query_index = seg_count + seg_start + jnp.arange(seg_rows, dtype=jnp.int32)
    sin_q, cos_q = angle_tables(query_index.astype(jnp.float32), feature_width)
    sin_query = sin_q[None, :, None, :]
    cos_query = cos_q[None, :, None, :]
    coeff_sin = rel_coeff[..., :half_width]
    coeff_cos = rel_coeff[..., half_width:]
    query_pos = jnp.concatenate(
        [
            coeff_sin * sin_query + coeff_cos * cos_query,
            coeff_cos * sin_query - coeff_sin * cos_query,
        ],
        axis=-1,
    ).astype(jnp.bfloat16)
    allowed = jnp.arange(2 * seg_count, dtype=jnp.int32)[None, :] <= query_index[:, None]

    def score_block():
        raw_scores = (
            jnp.einsum("sihe,sjhe->shij", query_u, key_heads, preferred_element_type=jnp.float32)
            + jnp.einsum("sihf,jf->shij", query_pos, key_pos, preferred_element_type=jnp.float32)
        ) * score_scale
        return jnp.where(allowed[None, None], raw_scores, -1e30)

    scores = score_block()
    row_top = jnp.max(scores, axis=-1, keepdims=True)
    expo = jnp.exp(scores - row_top)
    row_total = jnp.sum(expo, axis=-1, keepdims=True)
    log_total = row_top + jnp.log(row_total)
    att_probs = (expo / row_total).astype(jnp.bfloat16)
    att_mixed = jnp.einsum(
        "shij,sjhe->sihe", att_probs, value_heads, preferred_element_type=jnp.float32
    )
    mixed_low = att_mixed.reshape(seq_local, seg_rows, feature_width).astype(jnp.bfloat16)
    residual = pooled + jnp.einsum(
        "sid,de->sie", mixed_low, w_out, preferred_element_type=jnp.float32
    )
    normed_two = layer_norm(residual, gain_two_f, shift_two_f)
    two_low = normed_two.astype(jnp.bfloat16)
    ffn_inner = jnp.einsum(
        "sid,df->sif", two_low, w_up, preferred_element_type=jnp.float32
    ) + bias_up.astype(jnp.float32)
    hidden_low = smooth_gate(ffn_inner).astype(jnp.bfloat16)
    branch_out = jnp.einsum(
        "sif,fd->sid", hidden_low, w_down, preferred_element_type=jnp.float32
    ) + bias_down.astype(jnp.float32)
    out_low = (residual + branch_out).astype(jnp.bfloat16)
    rows_all = lax.all_gather(out_low, "blk", axis=1, tiled=True)
    picked = jnp.take_along_axis(rows_all, segment[:, :, None], axis=1)
    out_chars = (chars_f + picked.astype(jnp.float32)).astype(jnp.bfloat16)
    new_memory = pooled.astype(jnp.bfloat16)
    grad_table = jax.vmap(full_table)(grad_f, segment)
    grad_output = lax.psum_scatter(grad_table, "blk", scatter_dimension=1, tiled=True)
    grad_down_low = grad_output.astype(jnp.bfloat16)
    grad_bias_down = jnp.sum(grad_down_low.astype(jnp.float32), axis=(0, 1))
    grad_w_down = jnp.einsum(
        "sif,sid->fd", hidden_low, grad_down_low, preferred_element_type=jnp.float32
    )
    grad_hidden = jnp.einsum(
        "sid,fd->sif", grad_down_low, w_down, preferred_element_type=jnp.float32
    )
    unused_value, gate_back = jax.vjp(smooth_gate, ffn_inner)
    grad_inner = gate_back(grad_hidden)[0].astype(jnp.bfloat16)
    grad_bias_up = jnp.sum(grad_inner.astype(jnp.float32), axis=(0, 1))
    grad_w_up = jnp.einsum("sid,sif->df", two_low, grad_inner, preferred_element_type=jnp.float32)
    grad_normed_two = jnp.einsum(
        "sif,df->sid", grad_inner, w_up, preferred_element_type=jnp.float32
    )
    unused_norm, norm_two_back = jax.vjp(layer_norm, residual, gain_two_f, shift_two_f)
    grad_resid_norm, grad_gain_two, grad_shift_two = norm_two_back(grad_normed_two)
    grad_residual = grad_output + grad_resid_norm
    grad_att_low = grad_residual.astype(jnp.bfloat16)
    grad_w_out = jnp.einsum(
        "sid,sie->de", mixed_low, grad_att_low, preferred_element_type=jnp.float32
    )
    grad_mixed = jnp.einsum("sie,de->sid", grad_att_low, w_out, preferred_element_type=jnp.float32)
    grad_mixed = grad_mixed.astype(jnp.bfloat16).reshape(seq_local, seg_rows, head_count, head_dim)
    scores_again = score_block()
    probs_full = jnp.exp(scores_again - log_total)
    probs_low = probs_full.astype(jnp.bfloat16)
    grad_probs = jnp.einsum(
        "sihe,sjhe->shij", grad_mixed, value_heads, preferred_element_type=jnp.float32
    )
    grad_values = jnp.einsum(
        "shij,sihe->sjhe", probs_low, grad_mixed, preferred_element_type=jnp.float32
    )
    prob_delta = jnp.sum(probs_full * grad_probs, axis=-1, keepdims=True)
    grad_scores = (probs_full * (grad_probs - prob_delta)).astype(jnp.bfloat16)
    grad_query_u = (
        jnp.einsum("shij,sjhe->sihe", grad_scores, key_heads, preferred_element_type=jnp.float32)
        * score_scale
    )
    grad_keys = (
        jnp.einsum("shij,sihe->sjhe", grad_scores, query_u, preferred_element_type=jnp.float32)
        * score_scale
    )
    grad_query_pos = (
        jnp.einsum("shij,jf->sihf", grad_scores, key_pos, preferred_element_type=jnp.float32)
        * score_scale
    )
    grad_first = grad_query_pos[..., :half_width]
    grad_second = grad_query_pos[..., half_width:]
    grad_coeff = jnp.concatenate(
        [
            grad_first * sin_query - grad_second * cos_query,
            grad_first * cos_query + grad_second * sin_query,
        ],
        axis=-1,
    ).astype(jnp.bfloat16)
    grad_w_rel = jnp.einsum(
        "sihf,sihe->fhe", grad_coeff, query_v, preferred_element_type=jnp.float32
    ).reshape(feature_width, feature_width)
    grad_query_v = jnp.einsum(
        "sihf,fhe->sihe", grad_coeff, w_rel_heads, preferred_element_type=jnp.float32
    )
    grad_bias_u = jnp.sum(grad_query_u, axis=(0, 1))
    grad_bias_v = jnp.sum(grad_query_v, axis=(0, 1))
    grad_query = (
        (grad_query_u + grad_query_v)
        .reshape(seq_local, seg_rows, feature_width)
        .astype(jnp.bfloat16)
    )
    grad_w_query = jnp.einsum(
        "sid,sie->de", normed_low, grad_query, preferred_element_type=jnp.float32
    )
    grad_normed = jnp.einsum("sie,de->sid", grad_query, w_query, preferred_element_type=jnp.float32)
    key_share, value_share = (
        lax.psum_scatter(
            grad_keys.reshape(seq_local, 2, seg_count, feature_width),
            "blk",
            scatter_dimension=2,
            tiled=True,
        ),
        lax.psum_scatter(
            grad_values.reshape(seq_local, 2, seg_count, feature_width),
            "blk",
            scatter_dimension=2,
            tiled=True,
        ),
    )
    key_low = key_share.astype(jnp.bfloat16)
    value_low = value_share.astype(jnp.bfloat16)
    grad_w_key = jnp.einsum(
        "sid,sie->de", mem_low, key_low[:, 0], preferred_element_type=jnp.float32
    ) + jnp.einsum("sid,sie->de", normed_low, key_low[:, 1], preferred_element_type=jnp.float32)
    grad_w_value = jnp.einsum(
        "sid,sie->de", mem_low, value_low[:, 0], preferred_element_type=jnp.float32
    ) + jnp.einsum("sid,sie->de", normed_low, value_low[:, 1], preferred_element_type=jnp.float32)
    grad_normed = grad_normed + jnp.einsum(
        "sie,de->sid", key_low[:, 1], w_key, preferred_element_type=jnp.float32
    )
    grad_normed = grad_normed + jnp.einsum(
        "sie,de->sid", value_low[:, 1], w_value, preferred_element_type=jnp.float32
    )
    grad_mem_normed = jnp.einsum(
        "sie,de->sid", key_low[:, 0], w_key, preferred_element_type=jnp.float32
    ) + jnp.einsum("sie,de->sid", value_low[:, 0], w_value, preferred_element_type=jnp.float32)
    unused_one, norm_one_back = jax.vjp(layer_norm, pooled, gain_one_f, shift_one_f)
    grad_pooled_norm, grad_gain_one, grad_shift_one = norm_one_back(grad_normed)
    unused_mem, norm_mem_back = jax.vjp(layer_norm, memory_f, gain_one_f, shift_one_f)
    unused_grad, grad_gain_mem, grad_shift_mem = norm_mem_back(grad_mem_normed)
    grad_gain_one = grad_gain_one + grad_gain_mem
    grad_shift_one = grad_shift_one + grad_shift_mem
    grad_pooled = grad_residual + grad_pooled_norm
    grad_sum = grad_pooled / own_lengths[:, :, None]
    grad_sum_all = lax.all_gather(grad_sum, "blk", axis=1, tiled=True)
    grad_chars = grad_f + jnp.take_along_axis(grad_sum_all, segment[:, :, None], axis=1)
    (
        grad_w_query,
        grad_w_key,
        grad_w_value,
        grad_w_rel,
        grad_w_out,
        grad_w_up,
        grad_w_down,
        grad_bias_u,
        grad_bias_v,
        grad_gain_one,
        grad_shift_one,
        grad_gain_two,
        grad_shift_two,
        grad_bias_up,
        grad_bias_down,
    ) = lax.psum(
        (
            grad_w_query,
            grad_w_key,
            grad_w_value,
            grad_w_rel,
            grad_w_out,
            grad_w_up,
            grad_w_down,
            grad_bias_u,
            grad_bias_v,
            grad_gain_one,
            grad_shift_one,
            grad_gain_two,
            grad_shift_two,
            grad_bias_up,
            grad_bias_down,
        ),
        ("seq", "blk"),
    )
    return (
        out_chars,
        grad_chars,
        new_memory,
        grad_w_query,
        grad_w_key,
        grad_w_value,
        grad_w_rel,
        grad_w_out,
        grad_w_up,
        grad_w_down,
        grad_bias_u,
        grad_bias_v,
        grad_gain_one,
        grad_shift_one,
        grad_gain_two,
        grad_shift_two,
        grad_bias_up,
        grad_bias_down,
    )


def solution(mesh):
    placed = (
        P("seq", "blk", None),
        P("seq", None),
        P("seq", "blk", None),
        P("seq", "blk", None),
        P(),
        P(),
        P(),
        P(),
        P(),
        P(),
        P(),
        P(),
        P(),
        P(),
        P(),
        P(),
        P(),
        P(),
        P(),
    )
    return jax.shard_map(
        shards_whole if fits_whole(mesh) else shards,
        mesh=mesh,
        in_specs=placed,
        out_specs=(
            P("seq", "blk", None),
            P("seq", "blk", None),
            P("seq", "blk", None),
            P(),
            P(),
            P(),
            P(),
            P(),
            P(),
            P(),
            P(),
            P(),
            P(),
            P(),
            P(),
            P(),
            P(),
            P(),
        ),
        check_vma=False,
    )
```

```python
import functools
import math
import types

import jax
import jax.numpy as jnp
import numpy as np
from jax import lax
from jax.experimental import pallas as pl
from jax.experimental.pallas import tpu as pltpu
from jax.sharding import PartitionSpec as P

F32, BF16 = jnp.float32, jnp.bfloat16
NT = (((1,), (1,)), ((), ()))


def mm(a, b):
    return jnp.dot(a, b, preferred_element_type=F32)


def mm_nt(a, b):
    return lax.dot_general(a, b, NT, preferred_element_type=F32)


def normalize(value):
    center = value - jnp.mean(value, axis=-1, keepdims=True)
    inv = lax.rsqrt(jnp.mean(center * center, axis=-1, keepdims=True) + 1e-05)
    return center * inv, inv


def norm_back(grad, unit, inv, gain):
    scaled = grad * gain
    along = jnp.mean(scaled * unit, axis=-1, keepdims=True)
    return inv * (scaled - jnp.mean(scaled, axis=-1, keepdims=True) - unit * along)


def gelu_parts(value):
    gate = 0.5 + 0.5 * lax.erf(value * 0.7071067811865476)
    return gate, gate + value * jnp.exp(-0.5 * value * value) * 0.3989422804014327


def ramp(shape, dim):
    return lax.broadcasted_iota(jnp.int32, shape, dim)


MESH = pl.DeviceIdType.MESH
HALF = 256
PIECE = 512
UNITS = 13
STEPS = 11
VECTORS = ("bias_u", "bias_v", "gain_one", "shift_one", "gain_two", "shift_two", "bias_up", "bias_down")


class Place:
    def __init__(self):
        self.s = lax.axis_index("seq")
        self.b = lax.axis_index("blk")
        self.z, self.y = self.s // 2, self.s % 2
        self.x, self.c = self.b // 2, self.b % 2
        self.bit = dict(x=self.x, y=self.y, near=self.z % 2, far=self.z // 2)

    def group(self, k):
        return (self.s, (self.b + k) % 4)

    def core(self):
        return (self.s, self.b + 1 - 2 * self.c)

    def across(self):
        return (self.s, self.b + 2 - 4 * self.x)

    def move(self, axis):
        reach = dict(x=(0, 2), y=(1, 0), near=(2, 0), far=(4, 0))[axis]
        turn = 1 - 2 * self.bit[axis]
        return reach[0] * turn, reach[1] * turn

    def step(self, n):
        zero, one = ORDERS[0][n], ORDERS[1][n]
        away = [self.move(zero)[m] * (1 - self.c) + self.move(one)[m] * self.c for m in (0, 1)]
        bit = self.bit[zero] * (1 - self.c) + self.bit[one] * self.c
        return (self.s + away[0], self.b + away[1]), bit

    def pair(self, axis):
        away = self.move(axis)
        return (self.s + away[0], self.b + away[1])


ORDERS = (("y", "x", "near", "far"), ("near", "y", "x", "far"))
AXES = ("x", "y", "near", "far")


def rows_at(start, size):
    return pl.ds(pl.multiple_of(start, 16), size)


def remote(src, dst, send, recv, to):
    return pltpu.make_async_remote_copy(src, dst, send, recv, device_id=to, device_id_type=MESH)


class Sum:
    def __init__(self, place, total, land, out, send, recv, store):
        self.p, self.g, self.land, self.out = place, total, land, out
        self.send, self.recv, self.store = send, recv, store

    def offset(self, k, n):
        start = k * PIECE + self.p.c * 256
        for m in range(n):
            start = start + self.p.step(m)[1] * (128 >> m)
        return start

    def copies(self, step, k, landing=False):
        p, g, land = self.p, self.g, self.land

        def copy(src, dst, to):
            return remote(src, dst, self.send.at[k % 2, step], self.recv.at[k, step], to)

        if step == 0:
            return copy(g.at[rows_at(k * PIECE + (1 - p.c) * 256, 256)], land[0].at[k], p.core())
        if step <= 4:
            to, bit = p.step(step - 1)
            size = 256 >> step
            away = self.offset(k, step - 1) + (1 - bit) * size
            return copy(g.at[rows_at(away, size)], land[step].at[k], to)
        if step <= 8:
            n = 8 - step
            to, bit = p.step(n)
            size = 128 >> n
            side = rows_at((1 - bit if landing else bit) * size, size)
            src = land[3].at[k, rows_at(bit * 16, 16)] if n == 3 else land[n + 1].at[k]
            return copy(src, land[n].at[k, side], to)
        span = k * PIECE + (1 - p.c if landing else p.c) * 256
        return copy(land[0].at[k], self.out.at[rows_at(span, 256)], p.core())

    def own(self, k):
        span = rows_at(k * PIECE + self.p.c * 256, 256)
        return pltpu.make_async_copy(self.land[0].at[k], self.out.at[span], self.store.at[k % 2])

    def step(self, step, k):
        g, land = self.g, self.land
        if step > 0:
            self.copies(step - 1, k).wait_send()
            self.copies(step - 1, k, landing=True).wait_recv()
        if 1 <= step <= 4:
            size = 512 >> step
            span = rows_at(self.offset(k, step - 1), size)
            g[span] = (g[span].astype(F32) + land[step - 1][k].astype(F32)).astype(BF16)
        if step == 5:
            total = g[rows_at(self.offset(k, 4), 16)].astype(F32) + land[4][k].astype(F32)
            land[3][k, rows_at(self.p.step(3)[1] * 16, 16)] = total.astype(BF16)
        if 6 <= step <= 8:
            n = 8 - step
            size = 128 >> n
            land[n][k, rows_at(self.p.step(n)[1] * size, size)] = land[n + 1][k]
        if step < STEPS - 1:
            self.copies(step, k).start()
        if step == STEPS - 2:
            self.own(k).start()
        if step == STEPS - 1:
            self.own(k).wait()

    def tick(self, turn, units=UNITS):
        for step in range(STEPS - 1, -1, -1):
            k = turn - 2 * step
            if isinstance(k, int):
                if 0 <= k < units:
                    self.step(step, k)
            else:
                pl.when((k >= 0) & (k < units))(functools.partial(self.step, step, k))


def pair_lanes(p, start=0, size=128):
    if isinstance(p, int):
        return slice(p * 128 + start, p * 128 + start + size)
    return pl.ds(pl.multiple_of(p * 128 + start, size), size)


def lane_mask(par):
    lane = ramp((1, 128), 1)
    return jnp.where((lane >= 64) == bool(par), 1.0, 0.0).astype(BF16)


def flip_matrix():
    return jnp.where(ramp((HALF, HALF), 0) + ramp((HALF, HALF), 1) == HALF - 1, 1.0, 0.0).astype(BF16)


def flip(flip_low, value):
    return jnp.concatenate(
        [mm(flip_low, value[r : r + HALF]) for r in range(0, value.shape[0], HALF)], axis=0
    ).astype(value.dtype)


def pool_matrix(end, length, first_place, places):
    place = (ramp((end.shape[0], places), 1) + first_place).astype(F32)
    return jnp.where((place < end) & (place >= end - length), 1.0, 0.0).astype(BF16)


def query_block(n, seg):
    keys = seg + HALF * (n + 1)
    return slice(n * HALF, (n + 1) * HALF), keys, 2 * seg - keys


def attend_pair(p, n, seg, r):
    lanes = pair_lanes(p)
    seen = ramp((HALF, HALF), 1) <= ramp((HALF, HALF), 0)
    lane = ramp((HALF, 128), 1)
    rows, keys, skip = query_block(n, seg)
    key, value, place = r.key[0:keys, lanes], r.value[0:keys, lanes], r.place[skip : 2 * seg, lanes]
    mixed, scale = [], []
    for par in range(2):
        keep = lane_mask(par)
        near = mm_nt(r.query_u[rows, lanes] * keep, key)
        far = mm_nt(r.query_v[rows, lanes] * keep, place)
        scores = near + pltpu.roll(far, keys - (HALF - 1), 1, stride=1, stride_axis=0)
        scores = jnp.concatenate(
            [scores[:, : keys - HALF], jnp.where(seen, scores[:, keys - HALF :], -1e30)], axis=1
        )
        expo = jnp.exp(scores - jnp.max(scores, axis=1, keepdims=True))
        probs = expo.astype(BF16)
        scale.append(1.0 / jnp.sum(expo, axis=1, keepdims=True))
        r.probs[2 * p + par, rows, 0:keys] = probs
        mixed.append(mm(probs, value))
    scale = jnp.where(lane >= 64, scale[1], scale[0])
    r.scale[rows, lanes] = scale
    r.mixed[rows, lanes] = (jnp.where(lane >= 64, mixed[1], mixed[0]) * scale).astype(BF16)


def attend_back_pair(p, seg, r):
    lanes = pair_lanes(p)
    flip_low = flip_matrix()
    scale = 0.125
    lane = ramp((HALF, 128), 1)
    sums = [None] * 6
    bias = []
    for n in range(seg // HALF):
        rows, keys, skip = query_block(n, seg)
        key, value, place = r.key[0:keys, lanes], r.value[0:keys, lanes], r.place[skip : 2 * seg, lanes]
        grad_u, grad_v = [], []
        for par in range(2):
            keep = lane_mask(par)
            feats = pair_lanes(p, par * 64, 64)
            probs = r.probs[2 * p + par, rows, 0:keys]
            turned = mm(flip_low, probs)
            grad_mixed = r.grad_mixed[rows, lanes] * keep
            delta = jnp.sum(grad_mixed.astype(F32) * r.mixed_flip[rows, lanes].astype(F32), axis=1, keepdims=True)
            grad_scores = turned * (mm_nt(grad_mixed, value) - delta)
            near = grad_scores.astype(BF16)
            far = pltpu.roll(grad_scores, 0, 1, stride=1, stride_axis=0).astype(BF16)
            grad_u.append(mm(near, key) * scale)
            grad_v.append(mm(far, place) * scale)
            now = (
                mm(r.query_u_t[feats, rows], near),
                mm(r.grad_mixed_t[feats, rows], probs),
                mm(r.query_v_t[feats, rows], far),
            )
            for m in range(3):
                slot = par * 3 + m
                if n == 0:
                    sums[slot] = now[m]
                else:
                    old, new = sums[slot], now[m]
                    cut = old.shape[1]
                    if m < 2:
                        sums[slot] = jnp.concatenate([new[:, :cut] + old, new[:, cut:]], axis=1)
                    else:
                        sums[slot] = jnp.concatenate([new[:, :-cut], new[:, -cut:] + old], axis=1)
        grad_u = jnp.where(lane >= 64, grad_u[1], grad_u[0])
        grad_v = jnp.where(lane >= 64, grad_v[1], grad_v[0])
        bias.append((jnp.sum(grad_u, axis=0, keepdims=True), jnp.sum(grad_v, axis=0, keepdims=True)))
        r.grad_query[rows, lanes] = mm(flip_low, (grad_u + grad_v).astype(BF16)).astype(BF16)
    r.small[0:1, lanes] = sum(b[0] for b in bias)
    r.small[1:2, lanes] = sum(b[1] for b in bias)
    for par in range(2):
        feats = pair_lanes(p, par * 64, 64)
        for m, out in enumerate((r.grad_key_t, r.grad_value_t, r.grad_place_t)):
            out[feats, :] = sums[par * 3 + m].astype(BF16)


def pair_weights(p, seg, r, base):
    lanes = pair_lanes(p)
    grad_query_t = r.grad_query[:, lanes].astype(F32).T.astype(BF16)
    r.total[rows_at(base, 128)] = mm(grad_query_t, r.normed[seg : 2 * seg]).astype(BF16)
    r.total[rows_at(base + 128, 128)] = mm(r.grad_key_t[lanes, :], r.normed[...]).astype(BF16)
    r.total[rows_at(base + 256, 128)] = mm(r.grad_value_t[lanes, :], r.normed[...]).astype(BF16)
    r.total[rows_at(base + 384, 128)] = mm(r.grad_place_t[lanes, :], r.table[...]).astype(BF16)


def project_places(r):
    r.place[...] = mm(r.table[...], r.w_rel[...]).astype(BF16)


def project_memory(rows, r):
    unit, unused = normalize(r.memory[rows].astype(F32))
    low = (unit * r.vec("gain_one") + r.vec("shift_one")).astype(BF16)
    r.normed[rows] = low
    r.key[rows] = mm(low, r.w_key[...]).astype(BF16)
    r.value[rows] = mm(low, r.w_value[...]).astype(BF16)


def project_segments(n, seg, r):
    rows, keys, unused = query_block(n, seg)
    places = slice(keys - HALF, keys)
    unit, unused = normalize(r.pooled[rows])
    low = (unit * r.vec("gain_one") + r.vec("shift_one")).astype(BF16)
    r.normed[places] = low
    query = mm(low, r.w_query[...])
    scale = 0.125
    r.query_u[rows] = (query + r.vec("bias_u")).astype(BF16) * jnp.asarray(scale, BF16)
    r.query_v[rows] = (query + r.vec("bias_v")).astype(BF16) * jnp.asarray(scale, BF16)
    r.key[places] = mm(low, r.w_key[...]).astype(BF16)
    r.value[places] = mm(low, r.w_value[...]).astype(BF16)


def feed_forward_in(n, r):
    rows = slice(n * HALF, (n + 1) * HALF)
    residual = r.pooled[rows] + mm(r.mixed[rows], r.w_out[...])
    r.residual[rows] = residual
    unit, unused = normalize(residual)
    r.normed_two[rows] = (unit * r.vec("gain_two") + r.vec("shift_two")).astype(BF16)

    for m in range(r.w_up.shape[1] // 512):
        cols = slice(m * 512, (m + 1) * 512)
        inner = mm(r.normed_two[rows], r.w_up[:, cols]) + r.bias_up[0:1, cols]
        gate, slope = gelu_parts(inner)
        r.hidden[rows, cols] = (inner * gate).astype(BF16)
        r.slope[rows, cols] = slope.astype(BF16)


def feed_forward_back(n, r):
    cols = pl.ds(pl.multiple_of(n * 512, 512), 512)
    r.total[rows_at(n * 1024, 512)] = mm(r.grad_down_t[...], r.hidden[:, cols]).astype(BF16)
    grad_hidden = mm_nt(r.grad_down[...], r.w_down[cols, :])
    low = (grad_hidden * r.slope[:, cols].astype(F32)).astype(BF16)
    r.grad_inner[:, cols] = low
    r.small[pl.ds(7 + n, 1), :] = jnp.sum(low.astype(F32), axis=0, keepdims=True)
    r.total[rows_at(n * 1024 + 512, 512)] = mm(r.normed_two_t[...], low).astype(BF16)


def middle_back(r, base):
    grad_normed = mm_nt(r.grad_inner[...], r.w_up[...])
    unit, inv = normalize(r.residual[...])
    r.small[4:5, :] = jnp.sum(grad_normed * unit, axis=0, keepdims=True)
    r.small[5:6, :] = jnp.sum(grad_normed, axis=0, keepdims=True)
    grad = r.grad_output[...] + norm_back(grad_normed, unit, inv, r.vec("gain_two"))
    r.grad_residual[...] = grad
    low = grad.astype(BF16)
    mixed = r.mixed[...]
    r.total[rows_at(base, 512)] = mm(mixed.astype(F32).T.astype(BF16), low).astype(BF16)
    grad_mixed = (mm_nt(low, r.w_out[...]) * r.scale[...]).astype(BF16)
    r.grad_mixed_t[...] = grad_mixed.astype(F32).T.astype(BF16)
    flip_low = flip_matrix()
    r.grad_mixed[...] = flip(flip_low, grad_mixed)
    r.mixed_flip[...] = flip(flip_low, mixed)
    r.query_u_t[...] = flip(flip_low, r.query_u[...]).astype(F32).T.astype(BF16)
    r.query_v_t[...] = flip(flip_low, r.query_v[...]).astype(F32).T.astype(BF16)


def first_back(seg, r):
    grad_key = r.grad_key_t[...].astype(F32).T.astype(BF16)
    grad_value = r.grad_value_t[...].astype(F32).T.astype(BF16)
    grad_normed = mm_nt(r.grad_query[...], r.w_query[...])
    grad_normed += mm_nt(grad_key[seg:], r.w_key[...])
    grad_normed += mm_nt(grad_value[seg:], r.w_value[...])
    grad_mem = mm_nt(grad_key[:seg], r.w_key[...]) + mm_nt(grad_value[:seg], r.w_value[...])
    unit, inv = normalize(r.pooled[...])
    unit_mem, unused = normalize(r.memory[...].astype(F32))
    r.small[2:3, :] = jnp.sum(grad_normed * unit + grad_mem * unit_mem, axis=0, keepdims=True)
    r.small[3:4, :] = jnp.sum(grad_normed + grad_mem, axis=0, keepdims=True)
    return r.grad_residual[...] + norm_back(grad_normed, unit, inv, r.vec("gain_one"))


QUIET = 384


def sine_table(count, width):
    freqs = np.exp(np.arange(width // 2) * (-2.0 * math.log(10000.0) / width))
    angles = np.arange(count)[::-1, None] * freqs[None, :]
    return np.concatenate([np.sin(angles), np.cos(angles)], axis=1).astype(jnp.bfloat16)


def span_columns(lengths, low):
    seg = lengths.shape[1]
    lens = lengths.astype(F32).astype(BF16)
    row, col = ramp((seg - low, seg), 0) + low, ramp((seg - low, seg), 1)
    upto = jnp.where(col <= row, 1.0, 0.0).astype(BF16)
    same = jnp.where(col == row, 1.0, 0.0).astype(BF16)
    return mm_nt(upto, lens), mm_nt(same, lens)


def column(value, n):
    return jnp.sum(jnp.where(ramp(value.shape, 1) == n, value, 0.0), axis=1, keepdims=True)


WEIGHTS = ("w_query", "w_key", "w_value", "w_rel", "w_out", "w_up", "w_down")


def layer_scratch(seg, width, hidden):
    def low(*shape):
        return pltpu.VMEM(shape, BF16)

    def full(*shape):
        return pltpu.VMEM(shape, F32)

    return dict(
        table=low(2 * seg, width),
        w_query=low(width, width),
        w_key=low(width, width),
        w_value=low(width, width),
        w_rel=low(width, width),
        w_out=low(width, width),
        w_up=low(width, hidden),
        w_down=low(hidden, width),
        memory=low(seg, width),
        pooled=full(seg, width),
        normed=low(2 * seg, width),
        key=low(2 * seg, width),
        value=low(2 * seg, width),
        place=low(2 * seg, width),
        query_u=low(seg, width),
        query_v=low(seg, width),
        mixed=low(seg, width),
        probs=low(8, seg, 2 * seg),
        scale=full(seg, width),
        residual=full(seg, width),
        normed_two=low(seg, width),
        normed_two_t=low(width, seg),
        hidden=low(seg, hidden),
        slope=low(seg, hidden),
        grad_inner=low(seg, hidden),
        grad_output=full(seg, width),
        grad_down=low(seg, width),
        grad_down_t=low(width, seg),
        low_rows=low(seg, width),
        out_rows=low(seg, width),
        chars_quiet=low(QUIET, width),
        chars_parts=low(7, seg - QUIET, width),
        grads_quiet=low(QUIET, width),
        grads_parts=low(7, seg - QUIET, width),
        total=low(UNITS * PIECE, width),
        land_0=low(UNITS, 256, width),
        land_1=low(UNITS, 128, width),
        land_2=low(UNITS, 64, width),
        land_3=low(UNITS, 32, width),
        land_4=low(UNITS, 16, width),
        bias_up=full(1, hidden),
        vectors=full(16, width),
        small=full(16, width),
        small_sum=full(5, 16, width),
        small_land=full(5, 16, width),
        load_sem=pltpu.SemaphoreType.DMA((len(WEIGHTS) + 1,)),
        stage_sem=pltpu.SemaphoreType.DMA((2, 4)),
        memory_send=pltpu.SemaphoreType.DMA((4,)),
        memory_recv=pltpu.SemaphoreType.DMA((4,)),
        quiet_send=pltpu.SemaphoreType.DMA((2, 4, 2)),
        quiet_recv=pltpu.SemaphoreType.DMA((2, 2)),
        parts_send=pltpu.SemaphoreType.DMA((2, 3)),
        parts_recv=pltpu.SemaphoreType.DMA((2, 3)),
        kept_send=pltpu.SemaphoreType.DMA((4,)),
        kept_recv=pltpu.SemaphoreType.DMA((4,)),
        back_send=pltpu.SemaphoreType.DMA((2, 5)),
        back_recv=pltpu.SemaphoreType.DMA((2, 2, 4)),
        sum_send=pltpu.SemaphoreType.DMA((2, STEPS - 1)),
        sum_recv=pltpu.SemaphoreType.DMA((UNITS, STEPS - 1)),
        small_send=pltpu.SemaphoreType.DMA((5,)),
        small_recv=pltpu.SemaphoreType.DMA((5,)),
        store_sem=pltpu.SemaphoreType.DMA((2,)),
    )


class Rows:
    def __init__(self, r, place, way, source, stage, quiet, parts):
        self.r, self.p, self.way = r, place, way
        self.source, self.stage, self.quiet, self.parts = source, stage, quiet, parts

    def load(self, n):
        cols = pl.ds(pl.multiple_of(n * 512, 512), 512)
        return pltpu.make_async_copy(self.source.at[n], self.stage.at[:, cols], self.r.stage_sem.at[self.way, n])

    def quiet_copy(self, to, part):
        r = self.r
        span = pl.ds(0, HALF) if part == 0 else pl.ds(HALF, QUIET - HALF)
        src, dst = self.source.at[to, span], self.quiet.at[span]
        if to == 0:
            return pltpu.make_async_copy(src, dst, r.quiet_send.at[self.way, 0, part])
        return remote(src, dst, r.quiet_send.at[self.way, to, part], r.quiet_recv.at[self.way, part], (self.p.s, to))

    def start_quiet(self):
        @pl.when(self.p.b == 0)
        def _():
            for part in range(2):
                for to in (2, 3, 1, 0):
                    self.quiet_copy(to, part).start()

    def wait_quiet(self, part):
        @pl.when(self.p.b == 0)
        def _():
            self.quiet_copy(0, part).wait()

        @pl.when(self.p.b != 0)
        def _():
            self.quiet_copy(1, part).wait_recv()

    def parts_copy(self, n):
        src, dst, to = ((3, 1, self.p.core()), (4, 5, self.p.core()), (6, 2, self.p.across()))[n]
        return remote(
            self.parts.at[src],
            self.parts.at[dst],
            self.r.parts_send.at[self.way, n],
            self.r.parts_recv.at[self.way, n],
            to,
        )

    def part(self, to, ends, lens):
        self.load(to).wait()
        cols = pl.ds(pl.multiple_of(to * 512, 512), 512)
        chosen = pool_matrix(column(ends, to), column(lens, to), self.p.b * 512, 512)
        return mm(chosen, self.stage[:, cols])

    def start_parts(self, ends, lens):
        b, sibling, away = self.p.b, self.p.core()[1], self.p.across()[1]
        self.parts[4] = self.part(away + sibling - b, ends, lens).astype(BF16)
        self.parts_copy(1).start()
        self.parts[3] = self.part(sibling, ends, lens).astype(BF16)
        self.parts_copy(0).start()
        self.parts[6] = self.part(away, ends, lens).astype(BF16)
        self.parts[0] = self.part(b, ends, lens).astype(BF16)

    def join_parts(self):
        self.parts_copy(1).wait_recv()
        self.parts[6] = (self.parts[6].astype(F32) + self.parts[5].astype(F32)).astype(BF16)
        self.parts_copy(2).start()

    def wait_parts(self):
        self.parts_copy(0).wait_recv()
        self.parts_copy(2).wait_recv()
        return sum(self.parts[n].astype(F32) for n in range(3))

    def wait_sent(self):
        for n in range(3):
            self.parts_copy(n).wait_send()

        @pl.when(self.p.b == 0)
        def _():
            for part in range(2):
                for to in (1, 2, 3):
                    self.quiet_copy(to, part).wait_send()

    def back(self, rows, quiet_out, loud_out):
        self.rows, self.quiet_out, self.loud_out = rows, quiet_out, loud_out
        return self

    def loud_rows(self):
        return self.rows.at[pl.ds(QUIET, self.rows.shape[0] - QUIET)]

    def quiet_rows(self):
        return self.rows.at[pl.ds(0, QUIET)]

    def loud_copy(self, n, slot):
        r, p, way = self.r, self.p, self.way
        src = self.loud_out.at[slot] if n == 2 else self.loud_rows()
        to = p.across() if n == 1 else p.core()
        return remote(src, self.loud_out.at[slot], r.back_send.at[way, n], r.back_recv.at[way, 0, slot], to)

    def quiet_back(self, slot):
        r, way = self.r, self.way
        return remote(
            self.quiet_rows(),
            self.quiet_out.at[slot],
            r.back_send.at[way, 3],
            r.back_recv.at[way, 1, slot],
            (self.p.s, 0),
        )

    def own_copies(self):
        r, p, way = self.r, self.p, self.way
        loud = pltpu.make_async_copy(self.loud_rows(), self.loud_out.at[p.b], r.back_send.at[way, 4])
        quiet = pltpu.make_async_copy(self.quiet_rows(), self.quiet_out.at[0], r.back_send.at[way, 3])
        return loud, quiet

    def start_back(self):
        p = self.p
        loud, quiet = self.own_copies()
        self.loud_copy(1, p.b).start()
        self.loud_copy(0, p.b).start()
        pl.when(p.b != 0)(self.quiet_back(p.b).start)
        pl.when(p.b == 0)(quiet.start)
        loud.start()

    def pass_on(self):
        away = self.p.across()[1]
        self.loud_copy(1, away).wait_recv()
        self.loud_copy(2, away).start()

    def wait_back(self):
        p = self.p
        sibling, away = p.core()[1], p.across()[1]
        loud, quiet = self.own_copies()
        for n in (0, 1):
            self.loud_copy(n, p.b).wait_send()
        self.loud_copy(2, away).wait_send()
        loud.wait()
        pl.when(p.b != 0)(self.quiet_back(p.b).wait_send)
        pl.when(p.b == 0)(quiet.wait)
        self.loud_copy(0, sibling).wait_recv()
        self.loud_copy(2, away + sibling - p.b).wait_recv()

        @pl.when(p.b == 0)
        def _():
            for n in (1, 2, 3):
                self.quiet_back(n).wait_recv()


class Small:
    def __init__(self, r, place):
        self.r, self.p = r, place

    def source(self, step):
        return self.r.small if step == 0 else self.r.small_sum.at[step - 1]

    def copy(self, step):
        r, p = self.r, self.p
        to = p.core() if step == 0 else p.pair(AXES[step - 1])
        return remote(self.source(step), r.small_land.at[step], r.small_send.at[step], r.small_recv.at[step], to)

    def start(self, step):
        self.copy(step).start()

    def finish(self, step):
        self.copy(step).wait()
        self.r.small_sum[step] = self.source(step)[...] + self.r.small_land[step]


def layer_kernel(names, chars, lengths, memory, grad_out, *rest):
    count = len(VECTORS) + 1 + len(WEIGHTS)
    vectors, table, weights = rest[: len(VECTORS)], rest[len(VECTORS)], rest[len(VECTORS) + 1 : count]
    kept, out_quiet, out_loud, grad_quiet, grad_loud, total_out, small_out = rest[count : count + 7]
    r = types.SimpleNamespace(**dict(zip(names, rest[count + 7 :])))
    p = Place()
    seg, width = r.pooled.shape
    r.grad_residual, r.grad_mixed, r.grad_rows = r.grad_output, r.grad_down, r.normed_two
    for n, name in enumerate(("mixed_flip", "query_u_t", "query_v_t", "grad_mixed_t")):
        setattr(r, name, r.slope.at[:, n * width : (n + 1) * width])
    r.grad_key_t, r.grad_value_t = r.hidden.at[:, : 2 * seg], r.hidden.at[:, 2 * seg :]
    r.grad_place_t, r.grad_query = r.grad_inner.at[:, : 2 * seg], r.grad_inner.at[:, 2 * seg : 3 * seg]
    loads = [
        pltpu.make_async_copy(src, dst, r.load_sem.at[n])
        for n, (src, dst) in enumerate(
            zip((*weights, table), [getattr(r, name) for name in WEIGHTS] + [r.table])
        )
    ]
    chars_rows = Rows(r, p, 0, chars, r.hidden, r.chars_quiet, r.chars_parts).back(r.out_rows, out_quiet, out_loud)
    grads_rows = Rows(r, p, 1, grad_out, r.grad_inner, r.grads_quiet, r.grads_parts).back(
        r.grad_rows, grad_quiet, grad_loud
    )
    for n in range(4):
        chars_rows.load(n).start()
    for n in range(4):
        grads_rows.load(n).start()
    for copy in loads:
        copy.start()
    for n, name in enumerate(VECTORS):
        value = vectors[n][...].astype(F32)
        if name == "bias_up":
            r.bias_up[...] = value.reshape(1, -1)
        elif value.ndim == 2:
            r.vectors[n : n + 1, :] = jnp.concatenate([value[h : h + 1, :] for h in range(value.shape[0])], axis=1)
        else:
            r.vectors[n : n + 1, :] = value.reshape(1, -1)
    r.vec = lambda name: r.vectors[VECTORS.index(name) : VECTORS.index(name) + 1, :]

    barrier = pltpu.get_barrier_semaphore()
    others = [p.group(1), p.group(2), p.group(3), p.pair("y"), p.pair("near"), p.pair("far")]
    for other in others:
        pl.semaphore_signal(barrier, inc=1, device_id=other, device_id_type=MESH)
    pl.semaphore_wait(barrier, len(others))

    rows = memory.shape[1]

    def memory_copy(k, slot):
        to = (p.b + k) % 4
        return remote(
            memory.at[to], r.memory.at[rows_at(slot * rows, rows)], r.memory_send.at[k], r.memory_recv.at[slot], p.group(k)
        )

    own_memory = pltpu.make_async_copy(memory.at[p.b], r.memory.at[rows_at(p.b * rows, rows)], r.memory_send.at[0])
    for k in (2, 3, 1):
        memory_copy(k, p.b).start()
    own_memory.start()
    chars_rows.start_quiet()
    ends, lens = span_columns(lengths[...], QUIET)
    chars_rows.start_parts(ends, lens)
    for copy in loads:
        copy.wait()
    project_places(r)
    chars_rows.join_parts()
    grads_rows.start_quiet()
    grads_rows.start_parts(ends, lens)
    own_memory.wait()
    memory_copy(1, p.core()[1]).wait_recv()
    project_memory(rows_at(p.x * 2 * rows, 2 * rows), r)
    for slot in (2 * (1 - p.x), 2 * (1 - p.x) + 1):
        memory_copy(1, slot).wait_recv()
    project_memory(rows_at((1 - p.x) * 2 * rows, 2 * rows), r)
    own_lens = column(lens, p.b)

    def forward(block):
        project_segments(block, seg, r)
        for n in range(4):
            attend_pair(n, block, seg, r)
        feed_forward_in(block, r)

    chars_rows.wait_quiet(0)
    r.pooled[0:HALF] = chars_rows.quiet[0:HALF].astype(F32)
    forward(0)
    grads_rows.join_parts()
    chars_rows.wait_quiet(1)
    r.pooled[HALF:QUIET] = chars_rows.quiet[HALF:QUIET].astype(F32)
    r.pooled[QUIET:seg] = chars_rows.wait_parts() / own_lens
    r.low_rows[...] = r.pooled[...].astype(BF16)

    def kept_copy(k, slot):
        to = (p.b + k) % 4
        return remote(
            r.low_rows.at[rows_at(to * rows, rows)], kept.at[slot], r.kept_send.at[k], r.kept_recv.at[slot], p.group(k)
        )

    own_kept = pltpu.make_async_copy(r.low_rows.at[rows_at(p.b * rows, rows)], kept.at[p.b], r.kept_send.at[0])
    for k in (2, 3, 1):
        kept_copy(k, p.b).start()
    own_kept.start()
    forward(1)
    grads_rows.wait_quiet(0)
    grads_rows.wait_quiet(1)
    r.grad_output[0:QUIET] = grads_rows.quiet[...].astype(F32)
    r.grad_output[QUIET:seg] = grads_rows.wait_parts()
    low = r.grad_output[...].astype(BF16)
    r.grad_down[...] = low
    r.grad_down_t[...] = low.astype(F32).T.astype(BF16)
    r.normed_two_t[...] = r.normed_two[...].astype(F32).T.astype(BF16)
    r.small[...] = jnp.zeros(r.small.shape, F32)
    r.small[6:7, :] = jnp.sum(low.astype(F32), axis=0, keepdims=True)

    land = [getattr(r, f"land_{n}") for n in range(5)]
    sums = Sum(p, r.total, land, total_out, r.sum_send, r.sum_recv, r.store_sem)

    def feed_back(n, carry):
        feed_forward_back(n, r)
        sums.tick(2 * n)
        sums.tick(2 * n + 1)
        return carry

    lax.fori_loop(0, 4, feed_back, 0)
    r.out_rows[...] = (r.residual[...] + (mm(r.hidden[...], r.w_down[...]) + r.vec("bias_down"))).astype(BF16)
    chars_rows.start_back()
    middle_back(r, 8 * PIECE)
    sums.tick(8)

    def back(n, carry):
        attend_back_pair(n, seg, r)
        pair_weights(n, seg, r, (9 + n) * PIECE)
        sums.tick(9 + n)
        return carry

    lax.fori_loop(0, 4, back, 0)
    grad_pooled = first_back(seg, r)
    r.grad_rows[0:QUIET] = grad_pooled[:QUIET].astype(BF16)
    r.grad_rows[QUIET:seg] = (grad_pooled[QUIET:] / own_lens).astype(BF16)
    grads_rows.start_back()
    small = Small(r, p)
    small.start(0)
    chars_rows.pass_on()

    def tail(n, carry):
        sums.tick(UNITS + n)
        for step in range(5):

            @pl.when(n == 2 * step + 1)
            def _():
                small.finish(step)
                if step < 4:
                    small.start(step + 1)

        pl.when(n == 12)(grads_rows.pass_on)
        return carry

    lax.fori_loop(0, 2 * (STEPS - 1), tail, 0)
    small_out[...] = r.small_sum[4]
    for k in (1, 2, 3):
        memory_copy(k, p.b).wait_send()
        kept_copy(k, p.b).wait_send()
        kept_copy(k, (p.b + k) % 4).wait_recv()
    own_kept.wait()
    chars_rows.wait_sent()
    grads_rows.wait_sent()
    chars_rows.wait_back()
    grads_rows.wait_back()


def spread_kernel(
    lengths, chars, grad_out, rows, out_quiet, out_loud, grad_quiet, grad_loud, wide, flat, pairs, small,
    out_chars, grad_chars, kept, w_query, w_key, w_value, w_rel, w_out, w_up, w_down, bias_u, bias_v, *vectors,
):
    n = pl.program_id(0)
    b = lax.axis_index("blk")
    places = chars.shape[1]
    seg = lengths.shape[1]
    lens = lengths[...].astype(F32).astype(BF16)
    row, col = ramp((seg - QUIET, seg), 0) + QUIET, ramp((seg - QUIET, seg), 1)
    upto = jnp.where(col <= row, 1.0, 0.0).astype(BF16)
    same = jnp.where(col == row, 1.0, 0.0).astype(BF16)
    pick = ramp((lengths.shape[0], seg - QUIET), 0) == n
    end = jnp.sum(jnp.where(pick, mm_nt(lens, upto), 0.0), axis=0, keepdims=True)
    length = jnp.sum(jnp.where(pick, mm_nt(lens, same), 0.0), axis=0, keepdims=True)
    place = (ramp((places, seg - QUIET), 0) + b * places).astype(F32)
    chosen = jnp.where((place < end) & (place >= end - length), 1.0, 0.0).astype(BF16)
    first = b == 0
    kept[...] = rows[...]
    for source, quiet, loud, out in (
        (chars, out_quiet, out_loud, out_chars),
        (grad_out, grad_quiet, grad_loud, grad_chars),
    ):
        spread = mm(chosen, loud[0])
        whole = source[0].astype(F32) + spread
        out[0, QUIET:places] = whole[QUIET:].astype(out.dtype)
        out[0, 0:QUIET] = (whole[:QUIET] + jnp.where(first, quiet[0].astype(F32), 0.0)).astype(out.dtype)
    w_down[...] = wide[0:512].astype(F32).T
    w_up[...] = wide[512:1024].astype(F32)
    w_out[...] = flat[...].astype(F32)
    for m, out in enumerate((w_query, w_key, w_value, w_rel)):
        out[...] = pairs[m * 128 : (m + 1) * 128].astype(F32).T
    for m, out in enumerate((bias_u, bias_v)):
        out[...] = jnp.concatenate([small[m : m + 1, h * 64 : (h + 1) * 64] for h in range(8)], axis=0)
    for m, out in enumerate(vectors[:4]):
        out[...] = small[2 + m : 3 + m, :]
    vectors[4][...] = jnp.concatenate([small[m : m + 1, :] for m in range(7, 11)], axis=1)
    vectors[5][...] = small[6:7, :]


def shards_whole(
    chars, seg_lengths, memory, grad_out, w_query, w_key, w_value, w_rel, w_out, w_up, w_down,
    bias_u, bias_v, gain_one, shift_one, gain_two, shift_two, bias_up, bias_down,
):
    count, places, width = chars.shape
    seg, hidden = seg_lengths.shape[1], w_up.shape[1]
    rows = memory.shape[1]
    table = jnp.asarray(sine_table(2 * seg, width))
    scratch = layer_scratch(seg, width, hidden)
    anywhere, near = pl.BlockSpec(memory_space=pl.ANY), pl.BlockSpec(memory_space=pltpu.VMEM)
    loud = seg - QUIET
    kept, out_quiet, out_loud, grad_quiet, grad_loud, total, small = pl.pallas_call(
        functools.partial(layer_kernel, tuple(scratch)),
        out_shape=[
            jax.ShapeDtypeStruct((count, rows, width), BF16),
            jax.ShapeDtypeStruct((count, QUIET, width), BF16),
            jax.ShapeDtypeStruct((count, loud, width), BF16),
            jax.ShapeDtypeStruct((count, QUIET, width), BF16),
            jax.ShapeDtypeStruct((count, loud, width), BF16),
            jax.ShapeDtypeStruct((UNITS * PIECE, width), BF16),
            jax.ShapeDtypeStruct((16, width), F32),
        ],
        in_specs=[anywhere, near, anywhere, anywhere] + [near] * len(VECTORS) + [anywhere] * 8,
        out_specs=[anywhere] * 6 + [near],
        scratch_shapes=list(scratch.values()),
        compiler_params=pltpu.CompilerParams(
            collective_id=0, has_side_effects=True, vmem_limit_bytes=VMEM_BYTES
        ),
        name="layer",
    )(
        chars, seg_lengths, memory, grad_out,
        bias_u, bias_v, gain_one, shift_one, gain_two, shift_two, bias_up, bias_down, table,
        w_query, w_key, w_value, w_rel, w_out, w_up, w_down,
    )

    def block(shape, index):
        return pl.BlockSpec(shape, index)

    def each(*shape):
        return block((1, *shape), lambda n: (n, 0, 0))

    def whole(*shape):
        return block(shape, lambda n: (0, 0))

    vector = [(1, width)] * 4 + [(1, hidden), (1, width)]
    outs = pl.pallas_call(
        spread_kernel,
        grid=(count,),
        out_shape=[
            jax.ShapeDtypeStruct(chars.shape, BF16),
            jax.ShapeDtypeStruct(chars.shape, F32),
            jax.ShapeDtypeStruct(memory.shape, BF16),
            *[jax.ShapeDtypeStruct((width, width), F32)] * 5,
            jax.ShapeDtypeStruct((width, hidden), F32),
            jax.ShapeDtypeStruct((hidden, width), F32),
            *[jax.ShapeDtypeStruct(bias_u.shape, F32)] * 2,
            *[jax.ShapeDtypeStruct(shape, F32) for shape in vector],
        ],
        in_specs=[
            whole(*seg_lengths.shape),
            each(places, width),
            each(places, width),
            each(rows, width),
            each(QUIET, width),
            each(loud, width),
            each(QUIET, width),
            each(loud, width),
            block((2 * PIECE, width), lambda n: (n, 0)),
            block((128, width), lambda n: (8 * (PIECE // 128) + n, 0)),
            block((PIECE, width), lambda n: (9 + n, 0)),
            whole(16, width),
        ],
        out_specs=[
            each(places, width),
            each(places, width),
            each(rows, width),
            *[block((width, 128), lambda n: (0, n))] * 4,
            block((128, width), lambda n: (n, 0)),
            block((width, 512), lambda n: (0, n)),
            block((512, width), lambda n: (n, 0)),
            *[whole(*bias_u.shape)] * 2,
            *[whole(*shape) for shape in vector],
        ],
        compiler_params=pltpu.CompilerParams(vmem_limit_bytes=VMEM_BYTES),
        name="spread",
    )(seg_lengths, chars, grad_out, kept, out_quiet, out_loud, grad_quiet, grad_loud, total, total, total, small)
    return (*outs[:12], *[v.reshape(-1) for v in outs[12:]])


VMEM_BYTES = 64 * 2**20 - 2**16


def fits_whole(mesh):
    return dict(mesh.shape) == {"seq": 8, "blk": 4}


def layer_norm(value, gain, shift):
    center = value - jnp.mean(value, axis=-1, keepdims=True)
    spread = jnp.mean(center * center, axis=-1, keepdims=True)
    return center * lax.rsqrt(spread + 1e-05) * gain + shift


def angle_tables(places, feature_width):
    freqs = jnp.exp(
        jnp.arange(feature_width // 2, dtype=jnp.float32)
        * (-2.0 * math.log(10000.0) / feature_width)
    )
    angles = places[:, None] * freqs[None, :]
    return (jnp.sin(angles), jnp.cos(angles))


def smooth_gate(value):
    return jax.nn.gelu(value, approximate=False)


def segment_ids(seg_end, char_places):
    return jnp.sum((seg_end[:, None, :] <= char_places[None, :, None]).astype(jnp.int32), axis=2)


def shards(
    chars,
    seg_lengths,
    memory,
    grad_out,
    w_query,
    w_key,
    w_value,
    w_rel,
    w_out,
    w_up,
    w_down,
    bias_u,
    bias_v,
    gain_one,
    shift_one,
    gain_two,
    shift_two,
    bias_up,
    bias_down,
):
    blk_index = lax.axis_index("blk")
    seq_local, char_rows, feature_width = chars.shape
    seg_rows = memory.shape[1]
    seg_count = seg_lengths.shape[1]
    head_count, head_dim = bias_u.shape
    half_width = feature_width // 2
    score_scale = head_dim ** (-0.5)
    seg_start = blk_index * seg_rows
    gain_one_f = gain_one.astype(jnp.float32)
    shift_one_f = shift_one.astype(jnp.float32)
    gain_two_f = gain_two.astype(jnp.float32)
    shift_two_f = shift_two.astype(jnp.float32)
    seg_end = jnp.cumsum(seg_lengths, axis=1)
    char_places = blk_index * char_rows + jnp.arange(char_rows, dtype=jnp.int32)
    segment = segment_ids(seg_end, char_places)
    own_lengths = lax.dynamic_slice_in_dim(seg_lengths, seg_start, seg_rows, 1).astype(jnp.float32)
    chars_f = chars.astype(jnp.float32)
    grad_f = grad_out.astype(jnp.float32)

    def full_table(values, ids):
        return jax.ops.segment_sum(values, ids, num_segments=seg_count)

    part_sums = jax.vmap(full_table)(chars_f, segment)
    pooled_sum = lax.psum_scatter(part_sums, "blk", scatter_dimension=1, tiled=True)
    pooled = pooled_sum / own_lengths[:, :, None]
    normed = layer_norm(pooled, gain_one_f, shift_one_f)
    normed_low = normed.astype(jnp.bfloat16)
    memory_f = memory.astype(jnp.float32)
    mem_low = layer_norm(memory_f, gain_one_f, shift_one_f).astype(jnp.bfloat16)
    query_rows = jnp.einsum("sid,de->sie", normed_low, w_query, preferred_element_type=jnp.float32)
    key_local = jnp.stack(
        [
            jnp.einsum("sid,de->sie", mem_low, w_key, preferred_element_type=jnp.float32),
            jnp.einsum("sid,de->sie", normed_low, w_key, preferred_element_type=jnp.float32),
        ],
        axis=1,
    ).astype(jnp.bfloat16)
    value_local = jnp.stack(
        [
            jnp.einsum("sid,de->sie", mem_low, w_value, preferred_element_type=jnp.float32),
            jnp.einsum("sid,de->sie", normed_low, w_value, preferred_element_type=jnp.float32),
        ],
        axis=1,
    ).astype(jnp.bfloat16)
    key_all, value_all = (
        lax.all_gather(key_local, "blk", axis=2, tiled=True),
        lax.all_gather(value_local, "blk", axis=2, tiled=True),
    )
    key_heads = key_all.reshape(seq_local, 2 * seg_count, head_count, head_dim)
    value_heads = value_all.reshape(seq_local, 2 * seg_count, head_count, head_dim)
    query_u = (
        (query_rows + bias_u.astype(jnp.float32).reshape(-1))
        .astype(jnp.bfloat16)
        .reshape(seq_local, seg_rows, head_count, head_dim)
    )
    query_v = (
        (query_rows + bias_v.astype(jnp.float32).reshape(-1))
        .astype(jnp.bfloat16)
        .reshape(seq_local, seg_rows, head_count, head_dim)
    )
    w_rel_heads = w_rel.reshape(feature_width, head_count, head_dim)
    rel_coeff = jnp.einsum(
        "sihe,fhe->sihf", query_v, w_rel_heads, preferred_element_type=jnp.float32
    )
    sin_all, cos_all = angle_tables(jnp.arange(2 * seg_count).astype(jnp.float32), feature_width)
    key_pos = jnp.concatenate([cos_all, sin_all], axis=-1).astype(jnp.bfloat16)
    query_index = seg_count + seg_start + jnp.arange(seg_rows, dtype=jnp.int32)
    sin_q, cos_q = angle_tables(query_index.astype(jnp.float32), feature_width)
    sin_query = sin_q[None, :, None, :]
    cos_query = cos_q[None, :, None, :]
    coeff_sin = rel_coeff[..., :half_width]
    coeff_cos = rel_coeff[..., half_width:]
    query_pos = jnp.concatenate(
        [
            coeff_sin * sin_query + coeff_cos * cos_query,
            coeff_cos * sin_query - coeff_sin * cos_query,
        ],
        axis=-1,
    ).astype(jnp.bfloat16)
    allowed = jnp.arange(2 * seg_count, dtype=jnp.int32)[None, :] <= query_index[:, None]

    def score_block():
        raw_scores = (
            jnp.einsum("sihe,sjhe->shij", query_u, key_heads, preferred_element_type=jnp.float32)
            + jnp.einsum("sihf,jf->shij", query_pos, key_pos, preferred_element_type=jnp.float32)
        ) * score_scale
        return jnp.where(allowed[None, None], raw_scores, -1e30)

    scores = score_block()
    row_top = jnp.max(scores, axis=-1, keepdims=True)
    expo = jnp.exp(scores - row_top)
    row_total = jnp.sum(expo, axis=-1, keepdims=True)
    log_total = row_top + jnp.log(row_total)
    att_probs = (expo / row_total).astype(jnp.bfloat16)
    att_mixed = jnp.einsum(
        "shij,sjhe->sihe", att_probs, value_heads, preferred_element_type=jnp.float32
    )
    mixed_low = att_mixed.reshape(seq_local, seg_rows, feature_width).astype(jnp.bfloat16)
    residual = pooled + jnp.einsum(
        "sid,de->sie", mixed_low, w_out, preferred_element_type=jnp.float32
    )
    normed_two = layer_norm(residual, gain_two_f, shift_two_f)
    two_low = normed_two.astype(jnp.bfloat16)
    ffn_inner = jnp.einsum(
        "sid,df->sif", two_low, w_up, preferred_element_type=jnp.float32
    ) + bias_up.astype(jnp.float32)
    hidden_low = smooth_gate(ffn_inner).astype(jnp.bfloat16)
    branch_out = jnp.einsum(
        "sif,fd->sid", hidden_low, w_down, preferred_element_type=jnp.float32
    ) + bias_down.astype(jnp.float32)
    out_low = (residual + branch_out).astype(jnp.bfloat16)
    rows_all = lax.all_gather(out_low, "blk", axis=1, tiled=True)
    picked = jnp.take_along_axis(rows_all, segment[:, :, None], axis=1)
    out_chars = (chars_f + picked.astype(jnp.float32)).astype(jnp.bfloat16)
    new_memory = pooled.astype(jnp.bfloat16)
    grad_table = jax.vmap(full_table)(grad_f, segment)
    grad_output = lax.psum_scatter(grad_table, "blk", scatter_dimension=1, tiled=True)
    grad_down_low = grad_output.astype(jnp.bfloat16)
    grad_bias_down = jnp.sum(grad_down_low.astype(jnp.float32), axis=(0, 1))
    grad_w_down = jnp.einsum(
        "sif,sid->fd", hidden_low, grad_down_low, preferred_element_type=jnp.float32
    )
    grad_hidden = jnp.einsum(
        "sid,fd->sif", grad_down_low, w_down, preferred_element_type=jnp.float32
    )
    unused_value, gate_back = jax.vjp(smooth_gate, ffn_inner)
    grad_inner = gate_back(grad_hidden)[0].astype(jnp.bfloat16)
    grad_bias_up = jnp.sum(grad_inner.astype(jnp.float32), axis=(0, 1))
    grad_w_up = jnp.einsum("sid,sif->df", two_low, grad_inner, preferred_element_type=jnp.float32)
    grad_normed_two = jnp.einsum(
        "sif,df->sid", grad_inner, w_up, preferred_element_type=jnp.float32
    )
    unused_norm, norm_two_back = jax.vjp(layer_norm, residual, gain_two_f, shift_two_f)
    grad_resid_norm, grad_gain_two, grad_shift_two = norm_two_back(grad_normed_two)
    grad_residual = grad_output + grad_resid_norm
    grad_att_low = grad_residual.astype(jnp.bfloat16)
    grad_w_out = jnp.einsum(
        "sid,sie->de", mixed_low, grad_att_low, preferred_element_type=jnp.float32
    )
    grad_mixed = jnp.einsum("sie,de->sid", grad_att_low, w_out, preferred_element_type=jnp.float32)
    grad_mixed = grad_mixed.astype(jnp.bfloat16).reshape(seq_local, seg_rows, head_count, head_dim)
    scores_again = score_block()
    probs_full = jnp.exp(scores_again - log_total)
    probs_low = probs_full.astype(jnp.bfloat16)
    grad_probs = jnp.einsum(
        "sihe,sjhe->shij", grad_mixed, value_heads, preferred_element_type=jnp.float32
    )
    grad_values = jnp.einsum(
        "shij,sihe->sjhe", probs_low, grad_mixed, preferred_element_type=jnp.float32
    )
    prob_delta = jnp.sum(probs_full * grad_probs, axis=-1, keepdims=True)
    grad_scores = (probs_full * (grad_probs - prob_delta)).astype(jnp.bfloat16)
    grad_query_u = (
        jnp.einsum("shij,sjhe->sihe", grad_scores, key_heads, preferred_element_type=jnp.float32)
        * score_scale
    )
    grad_keys = (
        jnp.einsum("shij,sihe->sjhe", grad_scores, query_u, preferred_element_type=jnp.float32)
        * score_scale
    )
    grad_query_pos = (
        jnp.einsum("shij,jf->sihf", grad_scores, key_pos, preferred_element_type=jnp.float32)
        * score_scale
    )
    grad_first = grad_query_pos[..., :half_width]
    grad_second = grad_query_pos[..., half_width:]
    grad_coeff = jnp.concatenate(
        [
            grad_first * sin_query - grad_second * cos_query,
            grad_first * cos_query + grad_second * sin_query,
        ],
        axis=-1,
    ).astype(jnp.bfloat16)
    grad_w_rel = jnp.einsum(
        "sihf,sihe->fhe", grad_coeff, query_v, preferred_element_type=jnp.float32
    ).reshape(feature_width, feature_width)
    grad_query_v = jnp.einsum(
        "sihf,fhe->sihe", grad_coeff, w_rel_heads, preferred_element_type=jnp.float32
    )
    grad_bias_u = jnp.sum(grad_query_u, axis=(0, 1))
    grad_bias_v = jnp.sum(grad_query_v, axis=(0, 1))
    grad_query = (
        (grad_query_u + grad_query_v)
        .reshape(seq_local, seg_rows, feature_width)
        .astype(jnp.bfloat16)
    )
    grad_w_query = jnp.einsum(
        "sid,sie->de", normed_low, grad_query, preferred_element_type=jnp.float32
    )
    grad_normed = jnp.einsum("sie,de->sid", grad_query, w_query, preferred_element_type=jnp.float32)
    key_share, value_share = (
        lax.psum_scatter(
            grad_keys.reshape(seq_local, 2, seg_count, feature_width),
            "blk",
            scatter_dimension=2,
            tiled=True,
        ),
        lax.psum_scatter(
            grad_values.reshape(seq_local, 2, seg_count, feature_width),
            "blk",
            scatter_dimension=2,
            tiled=True,
        ),
    )
    key_low = key_share.astype(jnp.bfloat16)
    value_low = value_share.astype(jnp.bfloat16)
    grad_w_key = jnp.einsum(
        "sid,sie->de", mem_low, key_low[:, 0], preferred_element_type=jnp.float32
    ) + jnp.einsum("sid,sie->de", normed_low, key_low[:, 1], preferred_element_type=jnp.float32)
    grad_w_value = jnp.einsum(
        "sid,sie->de", mem_low, value_low[:, 0], preferred_element_type=jnp.float32
    ) + jnp.einsum("sid,sie->de", normed_low, value_low[:, 1], preferred_element_type=jnp.float32)
    grad_normed = grad_normed + jnp.einsum(
        "sie,de->sid", key_low[:, 1], w_key, preferred_element_type=jnp.float32
    )
    grad_normed = grad_normed + jnp.einsum(
        "sie,de->sid", value_low[:, 1], w_value, preferred_element_type=jnp.float32
    )
    grad_mem_normed = jnp.einsum(
        "sie,de->sid", key_low[:, 0], w_key, preferred_element_type=jnp.float32
    ) + jnp.einsum("sie,de->sid", value_low[:, 0], w_value, preferred_element_type=jnp.float32)
    unused_one, norm_one_back = jax.vjp(layer_norm, pooled, gain_one_f, shift_one_f)
    grad_pooled_norm, grad_gain_one, grad_shift_one = norm_one_back(grad_normed)
    unused_mem, norm_mem_back = jax.vjp(layer_norm, memory_f, gain_one_f, shift_one_f)
    unused_grad, grad_gain_mem, grad_shift_mem = norm_mem_back(grad_mem_normed)
    grad_gain_one = grad_gain_one + grad_gain_mem
    grad_shift_one = grad_shift_one + grad_shift_mem
    grad_pooled = grad_residual + grad_pooled_norm
    grad_sum = grad_pooled / own_lengths[:, :, None]
    grad_sum_all = lax.all_gather(grad_sum, "blk", axis=1, tiled=True)
    grad_chars = grad_f + jnp.take_along_axis(grad_sum_all, segment[:, :, None], axis=1)
    (
        grad_w_query,
        grad_w_key,
        grad_w_value,
        grad_w_rel,
        grad_w_out,
        grad_w_up,
        grad_w_down,
        grad_bias_u,
        grad_bias_v,
        grad_gain_one,
        grad_shift_one,
        grad_gain_two,
        grad_shift_two,
        grad_bias_up,
        grad_bias_down,
    ) = lax.psum(
        (
            grad_w_query,
            grad_w_key,
            grad_w_value,
            grad_w_rel,
            grad_w_out,
            grad_w_up,
            grad_w_down,
            grad_bias_u,
            grad_bias_v,
            grad_gain_one,
            grad_shift_one,
            grad_gain_two,
            grad_shift_two,
            grad_bias_up,
            grad_bias_down,
        ),
        ("seq", "blk"),
    )
    return (
        out_chars,
        grad_chars,
        new_memory,
        grad_w_query,
        grad_w_key,
        grad_w_value,
        grad_w_rel,
        grad_w_out,
        grad_w_up,
        grad_w_down,
        grad_bias_u,
        grad_bias_v,
        grad_gain_one,
        grad_shift_one,
        grad_gain_two,
        grad_shift_two,
        grad_bias_up,
        grad_bias_down,
    )


def solution(mesh):
    placed = (
        P("seq", "blk", None),
        P("seq", None),
        P("seq", "blk", None),
        P("seq", "blk", None),
        P(),
        P(),
        P(),
        P(),
        P(),
        P(),
        P(),
        P(),
        P(),
        P(),
        P(),
        P(),
        P(),
        P(),
        P(),
    )
    return jax.shard_map(
        shards_whole if fits_whole(mesh) else shards,
        mesh=mesh,
        in_specs=placed,
        out_specs=(
            P("seq", "blk", None),
            P("seq", "blk", None),
            P("seq", "blk", None),
            P(),
            P(),
            P(),
            P(),
            P(),
            P(),
            P(),
            P(),
            P(),
            P(),
            P(),
            P(),
            P(),
            P(),
            P(),
        ),
        check_vma=False,
    )
```

```python
import functools
import math
import types

import jax
import jax.numpy as jnp
import numpy as np
from jax import lax
from jax.experimental import pallas as pl
from jax.experimental.pallas import tpu as pltpu
from jax.sharding import PartitionSpec as P

F32, BF16 = jnp.float32, jnp.bfloat16
NT = (((1,), (1,)), ((), ()))


def mm(a, b):
    return jnp.dot(a, b, preferred_element_type=F32)


def mm_nt(a, b):
    return lax.dot_general(a, b, NT, preferred_element_type=F32)


def normalize(value):
    center = value - jnp.mean(value, axis=-1, keepdims=True)
    inv = lax.rsqrt(jnp.mean(center * center, axis=-1, keepdims=True) + 1e-05)
    return center * inv, inv


def norm_back(grad, unit, inv, gain):
    scaled = grad * gain
    along = jnp.mean(scaled * unit, axis=-1, keepdims=True)
    return inv * (scaled - jnp.mean(scaled, axis=-1, keepdims=True) - unit * along)


def gelu_parts(value):
    gate = 0.5 + 0.5 * lax.erf(value * 0.7071067811865476)
    return gate, gate + value * jnp.exp(-0.5 * value * value) * 0.3989422804014327


def ramp(shape, dim):
    return lax.broadcasted_iota(jnp.int32, shape, dim)


MESH = pl.DeviceIdType.MESH
HALF = 256
STEPS = 11
AXES = ("x", "y", "near", "far")
PIECES = tuple((1024, f"tile{n}") for n in range(4)) + ((512, "middle"),) + tuple((512, f"pair{n}") for n in range(4))
BASES = tuple(sum(rows for rows, unused in PIECES[:n]) for n in range(len(PIECES) + 1))
VECTORS = ("bias_u", "bias_v", "gain_one", "shift_one", "gain_two", "shift_two", "bias_up", "bias_down")
ORDERS = (
    (("y", "x", "near", "far"), ("x", "near", "y", "far")),
    (("near", "y", "far", "x"), ("x", "y", "near", "far")),
    (("near", "far", "y", "x"), ("y", "x", "near", "far")),
    (("far", "y", "x", "near"), ("y", "x", "near", "far")),
    (("y", "near", "x", "far"), ("x", "y", "far", "near")),
    (("y", "x", "near", "far"), ("y", "near", "x", "far")),
    (("near", "x", "y", "far"), ("x", "far", "y", "near")),
    (("y", "x", "near", "far"), ("near", "y", "x", "far")),
    (("y", "near", "x", "far"), ("near", "x", "y", "far")),
)
DURING = (
    ((0, 0),), ((1, 0),), ((2, 0),), ((0, 1), (3, 0)), ((1, 1),), ((2, 1), (3, 1), (4, 0)), ((0, 2),), (),
    (), ((1, 2), (4, 1)), ((5, 0),), (), ((2, 2),), (), ((5, 1),), ((6, 0),), ((0, 3), (3, 2)), (),
    ((1, 3), (6, 1)), ((4, 2),), ((7, 0), (2, 3)), (), ((5, 2),), ((0, 4), (7, 1)), ((1, 4), (3, 3)),
    ((8, 0), (4, 3), (6, 2)), ((2, 4),),
)
AFTER = (
    (8, 1), (0, 5), (7, 2), (5, 3), (1, 5), (3, 4), (4, 4), (6, 3), (2, 5), (8, 2), (7, 3), (5, 4), (0, 6),
    (1, 6), (6, 4), (3, 5), (4, 5), (8, 3), (2, 6), (0, 7), (7, 4), (5, 5), (8, 4), (1, 7), (6, 5), (3, 6),
    (4, 6), (2, 7), (0, 8), (7, 5), (5, 6), (8, 5), (6, 6), (3, 7), (1, 8), (4, 7), (2, 8), (7, 6), (0, 9),
    (6, 7), (5, 7), (8, 6), (3, 8), (4, 8), (0, 10), (1, 9), (2, 9), (7, 7), (8, 7), (5, 8), (1, 10), (6, 8),
    (2, 10), (4, 9), (7, 8), (3, 9), (8, 8), (4, 10), (5, 9), (6, 9), (3, 10), (7, 9), (5, 10), (8, 9),
    (6, 10), (7, 10), (8, 10),
)
BACK_DURING = (6, 8, 11, 13, 16, 21, 22, 24)
BACK_AFTER = (10, 14, 20, 45, 49, 55, 56, 61)


class Place:
    def __init__(self):
        self.s = lax.axis_index("seq")
        self.b = lax.axis_index("blk")
        self.z, self.y = self.s // 2, self.s % 2
        self.x, self.c = self.b // 2, self.b % 2
        self.bit = dict(x=self.x, y=self.y, near=self.z % 2, far=self.z // 2)

    def group(self, k):
        return (self.s, (self.b + k) % 4)

    def core(self):
        return (self.s, self.b + 1 - 2 * self.c)

    def across(self):
        return (self.s, self.b + 2 - 4 * self.x)

    def move(self, axis):
        reach = dict(x=(0, 2), y=(1, 0), near=(2, 0), far=(4, 0))[axis]
        turn = 1 - 2 * self.bit[axis]
        return reach[0] * turn, reach[1] * turn

    def step(self, zero, one):
        if zero == one:
            return self.pair(zero), self.bit[zero]
        away = [self.move(zero)[m] * (1 - self.c) + self.move(one)[m] * self.c for m in (0, 1)]
        bit = self.bit[zero] * (1 - self.c) + self.bit[one] * self.c
        return (self.s + away[0], self.b + away[1]), bit

    def pair(self, axis):
        away = self.move(axis)
        return (self.s + away[0], self.b + away[1])


def rows_at(start, size):
    return pl.ds(pl.multiple_of(start, 16), size)


def remote(src, dst, send, recv, to):
    return pltpu.make_async_remote_copy(src, dst, send, recv, device_id=to, device_id_type=MESH)


class Sum:
    def __init__(self, place, total, land, out, send, recv, store):
        self.p, self.g, self.land, self.out = place, total, land, out
        self.send, self.recv, self.store = send, recv, store
        self.steps = [[place.step(*axes) for axes in zip(*orders)] for orders in ORDERS]

    def offset(self, k, n):
        start = BASES[k] + self.p.c * (PIECES[k][0] // 2)
        for m in range(n):
            start = start + self.steps[k][m][1] * (PIECES[k][0] >> (m + 2))
        return start

    def lands(self, k, n, start=0, size=None):
        rows = PIECES[k][0] >> (n + 1)
        return self.land[n].at[rows_at((BASES[k] >> (n + 1)) + start, rows if size is None else size)]

    def copies(self, step, k, landing=False):
        p, g = self.p, self.g
        rows = PIECES[k][0]

        def copy(src, dst, to):
            return remote(src, dst, self.send.at[k, step], self.recv.at[k, step], to)

        if step == 0:
            half = rows // 2
            return copy(g.at[rows_at(BASES[k] + (1 - p.c) * half, half)], self.lands(k, 0), p.core())
        if step <= 4:
            to, bit = self.steps[k][step - 1]
            size = rows >> (step + 1)
            away = self.offset(k, step - 1) + (1 - bit) * size
            return copy(g.at[rows_at(away, size)], self.lands(k, step), to)
        if step <= 8:
            n = 8 - step
            to, bit = self.steps[k][n]
            size = rows >> (n + 2)
            dst = self.lands(k, n, (1 - bit if landing else bit) * size, size)
            src = self.lands(k, 3, bit * size, size) if n == 3 else self.lands(k, n + 1)
            return copy(src, dst, to)
        half = rows // 2
        span = BASES[k] + (1 - p.c if landing else p.c) * half
        return copy(self.lands(k, 0), self.out.at[rows_at(span, half)], p.core())

    def own(self, k):
        half = PIECES[k][0] // 2
        span = rows_at(BASES[k] + self.p.c * half, half)
        return pltpu.make_async_copy(self.lands(k, 0), self.out.at[span], self.store.at[k])

    def step(self, k, step):
        g = self.g
        rows = PIECES[k][0]
        if step > 0:
            self.copies(step - 1, k).wait_send()
            self.copies(step - 1, k, landing=True).wait_recv()
        if 1 <= step <= 4:
            span = rows_at(self.offset(k, step - 1), rows >> step)
            g[span] = (g[span].astype(F32) + self.lands(k, step - 1)[...].astype(F32)).astype(BF16)
        if step == 5:
            size = rows >> 5
            total = g[rows_at(self.offset(k, 4), size)].astype(F32) + self.lands(k, 4)[...].astype(F32)
            self.lands(k, 3, self.steps[k][3][1] * size, size)[...] = total.astype(BF16)
        if 6 <= step <= 8:
            n = 8 - step
            size = rows >> (n + 2)
            self.lands(k, n, self.steps[k][n][1] * size, size)[...] = self.lands(k, n + 1)[...]
        if step < STEPS - 1:
            self.copies(step, k).start()
        if step == STEPS - 2:
            self.own(k).start()
        if step == STEPS - 1:
            self.own(k).wait()


def pair_lanes(p, start=0, size=128):
    if isinstance(p, int):
        return slice(p * 128 + start, p * 128 + start + size)
    return pl.ds(pl.multiple_of(p * 128 + start, size), size)


def lane_mask(par):
    lane = ramp((1, 128), 1)
    return jnp.where((lane >= 64) == bool(par), 1.0, 0.0).astype(BF16)


def flip_matrix():
    return jnp.where(ramp((HALF, HALF), 0) + ramp((HALF, HALF), 1) == HALF - 1, 1.0, 0.0).astype(BF16)


def flip(flip_low, value):
    return jnp.concatenate(
        [mm(flip_low, value[r : r + HALF]) for r in range(0, value.shape[0], HALF)], axis=0
    ).astype(value.dtype)


def pool_matrix(end, length, first_place, places):
    place = (ramp((end.shape[0], places), 1) + first_place).astype(F32)
    return jnp.where((place < end) & (place >= end - length), 1.0, 0.0).astype(BF16)


def query_block(n, seg):
    keys = seg + HALF * (n + 1)
    return slice(n * HALF, (n + 1) * HALF), keys, 2 * seg - keys


def attend_pair(p, n, seg, r):
    lanes = pair_lanes(p)
    seen = ramp((HALF, HALF), 1) <= ramp((HALF, HALF), 0)
    lane = ramp((HALF, 128), 1)
    rows, keys, skip = query_block(n, seg)
    key, value, place = r.key[0:keys, lanes], r.value[0:keys, lanes], r.place[skip : 2 * seg, lanes]
    mixed, scale = [], []
    for par in range(2):
        keep = lane_mask(par)
        near = mm_nt(r.query_u[rows, lanes] * keep, key)
        far = mm_nt(r.query_v[rows, lanes] * keep, place)
        scores = near + pltpu.roll(far, keys - (HALF - 1), 1, stride=1, stride_axis=0)
        scores = jnp.concatenate(
            [scores[:, : keys - HALF], jnp.where(seen, scores[:, keys - HALF :], -1e30)], axis=1
        )
        expo = jnp.exp(scores - jnp.max(scores, axis=1, keepdims=True))
        probs = expo.astype(BF16)
        scale.append(1.0 / jnp.sum(expo, axis=1, keepdims=True))
        r.probs[2 * p + par, rows, 0:keys] = probs
        mixed.append(mm(probs, value))
    scale = jnp.where(lane >= 64, scale[1], scale[0])
    r.scale[rows, lanes] = scale
    r.mixed[rows, lanes] = (jnp.where(lane >= 64, mixed[1], mixed[0]) * scale).astype(BF16)


def attend_back_pair(p, seg, r, between):
    lanes = pair_lanes(p)
    flip_low = flip_matrix()
    scale = 0.125
    lane = ramp((HALF, 128), 1)
    sums = [None] * 6
    bias = []
    for n in range(seg // HALF):
        rows, keys, skip = query_block(n, seg)
        key, value, place = r.key[0:keys, lanes], r.value[0:keys, lanes], r.place[skip : 2 * seg, lanes]
        grad_u, grad_v = [], []
        for par in range(2):
            keep = lane_mask(par)
            feats = pair_lanes(p, par * 64, 64)
            probs = r.probs[2 * p + par, rows, 0:keys]
            turned = mm(flip_low, probs)
            grad_mixed = r.grad_mixed[rows, lanes] * keep
            delta = jnp.sum(grad_mixed.astype(F32) * r.mixed_flip[rows, lanes].astype(F32), axis=1, keepdims=True)
            grad_scores = turned * (mm_nt(grad_mixed, value) - delta)
            near = grad_scores.astype(BF16)
            far = pltpu.roll(grad_scores, 0, 1, stride=1, stride_axis=0).astype(BF16)
            grad_u.append(mm(near, key) * scale)
            grad_v.append(mm(far, place) * scale)
            now = (
                mm(r.query_u_t[feats, rows], near),
                mm(r.grad_mixed_t[feats, rows], probs),
                mm(r.query_v_t[feats, rows], far),
            )
            for m in range(3):
                slot = par * 3 + m
                if n == 0:
                    sums[slot] = now[m]
                else:
                    old, new = sums[slot], now[m]
                    cut = old.shape[1]
                    if m < 2:
                        sums[slot] = jnp.concatenate([new[:, :cut] + old, new[:, cut:]], axis=1)
                    else:
                        sums[slot] = jnp.concatenate([new[:, :-cut], new[:, -cut:] + old], axis=1)
            between()
        grad_u = jnp.where(lane >= 64, grad_u[1], grad_u[0])
        grad_v = jnp.where(lane >= 64, grad_v[1], grad_v[0])
        bias.append((jnp.sum(grad_u, axis=0, keepdims=True), jnp.sum(grad_v, axis=0, keepdims=True)))
        r.grad_query[rows, lanes] = mm(flip_low, (grad_u + grad_v).astype(BF16)).astype(BF16)
    r.small[0:1, lanes] = sum(b[0] for b in bias)
    r.small[1:2, lanes] = sum(b[1] for b in bias)
    for par in range(2):
        feats = pair_lanes(p, par * 64, 64)
        for m, out in enumerate((r.grad_key_t, r.grad_value_t, r.grad_place_t)):
            out[feats, :] = sums[par * 3 + m].astype(BF16)


def pair_weights(p, seg, r, base):
    lanes = pair_lanes(p)
    grad_query_t = r.grad_query[:, lanes].astype(F32).T.astype(BF16)
    r.total[rows_at(base, 128)] = mm(grad_query_t, r.normed[seg : 2 * seg]).astype(BF16)
    r.total[rows_at(base + 128, 128)] = mm(r.grad_key_t[lanes, :], r.normed[...]).astype(BF16)
    r.total[rows_at(base + 256, 128)] = mm(r.grad_value_t[lanes, :], r.normed[...]).astype(BF16)
    r.total[rows_at(base + 384, 128)] = mm(r.grad_place_t[lanes, :], r.table[...]).astype(BF16)


def project_places(r):
    r.place[...] = mm(r.table[...], r.w_rel[...]).astype(BF16)


def project_memory(rows, r):
    unit, unused = normalize(r.memory[rows].astype(F32))
    low = (unit * r.vec("gain_one") + r.vec("shift_one")).astype(BF16)
    r.normed[rows] = low
    r.key[rows] = mm(low, r.w_key[...]).astype(BF16)
    r.value[rows] = mm(low, r.w_value[...]).astype(BF16)


def project_segments(n, seg, r):
    rows, keys, unused = query_block(n, seg)
    places = slice(keys - HALF, keys)
    unit, unused = normalize(r.pooled[rows])
    low = (unit * r.vec("gain_one") + r.vec("shift_one")).astype(BF16)
    r.normed[places] = low
    query = mm(low, r.w_query[...])
    scale = 0.125
    r.query_u[rows] = (query + r.vec("bias_u")).astype(BF16) * jnp.asarray(scale, BF16)
    r.query_v[rows] = (query + r.vec("bias_v")).astype(BF16) * jnp.asarray(scale, BF16)
    r.key[places] = mm(low, r.w_key[...]).astype(BF16)
    r.value[places] = mm(low, r.w_value[...]).astype(BF16)


def feed_forward_in(n, r):
    rows = slice(n * HALF, (n + 1) * HALF)
    residual = r.pooled[rows] + mm(r.mixed[rows], r.w_out[...])
    r.residual[rows] = residual
    unit, unused = normalize(residual)
    r.normed_two[rows] = (unit * r.vec("gain_two") + r.vec("shift_two")).astype(BF16)

    for m in range(r.w_up.shape[1] // 512):
        cols = slice(m * 512, (m + 1) * 512)
        inner = mm(r.normed_two[rows], r.w_up[:, cols]) + r.bias_up[0:1, cols]
        gate, slope = gelu_parts(inner)
        r.hidden[rows, cols] = (inner * gate).astype(BF16)
        r.slope[rows, cols] = slope.astype(BF16)


def feed_forward_back(n, r):
    cols = slice(n * 512, (n + 1) * 512)
    r.total[rows_at(BASES[n], 512)] = mm(r.grad_down_t[...], r.hidden[:, cols]).astype(BF16)
    grad_hidden = mm_nt(r.grad_down[...], r.w_down[cols, :])
    low = (grad_hidden * r.slope[:, cols].astype(F32)).astype(BF16)
    r.grad_inner[:, cols] = low
    r.small[7 + n : 8 + n, :] = jnp.sum(low.astype(F32), axis=0, keepdims=True)
    r.total[rows_at(BASES[n] + 512, 512)] = mm(r.normed_two_t[...], low).astype(BF16)


def middle_back(r, base):
    grad_normed = mm_nt(r.grad_inner[...], r.w_up[...])
    unit, inv = normalize(r.residual[...])
    r.small[4:5, :] = jnp.sum(grad_normed * unit, axis=0, keepdims=True)
    r.small[5:6, :] = jnp.sum(grad_normed, axis=0, keepdims=True)
    grad = r.grad_output[...] + norm_back(grad_normed, unit, inv, r.vec("gain_two"))
    r.grad_residual[...] = grad
    low = grad.astype(BF16)
    mixed = r.mixed[...]
    r.total[rows_at(base, 512)] = mm(mixed.astype(F32).T.astype(BF16), low).astype(BF16)
    grad_mixed = (mm_nt(low, r.w_out[...]) * r.scale[...]).astype(BF16)
    r.grad_mixed_t[...] = grad_mixed.astype(F32).T.astype(BF16)
    flip_low = flip_matrix()
    r.grad_mixed[...] = flip(flip_low, grad_mixed)
    r.mixed_flip[...] = flip(flip_low, mixed)
    r.query_u_t[...] = flip(flip_low, r.query_u[...]).astype(F32).T.astype(BF16)
    r.query_v_t[...] = flip(flip_low, r.query_v[...]).astype(F32).T.astype(BF16)


def first_back(seg, r):
    grad_key = r.grad_key_t[...].astype(F32).T.astype(BF16)
    grad_value = r.grad_value_t[...].astype(F32).T.astype(BF16)
    grad_normed = mm_nt(r.grad_query[...], r.w_query[...])
    grad_normed += mm_nt(grad_key[seg:], r.w_key[...])
    grad_normed += mm_nt(grad_value[seg:], r.w_value[...])
    grad_mem = mm_nt(grad_key[:seg], r.w_key[...]) + mm_nt(grad_value[:seg], r.w_value[...])
    unit, inv = normalize(r.pooled[...])
    unit_mem, unused = normalize(r.memory[...].astype(F32))
    r.small[2:3, :] = jnp.sum(grad_normed * unit + grad_mem * unit_mem, axis=0, keepdims=True)
    r.small[3:4, :] = jnp.sum(grad_normed + grad_mem, axis=0, keepdims=True)
    return r.grad_residual[...] + norm_back(grad_normed, unit, inv, r.vec("gain_one"))


QUIET = 384
BACK_PARTS = 8
KEPT_DURING = (18, 9, 14)


def sine_table(count, width):
    freqs = np.exp(np.arange(width // 2) * (-2.0 * math.log(10000.0) / width))
    angles = np.arange(count)[::-1, None] * freqs[None, :]
    return np.concatenate([np.sin(angles), np.cos(angles)], axis=1).astype(jnp.bfloat16)


def span_columns(lengths, low):
    seg = lengths.shape[1]
    lens = lengths.astype(F32).astype(BF16)
    row, col = ramp((seg - low, seg), 0) + low, ramp((seg - low, seg), 1)
    upto = jnp.where(col <= row, 1.0, 0.0).astype(BF16)
    same = jnp.where(col == row, 1.0, 0.0).astype(BF16)
    return mm_nt(upto, lens), mm_nt(same, lens)


def column(value, n):
    return jnp.sum(jnp.where(ramp(value.shape, 1) == n, value, 0.0), axis=1, keepdims=True)


WEIGHTS = ("w_query", "w_key", "w_value", "w_rel", "w_out", "w_up", "w_down")


def layer_scratch(seg, width, hidden):
    def low(*shape):
        return pltpu.VMEM(shape, BF16)

    def full(*shape):
        return pltpu.VMEM(shape, F32)

    return dict(
        table=low(2 * seg, width),
        w_query=low(width, width),
        w_key=low(width, width),
        w_value=low(width, width),
        w_rel=low(width, width),
        w_out=low(width, width),
        w_up=low(width, hidden),
        w_down=low(hidden, width),
        memory=low(seg, width),
        pooled=full(seg, width),
        normed=low(2 * seg, width),
        key=low(2 * seg, width),
        value=low(2 * seg, width),
        place=low(2 * seg, width),
        query_u=low(seg, width),
        query_v=low(seg, width),
        mixed=low(seg, width),
        probs=low(8, seg, 2 * seg),
        scale=full(seg, width),
        residual=full(seg, width),
        normed_two=low(seg, width),
        normed_two_t=low(width, seg),
        hidden=low(seg, hidden),
        slope=low(seg, hidden),
        grad_inner=low(seg, hidden),
        grad_output=full(seg, width),
        grad_down=low(seg, width),
        grad_down_t=low(width, seg),
        low_rows=low(seg, width),
        out_rows=low(seg, width),
        chars_quiet=low(QUIET, width),
        chars_parts=low(7, seg - QUIET, width),
        grads_quiet=low(QUIET, width),
        grads_parts=low(7, seg - QUIET, width),
        total=low(BASES[-1], width),
        land_0=low(BASES[-1] >> 1, width),
        land_1=low(BASES[-1] >> 2, width),
        land_2=low(BASES[-1] >> 3, width),
        land_3=low(BASES[-1] >> 4, width),
        land_4=low(BASES[-1] >> 5, width),
        bias_up=full(1, hidden),
        vectors=full(16, width),
        small=full(16, width),
        small_sum=full(5, 16, width),
        small_land=full(5, 16, width),
        load_sem=pltpu.SemaphoreType.DMA((len(WEIGHTS) + 1,)),
        stage_sem=pltpu.SemaphoreType.DMA((2, 4)),
        memory_send=pltpu.SemaphoreType.DMA((4,)),
        memory_recv=pltpu.SemaphoreType.DMA((4,)),
        quiet_send=pltpu.SemaphoreType.DMA((2, 4, 2)),
        quiet_recv=pltpu.SemaphoreType.DMA((2, 2)),
        parts_send=pltpu.SemaphoreType.DMA((2, 3)),
        parts_recv=pltpu.SemaphoreType.DMA((2, 3)),
        kept_send=pltpu.SemaphoreType.DMA((6,)),
        kept_recv=pltpu.SemaphoreType.DMA((4,)),
        back_send=pltpu.SemaphoreType.DMA((2, 5)),
        back_recv=pltpu.SemaphoreType.DMA((2, 2, 4)),
        sum_send=pltpu.SemaphoreType.DMA((len(PIECES), STEPS - 1)),
        sum_recv=pltpu.SemaphoreType.DMA((len(PIECES), STEPS - 1)),
        small_send=pltpu.SemaphoreType.DMA((5,)),
        small_recv=pltpu.SemaphoreType.DMA((5,)),
        small_sem=pltpu.SemaphoreType.DMA,
        store_sem=pltpu.SemaphoreType.DMA((len(PIECES),)),
    )


class Rows:
    def __init__(self, r, place, way, source, stage, quiet, parts):
        self.r, self.p, self.way = r, place, way
        self.source, self.stage, self.quiet, self.parts = source, stage, quiet, parts

    def load(self, n):
        cols = pl.ds(pl.multiple_of(n * 512, 512), 512)
        return pltpu.make_async_copy(self.source.at[n], self.stage.at[:, cols], self.r.stage_sem.at[self.way, n])

    def quiet_copy(self, to, part):
        r = self.r
        span = pl.ds(0, HALF) if part == 0 else pl.ds(HALF, QUIET - HALF)
        src, dst = self.source.at[to, span], self.quiet.at[span]
        if to == 0:
            return pltpu.make_async_copy(src, dst, r.quiet_send.at[self.way, 0, part])
        return remote(src, dst, r.quiet_send.at[self.way, to, part], r.quiet_recv.at[self.way, part], (self.p.s, to))

    def start_quiet(self):
        @pl.when(self.p.b == 0)
        def _():
            for part in range(2):
                for to in (2, 3, 1, 0):
                    self.quiet_copy(to, part).start()

    def wait_quiet(self, part):
        @pl.when(self.p.b == 0)
        def _():
            self.quiet_copy(0, part).wait()

        @pl.when(self.p.b != 0)
        def _():
            self.quiet_copy(1, part).wait_recv()

    def parts_copy(self, n):
        src, dst, to = ((3, 1, self.p.core()), (4, 5, self.p.core()), (6, 2, self.p.across()))[n]
        return remote(
            self.parts.at[src],
            self.parts.at[dst],
            self.r.parts_send.at[self.way, n],
            self.r.parts_recv.at[self.way, n],
            to,
        )

    def part(self, to, ends, lens):
        self.load(to).wait()
        cols = pl.ds(pl.multiple_of(to * 512, 512), 512)
        chosen = pool_matrix(column(ends, to), column(lens, to), self.p.b * 512, 512)
        return mm(chosen, self.stage[:, cols])

    def start_parts(self, ends, lens):
        b, sibling, away = self.p.b, self.p.core()[1], self.p.across()[1]
        self.parts[4] = self.part(away + sibling - b, ends, lens).astype(BF16)
        self.parts_copy(1).start()
        self.parts[3] = self.part(sibling, ends, lens).astype(BF16)
        self.parts_copy(0).start()
        self.parts[6] = self.part(away, ends, lens).astype(BF16)
        self.parts[0] = self.part(b, ends, lens).astype(BF16)

    def join_parts(self):
        self.parts_copy(1).wait_recv()
        self.parts[6] = (self.parts[6].astype(F32) + self.parts[5].astype(F32)).astype(BF16)
        self.parts_copy(2).start()

    def wait_parts(self):
        self.parts_copy(0).wait_recv()
        self.parts_copy(2).wait_recv()
        return sum(self.parts[n].astype(F32) for n in range(3))

    def wait_sent(self):
        for n in range(3):
            self.parts_copy(n).wait_send()

        @pl.when(self.p.b == 0)
        def _():
            for part in range(2):
                for to in (1, 2, 3):
                    self.quiet_copy(to, part).wait_send()

    def back(self, rows, quiet_out, loud_out):
        self.rows, self.quiet_out, self.loud_out = rows, quiet_out, loud_out
        return self

    def loud_rows(self):
        return self.rows.at[pl.ds(QUIET, self.rows.shape[0] - QUIET)]

    def quiet_rows(self):
        return self.rows.at[pl.ds(0, QUIET)]

    def loud_copy(self, n, slot):
        r, p, way = self.r, self.p, self.way
        src = self.loud_out.at[slot] if n == 2 else self.loud_rows()
        to = p.across() if n == 1 else p.core()
        return remote(src, self.loud_out.at[slot], r.back_send.at[way, n], r.back_recv.at[way, 0, slot], to)

    def quiet_back(self, slot, start=0, size=QUIET):
        r, way = self.r, self.way
        span = pl.ds(start, size)
        return remote(
            self.rows.at[span],
            self.quiet_out.at[slot, span],
            r.back_send.at[way, 3],
            r.back_recv.at[way, 1, slot],
            (self.p.s, 0),
        )

    def own_copies(self):
        r, p, way = self.r, self.p, self.way
        loud = pltpu.make_async_copy(self.loud_rows(), self.loud_out.at[p.b], r.back_send.at[way, 4])
        quiet = pltpu.make_async_copy(self.quiet_rows(), self.quiet_out.at[0], r.back_send.at[way, 3])
        return loud, quiet

    def start_back(self):
        p = self.p
        loud, quiet = self.own_copies()
        self.loud_copy(1, p.b).start()
        self.loud_copy(0, p.b).start()
        pl.when(p.b == 0)(quiet.start)
        loud.start()

    def start_quiet_back(self, n):
        size = QUIET // BACK_PARTS
        pl.when(self.p.b != 0)(self.quiet_back(self.p.b, n * size, size).start)

    def pass_on(self):
        away = self.p.across()[1]
        self.loud_copy(1, away).wait_recv()
        self.loud_copy(2, away).start()

    def wait_back(self):
        p = self.p
        sibling, away = p.core()[1], p.across()[1]
        loud, quiet = self.own_copies()
        for n in (0, 1):
            self.loud_copy(n, p.b).wait_send()
        self.loud_copy(2, away).wait_send()
        loud.wait()
        pl.when(p.b != 0)(self.quiet_back(p.b).wait_send)
        pl.when(p.b == 0)(quiet.wait)
        self.loud_copy(0, sibling).wait_recv()
        self.loud_copy(2, away + sibling - p.b).wait_recv()

        @pl.when(p.b == 0)
        def _():
            for n in (1, 2, 3):
                self.quiet_back(n).wait_recv()


class Kept:
    def __init__(self, r, place, chars, kept):
        self.r, self.p, self.chars, self.kept = r, place, chars, kept
        self.count = kept.shape[1]

    def rows(self, to):
        return self.r.low_rows.at[pl.ds(to * self.count, self.count)]

    def late(self, to, slot):
        r = self.r
        return remote(self.rows(to), self.kept.at[slot], r.kept_send.at[4 + to - 2], r.kept_recv.at[slot], (self.p.s, to))

    def late_own(self, to):
        return pltpu.make_async_copy(self.rows(to), self.kept.at[to], self.r.kept_send.at[4 + to - 2])

    def early(self, slot):
        r = self.r
        src = self.chars.at[slot, pl.ds(self.count, self.count)]
        return remote(src, self.kept.at[slot], r.kept_send.at[slot], r.kept_recv.at[slot], (self.p.s, 1))

    def early_own(self, slot):
        src = self.chars.at[slot, pl.ds(0, self.count)]
        return pltpu.make_async_copy(src, self.kept.at[slot], self.r.kept_recv.at[slot])

    def start_late(self, to):
        pl.when(self.p.b != to)(self.late(to, self.p.b).start)
        pl.when(self.p.b == to)(self.late_own(to).start)

    def start_early(self):
        @pl.when(self.p.b == 0)
        def _():
            for slot in range(4):
                self.early_own(slot).start()
                self.early(slot).start()

    def wait(self):
        b = self.p.b

        @pl.when(b == 0)
        def _():
            for slot in range(4):
                self.early_own(slot).wait()
                self.early(slot).wait_send()

        @pl.when(b == 1)
        def _():
            for slot in range(4):
                self.early(slot).wait_recv()

        for to in (2, 3):
            pl.when(b != to)(self.late(to, b).wait_send)

            @pl.when(b == to)
            def _():
                self.late_own(to).wait()
                for slot in range(4):
                    if slot != to:
                        self.late(to, slot).wait_recv()


class Small:
    def __init__(self, r, place):
        self.r, self.p = r, place

    def source(self, step):
        return self.r.small if step == 0 else self.r.small_sum.at[step - 1]

    def copy(self, step):
        r, p = self.r, self.p
        to = p.core() if step == 0 else p.pair(AXES[step - 1])
        return remote(self.source(step), r.small_land.at[step], r.small_send.at[step], r.small_recv.at[step], to)

    def start(self, step):
        self.copy(step).start()

    def finish(self, step):
        self.copy(step).wait()
        self.r.small_sum[step] = self.source(step)[...] + self.r.small_land[step]


def layer_kernel(names, chars, lengths, memory, grad_out, *rest):
    count = len(VECTORS) + 1 + len(WEIGHTS)
    vectors, table, weights = rest[: len(VECTORS)], rest[len(VECTORS)], rest[len(VECTORS) + 1 : count]
    kept, out_quiet, out_loud, grad_quiet, grad_loud, total_out, small_out = rest[count : count + 7]
    r = types.SimpleNamespace(**dict(zip(names, rest[count + 7 :])))
    p = Place()
    seg, width = r.pooled.shape
    r.grad_residual, r.grad_mixed, r.grad_rows = r.grad_output, r.grad_down, r.normed_two
    for n, name in enumerate(("mixed_flip", "query_u_t", "query_v_t", "grad_mixed_t")):
        setattr(r, name, r.slope.at[:, n * width : (n + 1) * width])
    r.grad_key_t, r.grad_value_t = r.hidden.at[:, : 2 * seg], r.hidden.at[:, 2 * seg :]
    r.grad_place_t, r.grad_query = r.grad_inner.at[:, : 2 * seg], r.grad_inner.at[:, 2 * seg : 3 * seg]
    loads = [
        pltpu.make_async_copy(src, dst, r.load_sem.at[n])
        for n, (src, dst) in enumerate(
            zip((*weights, table), [getattr(r, name) for name in WEIGHTS] + [r.table])
        )
    ]
    chars_rows = Rows(r, p, 0, chars, r.hidden, r.chars_quiet, r.chars_parts).back(r.out_rows, out_quiet, out_loud)
    grads_rows = Rows(r, p, 1, grad_out, r.grad_inner, r.grads_quiet, r.grads_parts).back(
        r.grad_rows, grad_quiet, grad_loud
    )
    for n in range(4):
        chars_rows.load(n).start()
    for n in range(4):
        grads_rows.load(n).start()
    for copy in loads:
        copy.start()
    for n, name in enumerate(VECTORS):
        value = vectors[n][...].astype(F32)
        if name == "bias_up":
            r.bias_up[...] = value.reshape(1, -1)
        elif value.ndim == 2:
            r.vectors[n : n + 1, :] = jnp.concatenate([value[h : h + 1, :] for h in range(value.shape[0])], axis=1)
        else:
            r.vectors[n : n + 1, :] = value.reshape(1, -1)
    r.vec = lambda name: r.vectors[VECTORS.index(name) : VECTORS.index(name) + 1, :]

    barrier = pltpu.get_barrier_semaphore()
    others = [p.group(1), p.group(2), p.group(3), p.pair("y"), p.pair("near"), p.pair("far")]
    for other in others:
        pl.semaphore_signal(barrier, inc=1, device_id=other, device_id_type=MESH)
    pl.semaphore_wait(barrier, len(others))

    rows = memory.shape[1]

    def memory_copy(k, slot):
        to = (p.b + k) % 4
        return remote(
            memory.at[to], r.memory.at[rows_at(slot * rows, rows)], r.memory_send.at[k], r.memory_recv.at[slot], p.group(k)
        )

    own_memory = pltpu.make_async_copy(memory.at[p.b], r.memory.at[rows_at(p.b * rows, rows)], r.memory_send.at[0])
    for k in (2, 3, 1):
        memory_copy(k, p.b).start()
    own_memory.start()
    chars_rows.start_quiet()
    ends, lens = span_columns(lengths[...], QUIET)
    chars_rows.start_parts(ends, lens)
    for copy in loads:
        copy.wait()
    project_places(r)
    chars_rows.join_parts()
    grads_rows.start_quiet()
    grads_rows.start_parts(ends, lens)
    own_memory.wait()
    memory_copy(1, p.core()[1]).wait_recv()
    project_memory(rows_at(p.x * 2 * rows, 2 * rows), r)
    for slot in (2 * (1 - p.x), 2 * (1 - p.x) + 1):
        memory_copy(1, slot).wait_recv()
    project_memory(rows_at((1 - p.x) * 2 * rows, 2 * rows), r)
    own_lens = column(lens, p.b)

    def forward(block):
        project_segments(block, seg, r)
        for n in range(4):
            attend_pair(n, block, seg, r)
        feed_forward_in(block, r)

    chars_rows.wait_quiet(0)
    r.pooled[0:HALF] = chars_rows.quiet[0:HALF].astype(F32)
    forward(0)
    grads_rows.join_parts()
    chars_rows.wait_quiet(1)
    r.pooled[HALF:QUIET] = chars_rows.quiet[HALF:QUIET].astype(F32)
    r.pooled[QUIET:seg] = chars_rows.wait_parts() / own_lens
    r.low_rows[...] = r.pooled[...].astype(BF16)

    forward(1)
    grads_rows.wait_quiet(0)
    grads_rows.wait_quiet(1)
    r.grad_output[0:QUIET] = grads_rows.quiet[...].astype(F32)
    r.grad_output[QUIET:seg] = grads_rows.wait_parts()
    low = r.grad_output[...].astype(BF16)
    r.grad_down[...] = low
    r.grad_down_t[...] = low.astype(F32).T.astype(BF16)
    r.normed_two_t[...] = r.normed_two[...].astype(F32).T.astype(BF16)
    r.small[...] = jnp.zeros(r.small.shape, F32)
    r.small[6:7, :] = jnp.sum(low.astype(F32), axis=0, keepdims=True)

    land = [getattr(r, f"land_{n}") for n in range(5)]
    sums = Sum(p, r.total, land, total_out, r.sum_send, r.sum_recv, r.store_sem)
    turn = iter(range(len(DURING)))

    rows_kept = Kept(r, p, chars, kept)

    def between():
        n = next(turn)
        if n == KEPT_DURING[0]:
            rows_kept.start_early()
        for to in (2, 3):
            if n == KEPT_DURING[to - 1]:
                rows_kept.start_late(to)
        for part, at in enumerate(BACK_DURING):
            if at == n:
                chars_rows.start_quiet_back(part)
        for k, step in DURING[n]:
            sums.step(k, step)

    for n in range(4):
        feed_forward_back(n, r)
        between()
    r.out_rows[...] = (r.residual[...] + (mm(r.hidden[...], r.w_down[...]) + r.vec("bias_down"))).astype(BF16)
    chars_rows.start_back()
    between()
    middle_back(r, BASES[4])
    between()

    for n in range(4):
        attend_back_pair(n, seg, r, between)
        pair_weights(n, seg, r, BASES[5 + n])
        between()
    grad_pooled = first_back(seg, r)
    r.grad_rows[0:QUIET] = grad_pooled[:QUIET].astype(BF16)
    r.grad_rows[QUIET:seg] = (grad_pooled[QUIET:] / own_lens).astype(BF16)
    grads_rows.start_back()
    small = Small(r, p)
    small_store = pltpu.make_async_copy(r.small_sum.at[4], small_out, r.small_sem)
    small.start(0)
    between()
    every = len(AFTER) // 12
    for n, (k, step) in enumerate(AFTER):
        for part, at in enumerate(BACK_AFTER):
            if at == n:
                grads_rows.start_quiet_back(part)
        if n % every == every - 1 and n // every < 10:
            at = n // every
            if at % 2 == 1:
                small.finish(at // 2)
                if at // 2 < 4:
                    small.start(at // 2 + 1)
                else:
                    small_store.start()
            if at == 4:
                chars_rows.pass_on()
            if at == 8:
                grads_rows.pass_on()
        sums.step(k, step)
    for k in (1, 2, 3):
        memory_copy(k, p.b).wait_send()
    rows_kept.wait()
    chars_rows.wait_sent()
    grads_rows.wait_sent()
    chars_rows.wait_back()
    grads_rows.wait_back()
    small_store.wait()


def spread_kernel(
    lengths, chars, grad_out, rows, out_quiet, out_loud, grad_quiet, grad_loud, wide, flat, pairs, small,
    out_chars, grad_chars, kept, w_query, w_key, w_value, w_rel, w_out, w_up, w_down, bias_u, bias_v, *vectors,
):
    n = pl.program_id(0)
    b = lax.axis_index("blk")
    places = chars.shape[1]
    seg = lengths.shape[1]
    lens = lengths[...].astype(F32).astype(BF16)
    row, col = ramp((seg - QUIET, seg), 0) + QUIET, ramp((seg - QUIET, seg), 1)
    upto = jnp.where(col <= row, 1.0, 0.0).astype(BF16)
    same = jnp.where(col == row, 1.0, 0.0).astype(BF16)
    pick = ramp((lengths.shape[0], seg - QUIET), 0) == n
    end = jnp.sum(jnp.where(pick, mm_nt(lens, upto), 0.0), axis=0, keepdims=True)
    length = jnp.sum(jnp.where(pick, mm_nt(lens, same), 0.0), axis=0, keepdims=True)
    place = (ramp((places, seg - QUIET), 0) + b * places).astype(F32)
    chosen = jnp.where((place < end) & (place >= end - length), 1.0, 0.0).astype(BF16)
    first = b == 0
    kept[...] = rows[...]
    for source, quiet, loud, out in (
        (chars, out_quiet, out_loud, out_chars),
        (grad_out, grad_quiet, grad_loud, grad_chars),
    ):
        spread = mm(chosen, loud[0])
        whole = source[0].astype(F32) + spread
        out[0, QUIET:places] = whole[QUIET:].astype(out.dtype)
        out[0, 0:QUIET] = (whole[:QUIET] + jnp.where(first, quiet[0].astype(F32), 0.0)).astype(out.dtype)
    w_down[...] = wide[0:512].astype(F32).T
    w_up[...] = wide[512:1024].astype(F32)
    w_out[...] = flat[...].astype(F32)
    for m, out in enumerate((w_query, w_key, w_value, w_rel)):
        out[...] = pairs[m * 128 : (m + 1) * 128].astype(F32).T
    for m, out in enumerate((bias_u, bias_v)):
        out[...] = jnp.concatenate([small[m : m + 1, h * 64 : (h + 1) * 64] for h in range(8)], axis=0)
    for m, out in enumerate(vectors[:4]):
        out[...] = small[2 + m : 3 + m, :]
    vectors[4][...] = jnp.concatenate([small[m : m + 1, :] for m in range(7, 11)], axis=1)
    vectors[5][...] = small[6:7, :]


def shards_whole(
    chars, seg_lengths, memory, grad_out, w_query, w_key, w_value, w_rel, w_out, w_up, w_down,
    bias_u, bias_v, gain_one, shift_one, gain_two, shift_two, bias_up, bias_down,
):
    count, places, width = chars.shape
    seg, hidden = seg_lengths.shape[1], w_up.shape[1]
    rows = memory.shape[1]
    table = jnp.asarray(sine_table(2 * seg, width))
    scratch = layer_scratch(seg, width, hidden)
    anywhere, near = pl.BlockSpec(memory_space=pl.ANY), pl.BlockSpec(memory_space=pltpu.VMEM)
    loud = seg - QUIET
    kept, out_quiet, out_loud, grad_quiet, grad_loud, total, small = pl.pallas_call(
        functools.partial(layer_kernel, tuple(scratch)),
        out_shape=[
            jax.ShapeDtypeStruct((count, rows, width), BF16),
            jax.ShapeDtypeStruct((count, QUIET, width), BF16),
            jax.ShapeDtypeStruct((count, loud, width), BF16),
            jax.ShapeDtypeStruct((count, QUIET, width), BF16),
            jax.ShapeDtypeStruct((count, loud, width), BF16),
            jax.ShapeDtypeStruct((BASES[-1], width), BF16),
            jax.ShapeDtypeStruct((16, width), F32),
        ],
        in_specs=[anywhere, near, anywhere, anywhere] + [near] * len(VECTORS) + [anywhere] * 8,
        out_specs=[anywhere] * 7,
        scratch_shapes=list(scratch.values()),
        compiler_params=pltpu.CompilerParams(
            collective_id=0, has_side_effects=True, vmem_limit_bytes=VMEM_BYTES
        ),
        name="layer",
    )(
        chars, seg_lengths, memory, grad_out,
        bias_u, bias_v, gain_one, shift_one, gain_two, shift_two, bias_up, bias_down, table,
        w_query, w_key, w_value, w_rel, w_out, w_up, w_down,
    )

    def block(shape, index):
        return pl.BlockSpec(shape, index)

    def each(*shape):
        return block((1, *shape), lambda n: (n, 0, 0))

    def whole(*shape):
        return block(shape, lambda n: (0, 0))

    vector = [(1, width)] * 4 + [(1, hidden), (1, width)]
    outs = pl.pallas_call(
        spread_kernel,
        grid=(count,),
        out_shape=[
            jax.ShapeDtypeStruct(chars.shape, BF16),
            jax.ShapeDtypeStruct(chars.shape, F32),
            jax.ShapeDtypeStruct(memory.shape, BF16),
            *[jax.ShapeDtypeStruct((width, width), F32)] * 5,
            jax.ShapeDtypeStruct((width, hidden), F32),
            jax.ShapeDtypeStruct((hidden, width), F32),
            *[jax.ShapeDtypeStruct(bias_u.shape, F32)] * 2,
            *[jax.ShapeDtypeStruct(shape, F32) for shape in vector],
        ],
        in_specs=[
            whole(*seg_lengths.shape),
            each(places, width),
            each(places, width),
            each(rows, width),
            each(QUIET, width),
            each(loud, width),
            each(QUIET, width),
            each(loud, width),
            block((1024, width), lambda n: (n, 0)),
            block((128, width), lambda n: (BASES[4] // 128 + n, 0)),
            block((512, width), lambda n: (BASES[5] // 512 + n, 0)),
            whole(16, width),
        ],
        out_specs=[
            each(places, width),
            each(places, width),
            each(rows, width),
            *[block((width, 128), lambda n: (0, n))] * 4,
            block((128, width), lambda n: (n, 0)),
            block((width, 512), lambda n: (0, n)),
            block((512, width), lambda n: (n, 0)),
            *[whole(*bias_u.shape)] * 2,
            *[whole(*shape) for shape in vector],
        ],
        compiler_params=pltpu.CompilerParams(vmem_limit_bytes=VMEM_BYTES),
        name="spread",
    )(seg_lengths, chars, grad_out, kept, out_quiet, out_loud, grad_quiet, grad_loud, total, total, total, small)
    return (*outs[:12], *[v.reshape(-1) for v in outs[12:]])


VMEM_BYTES = 64 * 2**20 - 2**16


def fits_whole(mesh):
    return dict(mesh.shape) == {"seq": 8, "blk": 4}


def layer_norm(value, gain, shift):
    center = value - jnp.mean(value, axis=-1, keepdims=True)
    spread = jnp.mean(center * center, axis=-1, keepdims=True)
    return center * lax.rsqrt(spread + 1e-05) * gain + shift


def angle_tables(places, feature_width):
    freqs = jnp.exp(
        jnp.arange(feature_width // 2, dtype=jnp.float32)
        * (-2.0 * math.log(10000.0) / feature_width)
    )
    angles = places[:, None] * freqs[None, :]
    return (jnp.sin(angles), jnp.cos(angles))


def smooth_gate(value):
    return jax.nn.gelu(value, approximate=False)


def segment_ids(seg_end, char_places):
    return jnp.sum((seg_end[:, None, :] <= char_places[None, :, None]).astype(jnp.int32), axis=2)


def shards(
    chars,
    seg_lengths,
    memory,
    grad_out,
    w_query,
    w_key,
    w_value,
    w_rel,
    w_out,
    w_up,
    w_down,
    bias_u,
    bias_v,
    gain_one,
    shift_one,
    gain_two,
    shift_two,
    bias_up,
    bias_down,
):
    blk_index = lax.axis_index("blk")
    seq_local, char_rows, feature_width = chars.shape
    seg_rows = memory.shape[1]
    seg_count = seg_lengths.shape[1]
    head_count, head_dim = bias_u.shape
    half_width = feature_width // 2
    score_scale = head_dim ** (-0.5)
    seg_start = blk_index * seg_rows
    gain_one_f = gain_one.astype(jnp.float32)
    shift_one_f = shift_one.astype(jnp.float32)
    gain_two_f = gain_two.astype(jnp.float32)
    shift_two_f = shift_two.astype(jnp.float32)
    seg_end = jnp.cumsum(seg_lengths, axis=1)
    char_places = blk_index * char_rows + jnp.arange(char_rows, dtype=jnp.int32)
    segment = segment_ids(seg_end, char_places)
    own_lengths = lax.dynamic_slice_in_dim(seg_lengths, seg_start, seg_rows, 1).astype(jnp.float32)
    chars_f = chars.astype(jnp.float32)
    grad_f = grad_out.astype(jnp.float32)

    def full_table(values, ids):
        return jax.ops.segment_sum(values, ids, num_segments=seg_count)

    part_sums = jax.vmap(full_table)(chars_f, segment)
    pooled_sum = lax.psum_scatter(part_sums, "blk", scatter_dimension=1, tiled=True)
    pooled = pooled_sum / own_lengths[:, :, None]
    normed = layer_norm(pooled, gain_one_f, shift_one_f)
    normed_low = normed.astype(jnp.bfloat16)
    memory_f = memory.astype(jnp.float32)
    mem_low = layer_norm(memory_f, gain_one_f, shift_one_f).astype(jnp.bfloat16)
    query_rows = jnp.einsum("sid,de->sie", normed_low, w_query, preferred_element_type=jnp.float32)
    key_local = jnp.stack(
        [
            jnp.einsum("sid,de->sie", mem_low, w_key, preferred_element_type=jnp.float32),
            jnp.einsum("sid,de->sie", normed_low, w_key, preferred_element_type=jnp.float32),
        ],
        axis=1,
    ).astype(jnp.bfloat16)
    value_local = jnp.stack(
        [
            jnp.einsum("sid,de->sie", mem_low, w_value, preferred_element_type=jnp.float32),
            jnp.einsum("sid,de->sie", normed_low, w_value, preferred_element_type=jnp.float32),
        ],
        axis=1,
    ).astype(jnp.bfloat16)
    key_all, value_all = (
        lax.all_gather(key_local, "blk", axis=2, tiled=True),
        lax.all_gather(value_local, "blk", axis=2, tiled=True),
    )
    key_heads = key_all.reshape(seq_local, 2 * seg_count, head_count, head_dim)
    value_heads = value_all.reshape(seq_local, 2 * seg_count, head_count, head_dim)
    query_u = (
        (query_rows + bias_u.astype(jnp.float32).reshape(-1))
        .astype(jnp.bfloat16)
        .reshape(seq_local, seg_rows, head_count, head_dim)
    )
    query_v = (
        (query_rows + bias_v.astype(jnp.float32).reshape(-1))
        .astype(jnp.bfloat16)
        .reshape(seq_local, seg_rows, head_count, head_dim)
    )
    w_rel_heads = w_rel.reshape(feature_width, head_count, head_dim)
    rel_coeff = jnp.einsum(
        "sihe,fhe->sihf", query_v, w_rel_heads, preferred_element_type=jnp.float32
    )
    sin_all, cos_all = angle_tables(jnp.arange(2 * seg_count).astype(jnp.float32), feature_width)
    key_pos = jnp.concatenate([cos_all, sin_all], axis=-1).astype(jnp.bfloat16)
    query_index = seg_count + seg_start + jnp.arange(seg_rows, dtype=jnp.int32)
    sin_q, cos_q = angle_tables(query_index.astype(jnp.float32), feature_width)
    sin_query = sin_q[None, :, None, :]
    cos_query = cos_q[None, :, None, :]
    coeff_sin = rel_coeff[..., :half_width]
    coeff_cos = rel_coeff[..., half_width:]
    query_pos = jnp.concatenate(
        [
            coeff_sin * sin_query + coeff_cos * cos_query,
            coeff_cos * sin_query - coeff_sin * cos_query,
        ],
        axis=-1,
    ).astype(jnp.bfloat16)
    allowed = jnp.arange(2 * seg_count, dtype=jnp.int32)[None, :] <= query_index[:, None]

    def score_block():
        raw_scores = (
            jnp.einsum("sihe,sjhe->shij", query_u, key_heads, preferred_element_type=jnp.float32)
            + jnp.einsum("sihf,jf->shij", query_pos, key_pos, preferred_element_type=jnp.float32)
        ) * score_scale
        return jnp.where(allowed[None, None], raw_scores, -1e30)

    scores = score_block()
    row_top = jnp.max(scores, axis=-1, keepdims=True)
    expo = jnp.exp(scores - row_top)
    row_total = jnp.sum(expo, axis=-1, keepdims=True)
    log_total = row_top + jnp.log(row_total)
    att_probs = (expo / row_total).astype(jnp.bfloat16)
    att_mixed = jnp.einsum(
        "shij,sjhe->sihe", att_probs, value_heads, preferred_element_type=jnp.float32
    )
    mixed_low = att_mixed.reshape(seq_local, seg_rows, feature_width).astype(jnp.bfloat16)
    residual = pooled + jnp.einsum(
        "sid,de->sie", mixed_low, w_out, preferred_element_type=jnp.float32
    )
    normed_two = layer_norm(residual, gain_two_f, shift_two_f)
    two_low = normed_two.astype(jnp.bfloat16)
    ffn_inner = jnp.einsum(
        "sid,df->sif", two_low, w_up, preferred_element_type=jnp.float32
    ) + bias_up.astype(jnp.float32)
    hidden_low = smooth_gate(ffn_inner).astype(jnp.bfloat16)
    branch_out = jnp.einsum(
        "sif,fd->sid", hidden_low, w_down, preferred_element_type=jnp.float32
    ) + bias_down.astype(jnp.float32)
    out_low = (residual + branch_out).astype(jnp.bfloat16)
    rows_all = lax.all_gather(out_low, "blk", axis=1, tiled=True)
    picked = jnp.take_along_axis(rows_all, segment[:, :, None], axis=1)
    out_chars = (chars_f + picked.astype(jnp.float32)).astype(jnp.bfloat16)
    new_memory = pooled.astype(jnp.bfloat16)
    grad_table = jax.vmap(full_table)(grad_f, segment)
    grad_output = lax.psum_scatter(grad_table, "blk", scatter_dimension=1, tiled=True)
    grad_down_low = grad_output.astype(jnp.bfloat16)
    grad_bias_down = jnp.sum(grad_down_low.astype(jnp.float32), axis=(0, 1))
    grad_w_down = jnp.einsum(
        "sif,sid->fd", hidden_low, grad_down_low, preferred_element_type=jnp.float32
    )
    grad_hidden = jnp.einsum(
        "sid,fd->sif", grad_down_low, w_down, preferred_element_type=jnp.float32
    )
    unused_value, gate_back = jax.vjp(smooth_gate, ffn_inner)
    grad_inner = gate_back(grad_hidden)[0].astype(jnp.bfloat16)
    grad_bias_up = jnp.sum(grad_inner.astype(jnp.float32), axis=(0, 1))
    grad_w_up = jnp.einsum("sid,sif->df", two_low, grad_inner, preferred_element_type=jnp.float32)
    grad_normed_two = jnp.einsum(
        "sif,df->sid", grad_inner, w_up, preferred_element_type=jnp.float32
    )
    unused_norm, norm_two_back = jax.vjp(layer_norm, residual, gain_two_f, shift_two_f)
    grad_resid_norm, grad_gain_two, grad_shift_two = norm_two_back(grad_normed_two)
    grad_residual = grad_output + grad_resid_norm
    grad_att_low = grad_residual.astype(jnp.bfloat16)
    grad_w_out = jnp.einsum(
        "sid,sie->de", mixed_low, grad_att_low, preferred_element_type=jnp.float32
    )
    grad_mixed = jnp.einsum("sie,de->sid", grad_att_low, w_out, preferred_element_type=jnp.float32)
    grad_mixed = grad_mixed.astype(jnp.bfloat16).reshape(seq_local, seg_rows, head_count, head_dim)
    scores_again = score_block()
    probs_full = jnp.exp(scores_again - log_total)
    probs_low = probs_full.astype(jnp.bfloat16)
    grad_probs = jnp.einsum(
        "sihe,sjhe->shij", grad_mixed, value_heads, preferred_element_type=jnp.float32
    )
    grad_values = jnp.einsum(
        "shij,sihe->sjhe", probs_low, grad_mixed, preferred_element_type=jnp.float32
    )
    prob_delta = jnp.sum(probs_full * grad_probs, axis=-1, keepdims=True)
    grad_scores = (probs_full * (grad_probs - prob_delta)).astype(jnp.bfloat16)
    grad_query_u = (
        jnp.einsum("shij,sjhe->sihe", grad_scores, key_heads, preferred_element_type=jnp.float32)
        * score_scale
    )
    grad_keys = (
        jnp.einsum("shij,sihe->sjhe", grad_scores, query_u, preferred_element_type=jnp.float32)
        * score_scale
    )
    grad_query_pos = (
        jnp.einsum("shij,jf->sihf", grad_scores, key_pos, preferred_element_type=jnp.float32)
        * score_scale
    )
    grad_first = grad_query_pos[..., :half_width]
    grad_second = grad_query_pos[..., half_width:]
    grad_coeff = jnp.concatenate(
        [
            grad_first * sin_query - grad_second * cos_query,
            grad_first * cos_query + grad_second * sin_query,
        ],
        axis=-1,
    ).astype(jnp.bfloat16)
    grad_w_rel = jnp.einsum(
        "sihf,sihe->fhe", grad_coeff, query_v, preferred_element_type=jnp.float32
    ).reshape(feature_width, feature_width)
    grad_query_v = jnp.einsum(
        "sihf,fhe->sihe", grad_coeff, w_rel_heads, preferred_element_type=jnp.float32
    )
    grad_bias_u = jnp.sum(grad_query_u, axis=(0, 1))
    grad_bias_v = jnp.sum(grad_query_v, axis=(0, 1))
    grad_query = (
        (grad_query_u + grad_query_v)
        .reshape(seq_local, seg_rows, feature_width)
        .astype(jnp.bfloat16)
    )
    grad_w_query = jnp.einsum(
        "sid,sie->de", normed_low, grad_query, preferred_element_type=jnp.float32
    )
    grad_normed = jnp.einsum("sie,de->sid", grad_query, w_query, preferred_element_type=jnp.float32)
    key_share, value_share = (
        lax.psum_scatter(
            grad_keys.reshape(seq_local, 2, seg_count, feature_width),
            "blk",
            scatter_dimension=2,
            tiled=True,
        ),
        lax.psum_scatter(
            grad_values.reshape(seq_local, 2, seg_count, feature_width),
            "blk",
            scatter_dimension=2,
            tiled=True,
        ),
    )
    key_low = key_share.astype(jnp.bfloat16)
    value_low = value_share.astype(jnp.bfloat16)
    grad_w_key = jnp.einsum(
        "sid,sie->de", mem_low, key_low[:, 0], preferred_element_type=jnp.float32
    ) + jnp.einsum("sid,sie->de", normed_low, key_low[:, 1], preferred_element_type=jnp.float32)
    grad_w_value = jnp.einsum(
        "sid,sie->de", mem_low, value_low[:, 0], preferred_element_type=jnp.float32
    ) + jnp.einsum("sid,sie->de", normed_low, value_low[:, 1], preferred_element_type=jnp.float32)
    grad_normed = grad_normed + jnp.einsum(
        "sie,de->sid", key_low[:, 1], w_key, preferred_element_type=jnp.float32
    )
    grad_normed = grad_normed + jnp.einsum(
        "sie,de->sid", value_low[:, 1], w_value, preferred_element_type=jnp.float32
    )
    grad_mem_normed = jnp.einsum(
        "sie,de->sid", key_low[:, 0], w_key, preferred_element_type=jnp.float32
    ) + jnp.einsum("sie,de->sid", value_low[:, 0], w_value, preferred_element_type=jnp.float32)
    unused_one, norm_one_back = jax.vjp(layer_norm, pooled, gain_one_f, shift_one_f)
    grad_pooled_norm, grad_gain_one, grad_shift_one = norm_one_back(grad_normed)
    unused_mem, norm_mem_back = jax.vjp(layer_norm, memory_f, gain_one_f, shift_one_f)
    unused_grad, grad_gain_mem, grad_shift_mem = norm_mem_back(grad_mem_normed)
    grad_gain_one = grad_gain_one + grad_gain_mem
    grad_shift_one = grad_shift_one + grad_shift_mem
    grad_pooled = grad_residual + grad_pooled_norm
    grad_sum = grad_pooled / own_lengths[:, :, None]
    grad_sum_all = lax.all_gather(grad_sum, "blk", axis=1, tiled=True)
    grad_chars = grad_f + jnp.take_along_axis(grad_sum_all, segment[:, :, None], axis=1)
    (
        grad_w_query,
        grad_w_key,
        grad_w_value,
        grad_w_rel,
        grad_w_out,
        grad_w_up,
        grad_w_down,
        grad_bias_u,
        grad_bias_v,
        grad_gain_one,
        grad_shift_one,
        grad_gain_two,
        grad_shift_two,
        grad_bias_up,
        grad_bias_down,
    ) = lax.psum(
        (
            grad_w_query,
            grad_w_key,
            grad_w_value,
            grad_w_rel,
            grad_w_out,
            grad_w_up,
            grad_w_down,
            grad_bias_u,
            grad_bias_v,
            grad_gain_one,
            grad_shift_one,
            grad_gain_two,
            grad_shift_two,
            grad_bias_up,
            grad_bias_down,
        ),
        ("seq", "blk"),
    )
    return (
        out_chars,
        grad_chars,
        new_memory,
        grad_w_query,
        grad_w_key,
        grad_w_value,
        grad_w_rel,
        grad_w_out,
        grad_w_up,
        grad_w_down,
        grad_bias_u,
        grad_bias_v,
        grad_gain_one,
        grad_shift_one,
        grad_gain_two,
        grad_shift_two,
        grad_bias_up,
        grad_bias_down,
    )


def solution(mesh):
    placed = (
        P("seq", "blk", None),
        P("seq", None),
        P("seq", "blk", None),
        P("seq", "blk", None),
        P(),
        P(),
        P(),
        P(),
        P(),
        P(),
        P(),
        P(),
        P(),
        P(),
        P(),
        P(),
        P(),
        P(),
        P(),
    )
    return jax.shard_map(
        shards_whole if fits_whole(mesh) else shards,
        mesh=mesh,
        in_specs=placed,
        out_specs=(
            P("seq", "blk", None),
            P("seq", "blk", None),
            P("seq", "blk", None),
            P(),
            P(),
            P(),
            P(),
            P(),
            P(),
            P(),
            P(),
            P(),
            P(),
            P(),
            P(),
            P(),
            P(),
            P(),
        ),
        check_vma=False,
    )
```

```python
import functools
import math
import types

import jax
import jax.numpy as jnp
import numpy as np
from jax import lax
from jax.experimental import pallas as pl
from jax.experimental.pallas import tpu as pltpu
from jax.sharding import PartitionSpec as P

F32, BF16 = jnp.float32, jnp.bfloat16
NT = (((1,), (1,)), ((), ()))


def mm(a, b):
    return jnp.dot(a, b, preferred_element_type=F32)


def mm_nt(a, b):
    return lax.dot_general(a, b, NT, preferred_element_type=F32)


def normalize(value):
    center = value - jnp.mean(value, axis=-1, keepdims=True)
    inv = lax.rsqrt(jnp.mean(center * center, axis=-1, keepdims=True) + 1e-05)
    return center * inv, inv


def norm_back(grad, unit, inv, gain):
    scaled = grad * gain
    along = jnp.mean(scaled * unit, axis=-1, keepdims=True)
    return inv * (scaled - jnp.mean(scaled, axis=-1, keepdims=True) - unit * along)


def gelu_parts(value):
    gate = 0.5 + 0.5 * lax.erf(value * 0.7071067811865476)
    return gate, gate + value * jnp.exp(-0.5 * value * value) * 0.3989422804014327


def ramp(shape, dim):
    return lax.broadcasted_iota(jnp.int32, shape, dim)


MESH = pl.DeviceIdType.MESH
HALF = 256
STEPS = 11
AXES = ("x", "y", "near", "far")
PIECES = tuple((1024, f"tile{n}") for n in range(4)) + ((512, "middle"),) + tuple((512, f"pair{n}") for n in range(4))
BASES = tuple(sum(rows for rows, unused in PIECES[:n]) for n in range(len(PIECES) + 1))
VECTORS = ("bias_u", "bias_v", "gain_one", "shift_one", "gain_two", "shift_two", "bias_up", "bias_down")
ORDERS = (
    (("y", "x", "near", "far"), ("x", "near", "y", "far")),
    (("near", "y", "far", "x"), ("x", "y", "near", "far")),
    (("near", "far", "y", "x"), ("y", "x", "near", "far")),
    (("far", "y", "x", "near"), ("y", "x", "near", "far")),
    (("y", "near", "x", "far"), ("x", "y", "far", "near")),
    (("y", "x", "near", "far"), ("y", "near", "x", "far")),
    (("near", "x", "y", "far"), ("x", "far", "y", "near")),
    (("y", "x", "near", "far"), ("near", "y", "x", "far")),
    (("y", "near", "x", "far"), ("near", "x", "y", "far")),
)
DURING = (
    ((0, 0),), ((1, 0),), ((2, 0),), ((0, 1), (3, 0)), ((1, 1),), ((2, 1), (3, 1), (4, 0)), ((0, 2),), (),
    (), ((1, 2), (4, 1)), ((5, 0),), (), ((2, 2),), (), ((5, 1),), ((6, 0),), ((0, 3), (3, 2)), (),
    ((1, 3), (6, 1)), ((4, 2),), ((7, 0), (2, 3)), (), ((5, 2),), ((0, 4), (7, 1)), ((1, 4), (3, 3)),
    ((8, 0), (4, 3), (6, 2)), ((2, 4),),
)
AFTER = (
    (8, 1), (0, 5), (7, 2), (5, 3), (1, 5), (3, 4), (4, 4), (6, 3), (2, 5), (8, 2), (7, 3), (5, 4), (0, 6),
    (1, 6), (6, 4), (3, 5), (4, 5), (8, 3), (2, 6), (0, 7), (7, 4), (5, 5), (8, 4), (1, 7), (6, 5), (3, 6),
    (4, 6), (2, 7), (0, 8), (7, 5), (5, 6), (8, 5), (6, 6), (3, 7), (1, 8), (4, 7), (2, 8), (7, 6), (0, 9),
    (6, 7), (5, 7), (8, 6), (3, 8), (4, 8), (0, 10), (1, 9), (2, 9), (7, 7), (8, 7), (5, 8), (1, 10), (6, 8),
    (2, 10), (4, 9), (7, 8), (3, 9), (8, 8), (4, 10), (5, 9), (6, 9), (3, 10), (7, 9), (5, 10), (8, 9),
    (6, 10), (7, 10), (8, 10),
)
BACK_DURING = (6, 8, 11, 13, 16, 21, 22, 24)
BACK_AFTER = (10, 14, 20, 45, 49, 55, 56, 61)


class Place:
    def __init__(self):
        self.s = lax.axis_index("seq")
        self.b = lax.axis_index("blk")
        self.z, self.y = self.s // 2, self.s % 2
        self.x, self.c = self.b // 2, self.b % 2
        self.bit = dict(x=self.x, y=self.y, near=self.z % 2, far=self.z // 2)

    def group(self, k):
        return (self.s, (self.b + k) % 4)

    def core(self):
        return (self.s, self.b + 1 - 2 * self.c)

    def across(self):
        return (self.s, self.b + 2 - 4 * self.x)

    def move(self, axis):
        reach = dict(x=(0, 2), y=(1, 0), near=(2, 0), far=(4, 0))[axis]
        turn = 1 - 2 * self.bit[axis]
        return reach[0] * turn, reach[1] * turn

    def step(self, zero, one):
        if zero == one:
            return self.pair(zero), self.bit[zero]
        away = [self.move(zero)[m] * (1 - self.c) + self.move(one)[m] * self.c for m in (0, 1)]
        bit = self.bit[zero] * (1 - self.c) + self.bit[one] * self.c
        return (self.s + away[0], self.b + away[1]), bit

    def pair(self, axis):
        away = self.move(axis)
        return (self.s + away[0], self.b + away[1])


def rows_at(start, size):
    return pl.ds(pl.multiple_of(start, 16), size)


def remote(src, dst, send, recv, to):
    return pltpu.make_async_remote_copy(src, dst, send, recv, device_id=to, device_id_type=MESH)


class Sum:
    def __init__(self, place, total, land, out, send, recv, store):
        self.p, self.g, self.land, self.out = place, total, land, out
        self.send, self.recv, self.store = send, recv, store
        self.steps = [[place.step(*axes) for axes in zip(*orders)] for orders in ORDERS]

    def offset(self, k, n):
        start = BASES[k] + self.p.c * (PIECES[k][0] // 2)
        for m in range(n):
            start = start + self.steps[k][m][1] * (PIECES[k][0] >> (m + 2))
        return start

    def lands(self, k, n, start=0, size=None):
        rows = PIECES[k][0] >> (n + 1)
        return self.land[n].at[rows_at((BASES[k] >> (n + 1)) + start, rows if size is None else size)]

    def copies(self, step, k, landing=False):
        p, g = self.p, self.g
        rows = PIECES[k][0]

        def copy(src, dst, to):
            return remote(src, dst, self.send.at[k], self.recv.at[k, step], to)

        if step == 0:
            half = rows // 2
            return copy(g.at[rows_at(BASES[k] + (1 - p.c) * half, half)], self.lands(k, 0), p.core())
        if step <= 4:
            to, bit = self.steps[k][step - 1]
            size = rows >> (step + 1)
            away = self.offset(k, step - 1) + (1 - bit) * size
            return copy(g.at[rows_at(away, size)], self.lands(k, step), to)
        if step <= 8:
            n = 8 - step
            to, bit = self.steps[k][n]
            size = rows >> (n + 2)
            dst = self.lands(k, n, (1 - bit if landing else bit) * size, size)
            src = self.lands(k, 3, bit * size, size) if n == 3 else self.lands(k, n + 1)
            return copy(src, dst, to)
        half = rows // 2
        span = BASES[k] + (1 - p.c if landing else p.c) * half
        return copy(self.lands(k, 0), self.out.at[rows_at(span, half)], p.core())

    def own(self, k):
        half = PIECES[k][0] // 2
        span = rows_at(BASES[k] + self.p.c * half, half)
        return pltpu.make_async_copy(self.lands(k, 0), self.out.at[span], self.store.at[k])

    def add(self, k, n, start, size):
        span = rows_at(self.offset(k, n) + start, size)
        self.g[span] = (self.g[span].astype(F32) + self.lands(k, n, start, size)[...].astype(F32)).astype(BF16)

    def step(self, k, step):
        g = self.g
        rows = PIECES[k][0]
        if step > 0:
            self.copies(step - 1, k).wait_send()
            self.copies(step - 1, k, landing=True).wait_recv()
        if 1 <= step <= 4:
            half = rows >> (step + 1)
            bit = self.steps[k][step - 1][1]
            self.add(k, step - 1, (1 - bit) * half, half)
            self.copies(step, k).start()
            self.add(k, step - 1, bit * half, half)
        elif step == 5:
            size = rows >> 5
            total = g[rows_at(self.offset(k, 4), size)].astype(F32) + self.lands(k, 4)[...].astype(F32)
            self.lands(k, 3, self.steps[k][3][1] * size, size)[...] = total.astype(BF16)
            self.copies(step, k).start()
        elif step < STEPS - 1:
            self.copies(step, k).start()
        if 6 <= step <= 8:
            n = 8 - step
            size = rows >> (n + 2)
            self.lands(k, n, self.steps[k][n][1] * size, size)[...] = self.lands(k, n + 1)[...]
        if step == STEPS - 2:
            self.own(k).start()
        if step == STEPS - 1:
            self.own(k).wait()


def pair_lanes(p, start=0, size=128):
    if isinstance(p, int):
        return slice(p * 128 + start, p * 128 + start + size)
    return pl.ds(pl.multiple_of(p * 128 + start, size), size)


def lane_mask(par):
    lane = ramp((1, 128), 1)
    return jnp.where((lane >= 64) == bool(par), 1.0, 0.0).astype(BF16)


def flip_matrix():
    return jnp.where(ramp((HALF, HALF), 0) + ramp((HALF, HALF), 1) == HALF - 1, 1.0, 0.0).astype(BF16)


def flip(flip_low, value):
    return jnp.concatenate(
        [mm(flip_low, value[r : r + HALF]) for r in range(0, value.shape[0], HALF)], axis=0
    ).astype(value.dtype)


def pool_matrix(end, length, first_place, places):
    place = (ramp((end.shape[0], places), 1) + first_place).astype(F32)
    return jnp.where((place < end) & (place >= end - length), 1.0, 0.0).astype(BF16)


def query_block(n, seg):
    keys = seg + HALF * (n + 1)
    return slice(n * HALF, (n + 1) * HALF), keys, 2 * seg - keys


def attend(n, seg, r):
    seen = ramp((HALF, HALF), 1) <= ramp((HALF, HALF), 0)
    lane = ramp((HALF, 128), 1)
    rows, keys, skip = query_block(n, seg)

    def products(head):
        lanes, keep = pair_lanes(head // 2), lane_mask(head % 2)
        near = mm_nt(r.query_u[rows, lanes] * keep, r.key[0:keys, lanes])
        return near, mm_nt(r.query_v[rows, lanes] * keep, r.place[skip : 2 * seg, lanes])

    ahead = products(0)
    for p in range(4):
        mixed, scale = [], []
        for head in (2 * p, 2 * p + 1):
            near, far = ahead
            ahead = products(head + 1) if head < 7 else None
            scores = near + pltpu.roll(far, keys - (HALF - 1), 1, stride=1, stride_axis=0)
            scores = jnp.concatenate(
                [scores[:, : keys - HALF], jnp.where(seen, scores[:, keys - HALF :], -1e30)], axis=1
            )
            expo = jnp.exp(scores - jnp.max(scores, axis=1, keepdims=True))
            probs = expo.astype(BF16)
            r.probs[head, rows, 0:keys] = probs
            mixed.append(mm(probs, r.value[0:keys, pair_lanes(p)]))
            scale.append(1.0 / jnp.sum(expo, axis=1, keepdims=True))
        scale = jnp.where(lane >= 64, scale[1], scale[0])
        r.scale[rows, pair_lanes(p)] = scale
        r.mixed[rows, pair_lanes(p)] = (jnp.where(lane >= 64, mixed[1], mixed[0]) * scale).astype(BF16)


def attend_back_pair(p, seg, r, between):
    lanes = pair_lanes(p)
    flip_low = flip_matrix()
    scale = 0.125
    lane = ramp((HALF, 128), 1)
    sums = [None] * 6
    bias = []
    for n in range(seg // HALF):
        rows, keys, skip = query_block(n, seg)
        key, value, place = r.key[0:keys, lanes], r.value[0:keys, lanes], r.place[skip : 2 * seg, lanes]
        grad_u, grad_v = [], []
        for par in range(2):
            keep = lane_mask(par)
            feats = pair_lanes(p, par * 64, 64)
            probs = r.probs[2 * p + par, rows, 0:keys]
            turned = mm(flip_low, probs)
            grad_mixed = r.grad_mixed[rows, lanes] * keep
            delta = jnp.sum(grad_mixed.astype(F32) * r.mixed_flip[rows, lanes].astype(F32), axis=1, keepdims=True)
            grad_scores = turned * (mm_nt(grad_mixed, value) - delta)
            near = grad_scores.astype(BF16)
            far = pltpu.roll(grad_scores, 0, 1, stride=1, stride_axis=0).astype(BF16)
            grad_u.append(mm(near, key) * scale)
            grad_v.append(mm(far, place) * scale)
            now = (
                mm(r.query_u_t[feats, rows], near),
                mm(r.grad_mixed_t[feats, rows], probs),
                mm(r.query_v_t[feats, rows], far),
            )
            for m in range(3):
                slot = par * 3 + m
                if n == 0:
                    sums[slot] = now[m]
                else:
                    old, new = sums[slot], now[m]
                    cut = old.shape[1]
                    if m < 2:
                        sums[slot] = jnp.concatenate([new[:, :cut] + old, new[:, cut:]], axis=1)
                    else:
                        sums[slot] = jnp.concatenate([new[:, :-cut], new[:, -cut:] + old], axis=1)
            between(n * 2 + par)
        grad_u = jnp.where(lane >= 64, grad_u[1], grad_u[0])
        grad_v = jnp.where(lane >= 64, grad_v[1], grad_v[0])
        bias.append((jnp.sum(grad_u, axis=0, keepdims=True), jnp.sum(grad_v, axis=0, keepdims=True)))
        r.grad_query[rows, lanes] = mm(flip_low, (grad_u + grad_v).astype(BF16)).astype(BF16)
    r.small[0:1, lanes] = sum(b[0] for b in bias)
    r.small[1:2, lanes] = sum(b[1] for b in bias)
    for par in range(2):
        feats = pair_lanes(p, par * 64, 64)
        for m, out in enumerate((r.grad_key_t, r.grad_value_t, r.grad_place_t)):
            out[feats, :] = sums[par * 3 + m].astype(BF16)


def pair_weights(p, seg, r, base):
    lanes = pair_lanes(p)
    grad_query_t = r.grad_query[:, lanes].astype(F32).T.astype(BF16)
    r.total[rows_at(base, 128)] = mm(grad_query_t, r.normed[seg : 2 * seg]).astype(BF16)
    r.total[rows_at(base + 128, 128)] = mm(r.grad_key_t[lanes, :], r.normed[...]).astype(BF16)
    r.total[rows_at(base + 256, 128)] = mm(r.grad_value_t[lanes, :], r.normed[...]).astype(BF16)
    r.total[rows_at(base + 384, 128)] = mm(r.grad_place_t[lanes, :], r.table[...]).astype(BF16)


def project_places(r):
    r.place[...] = mm(r.table[...], r.w_rel[...]).astype(BF16)


def project_memory(rows, r):
    unit, unused = normalize(r.memory[rows].astype(F32))
    low = (unit * r.vec("gain_one") + r.vec("shift_one")).astype(BF16)
    r.normed[rows] = low
    r.key[rows] = mm(low, r.w_key[...]).astype(BF16)
    r.value[rows] = mm(low, r.w_value[...]).astype(BF16)


def project_segments(n, seg, r):
    rows, keys, unused = query_block(n, seg)
    places = slice(keys - HALF, keys)
    unit, unused = normalize(r.pooled[rows])
    low = (unit * r.vec("gain_one") + r.vec("shift_one")).astype(BF16)
    r.normed[places] = low
    query = mm(low, r.w_query[...])
    scale = 0.125
    r.query_u[rows] = (query + r.vec("bias_u")).astype(BF16) * jnp.asarray(scale, BF16)
    r.query_v[rows] = (query + r.vec("bias_v")).astype(BF16) * jnp.asarray(scale, BF16)
    r.key[places] = mm(low, r.w_key[...]).astype(BF16)
    r.value[places] = mm(low, r.w_value[...]).astype(BF16)


def feed_forward_in(n, r):
    rows = slice(n * HALF, (n + 1) * HALF)
    residual = r.pooled[rows] + mm(r.mixed[rows], r.w_out[...])
    r.residual[rows] = residual
    unit, unused = normalize(residual)
    r.normed_two[rows] = (unit * r.vec("gain_two") + r.vec("shift_two")).astype(BF16)

    for m in range(r.w_up.shape[1] // 512):
        cols = slice(m * 512, (m + 1) * 512)
        inner = mm(r.normed_two[rows], r.w_up[:, cols]) + r.bias_up[0:1, cols]
        gate, slope = gelu_parts(inner)
        r.hidden[rows, cols] = (inner * gate).astype(BF16)
        r.slope[rows, cols] = slope.astype(BF16)


def feed_forward_back(n, r):
    cols = slice(n * 512, (n + 1) * 512)
    r.total[rows_at(BASES[n], 512)] = mm(r.grad_down_t[...], r.hidden[:, cols]).astype(BF16)
    grad_hidden = mm_nt(r.grad_down[...], r.w_down[cols, :])
    low = (grad_hidden * r.slope[:, cols].astype(F32)).astype(BF16)
    r.grad_inner[:, cols] = low
    r.small[7 + n : 8 + n, :] = jnp.sum(low.astype(F32), axis=0, keepdims=True)
    r.total[rows_at(BASES[n] + 512, 512)] = mm(r.normed_two_t[...], low).astype(BF16)


def middle_back(r, base):
    grad_normed = mm_nt(r.grad_inner[...], r.w_up[...])
    unit, inv = normalize(r.residual[...])
    r.small[4:5, :] = jnp.sum(grad_normed * unit, axis=0, keepdims=True)
    r.small[5:6, :] = jnp.sum(grad_normed, axis=0, keepdims=True)
    grad = r.grad_output[...] + norm_back(grad_normed, unit, inv, r.vec("gain_two"))
    r.grad_residual[...] = grad
    low = grad.astype(BF16)
    mixed = r.mixed[...]
    r.total[rows_at(base, 512)] = mm(mixed.astype(F32).T.astype(BF16), low).astype(BF16)
    grad_mixed = (mm_nt(low, r.w_out[...]) * r.scale[...]).astype(BF16)
    r.grad_mixed_t[...] = grad_mixed.astype(F32).T.astype(BF16)
    flip_low = flip_matrix()
    r.grad_mixed[...] = flip(flip_low, grad_mixed)
    r.mixed_flip[...] = flip(flip_low, mixed)
    r.query_u_t[...] = flip(flip_low, r.query_u[...]).astype(F32).T.astype(BF16)
    r.query_v_t[...] = flip(flip_low, r.query_v[...]).astype(F32).T.astype(BF16)


def first_back(seg, r):
    grad_key = r.grad_key_t[...].astype(F32).T.astype(BF16)
    grad_value = r.grad_value_t[...].astype(F32).T.astype(BF16)
    grad_normed = mm_nt(r.grad_query[...], r.w_query[...])
    grad_normed += mm_nt(grad_key[seg:], r.w_key[...])
    grad_normed += mm_nt(grad_value[seg:], r.w_value[...])
    grad_mem = mm_nt(grad_key[:seg], r.w_key[...]) + mm_nt(grad_value[:seg], r.w_value[...])
    unit, inv = normalize(r.pooled[...])
    unit_mem, unused = normalize(r.memory[...].astype(F32))
    r.small[2:3, :] = jnp.sum(grad_normed * unit + grad_mem * unit_mem, axis=0, keepdims=True)
    r.small[3:4, :] = jnp.sum(grad_normed + grad_mem, axis=0, keepdims=True)
    return r.grad_residual[...] + norm_back(grad_normed, unit, inv, r.vec("gain_one"))


QUIET = 384
BACK_PARTS = 8
KEPT_DURING = (18, 9, 14)


def sine_table(count, width):
    freqs = np.exp(np.arange(width // 2) * (-2.0 * math.log(10000.0) / width))
    angles = np.arange(count)[::-1, None] * freqs[None, :]
    return np.concatenate([np.sin(angles), np.cos(angles)], axis=1).astype(jnp.bfloat16)


def span_columns(lengths, low):
    seg = lengths.shape[1]
    lens = lengths.astype(F32).astype(BF16)
    row, col = ramp((seg - low, seg), 0) + low, ramp((seg - low, seg), 1)
    upto = jnp.where(col <= row, 1.0, 0.0).astype(BF16)
    same = jnp.where(col == row, 1.0, 0.0).astype(BF16)
    return mm_nt(upto, lens), mm_nt(same, lens)


def column(value, n):
    return jnp.sum(jnp.where(ramp(value.shape, 1) == n, value, 0.0), axis=1, keepdims=True)


WEIGHTS = ("w_query", "w_key", "w_value", "w_rel", "w_out", "w_up", "w_down")


def layer_scratch(seg, width, hidden):
    def low(*shape):
        return pltpu.VMEM(shape, BF16)

    def full(*shape):
        return pltpu.VMEM(shape, F32)

    return dict(
        table=low(2 * seg, width),
        w_query=low(width, width),
        w_key=low(width, width),
        w_value=low(width, width),
        w_rel=low(width, width),
        w_out=low(width, width),
        w_up=low(width, hidden),
        w_down=low(hidden, width),
        memory=low(seg, width),
        pooled=full(seg, width),
        normed=low(2 * seg, width),
        key=low(2 * seg, width),
        value=low(2 * seg, width),
        place=low(2 * seg, width),
        query_u=low(seg, width),
        query_v=low(seg, width),
        mixed=low(seg, width),
        probs=low(8, seg, 2 * seg),
        scale=full(seg, width),
        residual=full(seg, width),
        normed_two=low(seg, width),
        normed_two_t=low(width, seg),
        hidden=low(seg, hidden),
        slope=low(seg, hidden),
        grad_inner=low(seg, hidden),
        grad_output=full(seg, width),
        grad_down=low(seg, width),
        grad_down_t=low(width, seg),
        low_rows=low(seg, width),
        out_rows=low(seg, width),
        chars_quiet=low(QUIET, width),
        chars_parts=low(7, seg - QUIET, width),
        grads_quiet=low(QUIET, width),
        grads_parts=low(7, seg - QUIET, width),
        total=low(BASES[-1], width),
        land_0=low(BASES[-1] >> 1, width),
        land_1=low(BASES[-1] >> 2, width),
        land_2=low(BASES[-1] >> 3, width),
        land_3=low(BASES[-1] >> 4, width),
        land_4=low(BASES[-1] >> 5, width),
        bias_up=full(1, hidden),
        vectors=full(16, width),
        small=full(16, width),
        small_sum=full(5, 16, width),
        small_land=full(5, 16, width),
        load_sem=pltpu.SemaphoreType.DMA((len(WEIGHTS) + 1,)),
        stage_sem=pltpu.SemaphoreType.DMA((2, 4)),
        memory_send=pltpu.SemaphoreType.DMA((4,)),
        memory_recv=pltpu.SemaphoreType.DMA((4,)),
        quiet_send=pltpu.SemaphoreType.DMA((2, 4, 2)),
        quiet_recv=pltpu.SemaphoreType.DMA((2, 2)),
        parts_send=pltpu.SemaphoreType.DMA((2, 3)),
        parts_recv=pltpu.SemaphoreType.DMA((2, 3)),
        kept_send=pltpu.SemaphoreType.DMA((6,)),
        kept_recv=pltpu.SemaphoreType.DMA((4,)),
        back_send=pltpu.SemaphoreType.DMA((2, 5)),
        back_recv=pltpu.SemaphoreType.DMA((2, 2, 4)),
        sum_send=pltpu.SemaphoreType.DMA((len(PIECES),)),
        sum_recv=pltpu.SemaphoreType.DMA((len(PIECES), STEPS - 1)),
        small_send=pltpu.SemaphoreType.DMA((5,)),
        small_recv=pltpu.SemaphoreType.DMA((5,)),
        small_sem=pltpu.SemaphoreType.DMA,
        store_sem=pltpu.SemaphoreType.DMA((len(PIECES),)),
    )


class Rows:
    def __init__(self, r, place, way, source, stage, quiet, parts):
        self.r, self.p, self.way = r, place, way
        self.source, self.stage, self.quiet, self.parts = source, stage, quiet, parts

    def load(self, n):
        cols = pl.ds(pl.multiple_of(n * 512, 512), 512)
        return pltpu.make_async_copy(self.source.at[n], self.stage.at[:, cols], self.r.stage_sem.at[self.way, n])

    def quiet_copy(self, to, part):
        r = self.r
        span = pl.ds(0, HALF) if part == 0 else pl.ds(HALF, QUIET - HALF)
        src, dst = self.source.at[to, span], self.quiet.at[span]
        if to == 0:
            return pltpu.make_async_copy(src, dst, r.quiet_send.at[self.way, 0, part])
        return remote(src, dst, r.quiet_send.at[self.way, to, part], r.quiet_recv.at[self.way, part], (self.p.s, to))

    def start_quiet(self):
        @pl.when(self.p.b == 0)
        def _():
            for part in range(2):
                for to in (2, 3, 1, 0):
                    self.quiet_copy(to, part).start()

    def wait_quiet(self, part):
        @pl.when(self.p.b == 0)
        def _():
            self.quiet_copy(0, part).wait()

        @pl.when(self.p.b != 0)
        def _():
            self.quiet_copy(1, part).wait_recv()

    def parts_copy(self, n):
        src, dst, to = ((3, 1, self.p.core()), (4, 5, self.p.core()), (6, 2, self.p.across()))[n]
        return remote(
            self.parts.at[src],
            self.parts.at[dst],
            self.r.parts_send.at[self.way, n],
            self.r.parts_recv.at[self.way, n],
            to,
        )

    def part(self, to, ends, lens):
        self.load(to).wait()
        cols = pl.ds(pl.multiple_of(to * 512, 512), 512)
        chosen = pool_matrix(column(ends, to), column(lens, to), self.p.b * 512, 512)
        return mm(chosen, self.stage[:, cols])

    def start_parts(self, ends, lens):
        b, sibling, away = self.p.b, self.p.core()[1], self.p.across()[1]
        self.parts[4] = self.part(away + sibling - b, ends, lens).astype(BF16)
        self.parts_copy(1).start()
        self.parts[3] = self.part(sibling, ends, lens).astype(BF16)
        self.parts_copy(0).start()
        self.parts[6] = self.part(away, ends, lens).astype(BF16)
        self.parts[0] = self.part(b, ends, lens).astype(BF16)

    def join_parts(self):
        self.parts_copy(1).wait_recv()
        self.parts[6] = (self.parts[6].astype(F32) + self.parts[5].astype(F32)).astype(BF16)
        self.parts_copy(2).start()

    def wait_parts(self):
        self.parts_copy(0).wait_recv()
        self.parts_copy(2).wait_recv()
        return sum(self.parts[n].astype(F32) for n in range(3))

    def wait_sent(self):
        for n in range(3):
            self.parts_copy(n).wait_send()

        @pl.when(self.p.b == 0)
        def _():
            for part in range(2):
                for to in (1, 2, 3):
                    self.quiet_copy(to, part).wait_send()

    def back(self, rows, quiet_out, loud_out):
        self.rows, self.quiet_out, self.loud_out = rows, quiet_out, loud_out
        return self

    def loud_rows(self):
        return self.rows.at[pl.ds(QUIET, self.rows.shape[0] - QUIET)]

    def quiet_rows(self):
        return self.rows.at[pl.ds(0, QUIET)]

    def loud_copy(self, n, slot):
        r, p, way = self.r, self.p, self.way
        src = self.loud_out.at[slot] if n == 2 else self.loud_rows()
        to = p.across() if n == 1 else p.core()
        return remote(src, self.loud_out.at[slot], r.back_send.at[way, n], r.back_recv.at[way, 0, slot], to)

    def quiet_back(self, slot, start=0, size=QUIET):
        r, way = self.r, self.way
        span = pl.ds(start, size)
        return remote(
            self.rows.at[span],
            self.quiet_out.at[slot, span],
            r.back_send.at[way, 3],
            r.back_recv.at[way, 1, slot],
            (self.p.s, 0),
        )

    def own_copies(self):
        r, p, way = self.r, self.p, self.way
        loud = pltpu.make_async_copy(self.loud_rows(), self.loud_out.at[p.b], r.back_send.at[way, 4])
        quiet = pltpu.make_async_copy(self.quiet_rows(), self.quiet_out.at[0], r.back_send.at[way, 3])
        return loud, quiet

    def start_back(self):
        p = self.p
        loud, quiet = self.own_copies()
        self.loud_copy(1, p.b).start()
        self.loud_copy(0, p.b).start()
        pl.when(p.b == 0)(quiet.start)
        loud.start()

    def start_quiet_back(self, n):
        size = QUIET // BACK_PARTS
        pl.when(self.p.b != 0)(self.quiet_back(self.p.b, n * size, size).start)

    def pass_on(self):
        away = self.p.across()[1]
        self.loud_copy(1, away).wait_recv()
        self.loud_copy(2, away).start()

    def wait_back(self):
        p = self.p
        sibling, away = p.core()[1], p.across()[1]
        loud, quiet = self.own_copies()
        for n in (0, 1):
            self.loud_copy(n, p.b).wait_send()
        self.loud_copy(2, away).wait_send()
        loud.wait()
        pl.when(p.b != 0)(self.quiet_back(p.b).wait_send)
        pl.when(p.b == 0)(quiet.wait)
        self.loud_copy(0, sibling).wait_recv()
        self.loud_copy(2, away + sibling - p.b).wait_recv()

        @pl.when(p.b == 0)
        def _():
            for n in (1, 2, 3):
                self.quiet_back(n).wait_recv()


class Kept:
    def __init__(self, r, place, chars, kept):
        self.r, self.p, self.chars, self.kept = r, place, chars, kept
        self.count = kept.shape[1]

    def rows(self, to):
        return self.r.low_rows.at[pl.ds(to * self.count, self.count)]

    def late(self, to, slot):
        r = self.r
        return remote(self.rows(to), self.kept.at[slot], r.kept_send.at[4 + to - 2], r.kept_recv.at[slot], (self.p.s, to))

    def late_own(self, to):
        return pltpu.make_async_copy(self.rows(to), self.kept.at[to], self.r.kept_send.at[4 + to - 2])

    def early(self, slot):
        r = self.r
        src = self.chars.at[slot, pl.ds(self.count, self.count)]
        return remote(src, self.kept.at[slot], r.kept_send.at[slot], r.kept_recv.at[slot], (self.p.s, 1))

    def early_own(self, slot):
        src = self.chars.at[slot, pl.ds(0, self.count)]
        return pltpu.make_async_copy(src, self.kept.at[slot], self.r.kept_recv.at[slot])

    def start_late(self, to):
        pl.when(self.p.b != to)(self.late(to, self.p.b).start)
        pl.when(self.p.b == to)(self.late_own(to).start)

    def start_early(self):
        @pl.when(self.p.b == 0)
        def _():
            for slot in range(4):
                self.early_own(slot).start()
                self.early(slot).start()

    def wait(self):
        b = self.p.b

        @pl.when(b == 0)
        def _():
            for slot in range(4):
                self.early_own(slot).wait()
                self.early(slot).wait_send()

        @pl.when(b == 1)
        def _():
            for slot in range(4):
                self.early(slot).wait_recv()

        for to in (2, 3):
            pl.when(b != to)(self.late(to, b).wait_send)

            @pl.when(b == to)
            def _():
                self.late_own(to).wait()
                for slot in range(4):
                    if slot != to:
                        self.late(to, slot).wait_recv()


class Small:
    def __init__(self, r, place):
        self.r, self.p = r, place

    def source(self, step):
        return self.r.small if step == 0 else self.r.small_sum.at[step - 1]

    def copy(self, step):
        r, p = self.r, self.p
        to = p.core() if step == 0 else p.pair(AXES[step - 1])
        return remote(self.source(step), r.small_land.at[step], r.small_send.at[step], r.small_recv.at[step], to)

    def start(self, step):
        self.copy(step).start()

    def finish(self, step):
        self.copy(step).wait()
        self.r.small_sum[step] = self.source(step)[...] + self.r.small_land[step]


def layer_kernel(names, chars, lengths, memory, grad_out, *rest):
    count = len(VECTORS) + 1 + len(WEIGHTS)
    vectors, table, weights = rest[: len(VECTORS)], rest[len(VECTORS)], rest[len(VECTORS) + 1 : count]
    kept, out_quiet, out_loud, grad_quiet, grad_loud, total_out, small_out = rest[count : count + 7]
    r = types.SimpleNamespace(**dict(zip(names, rest[count + 7 :])))
    p = Place()
    seg, width = r.pooled.shape
    r.grad_residual, r.grad_mixed, r.grad_rows = r.grad_output, r.grad_down, r.normed_two
    for n, name in enumerate(("mixed_flip", "query_u_t", "query_v_t", "grad_mixed_t")):
        setattr(r, name, r.slope.at[:, n * width : (n + 1) * width])
    r.grad_key_t, r.grad_value_t = r.hidden.at[:, : 2 * seg], r.hidden.at[:, 2 * seg :]
    r.grad_place_t, r.grad_query = r.grad_inner.at[:, : 2 * seg], r.grad_inner.at[:, 2 * seg : 3 * seg]
    loads = [
        pltpu.make_async_copy(src, dst, r.load_sem.at[n])
        for n, (src, dst) in enumerate(
            zip((*weights, table), [getattr(r, name) for name in WEIGHTS] + [r.table])
        )
    ]
    chars_rows = Rows(r, p, 0, chars, r.hidden, r.chars_quiet, r.chars_parts).back(r.out_rows, out_quiet, out_loud)
    grads_rows = Rows(r, p, 1, grad_out, r.grad_inner, r.grads_quiet, r.grads_parts).back(
        r.grad_rows, grad_quiet, grad_loud
    )
    for n in range(4):
        chars_rows.load(n).start()
    for n in range(4):
        grads_rows.load(n).start()
    for copy in loads:
        copy.start()
    for n, name in enumerate(VECTORS):
        value = vectors[n][...].astype(F32)
        if name == "bias_up":
            r.bias_up[...] = value.reshape(1, -1)
        elif value.ndim == 2:
            r.vectors[n : n + 1, :] = jnp.concatenate([value[h : h + 1, :] for h in range(value.shape[0])], axis=1)
        else:
            r.vectors[n : n + 1, :] = value.reshape(1, -1)
    r.vec = lambda name: r.vectors[VECTORS.index(name) : VECTORS.index(name) + 1, :]

    barrier = pltpu.get_barrier_semaphore()
    others = [p.group(1), p.group(2), p.group(3), p.pair("y"), p.pair("near"), p.pair("far")]
    for other in others:
        pl.semaphore_signal(barrier, inc=1, device_id=other, device_id_type=MESH)
    pl.semaphore_wait(barrier, len(others))

    rows = memory.shape[1]

    def memory_copy(k, slot):
        to = (p.b + k) % 4
        return remote(
            memory.at[to], r.memory.at[rows_at(slot * rows, rows)], r.memory_send.at[k], r.memory_recv.at[slot], p.group(k)
        )

    own_memory = pltpu.make_async_copy(memory.at[p.b], r.memory.at[rows_at(p.b * rows, rows)], r.memory_send.at[0])
    for k in (2, 3, 1):
        memory_copy(k, p.b).start()
    own_memory.start()
    chars_rows.start_quiet()
    ends, lens = span_columns(lengths[...], QUIET)
    chars_rows.start_parts(ends, lens)
    for copy in loads:
        copy.wait()
    project_places(r)
    chars_rows.join_parts()
    grads_rows.start_quiet()
    grads_rows.start_parts(ends, lens)
    own_memory.wait()
    memory_copy(1, p.core()[1]).wait_recv()
    project_memory(rows_at(p.x * 2 * rows, 2 * rows), r)
    for slot in (2 * (1 - p.x), 2 * (1 - p.x) + 1):
        memory_copy(1, slot).wait_recv()
    project_memory(rows_at((1 - p.x) * 2 * rows, 2 * rows), r)
    own_lens = column(lens, p.b)

    def forward(block):
        project_segments(block, seg, r)
        attend(block, seg, r)
        feed_forward_in(block, r)

    chars_rows.wait_quiet(0)
    r.pooled[0:HALF] = chars_rows.quiet[0:HALF].astype(F32)
    forward(0)
    grads_rows.join_parts()
    chars_rows.wait_quiet(1)
    r.pooled[HALF:QUIET] = chars_rows.quiet[HALF:QUIET].astype(F32)
    r.pooled[QUIET:seg] = chars_rows.wait_parts() / own_lens
    r.low_rows[...] = r.pooled[...].astype(BF16)

    forward(1)
    grads_rows.wait_quiet(0)
    grads_rows.wait_quiet(1)
    r.grad_output[0:QUIET] = grads_rows.quiet[...].astype(F32)
    r.grad_output[QUIET:seg] = grads_rows.wait_parts()
    low = r.grad_output[...].astype(BF16)
    r.grad_down[...] = low
    r.grad_down_t[...] = low.astype(F32).T.astype(BF16)
    r.normed_two_t[...] = r.normed_two[...].astype(F32).T.astype(BF16)
    r.small[...] = jnp.zeros(r.small.shape, F32)
    r.small[6:7, :] = jnp.sum(low.astype(F32), axis=0, keepdims=True)

    land = [getattr(r, f"land_{n}") for n in range(5)]
    sums = Sum(p, r.total, land, total_out, r.sum_send, r.sum_recv, r.store_sem)

    rows_kept = Kept(r, p, chars, kept)

    def take(n):
        if n == KEPT_DURING[0]:
            rows_kept.start_early()
        for to in (2, 3):
            if n == KEPT_DURING[to - 1]:
                rows_kept.start_late(to)
        for part, at in enumerate(BACK_DURING):
            if at == n:
                chars_rows.start_quiet_back(part)
        for k, step in DURING[n]:
            sums.step(k, step)

    def between(pair, unit):
        for n in range(4):
            at = n * 5 + 6 + unit
            if DURING[at] or at in BACK_DURING or at in KEPT_DURING:
                pl.when(pair == n)(functools.partial(take, at))

    for n in range(4):
        feed_forward_back(n, r)
        take(n)
    r.out_rows[...] = (r.residual[...] + (mm(r.hidden[...], r.w_down[...]) + r.vec("bias_down"))).astype(BF16)
    chars_rows.start_back()
    take(4)
    middle_back(r, BASES[4])
    take(5)

    def back(n, carry):
        attend_back_pair(n, seg, r, functools.partial(between, n))
        pair_weights(n, seg, r, BASES[5] + n * PIECES[5][0])
        between(n, 4)
        return carry

    lax.fori_loop(0, 4, back, 0)
    grad_pooled = first_back(seg, r)
    r.grad_rows[0:QUIET] = grad_pooled[:QUIET].astype(BF16)
    r.grad_rows[QUIET:seg] = (grad_pooled[QUIET:] / own_lens).astype(BF16)
    grads_rows.start_back()
    small = Small(r, p)
    small_store = pltpu.make_async_copy(r.small_sum.at[4], small_out, r.small_sem)
    small.start(0)
    take(26)
    every = len(AFTER) // 12
    for n, (k, step) in enumerate(AFTER):
        for part, at in enumerate(BACK_AFTER):
            if at == n:
                grads_rows.start_quiet_back(part)
        if n % every == every - 1 and n // every < 10:
            at = n // every
            if at % 2 == 1:
                small.finish(at // 2)
                if at // 2 < 4:
                    small.start(at // 2 + 1)
                else:
                    small_store.start()
            if at == 4:
                chars_rows.pass_on()
            if at == 8:
                grads_rows.pass_on()
        sums.step(k, step)
    for k in (1, 2, 3):
        memory_copy(k, p.b).wait_send()
    rows_kept.wait()
    chars_rows.wait_sent()
    grads_rows.wait_sent()
    chars_rows.wait_back()
    grads_rows.wait_back()
    small_store.wait()


def spread_kernel(
    lengths, chars, grad_out, rows, out_quiet, out_loud, grad_quiet, grad_loud, wide, flat, pairs, small,
    out_chars, grad_chars, kept, w_query, w_key, w_value, w_rel, w_out, w_up, w_down, bias_u, bias_v, *vectors,
):
    n = pl.program_id(0)
    b = lax.axis_index("blk")
    places = chars.shape[1]
    seg = lengths.shape[1]
    lens = lengths[...].astype(F32).astype(BF16)
    row, col = ramp((seg - QUIET, seg), 0) + QUIET, ramp((seg - QUIET, seg), 1)
    upto = jnp.where(col <= row, 1.0, 0.0).astype(BF16)
    same = jnp.where(col == row, 1.0, 0.0).astype(BF16)
    pick = ramp((lengths.shape[0], seg - QUIET), 0) == n
    end = jnp.sum(jnp.where(pick, mm_nt(lens, upto), 0.0), axis=0, keepdims=True)
    length = jnp.sum(jnp.where(pick, mm_nt(lens, same), 0.0), axis=0, keepdims=True)
    place = (ramp((places, seg - QUIET), 0) + b * places).astype(F32)
    chosen = jnp.where((place < end) & (place >= end - length), 1.0, 0.0).astype(BF16)
    first = b == 0
    kept[...] = rows[...]
    for source, quiet, loud, out in (
        (chars, out_quiet, out_loud, out_chars),
        (grad_out, grad_quiet, grad_loud, grad_chars),
    ):
        spread = mm(chosen, loud[0])
        whole = source[0].astype(F32) + spread
        out[0, QUIET:places] = whole[QUIET:].astype(out.dtype)
        out[0, 0:QUIET] = (whole[:QUIET] + jnp.where(first, quiet[0].astype(F32), 0.0)).astype(out.dtype)
    w_down[...] = wide[0:512].astype(F32).T
    w_up[...] = wide[512:1024].astype(F32)
    w_out[...] = flat[...].astype(F32)
    for m, out in enumerate((w_query, w_key, w_value, w_rel)):
        out[...] = pairs[m * 128 : (m + 1) * 128].astype(F32).T
    for m, out in enumerate((bias_u, bias_v)):
        out[...] = jnp.concatenate([small[m : m + 1, h * 64 : (h + 1) * 64] for h in range(8)], axis=0)
    for m, out in enumerate(vectors[:4]):
        out[...] = small[2 + m : 3 + m, :]
    vectors[4][...] = jnp.concatenate([small[m : m + 1, :] for m in range(7, 11)], axis=1)
    vectors[5][...] = small[6:7, :]


def shards_whole(
    chars, seg_lengths, memory, grad_out, w_query, w_key, w_value, w_rel, w_out, w_up, w_down,
    bias_u, bias_v, gain_one, shift_one, gain_two, shift_two, bias_up, bias_down,
):
    count, places, width = chars.shape
    seg, hidden = seg_lengths.shape[1], w_up.shape[1]
    rows = memory.shape[1]
    table = jnp.asarray(sine_table(2 * seg, width))
    scratch = layer_scratch(seg, width, hidden)
    anywhere, near = pl.BlockSpec(memory_space=pl.ANY), pl.BlockSpec(memory_space=pltpu.VMEM)
    loud = seg - QUIET
    kept, out_quiet, out_loud, grad_quiet, grad_loud, total, small = pl.pallas_call(
        functools.partial(layer_kernel, tuple(scratch)),
        out_shape=[
            jax.ShapeDtypeStruct((count, rows, width), BF16),
            jax.ShapeDtypeStruct((count, QUIET, width), BF16),
            jax.ShapeDtypeStruct((count, loud, width), BF16),
            jax.ShapeDtypeStruct((count, QUIET, width), BF16),
            jax.ShapeDtypeStruct((count, loud, width), BF16),
            jax.ShapeDtypeStruct((BASES[-1], width), BF16),
            jax.ShapeDtypeStruct((16, width), F32),
        ],
        in_specs=[anywhere, near, anywhere, anywhere] + [near] * len(VECTORS) + [anywhere] * 8,
        out_specs=[anywhere] * 7,
        scratch_shapes=list(scratch.values()),
        compiler_params=pltpu.CompilerParams(
            collective_id=0, has_side_effects=True, vmem_limit_bytes=VMEM_BYTES
        ),
        name="layer",
    )(
        chars, seg_lengths, memory, grad_out,
        bias_u, bias_v, gain_one, shift_one, gain_two, shift_two, bias_up, bias_down, table,
        w_query, w_key, w_value, w_rel, w_out, w_up, w_down,
    )

    def block(shape, index):
        return pl.BlockSpec(shape, index)

    def each(*shape):
        return block((1, *shape), lambda n: (n, 0, 0))

    def whole(*shape):
        return block(shape, lambda n: (0, 0))

    vector = [(1, width)] * 4 + [(1, hidden), (1, width)]
    outs = pl.pallas_call(
        spread_kernel,
        grid=(count,),
        out_shape=[
            jax.ShapeDtypeStruct(chars.shape, BF16),
            jax.ShapeDtypeStruct(chars.shape, F32),
            jax.ShapeDtypeStruct(memory.shape, BF16),
            *[jax.ShapeDtypeStruct((width, width), F32)] * 5,
            jax.ShapeDtypeStruct((width, hidden), F32),
            jax.ShapeDtypeStruct((hidden, width), F32),
            *[jax.ShapeDtypeStruct(bias_u.shape, F32)] * 2,
            *[jax.ShapeDtypeStruct(shape, F32) for shape in vector],
        ],
        in_specs=[
            whole(*seg_lengths.shape),
            each(places, width),
            each(places, width),
            each(rows, width),
            each(QUIET, width),
            each(loud, width),
            each(QUIET, width),
            each(loud, width),
            block((1024, width), lambda n: (n, 0)),
            block((128, width), lambda n: (BASES[4] // 128 + n, 0)),
            block((512, width), lambda n: (BASES[5] // 512 + n, 0)),
            whole(16, width),
        ],
        out_specs=[
            each(places, width),
            each(places, width),
            each(rows, width),
            *[block((width, 128), lambda n: (0, n))] * 4,
            block((128, width), lambda n: (n, 0)),
            block((width, 512), lambda n: (0, n)),
            block((512, width), lambda n: (n, 0)),
            *[whole(*bias_u.shape)] * 2,
            *[whole(*shape) for shape in vector],
        ],
        compiler_params=pltpu.CompilerParams(vmem_limit_bytes=VMEM_BYTES),
        name="spread",
    )(seg_lengths, chars, grad_out, kept, out_quiet, out_loud, grad_quiet, grad_loud, total, total, total, small)
    return (*outs[:12], *[v.reshape(-1) for v in outs[12:]])


VMEM_BYTES = 64 * 2**20 - 2**16


def fits_whole(mesh):
    return dict(mesh.shape) == {"seq": 8, "blk": 4}


def layer_norm(value, gain, shift):
    center = value - jnp.mean(value, axis=-1, keepdims=True)
    spread = jnp.mean(center * center, axis=-1, keepdims=True)
    return center * lax.rsqrt(spread + 1e-05) * gain + shift


def angle_tables(places, feature_width):
    freqs = jnp.exp(
        jnp.arange(feature_width // 2, dtype=jnp.float32)
        * (-2.0 * math.log(10000.0) / feature_width)
    )
    angles = places[:, None] * freqs[None, :]
    return (jnp.sin(angles), jnp.cos(angles))


def smooth_gate(value):
    return jax.nn.gelu(value, approximate=False)


def segment_ids(seg_end, char_places):
    return jnp.sum((seg_end[:, None, :] <= char_places[None, :, None]).astype(jnp.int32), axis=2)


def shards(
    chars,
    seg_lengths,
    memory,
    grad_out,
    w_query,
    w_key,
    w_value,
    w_rel,
    w_out,
    w_up,
    w_down,
    bias_u,
    bias_v,
    gain_one,
    shift_one,
    gain_two,
    shift_two,
    bias_up,
    bias_down,
):
    blk_index = lax.axis_index("blk")
    seq_local, char_rows, feature_width = chars.shape
    seg_rows = memory.shape[1]
    seg_count = seg_lengths.shape[1]
    head_count, head_dim = bias_u.shape
    half_width = feature_width // 2
    score_scale = head_dim ** (-0.5)
    seg_start = blk_index * seg_rows
    gain_one_f = gain_one.astype(jnp.float32)
    shift_one_f = shift_one.astype(jnp.float32)
    gain_two_f = gain_two.astype(jnp.float32)
    shift_two_f = shift_two.astype(jnp.float32)
    seg_end = jnp.cumsum(seg_lengths, axis=1)
    char_places = blk_index * char_rows + jnp.arange(char_rows, dtype=jnp.int32)
    segment = segment_ids(seg_end, char_places)
    own_lengths = lax.dynamic_slice_in_dim(seg_lengths, seg_start, seg_rows, 1).astype(jnp.float32)
    chars_f = chars.astype(jnp.float32)
    grad_f = grad_out.astype(jnp.float32)

    def full_table(values, ids):
        return jax.ops.segment_sum(values, ids, num_segments=seg_count)

    part_sums = jax.vmap(full_table)(chars_f, segment)
    pooled_sum = lax.psum_scatter(part_sums, "blk", scatter_dimension=1, tiled=True)
    pooled = pooled_sum / own_lengths[:, :, None]
    normed = layer_norm(pooled, gain_one_f, shift_one_f)
    normed_low = normed.astype(jnp.bfloat16)
    memory_f = memory.astype(jnp.float32)
    mem_low = layer_norm(memory_f, gain_one_f, shift_one_f).astype(jnp.bfloat16)
    query_rows = jnp.einsum("sid,de->sie", normed_low, w_query, preferred_element_type=jnp.float32)
    key_local = jnp.stack(
        [
            jnp.einsum("sid,de->sie", mem_low, w_key, preferred_element_type=jnp.float32),
            jnp.einsum("sid,de->sie", normed_low, w_key, preferred_element_type=jnp.float32),
        ],
        axis=1,
    ).astype(jnp.bfloat16)
    value_local = jnp.stack(
        [
            jnp.einsum("sid,de->sie", mem_low, w_value, preferred_element_type=jnp.float32),
            jnp.einsum("sid,de->sie", normed_low, w_value, preferred_element_type=jnp.float32),
        ],
        axis=1,
    ).astype(jnp.bfloat16)
    key_all, value_all = (
        lax.all_gather(key_local, "blk", axis=2, tiled=True),
        lax.all_gather(value_local, "blk", axis=2, tiled=True),
    )
    key_heads = key_all.reshape(seq_local, 2 * seg_count, head_count, head_dim)
    value_heads = value_all.reshape(seq_local, 2 * seg_count, head_count, head_dim)
    query_u = (
        (query_rows + bias_u.astype(jnp.float32).reshape(-1))
        .astype(jnp.bfloat16)
        .reshape(seq_local, seg_rows, head_count, head_dim)
    )
    query_v = (
        (query_rows + bias_v.astype(jnp.float32).reshape(-1))
        .astype(jnp.bfloat16)
        .reshape(seq_local, seg_rows, head_count, head_dim)
    )
    w_rel_heads = w_rel.reshape(feature_width, head_count, head_dim)
    rel_coeff = jnp.einsum(
        "sihe,fhe->sihf", query_v, w_rel_heads, preferred_element_type=jnp.float32
    )
    sin_all, cos_all = angle_tables(jnp.arange(2 * seg_count).astype(jnp.float32), feature_width)
    key_pos = jnp.concatenate([cos_all, sin_all], axis=-1).astype(jnp.bfloat16)
    query_index = seg_count + seg_start + jnp.arange(seg_rows, dtype=jnp.int32)
    sin_q, cos_q = angle_tables(query_index.astype(jnp.float32), feature_width)
    sin_query = sin_q[None, :, None, :]
    cos_query = cos_q[None, :, None, :]
    coeff_sin = rel_coeff[..., :half_width]
    coeff_cos = rel_coeff[..., half_width:]
    query_pos = jnp.concatenate(
        [
            coeff_sin * sin_query + coeff_cos * cos_query,
            coeff_cos * sin_query - coeff_sin * cos_query,
        ],
        axis=-1,
    ).astype(jnp.bfloat16)
    allowed = jnp.arange(2 * seg_count, dtype=jnp.int32)[None, :] <= query_index[:, None]

    def score_block():
        raw_scores = (
            jnp.einsum("sihe,sjhe->shij", query_u, key_heads, preferred_element_type=jnp.float32)
            + jnp.einsum("sihf,jf->shij", query_pos, key_pos, preferred_element_type=jnp.float32)
        ) * score_scale
        return jnp.where(allowed[None, None], raw_scores, -1e30)

    scores = score_block()
    row_top = jnp.max(scores, axis=-1, keepdims=True)
    expo = jnp.exp(scores - row_top)
    row_total = jnp.sum(expo, axis=-1, keepdims=True)
    log_total = row_top + jnp.log(row_total)
    att_probs = (expo / row_total).astype(jnp.bfloat16)
    att_mixed = jnp.einsum(
        "shij,sjhe->sihe", att_probs, value_heads, preferred_element_type=jnp.float32
    )
    mixed_low = att_mixed.reshape(seq_local, seg_rows, feature_width).astype(jnp.bfloat16)
    residual = pooled + jnp.einsum(
        "sid,de->sie", mixed_low, w_out, preferred_element_type=jnp.float32
    )
    normed_two = layer_norm(residual, gain_two_f, shift_two_f)
    two_low = normed_two.astype(jnp.bfloat16)
    ffn_inner = jnp.einsum(
        "sid,df->sif", two_low, w_up, preferred_element_type=jnp.float32
    ) + bias_up.astype(jnp.float32)
    hidden_low = smooth_gate(ffn_inner).astype(jnp.bfloat16)
    branch_out = jnp.einsum(
        "sif,fd->sid", hidden_low, w_down, preferred_element_type=jnp.float32
    ) + bias_down.astype(jnp.float32)
    out_low = (residual + branch_out).astype(jnp.bfloat16)
    rows_all = lax.all_gather(out_low, "blk", axis=1, tiled=True)
    picked = jnp.take_along_axis(rows_all, segment[:, :, None], axis=1)
    out_chars = (chars_f + picked.astype(jnp.float32)).astype(jnp.bfloat16)
    new_memory = pooled.astype(jnp.bfloat16)
    grad_table = jax.vmap(full_table)(grad_f, segment)
    grad_output = lax.psum_scatter(grad_table, "blk", scatter_dimension=1, tiled=True)
    grad_down_low = grad_output.astype(jnp.bfloat16)
    grad_bias_down = jnp.sum(grad_down_low.astype(jnp.float32), axis=(0, 1))
    grad_w_down = jnp.einsum(
        "sif,sid->fd", hidden_low, grad_down_low, preferred_element_type=jnp.float32
    )
    grad_hidden = jnp.einsum(
        "sid,fd->sif", grad_down_low, w_down, preferred_element_type=jnp.float32
    )
    unused_value, gate_back = jax.vjp(smooth_gate, ffn_inner)
    grad_inner = gate_back(grad_hidden)[0].astype(jnp.bfloat16)
    grad_bias_up = jnp.sum(grad_inner.astype(jnp.float32), axis=(0, 1))
    grad_w_up = jnp.einsum("sid,sif->df", two_low, grad_inner, preferred_element_type=jnp.float32)
    grad_normed_two = jnp.einsum(
        "sif,df->sid", grad_inner, w_up, preferred_element_type=jnp.float32
    )
    unused_norm, norm_two_back = jax.vjp(layer_norm, residual, gain_two_f, shift_two_f)
    grad_resid_norm, grad_gain_two, grad_shift_two = norm_two_back(grad_normed_two)
    grad_residual = grad_output + grad_resid_norm
    grad_att_low = grad_residual.astype(jnp.bfloat16)
    grad_w_out = jnp.einsum(
        "sid,sie->de", mixed_low, grad_att_low, preferred_element_type=jnp.float32
    )
    grad_mixed = jnp.einsum("sie,de->sid", grad_att_low, w_out, preferred_element_type=jnp.float32)
    grad_mixed = grad_mixed.astype(jnp.bfloat16).reshape(seq_local, seg_rows, head_count, head_dim)
    scores_again = score_block()
    probs_full = jnp.exp(scores_again - log_total)
    probs_low = probs_full.astype(jnp.bfloat16)
    grad_probs = jnp.einsum(
        "sihe,sjhe->shij", grad_mixed, value_heads, preferred_element_type=jnp.float32
    )
    grad_values = jnp.einsum(
        "shij,sihe->sjhe", probs_low, grad_mixed, preferred_element_type=jnp.float32
    )
    prob_delta = jnp.sum(probs_full * grad_probs, axis=-1, keepdims=True)
    grad_scores = (probs_full * (grad_probs - prob_delta)).astype(jnp.bfloat16)
    grad_query_u = (
        jnp.einsum("shij,sjhe->sihe", grad_scores, key_heads, preferred_element_type=jnp.float32)
        * score_scale
    )
    grad_keys = (
        jnp.einsum("shij,sihe->sjhe", grad_scores, query_u, preferred_element_type=jnp.float32)
        * score_scale
    )
    grad_query_pos = (
        jnp.einsum("shij,jf->sihf", grad_scores, key_pos, preferred_element_type=jnp.float32)
        * score_scale
    )
    grad_first = grad_query_pos[..., :half_width]
    grad_second = grad_query_pos[..., half_width:]
    grad_coeff = jnp.concatenate(
        [
            grad_first * sin_query - grad_second * cos_query,
            grad_first * cos_query + grad_second * sin_query,
        ],
        axis=-1,
    ).astype(jnp.bfloat16)
    grad_w_rel = jnp.einsum(
        "sihf,sihe->fhe", grad_coeff, query_v, preferred_element_type=jnp.float32
    ).reshape(feature_width, feature_width)
    grad_query_v = jnp.einsum(
        "sihf,fhe->sihe", grad_coeff, w_rel_heads, preferred_element_type=jnp.float32
    )
    grad_bias_u = jnp.sum(grad_query_u, axis=(0, 1))
    grad_bias_v = jnp.sum(grad_query_v, axis=(0, 1))
    grad_query = (
        (grad_query_u + grad_query_v)
        .reshape(seq_local, seg_rows, feature_width)
        .astype(jnp.bfloat16)
    )
    grad_w_query = jnp.einsum(
        "sid,sie->de", normed_low, grad_query, preferred_element_type=jnp.float32
    )
    grad_normed = jnp.einsum("sie,de->sid", grad_query, w_query, preferred_element_type=jnp.float32)
    key_share, value_share = (
        lax.psum_scatter(
            grad_keys.reshape(seq_local, 2, seg_count, feature_width),
            "blk",
            scatter_dimension=2,
            tiled=True,
        ),
        lax.psum_scatter(
            grad_values.reshape(seq_local, 2, seg_count, feature_width),
            "blk",
            scatter_dimension=2,
            tiled=True,
        ),
    )
    key_low = key_share.astype(jnp.bfloat16)
    value_low = value_share.astype(jnp.bfloat16)
    grad_w_key = jnp.einsum(
        "sid,sie->de", mem_low, key_low[:, 0], preferred_element_type=jnp.float32
    ) + jnp.einsum("sid,sie->de", normed_low, key_low[:, 1], preferred_element_type=jnp.float32)
    grad_w_value = jnp.einsum(
        "sid,sie->de", mem_low, value_low[:, 0], preferred_element_type=jnp.float32
    ) + jnp.einsum("sid,sie->de", normed_low, value_low[:, 1], preferred_element_type=jnp.float32)
    grad_normed = grad_normed + jnp.einsum(
        "sie,de->sid", key_low[:, 1], w_key, preferred_element_type=jnp.float32
    )
    grad_normed = grad_normed + jnp.einsum(
        "sie,de->sid", value_low[:, 1], w_value, preferred_element_type=jnp.float32
    )
    grad_mem_normed = jnp.einsum(
        "sie,de->sid", key_low[:, 0], w_key, preferred_element_type=jnp.float32
    ) + jnp.einsum("sie,de->sid", value_low[:, 0], w_value, preferred_element_type=jnp.float32)
    unused_one, norm_one_back = jax.vjp(layer_norm, pooled, gain_one_f, shift_one_f)
    grad_pooled_norm, grad_gain_one, grad_shift_one = norm_one_back(grad_normed)
    unused_mem, norm_mem_back = jax.vjp(layer_norm, memory_f, gain_one_f, shift_one_f)
    unused_grad, grad_gain_mem, grad_shift_mem = norm_mem_back(grad_mem_normed)
    grad_gain_one = grad_gain_one + grad_gain_mem
    grad_shift_one = grad_shift_one + grad_shift_mem
    grad_pooled = grad_residual + grad_pooled_norm
    grad_sum = grad_pooled / own_lengths[:, :, None]
    grad_sum_all = lax.all_gather(grad_sum, "blk", axis=1, tiled=True)
    grad_chars = grad_f + jnp.take_along_axis(grad_sum_all, segment[:, :, None], axis=1)
    (
        grad_w_query,
        grad_w_key,
        grad_w_value,
        grad_w_rel,
        grad_w_out,
        grad_w_up,
        grad_w_down,
        grad_bias_u,
        grad_bias_v,
        grad_gain_one,
        grad_shift_one,
        grad_gain_two,
        grad_shift_two,
        grad_bias_up,
        grad_bias_down,
    ) = lax.psum(
        (
            grad_w_query,
            grad_w_key,
            grad_w_value,
            grad_w_rel,
            grad_w_out,
            grad_w_up,
            grad_w_down,
            grad_bias_u,
            grad_bias_v,
            grad_gain_one,
            grad_shift_one,
            grad_gain_two,
            grad_shift_two,
            grad_bias_up,
            grad_bias_down,
        ),
        ("seq", "blk"),
    )
    return (
        out_chars,
        grad_chars,
        new_memory,
        grad_w_query,
        grad_w_key,
        grad_w_value,
        grad_w_rel,
        grad_w_out,
        grad_w_up,
        grad_w_down,
        grad_bias_u,
        grad_bias_v,
        grad_gain_one,
        grad_shift_one,
        grad_gain_two,
        grad_shift_two,
        grad_bias_up,
        grad_bias_down,
    )


def solution(mesh):
    placed = (
        P("seq", "blk", None),
        P("seq", None),
        P("seq", "blk", None),
        P("seq", "blk", None),
        P(),
        P(),
        P(),
        P(),
        P(),
        P(),
        P(),
        P(),
        P(),
        P(),
        P(),
        P(),
        P(),
        P(),
        P(),
    )
    return jax.shard_map(
        shards_whole if fits_whole(mesh) else shards,
        mesh=mesh,
        in_specs=placed,
        out_specs=(
            P("seq", "blk", None),
            P("seq", "blk", None),
            P("seq", "blk", None),
            P(),
            P(),
            P(),
            P(),
            P(),
            P(),
            P(),
            P(),
            P(),
            P(),
            P(),
            P(),
            P(),
            P(),
            P(),
        ),
        check_vma=False,
    )
```

```python
import functools
import math
import types

import jax
import jax.numpy as jnp
import numpy as np
from jax import lax
from jax.experimental import pallas as pl
from jax.experimental.pallas import tpu as pltpu
from jax.sharding import PartitionSpec as P

F32, BF16 = jnp.float32, jnp.bfloat16
NT = (((1,), (1,)), ((), ()))


def mm(a, b):
    return jnp.dot(a, b, preferred_element_type=F32)


def mm_nt(a, b):
    return lax.dot_general(a, b, NT, preferred_element_type=F32)


def normalize(value):
    center = value - jnp.mean(value, axis=-1, keepdims=True)
    inv = lax.rsqrt(jnp.mean(center * center, axis=-1, keepdims=True) + 1e-05)
    return center * inv, inv


def norm_back(grad, unit, inv, gain):
    scaled = grad * gain
    along = jnp.mean(scaled * unit, axis=-1, keepdims=True)
    return inv * (scaled - jnp.mean(scaled, axis=-1, keepdims=True) - unit * along)


def gelu_parts(value):
    gate = 0.5 + 0.5 * lax.erf(value * 0.7071067811865476)
    return gate, gate + value * jnp.exp(-0.5 * value * value) * 0.3989422804014327


def ramp(shape, dim):
    return lax.broadcasted_iota(jnp.int32, shape, dim)


MESH = pl.DeviceIdType.MESH
HALF = 256
STEPS = 11
AXES = ("x", "y", "near", "far")
PIECES = tuple((1024, f"tile{n}") for n in range(4)) + ((512, "middle"),) + tuple((512, f"pair{n}") for n in range(4))
BASES = tuple(sum(rows for rows, unused in PIECES[:n]) for n in range(len(PIECES) + 1))
VECTORS = ("bias_u", "bias_v", "gain_one", "shift_one", "gain_two", "shift_two", "bias_up", "bias_down")
ORDERS = (
    (("y", "x", "near", "far"), ("x", "near", "y", "far")),
    (("near", "y", "far", "x"), ("x", "y", "near", "far")),
    (("near", "far", "y", "x"), ("y", "x", "near", "far")),
    (("far", "y", "x", "near"), ("y", "x", "near", "far")),
    (("y", "near", "x", "far"), ("x", "y", "far", "near")),
    (("y", "x", "near", "far"), ("y", "near", "x", "far")),
    (("near", "x", "y", "far"), ("x", "far", "y", "near")),
    (("y", "x", "near", "far"), ("near", "y", "x", "far")),
    (("y", "near", "x", "far"), ("near", "x", "y", "far")),
)
DURING = (
    ((0, 0),), ((1, 0),), ((2, 0),), ((0, 1), (3, 0)), ((1, 1),), ((2, 1), (3, 1), (4, 0)), ((0, 2),), (),
    (), ((1, 2), (4, 1)), ((5, 0),), (), ((2, 2),), (), ((5, 1),), ((6, 0),), ((0, 3), (3, 2)), (),
    ((1, 3), (6, 1)), ((4, 2),), ((7, 0), (2, 3)), (), ((5, 2),), ((0, 4), (7, 1)), ((1, 4), (3, 3)),
    ((8, 0), (4, 3), (6, 2)), ((2, 4),),
)
AFTER = (
    (8, 1), (0, 5), (7, 2), (5, 3), (1, 5), (3, 4), (4, 4), (6, 3), (2, 5), (8, 2), (7, 3), (5, 4), (0, 6),
    (1, 6), (6, 4), (3, 5), (4, 5), (8, 3), (2, 6), (0, 7), (7, 4), (5, 5), (8, 4), (1, 7), (6, 5), (3, 6),
    (4, 6), (2, 7), (0, 8), (7, 5), (5, 6), (8, 5), (6, 6), (3, 7), (1, 8), (4, 7), (2, 8), (7, 6), (0, 9),
    (6, 7), (5, 7), (8, 6), (3, 8), (4, 8), (0, 10), (1, 9), (2, 9), (7, 7), (8, 7), (5, 8), (1, 10), (6, 8),
    (2, 10), (4, 9), (7, 8), (3, 9), (8, 8), (4, 10), (5, 9), (6, 9), (3, 10), (7, 9), (5, 10), (8, 9),
    (6, 10), (7, 10), (8, 10),
)
BACK_DURING = (6, 8, 11, 13, 16, 21, 22, 24)
BACK_AFTER = (10, 14, 20, 45, 49, 55, 56, 61)


class Place:
    def __init__(self):
        self.s = lax.axis_index("seq")
        self.b = lax.axis_index("blk")
        self.z, self.y = self.s // 2, self.s % 2
        self.x, self.c = self.b // 2, self.b % 2
        self.bit = dict(x=self.x, y=self.y, near=self.z % 2, far=self.z // 2)

    def group(self, k):
        return (self.s, (self.b + k) % 4)

    def core(self):
        return (self.s, self.b + 1 - 2 * self.c)

    def across(self):
        return (self.s, self.b + 2 - 4 * self.x)

    def move(self, axis):
        reach = dict(x=(0, 2), y=(1, 0), near=(2, 0), far=(4, 0))[axis]
        turn = 1 - 2 * self.bit[axis]
        return reach[0] * turn, reach[1] * turn

    def step(self, zero, one):
        if zero == one:
            return self.pair(zero), self.bit[zero]
        away = [self.move(zero)[m] * (1 - self.c) + self.move(one)[m] * self.c for m in (0, 1)]
        bit = self.bit[zero] * (1 - self.c) + self.bit[one] * self.c
        return (self.s + away[0], self.b + away[1]), bit

    def pair(self, axis):
        away = self.move(axis)
        return (self.s + away[0], self.b + away[1])


def rows_at(start, size):
    return pl.ds(pl.multiple_of(start, 16), size)


def remote(src, dst, send, recv, to):
    return pltpu.make_async_remote_copy(src, dst, send, recv, device_id=to, device_id_type=MESH)


class Sum:
    def __init__(self, place, total, land, out, send, recv, store):
        self.p, self.g, self.land, self.out = place, total, land, out
        self.send, self.recv, self.store = send, recv, store
        self.steps = [[place.step(*axes) for axes in zip(*orders)] for orders in ORDERS]

    def offset(self, k, n):
        start = BASES[k] + self.p.c * (PIECES[k][0] // 2)
        for m in range(n):
            start = start + self.steps[k][m][1] * (PIECES[k][0] >> (m + 2))
        return start

    def lands(self, k, n, start=0, size=None):
        rows = PIECES[k][0] >> (n + 1)
        return self.land[n].at[rows_at((BASES[k] >> (n + 1)) + start, rows if size is None else size)]

    def copies(self, step, k, landing=False):
        p, g = self.p, self.g
        rows = PIECES[k][0]

        def copy(src, dst, to):
            return remote(src, dst, self.send.at[k], self.recv.at[k, step], to)

        if step == 0:
            half = rows // 2
            return copy(g.at[rows_at(BASES[k] + (1 - p.c) * half, half)], self.lands(k, 0), p.core())
        if step <= 4:
            to, bit = self.steps[k][step - 1]
            size = rows >> (step + 1)
            away = self.offset(k, step - 1) + (1 - bit) * size
            return copy(g.at[rows_at(away, size)], self.lands(k, step), to)
        if step <= 8:
            n = 8 - step
            to, bit = self.steps[k][n]
            size = rows >> (n + 2)
            dst = self.lands(k, n, (1 - bit if landing else bit) * size, size)
            src = self.lands(k, 3, bit * size, size) if n == 3 else self.lands(k, n + 1)
            return copy(src, dst, to)
        half = rows // 2
        span = BASES[k] + (1 - p.c if landing else p.c) * half
        return copy(self.lands(k, 0), self.out.at[rows_at(span, half)], p.core())

    def own(self, k):
        half = PIECES[k][0] // 2
        span = rows_at(BASES[k] + self.p.c * half, half)
        return pltpu.make_async_copy(self.lands(k, 0), self.out.at[span], self.store.at[k])

    def add(self, k, n, start, size):
        span = rows_at(self.offset(k, n) + start, size)
        self.g[span] = self.g[span] + self.lands(k, n, start, size)[...]

    def step(self, k, step):
        rows = PIECES[k][0]
        if step > 0:
            self.copies(step - 1, k).wait_send()
            self.copies(step - 1, k, landing=True).wait_recv()
        if 1 <= step <= 4:
            half = rows >> (step + 1)
            bit = self.steps[k][step - 1][1]
            self.add(k, step - 1, (1 - bit) * half, half)
            self.copies(step, k).start()
            self.add(k, step - 1, bit * half, half)
        elif step == 5:
            size = rows >> 5
            total = self.g[rows_at(self.offset(k, 4), size)] + self.lands(k, 4)[...]
            self.lands(k, 3, self.steps[k][3][1] * size, size)[...] = total
            self.copies(step, k).start()
        elif step < STEPS - 1:
            self.copies(step, k).start()
        if 6 <= step <= 8:
            n = 8 - step
            size = rows >> (n + 2)
            self.lands(k, n, self.steps[k][n][1] * size, size)[...] = self.lands(k, n + 1)[...]
        if step == STEPS - 2:
            self.own(k).start()
        if step == STEPS - 1:
            self.own(k).wait()


def pair_lanes(p, start=0, size=128):
    if isinstance(p, int):
        return slice(p * 128 + start, p * 128 + start + size)
    return pl.ds(pl.multiple_of(p * 128 + start, size), size)


def lane_mask(par):
    lane = ramp((1, 128), 1)
    return jnp.where((lane >= 64) == bool(par), 1.0, 0.0).astype(BF16)


def flip_matrix():
    return jnp.where(ramp((HALF, HALF), 0) + ramp((HALF, HALF), 1) == HALF - 1, 1.0, 0.0).astype(BF16)


def flip(flip_low, value):
    return jnp.concatenate(
        [mm(flip_low, value[r : r + HALF]) for r in range(0, value.shape[0], HALF)], axis=0
    ).astype(value.dtype)


def pool_matrix(end, length, first_place, places):
    place = (ramp((end.shape[0], places), 1) + first_place).astype(F32)
    return jnp.where((place < end) & (place >= end - length), 1.0, 0.0).astype(BF16)


def query_block(n, seg):
    keys = seg + HALF * (n + 1)
    return slice(n * HALF, (n + 1) * HALF), keys, 2 * seg - keys


def attend(n, seg, r):
    seen = ramp((HALF, HALF), 1) <= ramp((HALF, HALF), 0)
    lane = ramp((HALF, 128), 1)
    rows, keys, skip = query_block(n, seg)

    def products(head):
        lanes, keep = pair_lanes(head // 2), lane_mask(head % 2)
        near = mm_nt(r.query_u[rows, lanes] * keep, r.key[0:keys, lanes])
        return near, mm_nt(r.query_v[rows, lanes] * keep, r.place[skip : 2 * seg, lanes])

    ahead = products(0)
    for p in range(4):
        mixed, scale = [], []
        for head in (2 * p, 2 * p + 1):
            near, far = ahead
            ahead = products(head + 1) if head < 7 else None
            scores = near + pltpu.roll(far, keys - (HALF - 1), 1, stride=1, stride_axis=0)
            scores = jnp.concatenate(
                [scores[:, : keys - HALF], jnp.where(seen, scores[:, keys - HALF :], -1e30)], axis=1
            )
            expo = jnp.exp(scores - jnp.max(scores, axis=1, keepdims=True))
            probs = expo.astype(BF16)
            r.probs[head, rows, 0:keys] = probs
            mixed.append(mm(probs, r.value[0:keys, pair_lanes(p)]))
            scale.append(1.0 / jnp.sum(expo, axis=1, keepdims=True))
        scale = jnp.where(lane >= 64, scale[1], scale[0])
        r.scale[rows, pair_lanes(p)] = scale
        r.mixed[rows, pair_lanes(p)] = (jnp.where(lane >= 64, mixed[1], mixed[0]) * scale).astype(BF16)


def attend_back_pair(p, seg, r, between):
    lanes = pair_lanes(p)
    flip_low = flip_matrix()
    scale = 0.125
    lane = ramp((HALF, 128), 1)
    sums = [None] * 6
    bias = []
    for n in range(seg // HALF):
        rows, keys, skip = query_block(n, seg)
        key, value, place = r.key[0:keys, lanes], r.value[0:keys, lanes], r.place[skip : 2 * seg, lanes]
        grad_u, grad_v = [], []
        for par in range(2):
            keep = lane_mask(par)
            feats = pair_lanes(p, par * 64, 64)
            probs = r.probs[2 * p + par, rows, 0:keys]
            turned = mm(flip_low, probs)
            grad_mixed = r.grad_mixed[rows, lanes] * keep
            delta = jnp.sum(grad_mixed.astype(F32) * r.mixed_flip[rows, lanes].astype(F32), axis=1, keepdims=True)
            grad_scores = turned * (mm_nt(grad_mixed, value) - delta)
            near = grad_scores.astype(BF16)
            far = pltpu.roll(grad_scores, 0, 1, stride=1, stride_axis=0).astype(BF16)
            grad_u.append(mm(near, key) * scale)
            grad_v.append(mm(far, place) * scale)
            now = (
                mm(r.query_u_t[feats, rows], near),
                mm(r.grad_mixed_t[feats, rows], probs),
                mm(r.query_v_t[feats, rows], far),
            )
            for m in range(3):
                slot = par * 3 + m
                if n == 0:
                    sums[slot] = now[m]
                else:
                    old, new = sums[slot], now[m]
                    cut = old.shape[1]
                    if m < 2:
                        sums[slot] = jnp.concatenate([new[:, :cut] + old, new[:, cut:]], axis=1)
                    else:
                        sums[slot] = jnp.concatenate([new[:, :-cut], new[:, -cut:] + old], axis=1)
            between(n * 2 + par)
        grad_u = jnp.where(lane >= 64, grad_u[1], grad_u[0])
        grad_v = jnp.where(lane >= 64, grad_v[1], grad_v[0])
        bias.append((jnp.sum(grad_u, axis=0, keepdims=True), jnp.sum(grad_v, axis=0, keepdims=True)))
        r.grad_query[rows, lanes] = mm(flip_low, (grad_u + grad_v).astype(BF16)).astype(BF16)
    r.small[0:1, lanes] = sum(b[0] for b in bias)
    r.small[1:2, lanes] = sum(b[1] for b in bias)
    for par in range(2):
        feats = pair_lanes(p, par * 64, 64)
        for m, out in enumerate((r.grad_key_t, r.grad_value_t, r.grad_place_t)):
            out[feats, :] = sums[par * 3 + m].astype(BF16)


def pair_weights(p, seg, r, base):
    lanes = pair_lanes(p)
    grad_query_t = r.grad_query[:, lanes].astype(F32).T.astype(BF16)
    r.total[rows_at(base, 128)] = mm(grad_query_t, r.normed[seg : 2 * seg]).astype(BF16)
    r.total[rows_at(base + 128, 128)] = mm(r.grad_key_t[lanes, :], r.normed[...]).astype(BF16)
    r.total[rows_at(base + 256, 128)] = mm(r.grad_value_t[lanes, :], r.normed[...]).astype(BF16)
    r.total[rows_at(base + 384, 128)] = mm(r.grad_place_t[lanes, :], r.table[...]).astype(BF16)


def project_places(r):
    r.place[...] = mm(r.table[...], r.w_rel[...]).astype(BF16)


def project_memory(rows, r):
    unit, unused = normalize(r.memory[rows].astype(F32))
    low = (unit * r.vec("gain_one") + r.vec("shift_one")).astype(BF16)
    r.normed[rows] = low
    r.key[rows] = mm(low, r.w_key[...]).astype(BF16)
    r.value[rows] = mm(low, r.w_value[...]).astype(BF16)


def project_segments(n, seg, r):
    rows, keys, unused = query_block(n, seg)
    places = slice(keys - HALF, keys)
    unit, unused = normalize(r.pooled[rows])
    low = (unit * r.vec("gain_one") + r.vec("shift_one")).astype(BF16)
    r.normed[places] = low
    query = mm(low, r.w_query[...])
    scale = 0.125
    r.query_u[rows] = (query + r.vec("bias_u")).astype(BF16) * jnp.asarray(scale, BF16)
    r.query_v[rows] = (query + r.vec("bias_v")).astype(BF16) * jnp.asarray(scale, BF16)
    r.key[places] = mm(low, r.w_key[...]).astype(BF16)
    r.value[places] = mm(low, r.w_value[...]).astype(BF16)


def feed_forward_in(n, r):
    rows = slice(n * HALF, (n + 1) * HALF)
    residual = r.pooled[rows] + mm(r.mixed[rows], r.w_out[...])
    r.residual[rows] = residual
    unit, unused = normalize(residual)
    r.normed_two[rows] = (unit * r.vec("gain_two") + r.vec("shift_two")).astype(BF16)

    for m in range(r.w_up.shape[1] // 512):
        cols = slice(m * 512, (m + 1) * 512)
        inner = mm(r.normed_two[rows], r.w_up[:, cols]) + r.bias_up[0:1, cols]
        gate, slope = gelu_parts(inner)
        r.hidden[rows, cols] = (inner * gate).astype(BF16)
        r.slope[rows, cols] = slope.astype(BF16)


def feed_forward_back(n, r):
    cols = slice(n * 512, (n + 1) * 512)
    r.total[rows_at(BASES[n], 512)] = mm(r.grad_down_t[...], r.hidden[:, cols]).astype(BF16)
    grad_hidden = mm_nt(r.grad_down[...], r.w_down[cols, :])
    low = (grad_hidden * r.slope[:, cols].astype(F32)).astype(BF16)
    r.grad_inner[:, cols] = low
    r.small[7 + n : 8 + n, :] = jnp.sum(low.astype(F32), axis=0, keepdims=True)
    r.total[rows_at(BASES[n] + 512, 512)] = mm(r.normed_two_t[...], low).astype(BF16)


def middle_back(r, base):
    grad_normed = mm_nt(r.grad_inner[...], r.w_up[...])
    unit, inv = normalize(r.residual[...])
    r.small[4:5, :] = jnp.sum(grad_normed * unit, axis=0, keepdims=True)
    r.small[5:6, :] = jnp.sum(grad_normed, axis=0, keepdims=True)
    grad = r.grad_output[...] + norm_back(grad_normed, unit, inv, r.vec("gain_two"))
    r.grad_residual[...] = grad
    low = grad.astype(BF16)
    mixed = r.mixed[...]
    r.total[rows_at(base, 512)] = mm(mixed.astype(F32).T.astype(BF16), low).astype(BF16)
    grad_mixed = (mm_nt(low, r.w_out[...]) * r.scale[...]).astype(BF16)
    r.grad_mixed_t[...] = grad_mixed.astype(F32).T.astype(BF16)
    flip_low = flip_matrix()
    r.grad_mixed[...] = flip(flip_low, grad_mixed)
    r.mixed_flip[...] = flip(flip_low, mixed)
    r.query_u_t[...] = flip(flip_low, r.query_u[...]).astype(F32).T.astype(BF16)
    r.query_v_t[...] = flip(flip_low, r.query_v[...]).astype(F32).T.astype(BF16)


def first_back(seg, r):
    grad_key = r.grad_key_t[...].astype(F32).T.astype(BF16)
    grad_value = r.grad_value_t[...].astype(F32).T.astype(BF16)
    grad_normed = mm_nt(r.grad_query[...], r.w_query[...])
    grad_normed += mm_nt(grad_key[seg:], r.w_key[...])
    grad_normed += mm_nt(grad_value[seg:], r.w_value[...])
    grad_mem = mm_nt(grad_key[:seg], r.w_key[...]) + mm_nt(grad_value[:seg], r.w_value[...])
    unit, inv = normalize(r.pooled[...])
    unit_mem, unused = normalize(r.memory[...].astype(F32))
    r.small[2:3, :] = jnp.sum(grad_normed * unit + grad_mem * unit_mem, axis=0, keepdims=True)
    r.small[3:4, :] = jnp.sum(grad_normed + grad_mem, axis=0, keepdims=True)
    return r.grad_residual[...] + norm_back(grad_normed, unit, inv, r.vec("gain_one"))


QUIET = 384
BACK_PARTS = 8
KEPT_DURING = (18, 9, 14)


def sine_table(count, width):
    freqs = np.exp(np.arange(width // 2) * (-2.0 * math.log(10000.0) / width))
    angles = np.arange(count)[::-1, None] * freqs[None, :]
    return np.concatenate([np.sin(angles), np.cos(angles)], axis=1).astype(jnp.bfloat16)


def span_columns(lengths, low):
    seg = lengths.shape[1]
    lens = lengths.astype(F32).astype(BF16)
    row, col = ramp((seg - low, seg), 0) + low, ramp((seg - low, seg), 1)
    upto = jnp.where(col <= row, 1.0, 0.0).astype(BF16)
    same = jnp.where(col == row, 1.0, 0.0).astype(BF16)
    return mm_nt(upto, lens), mm_nt(same, lens)


def column(value, n):
    return jnp.sum(jnp.where(ramp(value.shape, 1) == n, value, 0.0), axis=1, keepdims=True)


WEIGHTS = ("w_query", "w_key", "w_value", "w_rel", "w_out", "w_up", "w_down")


def layer_scratch(seg, width, hidden, shapes):
    def low(*shape):
        return pltpu.VMEM(shape, BF16)

    def full(*shape):
        return pltpu.VMEM(shape, F32)

    return dict(
        table=low(2 * seg, width),
        w_query=low(width, width),
        w_key=low(width, width),
        w_value=low(width, width),
        w_rel=low(width, width),
        w_out=low(width, width),
        w_up=low(width, hidden),
        w_down=low(hidden, width),
        memory=low(seg, width),
        pooled=full(seg, width),
        normed=low(2 * seg, width),
        key=low(2 * seg, width),
        value=low(2 * seg, width),
        place=low(2 * seg, width),
        query_u=low(seg, width),
        query_v=low(seg, width),
        mixed=low(seg, width),
        probs=low(8, seg, 2 * seg),
        scale=full(seg, width),
        residual=full(seg, width),
        normed_two=low(seg, width),
        normed_two_t=low(width, seg),
        hidden=low(seg, hidden),
        slope=low(seg, hidden),
        grad_inner=low(seg, hidden),
        grad_output=full(seg, width),
        grad_down=low(seg, width),
        grad_down_t=low(width, seg),
        low_rows=low(seg, width),
        out_rows=low(seg, width),
        chars_quiet=low(QUIET, width),
        chars_parts=low(7, seg - QUIET, width),
        grads_quiet=low(QUIET, width),
        grads_parts=low(7, seg - QUIET, width),
        total=low(BASES[-1], width),
        land_0=low(BASES[-1] >> 1, width),
        land_1=low(BASES[-1] >> 2, width),
        land_2=low(BASES[-1] >> 3, width),
        land_3=low(BASES[-1] >> 4, width),
        land_4=low(BASES[-1] >> 5, width),
        bias_up=full(1, hidden),
        vectors=full(16, width),
        lengths=pltpu.VMEM((4, seg), jnp.int32),
        **{f"raw_{name}": low(*shape) for name, shape in shapes.items()},
        small_load=pltpu.SemaphoreType.DMA((len(VECTORS) + 1,)),
        small=full(16, width),
        small_sum=full(5, 16, width),
        small_land=full(5, 16, width),
        load_sem=pltpu.SemaphoreType.DMA((len(WEIGHTS) + 1,)),
        stage_sem=pltpu.SemaphoreType.DMA((2, 4)),
        memory_send=pltpu.SemaphoreType.DMA((4,)),
        memory_recv=pltpu.SemaphoreType.DMA((4,)),
        quiet_send=pltpu.SemaphoreType.DMA((2, 4, 2)),
        quiet_recv=pltpu.SemaphoreType.DMA((2, 2)),
        parts_send=pltpu.SemaphoreType.DMA((2, 3)),
        parts_recv=pltpu.SemaphoreType.DMA((2, 3)),
        kept_send=pltpu.SemaphoreType.DMA((6,)),
        kept_recv=pltpu.SemaphoreType.DMA((4,)),
        back_send=pltpu.SemaphoreType.DMA((2, 5)),
        back_recv=pltpu.SemaphoreType.DMA((2, 2, 4)),
        sum_send=pltpu.SemaphoreType.DMA((len(PIECES),)),
        sum_recv=pltpu.SemaphoreType.DMA((len(PIECES), STEPS - 1)),
        small_send=pltpu.SemaphoreType.DMA((5,)),
        small_recv=pltpu.SemaphoreType.DMA((5,)),
        small_sem=pltpu.SemaphoreType.DMA,
        store_sem=pltpu.SemaphoreType.DMA((len(PIECES),)),
    )


class Rows:
    def __init__(self, r, place, way, source, stage, quiet, parts):
        self.r, self.p, self.way = r, place, way
        self.source, self.stage, self.quiet, self.parts = source, stage, quiet, parts

    def load(self, n):
        cols = pl.ds(pl.multiple_of(n * 512, 512), 512)
        return pltpu.make_async_copy(self.source.at[n], self.stage.at[:, cols], self.r.stage_sem.at[self.way, n])

    def quiet_copy(self, to, part):
        r = self.r
        span = pl.ds(0, HALF) if part == 0 else pl.ds(HALF, QUIET - HALF)
        src, dst = self.source.at[to, span], self.quiet.at[span]
        if to == 0:
            return pltpu.make_async_copy(src, dst, r.quiet_send.at[self.way, 0, part])
        return remote(src, dst, r.quiet_send.at[self.way, to, part], r.quiet_recv.at[self.way, part], (self.p.s, to))

    def start_quiet(self):
        @pl.when(self.p.b == 0)
        def _():
            for part in range(2):
                for to in (2, 3, 1, 0):
                    self.quiet_copy(to, part).start()

    def wait_quiet(self, part):
        @pl.when(self.p.b == 0)
        def _():
            self.quiet_copy(0, part).wait()

        @pl.when(self.p.b != 0)
        def _():
            self.quiet_copy(1, part).wait_recv()

    def parts_copy(self, n):
        src, dst, to = ((3, 1, self.p.core()), (4, 5, self.p.core()), (6, 2, self.p.across()))[n]
        return remote(
            self.parts.at[src],
            self.parts.at[dst],
            self.r.parts_send.at[self.way, n],
            self.r.parts_recv.at[self.way, n],
            to,
        )

    def part(self, to, ends, lens):
        self.load(to).wait()
        cols = pl.ds(pl.multiple_of(to * 512, 512), 512)
        chosen = pool_matrix(column(ends, to), column(lens, to), self.p.b * 512, 512)
        return mm(chosen, self.stage[:, cols])

    def start_parts(self, ends, lens):
        b, sibling, away = self.p.b, self.p.core()[1], self.p.across()[1]
        self.parts[4] = self.part(away + sibling - b, ends, lens).astype(BF16)
        self.parts_copy(1).start()
        self.parts[3] = self.part(sibling, ends, lens).astype(BF16)
        self.parts_copy(0).start()
        self.parts[6] = self.part(away, ends, lens).astype(BF16)
        self.parts[0] = self.part(b, ends, lens).astype(BF16)

    def join_parts(self):
        self.parts_copy(1).wait_recv()
        self.parts[6] = (self.parts[6].astype(F32) + self.parts[5].astype(F32)).astype(BF16)
        self.parts_copy(2).start()

    def wait_parts(self):
        self.parts_copy(0).wait_recv()
        self.parts_copy(2).wait_recv()
        return sum(self.parts[n].astype(F32) for n in range(3))

    def wait_sent(self):
        for n in range(3):
            self.parts_copy(n).wait_send()

        @pl.when(self.p.b == 0)
        def _():
            for part in range(2):
                for to in (1, 2, 3):
                    self.quiet_copy(to, part).wait_send()

    def back(self, rows, quiet_out, loud_out):
        self.rows, self.quiet_out, self.loud_out = rows, quiet_out, loud_out
        return self

    def loud_rows(self):
        return self.rows.at[pl.ds(QUIET, self.rows.shape[0] - QUIET)]

    def quiet_rows(self):
        return self.rows.at[pl.ds(0, QUIET)]

    def loud_copy(self, n, slot):
        r, p, way = self.r, self.p, self.way
        src = self.loud_out.at[slot] if n == 2 else self.loud_rows()
        to = p.across() if n == 1 else p.core()
        return remote(src, self.loud_out.at[slot], r.back_send.at[way, n], r.back_recv.at[way, 0, slot], to)

    def quiet_back(self, slot, start=0, size=QUIET):
        r, way = self.r, self.way
        span = pl.ds(start, size)
        return remote(
            self.rows.at[span],
            self.quiet_out.at[slot, span],
            r.back_send.at[way, 3],
            r.back_recv.at[way, 1, slot],
            (self.p.s, 0),
        )

    def own_copies(self):
        r, p, way = self.r, self.p, self.way
        loud = pltpu.make_async_copy(self.loud_rows(), self.loud_out.at[p.b], r.back_send.at[way, 4])
        quiet = pltpu.make_async_copy(self.quiet_rows(), self.quiet_out.at[0], r.back_send.at[way, 3])
        return loud, quiet

    def start_back(self):
        p = self.p
        loud, quiet = self.own_copies()
        self.loud_copy(1, p.b).start()
        self.loud_copy(0, p.b).start()
        pl.when(p.b == 0)(quiet.start)
        loud.start()

    def start_quiet_back(self, n):
        size = QUIET // BACK_PARTS
        pl.when(self.p.b != 0)(self.quiet_back(self.p.b, n * size, size).start)

    def pass_on(self):
        away = self.p.across()[1]
        self.loud_copy(1, away).wait_recv()
        self.loud_copy(2, away).start()

    def wait_back(self):
        p = self.p
        sibling, away = p.core()[1], p.across()[1]
        loud, quiet = self.own_copies()
        for n in (0, 1):
            self.loud_copy(n, p.b).wait_send()
        self.loud_copy(2, away).wait_send()
        loud.wait()
        pl.when(p.b != 0)(self.quiet_back(p.b).wait_send)
        pl.when(p.b == 0)(quiet.wait)
        self.loud_copy(0, sibling).wait_recv()
        self.loud_copy(2, away + sibling - p.b).wait_recv()

        @pl.when(p.b == 0)
        def _():
            for n in (1, 2, 3):
                self.quiet_back(n).wait_recv()


class Kept:
    def __init__(self, r, place, chars, kept):
        self.r, self.p, self.chars, self.kept = r, place, chars, kept
        self.count = kept.shape[1]

    def rows(self, to):
        return self.r.low_rows.at[pl.ds(to * self.count, self.count)]

    def late(self, to, slot):
        r = self.r
        return remote(self.rows(to), self.kept.at[slot], r.kept_send.at[4 + to - 2], r.kept_recv.at[slot], (self.p.s, to))

    def late_own(self, to):
        return pltpu.make_async_copy(self.rows(to), self.kept.at[to], self.r.kept_send.at[4 + to - 2])

    def early(self, slot):
        r = self.r
        src = self.chars.at[slot, pl.ds(self.count, self.count)]
        return remote(src, self.kept.at[slot], r.kept_send.at[slot], r.kept_recv.at[slot], (self.p.s, 1))

    def early_own(self, slot):
        src = self.chars.at[slot, pl.ds(0, self.count)]
        return pltpu.make_async_copy(src, self.kept.at[slot], self.r.kept_recv.at[slot])

    def start_late(self, to):
        pl.when(self.p.b != to)(self.late(to, self.p.b).start)
        pl.when(self.p.b == to)(self.late_own(to).start)

    def start_early(self):
        @pl.when(self.p.b == 0)
        def _():
            for slot in range(4):
                self.early_own(slot).start()
                self.early(slot).start()

    def wait(self):
        b = self.p.b

        @pl.when(b == 0)
        def _():
            for slot in range(4):
                self.early_own(slot).wait()
                self.early(slot).wait_send()

        @pl.when(b == 1)
        def _():
            for slot in range(4):
                self.early(slot).wait_recv()

        for to in (2, 3):
            pl.when(b != to)(self.late(to, b).wait_send)

            @pl.when(b == to)
            def _():
                self.late_own(to).wait()
                for slot in range(4):
                    if slot != to:
                        self.late(to, slot).wait_recv()


class Small:
    def __init__(self, r, place):
        self.r, self.p = r, place

    def source(self, step):
        return self.r.small if step == 0 else self.r.small_sum.at[step - 1]

    def copy(self, step):
        r, p = self.r, self.p
        to = p.core() if step == 0 else p.pair(AXES[step - 1])
        return remote(self.source(step), r.small_land.at[step], r.small_send.at[step], r.small_recv.at[step], to)

    def start(self, step):
        self.copy(step).start()

    def finish(self, step):
        self.copy(step).wait()
        self.r.small_sum[step] = self.source(step)[...] + self.r.small_land[step]


def layer_kernel(names, chars, lengths, memory, grad_out, *rest):
    count = len(VECTORS) + 1 + len(WEIGHTS)
    vectors, table, weights = rest[: len(VECTORS)], rest[len(VECTORS)], rest[len(VECTORS) + 1 : count]
    kept, out_quiet, out_loud, grad_quiet, grad_loud, total_out, small_out = rest[count : count + 7]
    r = types.SimpleNamespace(**dict(zip(names, rest[count + 7 :])))
    p = Place()
    seg, width = r.pooled.shape
    r.grad_residual, r.grad_mixed, r.grad_rows = r.grad_output, r.grad_down, r.normed_two
    for n, name in enumerate(("mixed_flip", "query_u_t", "query_v_t", "grad_mixed_t")):
        setattr(r, name, r.slope.at[:, n * width : (n + 1) * width])
    r.grad_key_t, r.grad_value_t = r.hidden.at[:, : 2 * seg], r.hidden.at[:, 2 * seg :]
    r.grad_place_t, r.grad_query = r.grad_inner.at[:, : 2 * seg], r.grad_inner.at[:, 2 * seg : 3 * seg]
    loads = [
        pltpu.make_async_copy(src, dst, r.load_sem.at[n])
        for n, (src, dst) in enumerate(
            zip((*weights, table), [getattr(r, name) for name in WEIGHTS] + [r.table])
        )
    ]
    chars_rows = Rows(r, p, 0, chars, r.hidden, r.chars_quiet, r.chars_parts).back(r.out_rows, out_quiet, out_loud)
    grads_rows = Rows(r, p, 1, grad_out, r.grad_inner, r.grads_quiet, r.grads_parts).back(
        r.grad_rows, grad_quiet, grad_loud
    )
    raw = [getattr(r, f"raw_{name}") for name in VECTORS]
    small_loads = [
        pltpu.make_async_copy(src, dst, r.small_load.at[n])
        for n, (src, dst) in enumerate(zip((*vectors, lengths), (*raw, r.lengths)))
    ]
    small_loads[-1].start()
    for n in range(4):
        chars_rows.load(n).start()
    for copy in small_loads[:-1]:
        copy.start()
    for n in range(4):
        grads_rows.load(n).start()
    for copy in loads:
        copy.start()
    r.vec = lambda name: r.vectors[VECTORS.index(name) : VECTORS.index(name) + 1, :]

    barrier = pltpu.get_barrier_semaphore()
    others = [p.group(1), p.group(2), p.group(3), p.pair("y"), p.pair("near"), p.pair("far")]
    for other in others:
        pl.semaphore_signal(barrier, inc=1, device_id=other, device_id_type=MESH)
    pl.semaphore_wait(barrier, len(others))

    rows = memory.shape[1]

    def memory_copy(k, slot):
        to = (p.b + k) % 4
        return remote(
            memory.at[to], r.memory.at[rows_at(slot * rows, rows)], r.memory_send.at[k], r.memory_recv.at[slot], p.group(k)
        )

    own_memory = pltpu.make_async_copy(memory.at[p.b], r.memory.at[rows_at(p.b * rows, rows)], r.memory_send.at[0])
    for k in (2, 3, 1):
        memory_copy(k, p.b).start()
    own_memory.start()
    chars_rows.start_quiet()
    small_loads[-1].wait()
    ends, lens = span_columns(r.lengths[...], QUIET)
    chars_rows.start_parts(ends, lens)
    for copy in loads:
        copy.wait()
    for copy in small_loads[:-1]:
        copy.wait()
    for n, name in enumerate(VECTORS):
        value = raw[n][...].astype(F32)
        if name == "bias_up":
            r.bias_up[...] = value.reshape(1, -1)
        elif value.ndim == 2:
            r.vectors[n : n + 1, :] = jnp.concatenate([value[h : h + 1, :] for h in range(value.shape[0])], axis=1)
        else:
            r.vectors[n : n + 1, :] = value.reshape(1, -1)
    project_places(r)
    waits = (1 - p.x) * p.c
    pl.when(waits == 0)(chars_rows.join_parts)
    grads_rows.start_quiet()
    grads_rows.start_parts(ends, lens)
    own_memory.wait()
    memory_copy(1, p.core()[1]).wait_recv()
    project_memory(rows_at(p.x * 2 * rows, 2 * rows), r)
    for slot in (2 * (1 - p.x), 2 * (1 - p.x) + 1):
        memory_copy(1, slot).wait_recv()
    project_memory(rows_at((1 - p.x) * 2 * rows, 2 * rows), r)
    own_lens = column(lens, p.b)

    def forward(block):
        project_segments(block, seg, r)
        attend(block, seg, r)
        if block == 0:
            pl.when(waits == 1)(chars_rows.join_parts)
        feed_forward_in(block, r)

    chars_rows.wait_quiet(0)
    r.pooled[0:HALF] = chars_rows.quiet[0:HALF].astype(F32)
    forward(0)
    grads_rows.join_parts()
    chars_rows.wait_quiet(1)
    r.pooled[HALF:QUIET] = chars_rows.quiet[HALF:QUIET].astype(F32)
    r.pooled[QUIET:seg] = chars_rows.wait_parts() / own_lens
    r.low_rows[...] = r.pooled[...].astype(BF16)

    forward(1)
    grads_rows.wait_quiet(0)
    grads_rows.wait_quiet(1)
    r.grad_output[0:QUIET] = grads_rows.quiet[...].astype(F32)
    r.grad_output[QUIET:seg] = grads_rows.wait_parts()
    low = r.grad_output[...].astype(BF16)
    r.grad_down[...] = low
    r.grad_down_t[...] = low.astype(F32).T.astype(BF16)
    r.normed_two_t[...] = r.normed_two[...].astype(F32).T.astype(BF16)
    r.small[...] = jnp.zeros(r.small.shape, F32)
    r.small[6:7, :] = jnp.sum(low.astype(F32), axis=0, keepdims=True)

    land = [getattr(r, f"land_{n}") for n in range(5)]
    sums = Sum(p, r.total, land, total_out, r.sum_send, r.sum_recv, r.store_sem)

    rows_kept = Kept(r, p, chars, kept)

    def take(n):
        if n == KEPT_DURING[0]:
            rows_kept.start_early()
        for to in (2, 3):
            if n == KEPT_DURING[to - 1]:
                rows_kept.start_late(to)
        for part, at in enumerate(BACK_DURING):
            if at == n:
                chars_rows.start_quiet_back(part)
        for k, step in DURING[n]:
            sums.step(k, step)

    def between(pair, unit):
        for n in range(4):
            at = n * 5 + 6 + unit
            if DURING[at] or at in BACK_DURING or at in KEPT_DURING:
                pl.when(pair == n)(functools.partial(take, at))

    for n in range(4):
        feed_forward_back(n, r)
        take(n)
    r.out_rows[...] = (r.residual[...] + (mm(r.hidden[...], r.w_down[...]) + r.vec("bias_down"))).astype(BF16)
    chars_rows.start_back()
    take(4)
    middle_back(r, BASES[4])
    take(5)

    def back(n, carry):
        attend_back_pair(n, seg, r, functools.partial(between, n))
        pair_weights(n, seg, r, BASES[5] + n * PIECES[5][0])
        between(n, 4)
        return carry

    lax.fori_loop(0, 4, back, 0)
    grad_pooled = first_back(seg, r)
    r.grad_rows[0:QUIET] = grad_pooled[:QUIET].astype(BF16)
    r.grad_rows[QUIET:seg] = (grad_pooled[QUIET:] / own_lens).astype(BF16)
    grads_rows.start_back()
    small = Small(r, p)
    small_store = pltpu.make_async_copy(r.small_sum.at[4], small_out, r.small_sem)
    small.start(0)
    take(26)
    every = len(AFTER) // 12
    for n, (k, step) in enumerate(AFTER):
        for part, at in enumerate(BACK_AFTER):
            if at == n:
                grads_rows.start_quiet_back(part)
        if n % every == every - 1 and n // every < 10:
            at = n // every
            if at % 2 == 1:
                small.finish(at // 2)
                if at // 2 < 4:
                    small.start(at // 2 + 1)
                else:
                    small_store.start()
            if at == 4:
                chars_rows.pass_on()
            if at == 8:
                grads_rows.pass_on()
        sums.step(k, step)
    for k in (1, 2, 3):
        memory_copy(k, p.b).wait_send()
    rows_kept.wait()
    chars_rows.wait_sent()
    grads_rows.wait_sent()
    chars_rows.wait_back()
    grads_rows.wait_back()
    small_store.wait()


def spread_kernel(
    lengths, chars, grad_out, rows, out_quiet, out_loud, grad_quiet, grad_loud, wide, flat, pairs, small,
    out_chars, grad_chars, kept, w_query, w_key, w_value, w_rel, w_out, w_up, w_down, bias_u, bias_v, *vectors,
):
    n = pl.program_id(0)
    b = lax.axis_index("blk")
    places = chars.shape[1]
    seg = lengths.shape[1]
    lens = lengths[...].astype(F32).astype(BF16)
    row, col = ramp((seg - QUIET, seg), 0) + QUIET, ramp((seg - QUIET, seg), 1)
    upto = jnp.where(col <= row, 1.0, 0.0).astype(BF16)
    same = jnp.where(col == row, 1.0, 0.0).astype(BF16)
    pick = ramp((lengths.shape[0], seg - QUIET), 0) == n
    end = jnp.sum(jnp.where(pick, mm_nt(lens, upto), 0.0), axis=0, keepdims=True)
    length = jnp.sum(jnp.where(pick, mm_nt(lens, same), 0.0), axis=0, keepdims=True)
    place = (ramp((places, seg - QUIET), 0) + b * places).astype(F32)
    chosen = jnp.where((place < end) & (place >= end - length), 1.0, 0.0).astype(BF16)
    first = b == 0
    kept[...] = rows[...]
    for source, quiet, loud, out in (
        (chars, out_quiet, out_loud, out_chars),
        (grad_out, grad_quiet, grad_loud, grad_chars),
    ):
        spread = mm(chosen, loud[0])
        whole = source[0].astype(F32) + spread
        out[0, QUIET:places] = whole[QUIET:].astype(out.dtype)
        out[0, 0:QUIET] = (whole[:QUIET] + jnp.where(first, quiet[0].astype(F32), 0.0)).astype(out.dtype)
    w_down[...] = wide[0:512].astype(F32).T
    w_up[...] = wide[512:1024].astype(F32)
    w_out[...] = flat[...].astype(F32)
    for m, out in enumerate((w_query, w_key, w_value, w_rel)):
        out[...] = pairs[m * 128 : (m + 1) * 128].astype(F32).T
    for m, out in enumerate((bias_u, bias_v)):
        out[...] = jnp.concatenate([small[m : m + 1, h * 64 : (h + 1) * 64] for h in range(8)], axis=0)
    for m, out in enumerate(vectors[:4]):
        out[...] = small[2 + m : 3 + m, :]
    vectors[4][...] = jnp.concatenate([small[m : m + 1, :] for m in range(7, 11)], axis=1)
    vectors[5][...] = small[6:7, :]


def shards_whole(
    chars, seg_lengths, memory, grad_out, w_query, w_key, w_value, w_rel, w_out, w_up, w_down,
    bias_u, bias_v, gain_one, shift_one, gain_two, shift_two, bias_up, bias_down,
):
    count, places, width = chars.shape
    seg, hidden = seg_lengths.shape[1], w_up.shape[1]
    rows = memory.shape[1]
    table = jnp.asarray(sine_table(2 * seg, width))
    vectors = (bias_u, bias_v, gain_one, shift_one, gain_two, shift_two, bias_up, bias_down)
    scratch = layer_scratch(seg, width, hidden, {name: v.shape for name, v in zip(VECTORS, vectors)})
    anywhere, near = pl.BlockSpec(memory_space=pl.ANY), pl.BlockSpec(memory_space=pltpu.VMEM)
    loud = seg - QUIET
    kept, out_quiet, out_loud, grad_quiet, grad_loud, total, small = pl.pallas_call(
        functools.partial(layer_kernel, tuple(scratch)),
        out_shape=[
            jax.ShapeDtypeStruct((count, rows, width), BF16),
            jax.ShapeDtypeStruct((count, QUIET, width), BF16),
            jax.ShapeDtypeStruct((count, loud, width), BF16),
            jax.ShapeDtypeStruct((count, QUIET, width), BF16),
            jax.ShapeDtypeStruct((count, loud, width), BF16),
            jax.ShapeDtypeStruct((BASES[-1], width), BF16),
            jax.ShapeDtypeStruct((16, width), F32),
        ],
        in_specs=[anywhere] * (12 + len(VECTORS)),
        out_specs=[anywhere] * 7,
        scratch_shapes=list(scratch.values()),
        compiler_params=pltpu.CompilerParams(
            collective_id=0, has_side_effects=True, vmem_limit_bytes=VMEM_BYTES
        ),
        name="layer",
    )(
        chars, seg_lengths, memory, grad_out,
        *vectors, table,
        w_query, w_key, w_value, w_rel, w_out, w_up, w_down,
    )

    def block(shape, index):
        return pl.BlockSpec(shape, index)

    def each(*shape):
        return block((1, *shape), lambda n: (n, 0, 0))

    def whole(*shape):
        return block(shape, lambda n: (0, 0))

    vector = [(1, width)] * 4 + [(1, hidden), (1, width)]
    outs = pl.pallas_call(
        spread_kernel,
        grid=(count,),
        out_shape=[
            jax.ShapeDtypeStruct(chars.shape, BF16),
            jax.ShapeDtypeStruct(chars.shape, F32),
            jax.ShapeDtypeStruct(memory.shape, BF16),
            *[jax.ShapeDtypeStruct((width, width), F32)] * 5,
            jax.ShapeDtypeStruct((width, hidden), F32),
            jax.ShapeDtypeStruct((hidden, width), F32),
            *[jax.ShapeDtypeStruct(bias_u.shape, F32)] * 2,
            *[jax.ShapeDtypeStruct(shape, F32) for shape in vector],
        ],
        in_specs=[
            whole(*seg_lengths.shape),
            each(places, width),
            each(places, width),
            each(rows, width),
            each(QUIET, width),
            each(loud, width),
            each(QUIET, width),
            each(loud, width),
            block((1024, width), lambda n: (n, 0)),
            block((128, width), lambda n: (BASES[4] // 128 + n, 0)),
            block((512, width), lambda n: (BASES[5] // 512 + n, 0)),
            whole(16, width),
        ],
        out_specs=[
            each(places, width),
            each(places, width),
            each(rows, width),
            *[block((width, 128), lambda n: (0, n))] * 4,
            block((128, width), lambda n: (n, 0)),
            block((width, 512), lambda n: (0, n)),
            block((512, width), lambda n: (n, 0)),
            *[whole(*bias_u.shape)] * 2,
            *[whole(*shape) for shape in vector],
        ],
        compiler_params=pltpu.CompilerParams(vmem_limit_bytes=VMEM_BYTES),
        name="spread",
    )(seg_lengths, chars, grad_out, kept, out_quiet, out_loud, grad_quiet, grad_loud, total, total, total, small)
    return (*outs[:12], *[v.reshape(-1) for v in outs[12:]])


VMEM_BYTES = 64 * 2**20 - 2**16


def fits_whole(mesh):
    return dict(mesh.shape) == {"seq": 8, "blk": 4}


def layer_norm(value, gain, shift):
    center = value - jnp.mean(value, axis=-1, keepdims=True)
    spread = jnp.mean(center * center, axis=-1, keepdims=True)
    return center * lax.rsqrt(spread + 1e-05) * gain + shift


def angle_tables(places, feature_width):
    freqs = jnp.exp(
        jnp.arange(feature_width // 2, dtype=jnp.float32)
        * (-2.0 * math.log(10000.0) / feature_width)
    )
    angles = places[:, None] * freqs[None, :]
    return (jnp.sin(angles), jnp.cos(angles))


def smooth_gate(value):
    return jax.nn.gelu(value, approximate=False)


def segment_ids(seg_end, char_places):
    return jnp.sum((seg_end[:, None, :] <= char_places[None, :, None]).astype(jnp.int32), axis=2)


def shards(
    chars,
    seg_lengths,
    memory,
    grad_out,
    w_query,
    w_key,
    w_value,
    w_rel,
    w_out,
    w_up,
    w_down,
    bias_u,
    bias_v,
    gain_one,
    shift_one,
    gain_two,
    shift_two,
    bias_up,
    bias_down,
):
    blk_index = lax.axis_index("blk")
    seq_local, char_rows, feature_width = chars.shape
    seg_rows = memory.shape[1]
    seg_count = seg_lengths.shape[1]
    head_count, head_dim = bias_u.shape
    half_width = feature_width // 2
    score_scale = head_dim ** (-0.5)
    seg_start = blk_index * seg_rows
    gain_one_f = gain_one.astype(jnp.float32)
    shift_one_f = shift_one.astype(jnp.float32)
    gain_two_f = gain_two.astype(jnp.float32)
    shift_two_f = shift_two.astype(jnp.float32)
    seg_end = jnp.cumsum(seg_lengths, axis=1)
    char_places = blk_index * char_rows + jnp.arange(char_rows, dtype=jnp.int32)
    segment = segment_ids(seg_end, char_places)
    own_lengths = lax.dynamic_slice_in_dim(seg_lengths, seg_start, seg_rows, 1).astype(jnp.float32)
    chars_f = chars.astype(jnp.float32)
    grad_f = grad_out.astype(jnp.float32)

    def full_table(values, ids):
        return jax.ops.segment_sum(values, ids, num_segments=seg_count)

    part_sums = jax.vmap(full_table)(chars_f, segment)
    pooled_sum = lax.psum_scatter(part_sums, "blk", scatter_dimension=1, tiled=True)
    pooled = pooled_sum / own_lengths[:, :, None]
    normed = layer_norm(pooled, gain_one_f, shift_one_f)
    normed_low = normed.astype(jnp.bfloat16)
    memory_f = memory.astype(jnp.float32)
    mem_low = layer_norm(memory_f, gain_one_f, shift_one_f).astype(jnp.bfloat16)
    query_rows = jnp.einsum("sid,de->sie", normed_low, w_query, preferred_element_type=jnp.float32)
    key_local = jnp.stack(
        [
            jnp.einsum("sid,de->sie", mem_low, w_key, preferred_element_type=jnp.float32),
            jnp.einsum("sid,de->sie", normed_low, w_key, preferred_element_type=jnp.float32),
        ],
        axis=1,
    ).astype(jnp.bfloat16)
    value_local = jnp.stack(
        [
            jnp.einsum("sid,de->sie", mem_low, w_value, preferred_element_type=jnp.float32),
            jnp.einsum("sid,de->sie", normed_low, w_value, preferred_element_type=jnp.float32),
        ],
        axis=1,
    ).astype(jnp.bfloat16)
    key_all, value_all = (
        lax.all_gather(key_local, "blk", axis=2, tiled=True),
        lax.all_gather(value_local, "blk", axis=2, tiled=True),
    )
    key_heads = key_all.reshape(seq_local, 2 * seg_count, head_count, head_dim)
    value_heads = value_all.reshape(seq_local, 2 * seg_count, head_count, head_dim)
    query_u = (
        (query_rows + bias_u.astype(jnp.float32).reshape(-1))
        .astype(jnp.bfloat16)
        .reshape(seq_local, seg_rows, head_count, head_dim)
    )
    query_v = (
        (query_rows + bias_v.astype(jnp.float32).reshape(-1))
        .astype(jnp.bfloat16)
        .reshape(seq_local, seg_rows, head_count, head_dim)
    )
    w_rel_heads = w_rel.reshape(feature_width, head_count, head_dim)
    rel_coeff = jnp.einsum(
        "sihe,fhe->sihf", query_v, w_rel_heads, preferred_element_type=jnp.float32
    )
    sin_all, cos_all = angle_tables(jnp.arange(2 * seg_count).astype(jnp.float32), feature_width)
    key_pos = jnp.concatenate([cos_all, sin_all], axis=-1).astype(jnp.bfloat16)
    query_index = seg_count + seg_start + jnp.arange(seg_rows, dtype=jnp.int32)
    sin_q, cos_q = angle_tables(query_index.astype(jnp.float32), feature_width)
    sin_query = sin_q[None, :, None, :]
    cos_query = cos_q[None, :, None, :]
    coeff_sin = rel_coeff[..., :half_width]
    coeff_cos = rel_coeff[..., half_width:]
    query_pos = jnp.concatenate(
        [
            coeff_sin * sin_query + coeff_cos * cos_query,
            coeff_cos * sin_query - coeff_sin * cos_query,
        ],
        axis=-1,
    ).astype(jnp.bfloat16)
    allowed = jnp.arange(2 * seg_count, dtype=jnp.int32)[None, :] <= query_index[:, None]

    def score_block():
        raw_scores = (
            jnp.einsum("sihe,sjhe->shij", query_u, key_heads, preferred_element_type=jnp.float32)
            + jnp.einsum("sihf,jf->shij", query_pos, key_pos, preferred_element_type=jnp.float32)
        ) * score_scale
        return jnp.where(allowed[None, None], raw_scores, -1e30)

    scores = score_block()
    row_top = jnp.max(scores, axis=-1, keepdims=True)
    expo = jnp.exp(scores - row_top)
    row_total = jnp.sum(expo, axis=-1, keepdims=True)
    log_total = row_top + jnp.log(row_total)
    att_probs = (expo / row_total).astype(jnp.bfloat16)
    att_mixed = jnp.einsum(
        "shij,sjhe->sihe", att_probs, value_heads, preferred_element_type=jnp.float32
    )
    mixed_low = att_mixed.reshape(seq_local, seg_rows, feature_width).astype(jnp.bfloat16)
    residual = pooled + jnp.einsum(
        "sid,de->sie", mixed_low, w_out, preferred_element_type=jnp.float32
    )
    normed_two = layer_norm(residual, gain_two_f, shift_two_f)
    two_low = normed_two.astype(jnp.bfloat16)
    ffn_inner = jnp.einsum(
        "sid,df->sif", two_low, w_up, preferred_element_type=jnp.float32
    ) + bias_up.astype(jnp.float32)
    hidden_low = smooth_gate(ffn_inner).astype(jnp.bfloat16)
    branch_out = jnp.einsum(
        "sif,fd->sid", hidden_low, w_down, preferred_element_type=jnp.float32
    ) + bias_down.astype(jnp.float32)
    out_low = (residual + branch_out).astype(jnp.bfloat16)
    rows_all = lax.all_gather(out_low, "blk", axis=1, tiled=True)
    picked = jnp.take_along_axis(rows_all, segment[:, :, None], axis=1)
    out_chars = (chars_f + picked.astype(jnp.float32)).astype(jnp.bfloat16)
    new_memory = pooled.astype(jnp.bfloat16)
    grad_table = jax.vmap(full_table)(grad_f, segment)
    grad_output = lax.psum_scatter(grad_table, "blk", scatter_dimension=1, tiled=True)
    grad_down_low = grad_output.astype(jnp.bfloat16)
    grad_bias_down = jnp.sum(grad_down_low.astype(jnp.float32), axis=(0, 1))
    grad_w_down = jnp.einsum(
        "sif,sid->fd", hidden_low, grad_down_low, preferred_element_type=jnp.float32
    )
    grad_hidden = jnp.einsum(
        "sid,fd->sif", grad_down_low, w_down, preferred_element_type=jnp.float32
    )
    unused_value, gate_back = jax.vjp(smooth_gate, ffn_inner)
    grad_inner = gate_back(grad_hidden)[0].astype(jnp.bfloat16)
    grad_bias_up = jnp.sum(grad_inner.astype(jnp.float32), axis=(0, 1))
    grad_w_up = jnp.einsum("sid,sif->df", two_low, grad_inner, preferred_element_type=jnp.float32)
    grad_normed_two = jnp.einsum(
        "sif,df->sid", grad_inner, w_up, preferred_element_type=jnp.float32
    )
    unused_norm, norm_two_back = jax.vjp(layer_norm, residual, gain_two_f, shift_two_f)
    grad_resid_norm, grad_gain_two, grad_shift_two = norm_two_back(grad_normed_two)
    grad_residual = grad_output + grad_resid_norm
    grad_att_low = grad_residual.astype(jnp.bfloat16)
    grad_w_out = jnp.einsum(
        "sid,sie->de", mixed_low, grad_att_low, preferred_element_type=jnp.float32
    )
    grad_mixed = jnp.einsum("sie,de->sid", grad_att_low, w_out, preferred_element_type=jnp.float32)
    grad_mixed = grad_mixed.astype(jnp.bfloat16).reshape(seq_local, seg_rows, head_count, head_dim)
    scores_again = score_block()
    probs_full = jnp.exp(scores_again - log_total)
    probs_low = probs_full.astype(jnp.bfloat16)
    grad_probs = jnp.einsum(
        "sihe,sjhe->shij", grad_mixed, value_heads, preferred_element_type=jnp.float32
    )
    grad_values = jnp.einsum(
        "shij,sihe->sjhe", probs_low, grad_mixed, preferred_element_type=jnp.float32
    )
    prob_delta = jnp.sum(probs_full * grad_probs, axis=-1, keepdims=True)
    grad_scores = (probs_full * (grad_probs - prob_delta)).astype(jnp.bfloat16)
    grad_query_u = (
        jnp.einsum("shij,sjhe->sihe", grad_scores, key_heads, preferred_element_type=jnp.float32)
        * score_scale
    )
    grad_keys = (
        jnp.einsum("shij,sihe->sjhe", grad_scores, query_u, preferred_element_type=jnp.float32)
        * score_scale
    )
    grad_query_pos = (
        jnp.einsum("shij,jf->sihf", grad_scores, key_pos, preferred_element_type=jnp.float32)
        * score_scale
    )
    grad_first = grad_query_pos[..., :half_width]
    grad_second = grad_query_pos[..., half_width:]
    grad_coeff = jnp.concatenate(
        [
            grad_first * sin_query - grad_second * cos_query,
            grad_first * cos_query + grad_second * sin_query,
        ],
        axis=-1,
    ).astype(jnp.bfloat16)
    grad_w_rel = jnp.einsum(
        "sihf,sihe->fhe", grad_coeff, query_v, preferred_element_type=jnp.float32
    ).reshape(feature_width, feature_width)
    grad_query_v = jnp.einsum(
        "sihf,fhe->sihe", grad_coeff, w_rel_heads, preferred_element_type=jnp.float32
    )
    grad_bias_u = jnp.sum(grad_query_u, axis=(0, 1))
    grad_bias_v = jnp.sum(grad_query_v, axis=(0, 1))
    grad_query = (
        (grad_query_u + grad_query_v)
        .reshape(seq_local, seg_rows, feature_width)
        .astype(jnp.bfloat16)
    )
    grad_w_query = jnp.einsum(
        "sid,sie->de", normed_low, grad_query, preferred_element_type=jnp.float32
    )
    grad_normed = jnp.einsum("sie,de->sid", grad_query, w_query, preferred_element_type=jnp.float32)
    key_share, value_share = (
        lax.psum_scatter(
            grad_keys.reshape(seq_local, 2, seg_count, feature_width),
            "blk",
            scatter_dimension=2,
            tiled=True,
        ),
        lax.psum_scatter(
            grad_values.reshape(seq_local, 2, seg_count, feature_width),
            "blk",
            scatter_dimension=2,
            tiled=True,
        ),
    )
    key_low = key_share.astype(jnp.bfloat16)
    value_low = value_share.astype(jnp.bfloat16)
    grad_w_key = jnp.einsum(
        "sid,sie->de", mem_low, key_low[:, 0], preferred_element_type=jnp.float32
    ) + jnp.einsum("sid,sie->de", normed_low, key_low[:, 1], preferred_element_type=jnp.float32)
    grad_w_value = jnp.einsum(
        "sid,sie->de", mem_low, value_low[:, 0], preferred_element_type=jnp.float32
    ) + jnp.einsum("sid,sie->de", normed_low, value_low[:, 1], preferred_element_type=jnp.float32)
    grad_normed = grad_normed + jnp.einsum(
        "sie,de->sid", key_low[:, 1], w_key, preferred_element_type=jnp.float32
    )
    grad_normed = grad_normed + jnp.einsum(
        "sie,de->sid", value_low[:, 1], w_value, preferred_element_type=jnp.float32
    )
    grad_mem_normed = jnp.einsum(
        "sie,de->sid", key_low[:, 0], w_key, preferred_element_type=jnp.float32
    ) + jnp.einsum("sie,de->sid", value_low[:, 0], w_value, preferred_element_type=jnp.float32)
    unused_one, norm_one_back = jax.vjp(layer_norm, pooled, gain_one_f, shift_one_f)
    grad_pooled_norm, grad_gain_one, grad_shift_one = norm_one_back(grad_normed)
    unused_mem, norm_mem_back = jax.vjp(layer_norm, memory_f, gain_one_f, shift_one_f)
    unused_grad, grad_gain_mem, grad_shift_mem = norm_mem_back(grad_mem_normed)
    grad_gain_one = grad_gain_one + grad_gain_mem
    grad_shift_one = grad_shift_one + grad_shift_mem
    grad_pooled = grad_residual + grad_pooled_norm
    grad_sum = grad_pooled / own_lengths[:, :, None]
    grad_sum_all = lax.all_gather(grad_sum, "blk", axis=1, tiled=True)
    grad_chars = grad_f + jnp.take_along_axis(grad_sum_all, segment[:, :, None], axis=1)
    (
        grad_w_query,
        grad_w_key,
        grad_w_value,
        grad_w_rel,
        grad_w_out,
        grad_w_up,
        grad_w_down,
        grad_bias_u,
        grad_bias_v,
        grad_gain_one,
        grad_shift_one,
        grad_gain_two,
        grad_shift_two,
        grad_bias_up,
        grad_bias_down,
    ) = lax.psum(
        (
            grad_w_query,
            grad_w_key,
            grad_w_value,
            grad_w_rel,
            grad_w_out,
            grad_w_up,
            grad_w_down,
            grad_bias_u,
            grad_bias_v,
            grad_gain_one,
            grad_shift_one,
            grad_gain_two,
            grad_shift_two,
            grad_bias_up,
            grad_bias_down,
        ),
        ("seq", "blk"),
    )
    return (
        out_chars,
        grad_chars,
        new_memory,
        grad_w_query,
        grad_w_key,
        grad_w_value,
        grad_w_rel,
        grad_w_out,
        grad_w_up,
        grad_w_down,
        grad_bias_u,
        grad_bias_v,
        grad_gain_one,
        grad_shift_one,
        grad_gain_two,
        grad_shift_two,
        grad_bias_up,
        grad_bias_down,
    )


def solution(mesh):
    placed = (
        P("seq", "blk", None),
        P("seq", None),
        P("seq", "blk", None),
        P("seq", "blk", None),
        P(),
        P(),
        P(),
        P(),
        P(),
        P(),
        P(),
        P(),
        P(),
        P(),
        P(),
        P(),
        P(),
        P(),
        P(),
    )
    return jax.shard_map(
        shards_whole if fits_whole(mesh) else shards,
        mesh=mesh,
        in_specs=placed,
        out_specs=(
            P("seq", "blk", None),
            P("seq", "blk", None),
            P("seq", "blk", None),
            P(),
            P(),
            P(),
            P(),
            P(),
            P(),
            P(),
            P(),
            P(),
            P(),
            P(),
            P(),
            P(),
            P(),
            P(),
        ),
        check_vma=False,
    )
```

```python
import functools
import math
import types

import jax
import jax.numpy as jnp
import numpy as np
from jax import lax
from jax.experimental import pallas as pl
from jax.experimental.pallas import tpu as pltpu
from jax.sharding import PartitionSpec as P

F32, BF16 = jnp.float32, jnp.bfloat16
NT = (((1,), (1,)), ((), ()))


def mm(a, b):
    return jnp.dot(a, b, preferred_element_type=F32)


def mm_nt(a, b):
    return lax.dot_general(a, b, NT, preferred_element_type=F32)


def normalize(value):
    center = value - jnp.mean(value, axis=-1, keepdims=True)
    inv = lax.rsqrt(jnp.mean(center * center, axis=-1, keepdims=True) + 1e-05)
    return center * inv, inv


def norm_back(grad, unit, inv, gain):
    scaled = grad * gain
    along = jnp.mean(scaled * unit, axis=-1, keepdims=True)
    return inv * (scaled - jnp.mean(scaled, axis=-1, keepdims=True) - unit * along)


def gelu_parts(value):
    gate = 0.5 + 0.5 * lax.erf(value * 0.7071067811865476)
    return gate, gate + value * jnp.exp(-0.5 * value * value) * 0.3989422804014327


def ramp(shape, dim):
    return lax.broadcasted_iota(jnp.int32, shape, dim)


MESH = pl.DeviceIdType.MESH
HALF = 256
FACTOR = dict(x=2, y=2, near=2, far=2, z=4, xy=4)
AXES = ("x", "y", "near", "far")
PIECES = tuple((1024, f"tile{n}") for n in range(4)) + ((512, "middle"),) + tuple((512, f"pair{n}") for n in range(4))
BASES = tuple(sum(rows for rows, unused in PIECES[:n]) for n in range(len(PIECES) + 1))
VECTORS = ("bias_u", "bias_v", "gain_one", "shift_one", "gain_two", "shift_two", "bias_up", "bias_down")
ORDERS = (
    (("y", "near", "x", "far"), ("near", "y", "far", "x")),
    (("far", "y", "x", "near"), ("near", "x", "y", "far")),
    (("y", "x", "z"), ("x", "y", "z")),
    (("x", "y", "z"), ("y", "x", "z")),
    (("near", "far", "xy"), ("far", "near", "xy")),
    (("y", "x", "near", "far"), ("far", "x", "y", "near")),
    (("xy", "near", "far"), ("xy", "near", "far")),
    (("y", "x", "z"), ("x", "y", "z")),
    (("y", "x", "z"), ("y", "x", "z")),
)
DURING = (
    ((0, 0),), ((1, 0),), ((2, 0),), ((3, 0), (0, 1)), (), ((1, 1), (2, 1), (4, 0)), ((3, 1),), (),
    ((0, 2), (4, 1)), (), ((5, 0),), (), ((2, 2),), (), ((5, 1),), ((6, 0),), ((3, 2), (1, 2)), ((0, 3),),
    ((6, 1),), ((2, 3),), ((7, 0),), ((4, 2),), ((3, 3), (5, 2)), ((1, 3), (7, 1)), ((0, 4),), ((8, 0),),
    ((2, 4),),
)
AFTER = (
    (6, 2), (8, 1), (5, 3), (4, 3), (1, 4), (7, 2), (3, 4), (6, 3), (8, 2), (0, 5), (5, 4), (2, 5), (1, 5),
    (7, 3), (4, 4), (8, 3), (3, 5), (6, 4), (0, 6), (2, 6), (5, 5), (1, 6), (4, 5), (7, 4), (3, 6), (8, 4),
    (6, 5), (0, 7), (5, 6), (2, 7), (1, 7), (4, 6), (6, 6), (2, 8), (7, 5), (3, 7), (0, 8), (8, 5), (5, 7),
    (1, 8), (3, 8), (4, 7), (7, 6), (6, 7), (8, 6), (4, 8), (5, 8), (6, 8), (0, 9), (7, 7), (0, 10), (1, 9),
    (7, 8), (8, 7), (5, 9), (1, 10), (8, 8), (5, 10),
)
BACK_DURING = (10, 14)
BACK_AFTER = (6, 40, 44, 45, 46, 46)


class Place:
    def __init__(self):
        self.s = lax.axis_index("seq")
        self.b = lax.axis_index("blk")
        self.z, self.y = self.s // 2, self.s % 2
        self.x, self.c = self.b // 2, self.b % 2
        self.bit = dict(x=self.x, y=self.y, near=self.z % 2, far=self.z // 2)

    def group(self, k):
        return (self.s, (self.b + k) % 4)

    def core(self):
        return (self.s, self.b + 1 - 2 * self.c)

    def across(self):
        return (self.s, self.b + 2 - 4 * self.x)

    def move(self, axis):
        reach = dict(x=(0, 2), y=(1, 0), near=(2, 0), far=(4, 0))[axis]
        turn = 1 - 2 * self.bit[axis]
        return reach[0] * turn, reach[1] * turn

    def peers(self, axis):
        if axis == "z":
            return self.z, [(self.line(j), (self.z + j) % 4, (self.z + 4 - j) % 4) for j in (1, 2, 3)]
        if axis == "xy":
            out = []
            for across, along in ((1, 0), (0, 1), (1, 1)):
                x, y = self.x + across * (1 - 2 * self.x), self.y + along * (1 - 2 * self.y)
                device = (self.s + along * (1 - 2 * self.y), self.b + across * 2 * (1 - 2 * self.x))
                out.append((device, x + 2 * y, x + 2 * y))
            return self.x + 2 * self.y, out
        bit = self.bit[axis]
        return bit, [(self.pair(axis), 1 - bit, 1 - bit)]

    def stage(self, zero, one):
        if zero == one:
            return self.peers(zero)

        def pick(a, b):
            return a * (1 - self.c) + b * self.c

        (own_zero, peers_zero), (own_one, peers_one) = self.peers(zero), self.peers(one)
        peers = [
            ((pick(d[0], e[0]), pick(d[1], e[1])), pick(i, j), pick(f, g))
            for (d, i, f), (e, j, g) in zip(peers_zero, peers_one)
        ]
        return pick(own_zero, own_one), peers

    def line(self, j):
        return (((self.z + j) % 4) * 2 + self.y, self.b)

    def pair(self, axis):
        away = self.move(axis)
        return (self.s + away[0], self.b + away[1])


def rows_at(start, size):
    return pl.ds(pl.multiple_of(start, 16), size)


def remote(src, dst, send, recv, to):
    return pltpu.make_async_remote_copy(src, dst, send, recv, device_id=to, device_id_type=MESH)


def piece_rows(k):
    rows = [PIECES[k][0] // 2]
    for axis in ORDERS[k][0]:
        rows.append(rows[-1] // FACTOR[axis])
    return rows


def piece_lands(k):
    rows = piece_rows(k)
    return [rows[0]] + [(FACTOR[axis] - 1) * rows[n + 1] for n, axis in enumerate(ORDERS[k][0])]


LANDS = [[], 0]
for _k in range(len(PIECES)):
    LANDS[0].append([])
    for _rows in piece_lands(_k):
        LANDS[0][-1].append(LANDS[1])
        LANDS[1] += _rows


class Sum:
    def __init__(self, place, total, land, out, send, recv, store):
        self.p, self.g, self.land, self.out = place, total, land, out
        self.send, self.recv, self.store = send, recv, store
        known = {}
        self.stages = []
        for orders in ORDERS:
            for axes in zip(*orders):
                if axes not in known:
                    known[axes] = place.stage(*axes)
            self.stages.append([known[axes] for axes in zip(*orders)])

    def offset(self, k, n):
        rows = piece_rows(k)
        start = BASES[k] + self.p.c * rows[0]
        for m in range(n):
            start = start + self.stages[k][m][0] * rows[m + 1]
        return start

    def lands(self, k, n, start, size):
        return self.land.at[rows_at(LANDS[0][k][n] + start, size)]

    def copies(self, step, k, landing=False):
        p, rows = self.p, piece_rows(k)
        count = len(rows) - 1

        def copy(src, dst, to, j=0):
            return remote(src, dst, self.send.at[k, j], self.recv.at[k, step, j], to)

        if step == 0:
            src = self.g.at[rows_at(BASES[k] + (1 - p.c) * rows[0], rows[0])]
            return [copy(src, self.lands(k, 0, 0, rows[0]), p.core())]
        if step == 2 * count + 1:
            span = BASES[k] + (1 - p.c if landing else p.c) * rows[0]
            return [copy(self.lands(k, 0, 0, rows[0]), self.out.at[rows_at(span, rows[0])], p.core())]
        n = step - 1 if step <= count else 2 * count - step
        size = rows[n + 1]
        own, peers = self.stages[k][n]
        if step <= count:
            start = self.offset(k, n)
            return [
                copy(self.g.at[rows_at(start + at * size, size)], self.lands(k, n + 1, j * size, size), to, j)
                for j, (to, at, unused) in enumerate(peers)
            ]
        src = self.lands(k, n, own * size, size) if n == count - 1 else self.lands(k, n + 1, 0, size)
        return [
            copy(src, self.lands(k, n, (back if landing else own) * size, size), to, j)
            for j, (to, unused, back) in enumerate(peers)
        ]

    def own(self, k):
        rows = piece_rows(k)[0]
        span = rows_at(BASES[k] + self.p.c * rows, rows)
        return pltpu.make_async_copy(self.lands(k, 0, 0, rows), self.out.at[span], self.store.at[k])

    def added(self, k, n, start, size):
        mine = self.g[rows_at(self.offset(k, n) + start, size)]
        if n == 0 or len(self.stages[k][n - 1][1]) == 1:
            return mine + self.lands(k, n, start, size)[...]
        whole = piece_rows(k)[n]
        mine = mine.astype(F32)
        for j in range(len(self.stages[k][n - 1][1])):
            mine = mine + self.lands(k, n, j * whole + start, size)[...].astype(F32)
        return mine.astype(BF16)

    def step(self, k, step):
        rows = piece_rows(k)
        count = len(rows) - 1
        if step > 0:
            for copy in self.copies(step - 1, k):
                copy.wait_send()
            for copy in self.copies(step - 1, k, landing=True):
                copy.wait_recv()
        if 1 <= step <= count:
            n, size = step - 1, rows[step]
            own, peers = self.stages[k][n]
            copies = self.copies(step, k)
            for index, copy in zip([at for unused, at, other in peers] + [own], copies + [None]):
                part = self.added(k, n, index * size, size)
                self.g[rows_at(self.offset(k, n) + index * size, size)] = part
                if copy is not None:
                    copy.start()
        elif step <= 2 * count + 1:
            if step == count + 1:
                size = rows[count]
                self.lands(k, count - 1, self.stages[k][count - 1][0] * size, size)[...] = self.added(k, count, 0, size)
            for copy in self.copies(step, k):
                copy.start()
        if count + 2 <= step <= 2 * count:
            n = 2 * count - step
            size = rows[n + 1]
            self.lands(k, n, self.stages[k][n][0] * size, size)[...] = self.lands(k, n + 1, 0, size)[...]
        if step == 2 * count + 1:
            self.own(k).start()
        if step == 2 * count + 2:
            self.own(k).wait()


def pair_lanes(p, start=0, size=128):
    if isinstance(p, int):
        return slice(p * 128 + start, p * 128 + start + size)
    return pl.ds(pl.multiple_of(p * 128 + start, size), size)


def lane_mask(par):
    lane = ramp((1, 128), 1)
    return jnp.where((lane >= 64) == bool(par), 1.0, 0.0).astype(BF16)


def flip_matrix():
    return jnp.where(ramp((HALF, HALF), 0) + ramp((HALF, HALF), 1) == HALF - 1, 1.0, 0.0).astype(BF16)


def flip(flip_low, value):
    return jnp.concatenate(
        [mm(flip_low, value[r : r + HALF]) for r in range(0, value.shape[0], HALF)], axis=0
    ).astype(value.dtype)


def pool_matrix(end, length, first_place, places):
    place = (ramp((end.shape[0], places), 1) + first_place).astype(F32)
    return jnp.where((place < end) & (place >= end - length), 1.0, 0.0).astype(BF16)


def query_block(n, seg):
    keys = seg + HALF * (n + 1)
    return slice(n * HALF, (n + 1) * HALF), keys, 2 * seg - keys


def attend(n, seg, r):
    seen = ramp((HALF, HALF), 1) <= ramp((HALF, HALF), 0)
    lane = ramp((HALF, 128), 1)
    rows, keys, skip = query_block(n, seg)

    def products(head):
        lanes, keep = pair_lanes(head // 2), lane_mask(head % 2)
        near = mm_nt(r.query_u[rows, lanes] * keep, r.key[0:keys, lanes])
        return near, mm_nt(r.query_v[rows, lanes] * keep, r.place[skip : 2 * seg, lanes])

    ahead = products(0)
    for p in range(4):
        mixed, scale = [], []
        for head in (2 * p, 2 * p + 1):
            near, far = ahead
            ahead = products(head + 1) if head < 7 else None
            scores = near + pltpu.roll(far, keys - (HALF - 1), 1, stride=1, stride_axis=0)
            scores = jnp.concatenate(
                [scores[:, : keys - HALF], jnp.where(seen, scores[:, keys - HALF :], -1e30)], axis=1
            )
            expo = jnp.exp(scores - jnp.max(scores, axis=1, keepdims=True))
            probs = expo.astype(BF16)
            r.probs[head, rows, 0:keys] = probs
            mixed.append(mm(probs, r.value[0:keys, pair_lanes(p)]))
            scale.append(1.0 / jnp.sum(expo, axis=1, keepdims=True))
        scale = jnp.where(lane >= 64, scale[1], scale[0])
        r.scale[rows, pair_lanes(p)] = scale
        r.mixed[rows, pair_lanes(p)] = (jnp.where(lane >= 64, mixed[1], mixed[0]) * scale).astype(BF16)


def attend_back_pair(p, seg, r, between):
    lanes = pair_lanes(p)
    flip_low = flip_matrix()
    scale = 0.125
    lane = ramp((HALF, 128), 1)
    sums = [None] * 6
    bias = []
    for n in range(seg // HALF):
        rows, keys, skip = query_block(n, seg)
        key, value, place = r.key[0:keys, lanes], r.value[0:keys, lanes], r.place[skip : 2 * seg, lanes]
        grad_u, grad_v = [], []
        for par in range(2):
            keep = lane_mask(par)
            feats = pair_lanes(p, par * 64, 64)
            probs = r.probs[2 * p + par, rows, 0:keys]
            turned = mm(flip_low, probs)
            grad_mixed = r.grad_mixed[rows, lanes] * keep
            delta = jnp.sum(grad_mixed.astype(F32) * r.mixed_flip[rows, lanes].astype(F32), axis=1, keepdims=True)
            grad_scores = turned * (mm_nt(grad_mixed, value) - delta)
            near = grad_scores.astype(BF16)
            far = pltpu.roll(grad_scores, 0, 1, stride=1, stride_axis=0).astype(BF16)
            grad_u.append(mm(near, key) * scale)
            grad_v.append(mm(far, place) * scale)
            now = (
                mm(r.query_u_t[feats, rows], near),
                mm(r.grad_mixed_t[feats, rows], probs),
                mm(r.query_v_t[feats, rows], far),
            )
            for m in range(3):
                slot = par * 3 + m
                if n == 0:
                    sums[slot] = now[m]
                else:
                    old, new = sums[slot], now[m]
                    cut = old.shape[1]
                    if m < 2:
                        sums[slot] = jnp.concatenate([new[:, :cut] + old, new[:, cut:]], axis=1)
                    else:
                        sums[slot] = jnp.concatenate([new[:, :-cut], new[:, -cut:] + old], axis=1)
            between(n * 2 + par)
        grad_u = jnp.where(lane >= 64, grad_u[1], grad_u[0])
        grad_v = jnp.where(lane >= 64, grad_v[1], grad_v[0])
        bias.append((jnp.sum(grad_u, axis=0, keepdims=True), jnp.sum(grad_v, axis=0, keepdims=True)))
        r.grad_query[rows, lanes] = mm(flip_low, (grad_u + grad_v).astype(BF16)).astype(BF16)
    r.small[0:1, lanes] = sum(b[0] for b in bias)
    r.small[1:2, lanes] = sum(b[1] for b in bias)
    for par in range(2):
        feats = pair_lanes(p, par * 64, 64)
        for m, out in enumerate((r.grad_key_t, r.grad_value_t, r.grad_place_t)):
            out[feats, :] = sums[par * 3 + m].astype(BF16)


def pair_weights(p, seg, r, base):
    lanes = pair_lanes(p)
    grad_query_t = r.grad_query[:, lanes].astype(F32).T.astype(BF16)
    r.total[rows_at(base, 128)] = mm(grad_query_t, r.normed[seg : 2 * seg]).astype(BF16)
    r.total[rows_at(base + 128, 128)] = mm(r.grad_key_t[lanes, :], r.normed[...]).astype(BF16)
    r.total[rows_at(base + 256, 128)] = mm(r.grad_value_t[lanes, :], r.normed[...]).astype(BF16)
    r.total[rows_at(base + 384, 128)] = mm(r.grad_place_t[lanes, :], r.table[...]).astype(BF16)


def project_places(r):
    r.place[...] = mm(r.table[...], r.w_rel[...]).astype(BF16)


def project_memory(rows, r):
    unit, unused = normalize(r.memory[rows].astype(F32))
    low = (unit * r.vec("gain_one") + r.vec("shift_one")).astype(BF16)
    r.normed[rows] = low
    r.key[rows] = mm(low, r.w_key[...]).astype(BF16)
    r.value[rows] = mm(low, r.w_value[...]).astype(BF16)


def project_segments(n, seg, r):
    rows, keys, unused = query_block(n, seg)
    places = slice(keys - HALF, keys)
    unit, unused = normalize(r.pooled[rows])
    low = (unit * r.vec("gain_one") + r.vec("shift_one")).astype(BF16)
    r.normed[places] = low
    query = mm(low, r.w_query[...])
    scale = 0.125
    r.query_u[rows] = (query + r.vec("bias_u")).astype(BF16) * jnp.asarray(scale, BF16)
    r.query_v[rows] = (query + r.vec("bias_v")).astype(BF16) * jnp.asarray(scale, BF16)
    r.key[places] = mm(low, r.w_key[...]).astype(BF16)
    r.value[places] = mm(low, r.w_value[...]).astype(BF16)


def feed_forward_in(n, r):
    rows = slice(n * HALF, (n + 1) * HALF)
    residual = r.pooled[rows] + mm(r.mixed[rows], r.w_out[...])
    r.residual[rows] = residual
    unit, unused = normalize(residual)
    r.normed_two[rows] = (unit * r.vec("gain_two") + r.vec("shift_two")).astype(BF16)

    for m in range(r.w_up.shape[1] // 512):
        cols = slice(m * 512, (m + 1) * 512)
        inner = mm(r.normed_two[rows], r.w_up[:, cols]) + r.bias_up[0:1, cols]
        gate, slope = gelu_parts(inner)
        r.hidden[rows, cols] = (inner * gate).astype(BF16)
        r.slope[rows, cols] = slope.astype(BF16)


def feed_forward_out(n, r):
    rows = slice(n * HALF, (n + 1) * HALF)
    branch = mm(r.hidden[rows], r.w_down[...]) + r.vec("bias_down")
    r.out_rows[rows] = (r.residual[rows] + branch).astype(BF16)


def feed_forward_back(n, r):
    cols = slice(n * 512, (n + 1) * 512)
    r.total[rows_at(BASES[n], 512)] = mm(r.grad_down_t[...], r.hidden[:, cols]).astype(BF16)
    grad_hidden = mm_nt(r.grad_down[...], r.w_down[cols, :])
    low = (grad_hidden * r.slope[:, cols].astype(F32)).astype(BF16)
    r.grad_inner[:, cols] = low
    r.small[7 + n : 8 + n, :] = jnp.sum(low.astype(F32), axis=0, keepdims=True)
    r.total[rows_at(BASES[n] + 512, 512)] = mm(r.normed_two_t[...], low).astype(BF16)


def middle_back(r, base):
    grad_normed = mm_nt(r.grad_inner[...], r.w_up[...])
    unit, inv = normalize(r.residual[...])
    r.small[4:5, :] = jnp.sum(grad_normed * unit, axis=0, keepdims=True)
    r.small[5:6, :] = jnp.sum(grad_normed, axis=0, keepdims=True)
    grad = r.grad_output[...] + norm_back(grad_normed, unit, inv, r.vec("gain_two"))
    r.grad_residual[...] = grad
    low = grad.astype(BF16)
    mixed = r.mixed[...]
    r.total[rows_at(base, 512)] = mm(mixed.astype(F32).T.astype(BF16), low).astype(BF16)
    grad_mixed = (mm_nt(low, r.w_out[...]) * r.scale[...]).astype(BF16)
    r.grad_mixed_t[...] = grad_mixed.astype(F32).T.astype(BF16)
    flip_low = flip_matrix()
    r.grad_mixed[...] = flip(flip_low, grad_mixed)
    r.mixed_flip[...] = flip(flip_low, mixed)
    r.query_u_t[...] = flip(flip_low, r.query_u[...]).astype(F32).T.astype(BF16)
    r.query_v_t[...] = flip(flip_low, r.query_v[...]).astype(F32).T.astype(BF16)


def first_back(seg, r):
    grad_key = r.grad_key_t[...].astype(F32).T.astype(BF16)
    grad_value = r.grad_value_t[...].astype(F32).T.astype(BF16)
    grad_normed = mm_nt(r.grad_query[...], r.w_query[...])
    grad_normed += mm_nt(grad_key[seg:], r.w_key[...])
    grad_normed += mm_nt(grad_value[seg:], r.w_value[...])
    grad_mem = mm_nt(grad_key[:seg], r.w_key[...]) + mm_nt(grad_value[:seg], r.w_value[...])
    unit, inv = normalize(r.pooled[...])
    unit_mem, unused = normalize(r.memory[...].astype(F32))
    r.small[2:3, :] = jnp.sum(grad_normed * unit + grad_mem * unit_mem, axis=0, keepdims=True)
    r.small[3:4, :] = jnp.sum(grad_normed + grad_mem, axis=0, keepdims=True)
    return r.grad_residual[...] + norm_back(grad_normed, unit, inv, r.vec("gain_one"))


QUIET = 384
BACK_PARTS = 6
BACK_EARLY = BACK_PARTS * HALF // QUIET
KEPT_DURING = (18, 9, 14)


def sine_table(count, width):
    freqs = np.exp(np.arange(width // 2) * (-2.0 * math.log(10000.0) / width))
    angles = np.arange(count)[::-1, None] * freqs[None, :]
    return np.concatenate([np.sin(angles), np.cos(angles)], axis=1).astype(jnp.bfloat16)


def span_columns(lengths, low):
    seg = lengths.shape[1]
    lens = lengths.astype(F32).astype(BF16)
    row, col = ramp((seg - low, seg), 0) + low, ramp((seg - low, seg), 1)
    upto = jnp.where(col <= row, 1.0, 0.0).astype(BF16)
    same = jnp.where(col == row, 1.0, 0.0).astype(BF16)
    return mm_nt(upto, lens), mm_nt(same, lens)


def column(value, n):
    return jnp.sum(jnp.where(ramp(value.shape, 1) == n, value, 0.0), axis=1, keepdims=True)


WEIGHTS = ("w_query", "w_key", "w_value", "w_rel", "w_out", "w_up", "w_down")


def layer_scratch(seg, width, hidden, shapes):
    def low(*shape):
        return pltpu.VMEM(shape, BF16)

    def full(*shape):
        return pltpu.VMEM(shape, F32)

    return dict(
        table=low(2 * seg, width),
        w_query=low(width, width),
        w_key=low(width, width),
        w_value=low(width, width),
        w_rel=low(width, width),
        w_out=low(width, width),
        w_up=low(width, hidden),
        w_down=low(hidden, width),
        memory=low(seg, width),
        pooled=full(seg, width),
        normed=low(2 * seg, width),
        key=low(2 * seg, width),
        value=low(2 * seg, width),
        place=low(2 * seg, width),
        query_u=low(seg, width),
        query_v=low(seg, width),
        mixed=low(seg, width),
        probs=low(8, seg, 2 * seg),
        scale=full(seg, width),
        residual=full(seg, width),
        normed_two=low(seg, width),
        normed_two_t=low(width, seg),
        hidden=low(seg, hidden),
        slope=low(seg, hidden),
        grad_inner=low(seg, hidden),
        grad_output=full(seg, width),
        grad_down=low(seg, width),
        grad_down_t=low(width, seg),
        low_rows=low(seg, width),
        out_rows=low(seg, width),
        chars_quiet=low(QUIET, width),
        chars_parts=low(7, seg - QUIET, width),
        grads_quiet=low(QUIET, width),
        grads_parts=low(7, seg - QUIET, width),
        total=low(BASES[-1], width),
        land=low(LANDS[1], width),
        bias_up=full(1, hidden),
        vectors=full(16, width),
        lengths=pltpu.VMEM((4, seg), jnp.int32),
        **{f"raw_{name}": low(*shape) for name, shape in shapes.items()},
        small_load=pltpu.SemaphoreType.DMA((len(VECTORS) + 1,)),
        small=full(16, width),
        small_sum=full(5, 16, width),
        small_land=full(5, 16, width),
        load_sem=pltpu.SemaphoreType.DMA((len(WEIGHTS) + 1,)),
        stage_sem=pltpu.SemaphoreType.DMA((2, 4)),
        memory_send=pltpu.SemaphoreType.DMA((4,)),
        memory_recv=pltpu.SemaphoreType.DMA((4,)),
        quiet_send=pltpu.SemaphoreType.DMA((2, 4, 2)),
        quiet_recv=pltpu.SemaphoreType.DMA((2, 2)),
        parts_send=pltpu.SemaphoreType.DMA((2, 3)),
        parts_recv=pltpu.SemaphoreType.DMA((2, 3)),
        kept_send=pltpu.SemaphoreType.DMA((6,)),
        kept_recv=pltpu.SemaphoreType.DMA((4,)),
        back_send=pltpu.SemaphoreType.DMA((2, 5)),
        back_recv=pltpu.SemaphoreType.DMA((2, 2, 4)),
        sum_send=pltpu.SemaphoreType.DMA((len(PIECES), 3)),
        sum_recv=pltpu.SemaphoreType.DMA((len(PIECES), 10, 3)),
        small_send=pltpu.SemaphoreType.DMA((5,)),
        small_recv=pltpu.SemaphoreType.DMA((5,)),
        small_sem=pltpu.SemaphoreType.DMA,
        store_sem=pltpu.SemaphoreType.DMA((len(PIECES),)),
    )


class Rows:
    def __init__(self, r, place, way, source, stage, quiet, parts):
        self.r, self.p, self.way = r, place, way
        self.source, self.stage, self.quiet, self.parts = source, stage, quiet, parts

    def load(self, n):
        cols = pl.ds(pl.multiple_of(n * 512, 512), 512)
        return pltpu.make_async_copy(self.source.at[n], self.stage.at[:, cols], self.r.stage_sem.at[self.way, n])

    def quiet_copy(self, to, part):
        r = self.r
        span = pl.ds(0, HALF) if part == 0 else pl.ds(HALF, QUIET - HALF)
        src, dst = self.source.at[to, span], self.quiet.at[span]
        if to == 0:
            return pltpu.make_async_copy(src, dst, r.quiet_send.at[self.way, 0, part])
        return remote(src, dst, r.quiet_send.at[self.way, to, part], r.quiet_recv.at[self.way, part], (self.p.s, to))

    def start_quiet(self):
        @pl.when(self.p.b == 0)
        def _():
            for part in range(2):
                for to in (2, 3, 1, 0):
                    self.quiet_copy(to, part).start()

    def wait_quiet(self, part):
        @pl.when(self.p.b == 0)
        def _():
            self.quiet_copy(0, part).wait()

        @pl.when(self.p.b != 0)
        def _():
            self.quiet_copy(1, part).wait_recv()

    def parts_copy(self, n):
        src, dst, to = ((3, 1, self.p.core()), (4, 5, self.p.core()), (6, 2, self.p.across()))[n]
        return remote(
            self.parts.at[src],
            self.parts.at[dst],
            self.r.parts_send.at[self.way, n],
            self.r.parts_recv.at[self.way, n],
            to,
        )

    def part(self, to, ends, lens):
        self.load(to).wait()
        cols = pl.ds(pl.multiple_of(to * 512, 512), 512)
        chosen = pool_matrix(column(ends, to), column(lens, to), self.p.b * 512, 512)
        return mm(chosen, self.stage[:, cols])

    def start_parts(self, ends, lens):
        b, sibling, away = self.p.b, self.p.core()[1], self.p.across()[1]
        self.parts[4] = self.part(away + sibling - b, ends, lens).astype(BF16)
        self.parts_copy(1).start()
        self.parts[3] = self.part(sibling, ends, lens).astype(BF16)
        self.parts_copy(0).start()
        self.parts[6] = self.part(away, ends, lens).astype(BF16)
        self.parts[0] = self.part(b, ends, lens).astype(BF16)

    def join_parts(self):
        self.parts_copy(1).wait_recv()
        self.parts[6] = (self.parts[6].astype(F32) + self.parts[5].astype(F32)).astype(BF16)
        self.parts_copy(2).start()

    def wait_parts(self):
        self.parts_copy(0).wait_recv()
        self.parts_copy(2).wait_recv()
        return sum(self.parts[n].astype(F32) for n in range(3))

    def wait_sent(self):
        for n in range(3):
            self.parts_copy(n).wait_send()

        @pl.when(self.p.b == 0)
        def _():
            for part in range(2):
                for to in (1, 2, 3):
                    self.quiet_copy(to, part).wait_send()

    def back(self, rows, quiet_out, loud_out):
        self.rows, self.quiet_out, self.loud_out = rows, quiet_out, loud_out
        return self

    def loud_rows(self):
        return self.rows.at[pl.ds(QUIET, self.rows.shape[0] - QUIET)]

    def quiet_rows(self):
        return self.rows.at[pl.ds(0, QUIET)]

    def loud_copy(self, n, slot):
        r, p, way = self.r, self.p, self.way
        src = self.loud_out.at[slot] if n == 2 else self.loud_rows()
        to = p.across() if n == 1 else p.core()
        return remote(src, self.loud_out.at[slot], r.back_send.at[way, n], r.back_recv.at[way, 0, slot], to)

    def quiet_back(self, slot, start=0, size=QUIET):
        r, way = self.r, self.way
        span = pl.ds(start, size)
        return remote(
            self.rows.at[span],
            self.quiet_out.at[slot, span],
            r.back_send.at[way, 3],
            r.back_recv.at[way, 1, slot],
            (self.p.s, 0),
        )

    def own_copies(self):
        r, p, way = self.r, self.p, self.way
        loud = pltpu.make_async_copy(self.loud_rows(), self.loud_out.at[p.b], r.back_send.at[way, 4])
        quiet = pltpu.make_async_copy(self.quiet_rows(), self.quiet_out.at[0], r.back_send.at[way, 3])
        return loud, quiet

    def start_back(self):
        p = self.p
        loud, quiet = self.own_copies()
        self.loud_copy(1, p.b).start()
        self.loud_copy(0, p.b).start()
        pl.when(p.b == 0)(quiet.start)
        loud.start()

    def start_quiet_back(self, n):
        size = QUIET // BACK_PARTS
        pl.when(self.p.b != 0)(self.quiet_back(self.p.b, n * size, size).start)

    def pass_on(self):
        away = self.p.across()[1]
        self.loud_copy(1, away).wait_recv()
        self.loud_copy(2, away).start()

    def wait_back(self):
        p = self.p
        sibling, away = p.core()[1], p.across()[1]
        loud, quiet = self.own_copies()
        for n in (0, 1):
            self.loud_copy(n, p.b).wait_send()
        self.loud_copy(2, away).wait_send()
        loud.wait()
        pl.when(p.b != 0)(self.quiet_back(p.b).wait_send)
        pl.when(p.b == 0)(quiet.wait)
        self.loud_copy(0, sibling).wait_recv()
        self.loud_copy(2, away + sibling - p.b).wait_recv()

        @pl.when(p.b == 0)
        def _():
            for n in (1, 2, 3):
                self.quiet_back(n).wait_recv()


class Kept:
    def __init__(self, r, place, chars, kept):
        self.r, self.p, self.chars, self.kept = r, place, chars, kept
        self.count = kept.shape[1]

    def rows(self, to):
        return self.r.low_rows.at[pl.ds(to * self.count, self.count)]

    def late(self, to, slot):
        r = self.r
        return remote(self.rows(to), self.kept.at[slot], r.kept_send.at[4 + to - 2], r.kept_recv.at[slot], (self.p.s, to))

    def late_own(self, to):
        return pltpu.make_async_copy(self.rows(to), self.kept.at[to], self.r.kept_send.at[4 + to - 2])

    def early(self, slot):
        r = self.r
        src = self.chars.at[slot, pl.ds(self.count, self.count)]
        return remote(src, self.kept.at[slot], r.kept_send.at[slot], r.kept_recv.at[slot], (self.p.s, 1))

    def early_own(self, slot):
        src = self.chars.at[slot, pl.ds(0, self.count)]
        return pltpu.make_async_copy(src, self.kept.at[slot], self.r.kept_recv.at[slot])

    def start_late(self, to):
        pl.when(self.p.b != to)(self.late(to, self.p.b).start)
        pl.when(self.p.b == to)(self.late_own(to).start)

    def start_early(self):
        @pl.when(self.p.b == 0)
        def _():
            for slot in range(4):
                self.early_own(slot).start()
                self.early(slot).start()

    def wait(self):
        b = self.p.b

        @pl.when(b == 0)
        def _():
            for slot in range(4):
                self.early_own(slot).wait()
                self.early(slot).wait_send()

        @pl.when(b == 1)
        def _():
            for slot in range(4):
                self.early(slot).wait_recv()

        for to in (2, 3):
            pl.when(b != to)(self.late(to, b).wait_send)

            @pl.when(b == to)
            def _():
                self.late_own(to).wait()
                for slot in range(4):
                    if slot != to:
                        self.late(to, slot).wait_recv()


class Small:
    def __init__(self, r, place):
        self.r, self.p = r, place

    def source(self, step):
        return self.r.small if step == 0 else self.r.small_sum.at[step - 1]

    def copy(self, step):
        r, p = self.r, self.p
        to = p.core() if step == 0 else p.pair(AXES[step - 1])
        return remote(self.source(step), r.small_land.at[step], r.small_send.at[step], r.small_recv.at[step], to)

    def start(self, step):
        self.copy(step).start()

    def finish(self, step):
        self.copy(step).wait()
        self.r.small_sum[step] = self.source(step)[...] + self.r.small_land[step]


def layer_kernel(names, chars, lengths, memory, grad_out, *rest):
    count = len(VECTORS) + 1 + len(WEIGHTS)
    vectors, table, weights = rest[: len(VECTORS)], rest[len(VECTORS)], rest[len(VECTORS) + 1 : count]
    kept, out_quiet, out_loud, grad_quiet, grad_loud, total_out, small_out = rest[count : count + 7]
    r = types.SimpleNamespace(**dict(zip(names, rest[count + 7 :])))
    p = Place()
    seg, width = r.pooled.shape
    r.grad_residual, r.grad_mixed, r.grad_rows = r.grad_output, r.grad_down, r.normed_two
    for n, name in enumerate(("mixed_flip", "query_u_t", "query_v_t", "grad_mixed_t")):
        setattr(r, name, r.slope.at[:, n * width : (n + 1) * width])
    r.grad_key_t, r.grad_value_t = r.hidden.at[:, : 2 * seg], r.hidden.at[:, 2 * seg :]
    r.grad_place_t, r.grad_query = r.grad_inner.at[:, : 2 * seg], r.grad_inner.at[:, 2 * seg : 3 * seg]
    loads = [
        pltpu.make_async_copy(src, dst, r.load_sem.at[n])
        for n, (src, dst) in enumerate(
            zip((*weights, table), [getattr(r, name) for name in WEIGHTS] + [r.table])
        )
    ]
    chars_rows = Rows(r, p, 0, chars, r.hidden, r.chars_quiet, r.chars_parts).back(r.out_rows, out_quiet, out_loud)
    grads_rows = Rows(r, p, 1, grad_out, r.grad_inner, r.grads_quiet, r.grads_parts).back(
        r.grad_rows, grad_quiet, grad_loud
    )
    raw = [getattr(r, f"raw_{name}") for name in VECTORS]
    small_loads = [
        pltpu.make_async_copy(src, dst, r.small_load.at[n])
        for n, (src, dst) in enumerate(zip((*vectors, lengths), (*raw, r.lengths)))
    ]
    small_loads[-1].start()
    for n in range(4):
        chars_rows.load(n).start()
    for copy in small_loads[:-1]:
        copy.start()
    for n in range(4):
        grads_rows.load(n).start()
    for copy in loads:
        copy.start()
    r.vec = lambda name: r.vectors[VECTORS.index(name) : VECTORS.index(name) + 1, :]

    barrier = pltpu.get_barrier_semaphore()
    others = [p.group(1), p.group(2), p.group(3), *(to for to, unused, other in p.peers("xy")[1][1:]), p.line(1), p.line(2), p.line(3)]
    for other in others:
        pl.semaphore_signal(barrier, inc=1, device_id=other, device_id_type=MESH)
    pl.semaphore_wait(barrier, len(others))

    rows = memory.shape[1]

    def memory_copy(k, slot):
        to = (p.b + k) % 4
        return remote(
            memory.at[to], r.memory.at[rows_at(slot * rows, rows)], r.memory_send.at[k], r.memory_recv.at[slot], p.group(k)
        )

    own_memory = pltpu.make_async_copy(memory.at[p.b], r.memory.at[rows_at(p.b * rows, rows)], r.memory_send.at[0])
    for k in (2, 3, 1):
        memory_copy(k, p.b).start()
    own_memory.start()
    chars_rows.start_quiet()
    small_loads[-1].wait()
    ends, lens = span_columns(r.lengths[...], QUIET)
    chars_rows.start_parts(ends, lens)
    for copy in loads:
        copy.wait()
    for copy in small_loads[:-1]:
        copy.wait()
    for n, name in enumerate(VECTORS):
        value = raw[n][...].astype(F32)
        if name == "bias_up":
            r.bias_up[...] = value.reshape(1, -1)
        elif value.ndim == 2:
            r.vectors[n : n + 1, :] = jnp.concatenate([value[h : h + 1, :] for h in range(value.shape[0])], axis=1)
        else:
            r.vectors[n : n + 1, :] = value.reshape(1, -1)
    project_places(r)
    waits = (1 - p.x) * p.c
    pl.when(waits == 0)(chars_rows.join_parts)
    grads_rows.start_quiet()
    grads_rows.start_parts(ends, lens)
    own_memory.wait()
    memory_copy(1, p.core()[1]).wait_recv()
    project_memory(rows_at(p.x * 2 * rows, 2 * rows), r)
    for slot in (2 * (1 - p.x), 2 * (1 - p.x) + 1):
        memory_copy(1, slot).wait_recv()
    project_memory(rows_at((1 - p.x) * 2 * rows, 2 * rows), r)
    own_lens = column(lens, p.b)

    def forward(block):
        project_segments(block, seg, r)
        attend(block, seg, r)
        if block == 0:
            pl.when(waits == 1)(chars_rows.join_parts)
        feed_forward_in(block, r)

    chars_rows.wait_quiet(0)
    r.pooled[0:HALF] = chars_rows.quiet[0:HALF].astype(F32)
    forward(0)
    grads_rows.join_parts()
    feed_forward_out(0, r)
    for part in range(BACK_EARLY):
        chars_rows.start_quiet_back(part)
    chars_rows.wait_quiet(1)
    r.pooled[HALF:QUIET] = chars_rows.quiet[HALF:QUIET].astype(F32)
    r.pooled[QUIET:seg] = chars_rows.wait_parts() / own_lens
    r.low_rows[...] = r.pooled[...].astype(BF16)

    forward(1)
    grads_rows.wait_quiet(0)
    grads_rows.wait_quiet(1)
    r.grad_output[0:QUIET] = grads_rows.quiet[...].astype(F32)
    r.grad_output[QUIET:seg] = grads_rows.wait_parts()
    low = r.grad_output[...].astype(BF16)
    r.grad_down[...] = low
    r.grad_down_t[...] = low.astype(F32).T.astype(BF16)
    r.normed_two_t[...] = r.normed_two[...].astype(F32).T.astype(BF16)
    r.small[...] = jnp.zeros(r.small.shape, F32)
    r.small[6:7, :] = jnp.sum(low.astype(F32), axis=0, keepdims=True)

    sums = Sum(p, r.total, r.land, total_out, r.sum_send, r.sum_recv, r.store_sem)

    rows_kept = Kept(r, p, chars, kept)

    def take(n):
        if n == KEPT_DURING[0]:
            rows_kept.start_early()
        for to in (2, 3):
            if n == KEPT_DURING[to - 1]:
                rows_kept.start_late(to)
        for part, at in enumerate(BACK_DURING):
            if at == n:
                chars_rows.start_quiet_back(BACK_EARLY + part)
        for k, step in DURING[n]:
            sums.step(k, step)

    def between(pair, unit):
        for n in range(4):
            at = n * 5 + 6 + unit
            if DURING[at] or at in BACK_DURING or at in KEPT_DURING:
                pl.when(pair == n)(functools.partial(take, at))

    for n in range(4):
        feed_forward_back(n, r)
        take(n)
    feed_forward_out(1, r)
    chars_rows.start_back()
    take(4)
    middle_back(r, BASES[4])
    take(5)

    def back(n, carry):
        attend_back_pair(n, seg, r, functools.partial(between, n))
        pair_weights(n, seg, r, BASES[5] + n * PIECES[5][0])
        between(n, 4)
        return carry

    lax.fori_loop(0, 4, back, 0)
    grad_pooled = first_back(seg, r)
    r.grad_rows[0:QUIET] = grad_pooled[:QUIET].astype(BF16)
    r.grad_rows[QUIET:seg] = (grad_pooled[QUIET:] / own_lens).astype(BF16)
    grads_rows.start_back()
    small = Small(r, p)
    small_store = pltpu.make_async_copy(r.small_sum.at[4], small_out, r.small_sem)
    small.start(0)
    take(26)
    every = len(AFTER) // 12
    for n, (k, step) in enumerate(AFTER):
        for part, at in enumerate(BACK_AFTER):
            if at == n:
                grads_rows.start_quiet_back(part)
        if n % every == every - 1 and n // every < 10:
            at = n // every
            if at % 2 == 1:
                small.finish(at // 2)
                if at // 2 < 4:
                    small.start(at // 2 + 1)
                else:
                    small_store.start()
            if at == 4:
                chars_rows.pass_on()
            if at == 8:
                grads_rows.pass_on()
        sums.step(k, step)
    for k in (1, 2, 3):
        memory_copy(k, p.b).wait_send()
    rows_kept.wait()
    chars_rows.wait_sent()
    grads_rows.wait_sent()
    chars_rows.wait_back()
    grads_rows.wait_back()
    small_store.wait()


def spread_kernel(
    lengths, chars, grad_out, rows, out_quiet, out_loud, grad_quiet, grad_loud, wide, flat, pairs, small,
    out_chars, grad_chars, kept, w_query, w_key, w_value, w_rel, w_out, w_up, w_down, bias_u, bias_v, *vectors,
):
    n = pl.program_id(0)
    b = lax.axis_index("blk")
    places = chars.shape[1]
    seg = lengths.shape[1]
    lens = lengths[...].astype(F32).astype(BF16)
    row, col = ramp((seg - QUIET, seg), 0) + QUIET, ramp((seg - QUIET, seg), 1)
    upto = jnp.where(col <= row, 1.0, 0.0).astype(BF16)
    same = jnp.where(col == row, 1.0, 0.0).astype(BF16)
    pick = ramp((lengths.shape[0], seg - QUIET), 0) == n
    end = jnp.sum(jnp.where(pick, mm_nt(lens, upto), 0.0), axis=0, keepdims=True)
    length = jnp.sum(jnp.where(pick, mm_nt(lens, same), 0.0), axis=0, keepdims=True)
    place = (ramp((places, seg - QUIET), 0) + b * places).astype(F32)
    chosen = jnp.where((place < end) & (place >= end - length), 1.0, 0.0).astype(BF16)
    first = b == 0
    kept[...] = rows[...]
    for source, quiet, loud, out in (
        (chars, out_quiet, out_loud, out_chars),
        (grad_out, grad_quiet, grad_loud, grad_chars),
    ):
        spread = mm(chosen, loud[0])
        whole = source[0].astype(F32) + spread
        out[0, QUIET:places] = whole[QUIET:].astype(out.dtype)
        out[0, 0:QUIET] = (whole[:QUIET] + jnp.where(first, quiet[0].astype(F32), 0.0)).astype(out.dtype)
    w_down[...] = wide[0:512].astype(F32).T
    w_up[...] = wide[512:1024].astype(F32)
    w_out[...] = flat[...].astype(F32)
    for m, out in enumerate((w_query, w_key, w_value, w_rel)):
        out[...] = pairs[m * 128 : (m + 1) * 128].astype(F32).T
    for m, out in enumerate((bias_u, bias_v)):
        out[...] = jnp.concatenate([small[m : m + 1, h * 64 : (h + 1) * 64] for h in range(8)], axis=0)
    for m, out in enumerate(vectors[:4]):
        out[...] = small[2 + m : 3 + m, :]
    vectors[4][...] = jnp.concatenate([small[m : m + 1, :] for m in range(7, 11)], axis=1)
    vectors[5][...] = small[6:7, :]


def shards_whole(
    chars, seg_lengths, memory, grad_out, w_query, w_key, w_value, w_rel, w_out, w_up, w_down,
    bias_u, bias_v, gain_one, shift_one, gain_two, shift_two, bias_up, bias_down,
):
    count, places, width = chars.shape
    seg, hidden = seg_lengths.shape[1], w_up.shape[1]
    rows = memory.shape[1]
    table = jnp.asarray(sine_table(2 * seg, width))
    vectors = (bias_u, bias_v, gain_one, shift_one, gain_two, shift_two, bias_up, bias_down)
    scratch = layer_scratch(seg, width, hidden, {name: v.shape for name, v in zip(VECTORS, vectors)})
    anywhere, near = pl.BlockSpec(memory_space=pl.ANY), pl.BlockSpec(memory_space=pltpu.VMEM)
    loud = seg - QUIET
    kept, out_quiet, out_loud, grad_quiet, grad_loud, total, small = pl.pallas_call(
        functools.partial(layer_kernel, tuple(scratch)),
        out_shape=[
            jax.ShapeDtypeStruct((count, rows, width), BF16),
            jax.ShapeDtypeStruct((count, QUIET, width), BF16),
            jax.ShapeDtypeStruct((count, loud, width), BF16),
            jax.ShapeDtypeStruct((count, QUIET, width), BF16),
            jax.ShapeDtypeStruct((count, loud, width), BF16),
            jax.ShapeDtypeStruct((BASES[-1], width), BF16),
            jax.ShapeDtypeStruct((16, width), F32),
        ],
        in_specs=[anywhere] * (12 + len(VECTORS)),
        out_specs=[anywhere] * 7,
        scratch_shapes=list(scratch.values()),
        compiler_params=pltpu.CompilerParams(
            collective_id=0, has_side_effects=True, vmem_limit_bytes=VMEM_BYTES
        ),
        name="layer",
    )(
        chars, seg_lengths, memory, grad_out,
        *vectors, table,
        w_query, w_key, w_value, w_rel, w_out, w_up, w_down,
    )

    def block(shape, index):
        return pl.BlockSpec(shape, index)

    def each(*shape):
        return block((1, *shape), lambda n: (n, 0, 0))

    def whole(*shape):
        return block(shape, lambda n: (0, 0))

    vector = [(1, width)] * 4 + [(1, hidden), (1, width)]
    outs = pl.pallas_call(
        spread_kernel,
        grid=(count,),
        out_shape=[
            jax.ShapeDtypeStruct(chars.shape, BF16),
            jax.ShapeDtypeStruct(chars.shape, F32),
            jax.ShapeDtypeStruct(memory.shape, BF16),
            *[jax.ShapeDtypeStruct((width, width), F32)] * 5,
            jax.ShapeDtypeStruct((width, hidden), F32),
            jax.ShapeDtypeStruct((hidden, width), F32),
            *[jax.ShapeDtypeStruct(bias_u.shape, F32)] * 2,
            *[jax.ShapeDtypeStruct(shape, F32) for shape in vector],
        ],
        in_specs=[
            whole(*seg_lengths.shape),
            each(places, width),
            each(places, width),
            each(rows, width),
            each(QUIET, width),
            each(loud, width),
            each(QUIET, width),
            each(loud, width),
            block((1024, width), lambda n: (n, 0)),
            block((128, width), lambda n: (BASES[4] // 128 + n, 0)),
            block((512, width), lambda n: (BASES[5] // 512 + n, 0)),
            whole(16, width),
        ],
        out_specs=[
            each(places, width),
            each(places, width),
            each(rows, width),
            *[block((width, 128), lambda n: (0, n))] * 4,
            block((128, width), lambda n: (n, 0)),
            block((width, 512), lambda n: (0, n)),
            block((512, width), lambda n: (n, 0)),
            *[whole(*bias_u.shape)] * 2,
            *[whole(*shape) for shape in vector],
        ],
        compiler_params=pltpu.CompilerParams(vmem_limit_bytes=VMEM_BYTES),
        name="spread",
    )(seg_lengths, chars, grad_out, kept, out_quiet, out_loud, grad_quiet, grad_loud, total, total, total, small)
    return (*outs[:12], *[v.reshape(-1) for v in outs[12:]])


VMEM_BYTES = 64 * 2**20 - 2**16


def fits_whole(mesh):
    return dict(mesh.shape) == {"seq": 8, "blk": 4}


def layer_norm(value, gain, shift):
    center = value - jnp.mean(value, axis=-1, keepdims=True)
    spread = jnp.mean(center * center, axis=-1, keepdims=True)
    return center * lax.rsqrt(spread + 1e-05) * gain + shift


def angle_tables(places, feature_width):
    freqs = jnp.exp(
        jnp.arange(feature_width // 2, dtype=jnp.float32)
        * (-2.0 * math.log(10000.0) / feature_width)
    )
    angles = places[:, None] * freqs[None, :]
    return (jnp.sin(angles), jnp.cos(angles))


def smooth_gate(value):
    return jax.nn.gelu(value, approximate=False)


def segment_ids(seg_end, char_places):
    return jnp.sum((seg_end[:, None, :] <= char_places[None, :, None]).astype(jnp.int32), axis=2)


def shards(
    chars,
    seg_lengths,
    memory,
    grad_out,
    w_query,
    w_key,
    w_value,
    w_rel,
    w_out,
    w_up,
    w_down,
    bias_u,
    bias_v,
    gain_one,
    shift_one,
    gain_two,
    shift_two,
    bias_up,
    bias_down,
):
    blk_index = lax.axis_index("blk")
    seq_local, char_rows, feature_width = chars.shape
    seg_rows = memory.shape[1]
    seg_count = seg_lengths.shape[1]
    head_count, head_dim = bias_u.shape
    half_width = feature_width // 2
    score_scale = head_dim ** (-0.5)
    seg_start = blk_index * seg_rows
    gain_one_f = gain_one.astype(jnp.float32)
    shift_one_f = shift_one.astype(jnp.float32)
    gain_two_f = gain_two.astype(jnp.float32)
    shift_two_f = shift_two.astype(jnp.float32)
    seg_end = jnp.cumsum(seg_lengths, axis=1)
    char_places = blk_index * char_rows + jnp.arange(char_rows, dtype=jnp.int32)
    segment = segment_ids(seg_end, char_places)
    own_lengths = lax.dynamic_slice_in_dim(seg_lengths, seg_start, seg_rows, 1).astype(jnp.float32)
    chars_f = chars.astype(jnp.float32)
    grad_f = grad_out.astype(jnp.float32)

    def full_table(values, ids):
        return jax.ops.segment_sum(values, ids, num_segments=seg_count)

    part_sums = jax.vmap(full_table)(chars_f, segment)
    pooled_sum = lax.psum_scatter(part_sums, "blk", scatter_dimension=1, tiled=True)
    pooled = pooled_sum / own_lengths[:, :, None]
    normed = layer_norm(pooled, gain_one_f, shift_one_f)
    normed_low = normed.astype(jnp.bfloat16)
    memory_f = memory.astype(jnp.float32)
    mem_low = layer_norm(memory_f, gain_one_f, shift_one_f).astype(jnp.bfloat16)
    query_rows = jnp.einsum("sid,de->sie", normed_low, w_query, preferred_element_type=jnp.float32)
    key_local = jnp.stack(
        [
            jnp.einsum("sid,de->sie", mem_low, w_key, preferred_element_type=jnp.float32),
            jnp.einsum("sid,de->sie", normed_low, w_key, preferred_element_type=jnp.float32),
        ],
        axis=1,
    ).astype(jnp.bfloat16)
    value_local = jnp.stack(
        [
            jnp.einsum("sid,de->sie", mem_low, w_value, preferred_element_type=jnp.float32),
            jnp.einsum("sid,de->sie", normed_low, w_value, preferred_element_type=jnp.float32),
        ],
        axis=1,
    ).astype(jnp.bfloat16)
    key_all, value_all = (
        lax.all_gather(key_local, "blk", axis=2, tiled=True),
        lax.all_gather(value_local, "blk", axis=2, tiled=True),
    )
    key_heads = key_all.reshape(seq_local, 2 * seg_count, head_count, head_dim)
    value_heads = value_all.reshape(seq_local, 2 * seg_count, head_count, head_dim)
    query_u = (
        (query_rows + bias_u.astype(jnp.float32).reshape(-1))
        .astype(jnp.bfloat16)
        .reshape(seq_local, seg_rows, head_count, head_dim)
    )
    query_v = (
        (query_rows + bias_v.astype(jnp.float32).reshape(-1))
        .astype(jnp.bfloat16)
        .reshape(seq_local, seg_rows, head_count, head_dim)
    )
    w_rel_heads = w_rel.reshape(feature_width, head_count, head_dim)
    rel_coeff = jnp.einsum(
        "sihe,fhe->sihf", query_v, w_rel_heads, preferred_element_type=jnp.float32
    )
    sin_all, cos_all = angle_tables(jnp.arange(2 * seg_count).astype(jnp.float32), feature_width)
    key_pos = jnp.concatenate([cos_all, sin_all], axis=-1).astype(jnp.bfloat16)
    query_index = seg_count + seg_start + jnp.arange(seg_rows, dtype=jnp.int32)
    sin_q, cos_q = angle_tables(query_index.astype(jnp.float32), feature_width)
    sin_query = sin_q[None, :, None, :]
    cos_query = cos_q[None, :, None, :]
    coeff_sin = rel_coeff[..., :half_width]
    coeff_cos = rel_coeff[..., half_width:]
    query_pos = jnp.concatenate(
        [
            coeff_sin * sin_query + coeff_cos * cos_query,
            coeff_cos * sin_query - coeff_sin * cos_query,
        ],
        axis=-1,
    ).astype(jnp.bfloat16)
    allowed = jnp.arange(2 * seg_count, dtype=jnp.int32)[None, :] <= query_index[:, None]

    def score_block():
        raw_scores = (
            jnp.einsum("sihe,sjhe->shij", query_u, key_heads, preferred_element_type=jnp.float32)
            + jnp.einsum("sihf,jf->shij", query_pos, key_pos, preferred_element_type=jnp.float32)
        ) * score_scale
        return jnp.where(allowed[None, None], raw_scores, -1e30)

    scores = score_block()
    row_top = jnp.max(scores, axis=-1, keepdims=True)
    expo = jnp.exp(scores - row_top)
    row_total = jnp.sum(expo, axis=-1, keepdims=True)
    log_total = row_top + jnp.log(row_total)
    att_probs = (expo / row_total).astype(jnp.bfloat16)
    att_mixed = jnp.einsum(
        "shij,sjhe->sihe", att_probs, value_heads, preferred_element_type=jnp.float32
    )
    mixed_low = att_mixed.reshape(seq_local, seg_rows, feature_width).astype(jnp.bfloat16)
    residual = pooled + jnp.einsum(
        "sid,de->sie", mixed_low, w_out, preferred_element_type=jnp.float32
    )
    normed_two = layer_norm(residual, gain_two_f, shift_two_f)
    two_low = normed_two.astype(jnp.bfloat16)
    ffn_inner = jnp.einsum(
        "sid,df->sif", two_low, w_up, preferred_element_type=jnp.float32
    ) + bias_up.astype(jnp.float32)
    hidden_low = smooth_gate(ffn_inner).astype(jnp.bfloat16)
    branch_out = jnp.einsum(
        "sif,fd->sid", hidden_low, w_down, preferred_element_type=jnp.float32
    ) + bias_down.astype(jnp.float32)
    out_low = (residual + branch_out).astype(jnp.bfloat16)
    rows_all = lax.all_gather(out_low, "blk", axis=1, tiled=True)
    picked = jnp.take_along_axis(rows_all, segment[:, :, None], axis=1)
    out_chars = (chars_f + picked.astype(jnp.float32)).astype(jnp.bfloat16)
    new_memory = pooled.astype(jnp.bfloat16)
    grad_table = jax.vmap(full_table)(grad_f, segment)
    grad_output = lax.psum_scatter(grad_table, "blk", scatter_dimension=1, tiled=True)
    grad_down_low = grad_output.astype(jnp.bfloat16)
    grad_bias_down = jnp.sum(grad_down_low.astype(jnp.float32), axis=(0, 1))
    grad_w_down = jnp.einsum(
        "sif,sid->fd", hidden_low, grad_down_low, preferred_element_type=jnp.float32
    )
    grad_hidden = jnp.einsum(
        "sid,fd->sif", grad_down_low, w_down, preferred_element_type=jnp.float32
    )
    unused_value, gate_back = jax.vjp(smooth_gate, ffn_inner)
    grad_inner = gate_back(grad_hidden)[0].astype(jnp.bfloat16)
    grad_bias_up = jnp.sum(grad_inner.astype(jnp.float32), axis=(0, 1))
    grad_w_up = jnp.einsum("sid,sif->df", two_low, grad_inner, preferred_element_type=jnp.float32)
    grad_normed_two = jnp.einsum(
        "sif,df->sid", grad_inner, w_up, preferred_element_type=jnp.float32
    )
    unused_norm, norm_two_back = jax.vjp(layer_norm, residual, gain_two_f, shift_two_f)
    grad_resid_norm, grad_gain_two, grad_shift_two = norm_two_back(grad_normed_two)
    grad_residual = grad_output + grad_resid_norm
    grad_att_low = grad_residual.astype(jnp.bfloat16)
    grad_w_out = jnp.einsum(
        "sid,sie->de", mixed_low, grad_att_low, preferred_element_type=jnp.float32
    )
    grad_mixed = jnp.einsum("sie,de->sid", grad_att_low, w_out, preferred_element_type=jnp.float32)
    grad_mixed = grad_mixed.astype(jnp.bfloat16).reshape(seq_local, seg_rows, head_count, head_dim)
    scores_again = score_block()
    probs_full = jnp.exp(scores_again - log_total)
    probs_low = probs_full.astype(jnp.bfloat16)
    grad_probs = jnp.einsum(
        "sihe,sjhe->shij", grad_mixed, value_heads, preferred_element_type=jnp.float32
    )
    grad_values = jnp.einsum(
        "shij,sihe->sjhe", probs_low, grad_mixed, preferred_element_type=jnp.float32
    )
    prob_delta = jnp.sum(probs_full * grad_probs, axis=-1, keepdims=True)
    grad_scores = (probs_full * (grad_probs - prob_delta)).astype(jnp.bfloat16)
    grad_query_u = (
        jnp.einsum("shij,sjhe->sihe", grad_scores, key_heads, preferred_element_type=jnp.float32)
        * score_scale
    )
    grad_keys = (
        jnp.einsum("shij,sihe->sjhe", grad_scores, query_u, preferred_element_type=jnp.float32)
        * score_scale
    )
    grad_query_pos = (
        jnp.einsum("shij,jf->sihf", grad_scores, key_pos, preferred_element_type=jnp.float32)
        * score_scale
    )
    grad_first = grad_query_pos[..., :half_width]
    grad_second = grad_query_pos[..., half_width:]
    grad_coeff = jnp.concatenate(
        [
            grad_first * sin_query - grad_second * cos_query,
            grad_first * cos_query + grad_second * sin_query,
        ],
        axis=-1,
    ).astype(jnp.bfloat16)
    grad_w_rel = jnp.einsum(
        "sihf,sihe->fhe", grad_coeff, query_v, preferred_element_type=jnp.float32
    ).reshape(feature_width, feature_width)
    grad_query_v = jnp.einsum(
        "sihf,fhe->sihe", grad_coeff, w_rel_heads, preferred_element_type=jnp.float32
    )
    grad_bias_u = jnp.sum(grad_query_u, axis=(0, 1))
    grad_bias_v = jnp.sum(grad_query_v, axis=(0, 1))
    grad_query = (
        (grad_query_u + grad_query_v)
        .reshape(seq_local, seg_rows, feature_width)
        .astype(jnp.bfloat16)
    )
    grad_w_query = jnp.einsum(
        "sid,sie->de", normed_low, grad_query, preferred_element_type=jnp.float32
    )
    grad_normed = jnp.einsum("sie,de->sid", grad_query, w_query, preferred_element_type=jnp.float32)
    key_share, value_share = (
        lax.psum_scatter(
            grad_keys.reshape(seq_local, 2, seg_count, feature_width),
            "blk",
            scatter_dimension=2,
            tiled=True,
        ),
        lax.psum_scatter(
            grad_values.reshape(seq_local, 2, seg_count, feature_width),
            "blk",
            scatter_dimension=2,
            tiled=True,
        ),
    )
    key_low = key_share.astype(jnp.bfloat16)
    value_low = value_share.astype(jnp.bfloat16)
    grad_w_key = jnp.einsum(
        "sid,sie->de", mem_low, key_low[:, 0], preferred_element_type=jnp.float32
    ) + jnp.einsum("sid,sie->de", normed_low, key_low[:, 1], preferred_element_type=jnp.float32)
    grad_w_value = jnp.einsum(
        "sid,sie->de", mem_low, value_low[:, 0], preferred_element_type=jnp.float32
    ) + jnp.einsum("sid,sie->de", normed_low, value_low[:, 1], preferred_element_type=jnp.float32)
    grad_normed = grad_normed + jnp.einsum(
        "sie,de->sid", key_low[:, 1], w_key, preferred_element_type=jnp.float32
    )
    grad_normed = grad_normed + jnp.einsum(
        "sie,de->sid", value_low[:, 1], w_value, preferred_element_type=jnp.float32
    )
    grad_mem_normed = jnp.einsum(
        "sie,de->sid", key_low[:, 0], w_key, preferred_element_type=jnp.float32
    ) + jnp.einsum("sie,de->sid", value_low[:, 0], w_value, preferred_element_type=jnp.float32)
    unused_one, norm_one_back = jax.vjp(layer_norm, pooled, gain_one_f, shift_one_f)
    grad_pooled_norm, grad_gain_one, grad_shift_one = norm_one_back(grad_normed)
    unused_mem, norm_mem_back = jax.vjp(layer_norm, memory_f, gain_one_f, shift_one_f)
    unused_grad, grad_gain_mem, grad_shift_mem = norm_mem_back(grad_mem_normed)
    grad_gain_one = grad_gain_one + grad_gain_mem
    grad_shift_one = grad_shift_one + grad_shift_mem
    grad_pooled = grad_residual + grad_pooled_norm
    grad_sum = grad_pooled / own_lengths[:, :, None]
    grad_sum_all = lax.all_gather(grad_sum, "blk", axis=1, tiled=True)
    grad_chars = grad_f + jnp.take_along_axis(grad_sum_all, segment[:, :, None], axis=1)
    (
        grad_w_query,
        grad_w_key,
        grad_w_value,
        grad_w_rel,
        grad_w_out,
        grad_w_up,
        grad_w_down,
        grad_bias_u,
        grad_bias_v,
        grad_gain_one,
        grad_shift_one,
        grad_gain_two,
        grad_shift_two,
        grad_bias_up,
        grad_bias_down,
    ) = lax.psum(
        (
            grad_w_query,
            grad_w_key,
            grad_w_value,
            grad_w_rel,
            grad_w_out,
            grad_w_up,
            grad_w_down,
            grad_bias_u,
            grad_bias_v,
            grad_gain_one,
            grad_shift_one,
            grad_gain_two,
            grad_shift_two,
            grad_bias_up,
            grad_bias_down,
        ),
        ("seq", "blk"),
    )
    return (
        out_chars,
        grad_chars,
        new_memory,
        grad_w_query,
        grad_w_key,
        grad_w_value,
        grad_w_rel,
        grad_w_out,
        grad_w_up,
        grad_w_down,
        grad_bias_u,
        grad_bias_v,
        grad_gain_one,
        grad_shift_one,
        grad_gain_two,
        grad_shift_two,
        grad_bias_up,
        grad_bias_down,
    )


def solution(mesh):
    placed = (
        P("seq", "blk", None),
        P("seq", None),
        P("seq", "blk", None),
        P("seq", "blk", None),
        P(),
        P(),
        P(),
        P(),
        P(),
        P(),
        P(),
        P(),
        P(),
        P(),
        P(),
        P(),
        P(),
        P(),
        P(),
    )
    return jax.shard_map(
        shards_whole if fits_whole(mesh) else shards,
        mesh=mesh,
        in_specs=placed,
        out_specs=(
            P("seq", "blk", None),
            P("seq", "blk", None),
            P("seq", "blk", None),
            P(),
            P(),
            P(),
            P(),
            P(),
            P(),
            P(),
            P(),
            P(),
            P(),
            P(),
            P(),
            P(),
            P(),
            P(),
        ),
        check_vma=False,
    )
```

```python
import functools
import math
import types

import jax
import jax.numpy as jnp
import numpy as np
from jax import lax
from jax.experimental import pallas as pl
from jax.experimental.pallas import tpu as pltpu
from jax.sharding import PartitionSpec as P

F32, BF16 = jnp.float32, jnp.bfloat16
NT = (((1,), (1,)), ((), ()))


def mm(a, b):
    return jnp.dot(a, b, preferred_element_type=F32)


def mm_nt(a, b):
    return lax.dot_general(a, b, NT, preferred_element_type=F32)


def normalize(value):
    center = value - jnp.mean(value, axis=-1, keepdims=True)
    inv = lax.rsqrt(jnp.mean(center * center, axis=-1, keepdims=True) + 1e-05)
    return center * inv, inv


def norm_back(grad, unit, inv, gain):
    scaled = grad * gain
    along = jnp.mean(scaled * unit, axis=-1, keepdims=True)
    return inv * (scaled - jnp.mean(scaled, axis=-1, keepdims=True) - unit * along)


def gelu_parts(value):
    gate = 0.5 + 0.5 * lax.erf(value * 0.7071067811865476)
    return gate, gate + value * jnp.exp(-0.5 * value * value) * 0.3989422804014327


def ramp(shape, dim):
    return lax.broadcasted_iota(jnp.int32, shape, dim)


MESH = pl.DeviceIdType.MESH
HALF = 256
FACTOR = dict(x=2, y=2, near=2, far=2, z=4, xy=4)
AXES = ("x", "y", "near", "far")
PIECES = tuple((1024, f"tile{n}") for n in range(4)) + ((512, "middle"),) + tuple((512, f"pair{n}") for n in range(4))
BASES = tuple(sum(rows for rows, unused in PIECES[:n]) for n in range(len(PIECES) + 1))
VECTORS = ("bias_u", "bias_v", "gain_one", "shift_one", "gain_two", "shift_two", "bias_up", "bias_down")
ORDERS = (
    (("y", "near", "x", "far"), ("near", "y", "far", "x")),
    (("far", "y", "x", "near"), ("near", "x", "y", "far")),
    (("y", "x", "z"), ("x", "y", "z")),
    (("x", "y", "z"), ("y", "x", "z")),
    (("near", "far", "xy"), ("far", "near", "xy")),
    (("y", "x", "near", "far"), ("far", "x", "y", "near")),
    (("xy", "near", "far"), ("xy", "near", "far")),
    (("y", "x", "z"), ("x", "y", "z")),
    (("y", "x", "z"), ("y", "x", "z")),
)
DURING = (
    ((0, 0),), ((1, 0),), ((2, 0),), ((3, 0), (0, 1)), (), ((1, 1), (2, 1), (4, 0)), ((3, 1),), (),
    ((0, 2), (4, 1)), (), ((5, 0),), (), ((2, 2),), (), ((5, 1),), ((6, 0),), ((3, 2), (1, 2)), ((0, 3),),
    ((6, 1),), ((2, 3),), ((7, 0),), ((4, 2),), ((3, 3), (5, 2)), ((1, 3), (7, 1)), ((0, 4),), ((8, 0),),
    ((2, 4),),
)
AFTER = (
    (6, 2), (8, 1), (5, 3), (4, 3), (1, 4), (7, 2), (3, 4), (6, 3), (8, 2), (0, 5), (5, 4), (2, 5), (1, 5),
    (7, 3), (4, 4), (8, 3), (3, 5), (6, 4), (0, 6), (2, 6), (5, 5), (1, 6), (4, 5), (7, 4), (3, 6), (8, 4),
    (6, 5), (0, 7), (5, 6), (2, 7), (1, 7), (4, 6), (6, 6), (2, 8), (7, 5), (3, 7), (0, 8), (8, 5), (5, 7),
    (1, 8), (3, 8), (4, 7), (7, 6), (6, 7), (8, 6), (4, 8), (5, 8), (6, 8), (0, 9), (7, 7), (0, 10), (1, 9),
    (7, 8), (8, 7), (5, 9), (1, 10), (8, 8), (5, 10),
)
BACK_DURING = (10, 14)
BACK_AFTER = (6, 40, 44, 45, 46, 46)


class Place:
    def __init__(self):
        self.s = lax.axis_index("seq")
        self.b = lax.axis_index("blk")
        self.z, self.y = self.s // 2, self.s % 2
        self.x, self.c = self.b // 2, self.b % 2
        self.bit = dict(x=self.x, y=self.y, near=self.z % 2, far=self.z // 2)

    def group(self, k):
        return (self.s, (self.b + k) % 4)

    def core(self):
        return (self.s, self.b + 1 - 2 * self.c)

    def across(self):
        return (self.s, self.b + 2 - 4 * self.x)

    def move(self, axis):
        reach = dict(x=(0, 2), y=(1, 0), near=(2, 0), far=(4, 0))[axis]
        turn = 1 - 2 * self.bit[axis]
        return reach[0] * turn, reach[1] * turn

    def peers(self, axis):
        if axis == "z":
            return self.z, [(self.line(j), (self.z + j) % 4, (self.z + 4 - j) % 4) for j in (1, 2, 3)]
        if axis == "xy":
            out = []
            for across, along in ((1, 0), (0, 1), (1, 1)):
                x, y = self.x + across * (1 - 2 * self.x), self.y + along * (1 - 2 * self.y)
                device = (self.s + along * (1 - 2 * self.y), self.b + across * 2 * (1 - 2 * self.x))
                out.append((device, x + 2 * y, x + 2 * y))
            return self.x + 2 * self.y, out
        bit = self.bit[axis]
        return bit, [(self.pair(axis), 1 - bit, 1 - bit)]

    def stage(self, zero, one):
        if zero == one:
            return self.peers(zero)

        def pick(a, b):
            return a * (1 - self.c) + b * self.c

        (own_zero, peers_zero), (own_one, peers_one) = self.peers(zero), self.peers(one)
        peers = [
            ((pick(d[0], e[0]), pick(d[1], e[1])), pick(i, j), pick(f, g))
            for (d, i, f), (e, j, g) in zip(peers_zero, peers_one)
        ]
        return pick(own_zero, own_one), peers

    def line(self, j):
        return (((self.z + j) % 4) * 2 + self.y, self.b)

    def pair(self, axis):
        away = self.move(axis)
        return (self.s + away[0], self.b + away[1])


def rows_at(start, size):
    return pl.ds(pl.multiple_of(start, 16), size)


def remote(src, dst, send, recv, to):
    return pltpu.make_async_remote_copy(src, dst, send, recv, device_id=to, device_id_type=MESH)


def piece_rows(k):
    rows = [PIECES[k][0] // 2]
    for axis in ORDERS[k][0]:
        rows.append(rows[-1] // FACTOR[axis])
    return rows


def piece_lands(k):
    rows = piece_rows(k)
    return [rows[0]] + [(FACTOR[axis] - 1) * rows[n + 1] for n, axis in enumerate(ORDERS[k][0])]


def piece_peers(k):
    stages = [FACTOR[axis] - 1 for axis in ORDERS[k][0]]
    return [1, *stages, *stages[::-1], 1]


def starts(counts):
    out, end = [], 0
    for piece in counts:
        out.append([])
        for count in piece:
            out[-1].append(end)
            end += count
    return out, end


LANDS = starts([piece_lands(k) for k in range(len(PIECES))])
SENDS = starts([[max(piece_peers(k))] for k in range(len(PIECES))])
RECVS = starts([piece_peers(k) for k in range(len(PIECES))])


class Sum:
    def __init__(self, place, total, land, out, send, recv, store):
        self.p, self.g, self.land, self.out = place, total, land, out
        self.send, self.recv, self.store = send, recv, store
        known = {}
        self.stages = []
        for orders in ORDERS:
            for axes in zip(*orders):
                if axes not in known:
                    known[axes] = place.stage(*axes)
            self.stages.append([known[axes] for axes in zip(*orders)])

    def offset(self, k, n):
        rows = piece_rows(k)
        start = BASES[k] + self.p.c * rows[0]
        for m in range(n):
            start = start + self.stages[k][m][0] * rows[m + 1]
        return start

    def lands(self, k, n, start, size):
        return self.land.at[rows_at(LANDS[0][k][n] + start, size)]

    def copies(self, step, k, landing=False):
        p, rows = self.p, piece_rows(k)
        count = len(rows) - 1

        def copy(src, dst, to, j=0):
            return remote(src, dst, self.send.at[SENDS[0][k][0] + j], self.recv.at[RECVS[0][k][step] + j], to)

        if step == 0:
            src = self.g.at[rows_at(BASES[k] + (1 - p.c) * rows[0], rows[0])]
            return [copy(src, self.lands(k, 0, 0, rows[0]), p.core())]
        if step == 2 * count + 1:
            span = BASES[k] + (1 - p.c if landing else p.c) * rows[0]
            return [copy(self.lands(k, 0, 0, rows[0]), self.out.at[rows_at(span, rows[0])], p.core())]
        n = step - 1 if step <= count else 2 * count - step
        size = rows[n + 1]
        own, peers = self.stages[k][n]
        if step <= count:
            start = self.offset(k, n)
            return [
                copy(self.g.at[rows_at(start + at * size, size)], self.lands(k, n + 1, j * size, size), to, j)
                for j, (to, at, unused) in enumerate(peers)
            ]
        src = self.lands(k, n, own * size, size) if n == count - 1 else self.lands(k, n + 1, 0, size)
        return [
            copy(src, self.lands(k, n, (back if landing else own) * size, size), to, j)
            for j, (to, unused, back) in enumerate(peers)
        ]

    def own(self, k):
        rows = piece_rows(k)[0]
        span = rows_at(BASES[k] + self.p.c * rows, rows)
        return pltpu.make_async_copy(self.lands(k, 0, 0, rows), self.out.at[span], self.store.at[k])

    def added(self, k, n, start, size):
        mine = self.g[rows_at(self.offset(k, n) + start, size)]
        if n == 0 or len(self.stages[k][n - 1][1]) == 1:
            return mine + self.lands(k, n, start, size)[...]
        whole = piece_rows(k)[n]
        mine = mine.astype(F32)
        for j in range(len(self.stages[k][n - 1][1])):
            mine = mine + self.lands(k, n, j * whole + start, size)[...].astype(F32)
        return mine.astype(BF16)

    def step(self, k, step):
        rows = piece_rows(k)
        count = len(rows) - 1
        if step > 0:
            for copy in self.copies(step - 1, k):
                copy.wait_send()
            for copy in self.copies(step - 1, k, landing=True):
                copy.wait_recv()
        if 1 <= step <= count:
            n, size = step - 1, rows[step]
            own, peers = self.stages[k][n]
            copies = self.copies(step, k)
            for index, copy in zip([at for unused, at, other in peers] + [own], copies + [None]):
                part = self.added(k, n, index * size, size)
                self.g[rows_at(self.offset(k, n) + index * size, size)] = part
                if copy is not None:
                    copy.start()
        elif step <= 2 * count + 1:
            if step == count + 1:
                size = rows[count]
                self.lands(k, count - 1, self.stages[k][count - 1][0] * size, size)[...] = self.added(k, count, 0, size)
            for copy in self.copies(step, k):
                copy.start()
        if count + 2 <= step <= 2 * count:
            n = 2 * count - step
            size = rows[n + 1]
            self.lands(k, n, self.stages[k][n][0] * size, size)[...] = self.lands(k, n + 1, 0, size)[...]
        if step == 2 * count + 1:
            self.own(k).start()
        if step == 2 * count + 2:
            self.own(k).wait()


def pair_lanes(p, start=0, size=128):
    if isinstance(p, int):
        return slice(p * 128 + start, p * 128 + start + size)
    return pl.ds(pl.multiple_of(p * 128 + start, size), size)


def lane_mask(par):
    lane = ramp((1, 128), 1)
    return jnp.where((lane >= 64) == bool(par), 1.0, 0.0).astype(BF16)


def flip_matrix():
    return jnp.where(ramp((HALF, HALF), 0) + ramp((HALF, HALF), 1) == HALF - 1, 1.0, 0.0).astype(BF16)


def flip(flip_low, value):
    return jnp.concatenate(
        [mm(flip_low, value[r : r + HALF]) for r in range(0, value.shape[0], HALF)], axis=0
    ).astype(value.dtype)


def pool_matrix(end, length, first_place, places):
    place = (ramp((end.shape[0], places), 1) + first_place).astype(F32)
    return jnp.where((place < end) & (place >= end - length), 1.0, 0.0).astype(BF16)


def query_block(n, seg):
    keys = seg + HALF * (n + 1)
    return slice(n * HALF, (n + 1) * HALF), keys, 2 * seg - keys


def attend(n, seg, r):
    seen = ramp((HALF, HALF), 1) <= ramp((HALF, HALF), 0)
    lane = ramp((HALF, 128), 1)
    rows, keys, skip = query_block(n, seg)

    def products(head):
        lanes, keep = pair_lanes(head // 2), lane_mask(head % 2)
        near = mm_nt(r.query_u[rows, lanes] * keep, r.key[0:keys, lanes])
        return near, mm_nt(r.query_v[rows, lanes] * keep, r.place[skip : 2 * seg, lanes])

    ahead = products(0)
    for p in range(4):
        mixed, scale = [], []
        for head in (2 * p, 2 * p + 1):
            near, far = ahead
            ahead = products(head + 1) if head < 7 else None
            scores = near + pltpu.roll(far, keys - (HALF - 1), 1, stride=1, stride_axis=0)
            scores = jnp.concatenate(
                [scores[:, : keys - HALF], jnp.where(seen, scores[:, keys - HALF :], -1e30)], axis=1
            )
            expo = jnp.exp(scores - jnp.max(scores, axis=1, keepdims=True))
            probs = expo.astype(BF16)
            r.probs[head, rows, 0:keys] = probs
            mixed.append(mm(probs, r.value[0:keys, pair_lanes(p)]))
            scale.append(1.0 / jnp.sum(expo, axis=1, keepdims=True))
        scale = jnp.where(lane >= 64, scale[1], scale[0])
        r.scale[rows, pair_lanes(p)] = scale
        r.mixed[rows, pair_lanes(p)] = (jnp.where(lane >= 64, mixed[1], mixed[0]) * scale).astype(BF16)


def attend_back_pair(p, seg, r, between):
    lanes = pair_lanes(p)
    flip_low = flip_matrix()
    scale = 0.125
    lane = ramp((HALF, 128), 1)
    sums = [None] * 6
    bias = []
    for n in range(seg // HALF):
        rows, keys, skip = query_block(n, seg)
        key, value, place = r.key[0:keys, lanes], r.value[0:keys, lanes], r.place[skip : 2 * seg, lanes]
        grad_u, grad_v = [], []
        for par in range(2):
            keep = lane_mask(par)
            feats = pair_lanes(p, par * 64, 64)
            probs = r.probs[2 * p + par, rows, 0:keys]
            turned = mm(flip_low, probs)
            grad_mixed = r.grad_mixed[rows, lanes] * keep
            delta = jnp.sum(grad_mixed.astype(F32) * r.mixed_flip[rows, lanes].astype(F32), axis=1, keepdims=True)
            grad_scores = turned * (mm_nt(grad_mixed, value) - delta)
            near = grad_scores.astype(BF16)
            far = pltpu.roll(grad_scores, 0, 1, stride=1, stride_axis=0).astype(BF16)
            grad_u.append(mm(near, key) * scale)
            grad_v.append(mm(far, place) * scale)
            now = (
                mm(r.query_u_t[feats, rows], near),
                mm(r.grad_mixed_t[feats, rows], probs),
                mm(r.query_v_t[feats, rows], far),
            )
            for m in range(3):
                slot = par * 3 + m
                if n == 0:
                    sums[slot] = now[m]
                else:
                    old, new = sums[slot], now[m]
                    cut = old.shape[1]
                    if m < 2:
                        sums[slot] = jnp.concatenate([new[:, :cut] + old, new[:, cut:]], axis=1)
                    else:
                        sums[slot] = jnp.concatenate([new[:, :-cut], new[:, -cut:] + old], axis=1)
            between(n * 2 + par)
        grad_u = jnp.where(lane >= 64, grad_u[1], grad_u[0])
        grad_v = jnp.where(lane >= 64, grad_v[1], grad_v[0])
        bias.append((jnp.sum(grad_u, axis=0, keepdims=True), jnp.sum(grad_v, axis=0, keepdims=True)))
        r.grad_query[rows, lanes] = mm(flip_low, (grad_u + grad_v).astype(BF16)).astype(BF16)
    r.small[0:1, lanes] = sum(b[0] for b in bias)
    r.small[1:2, lanes] = sum(b[1] for b in bias)
    for par in range(2):
        feats = pair_lanes(p, par * 64, 64)
        for m, out in enumerate((r.grad_key_t, r.grad_value_t, r.grad_place_t)):
            out[feats, :] = sums[par * 3 + m].astype(BF16)


def pair_weights(p, seg, r, base):
    lanes = pair_lanes(p)
    grad_query_t = r.grad_query[:, lanes].astype(F32).T.astype(BF16)
    r.total[rows_at(base, 128)] = mm(grad_query_t, r.normed[seg : 2 * seg]).astype(BF16)
    r.total[rows_at(base + 128, 128)] = mm(r.grad_key_t[lanes, :], r.normed[...]).astype(BF16)
    r.total[rows_at(base + 256, 128)] = mm(r.grad_value_t[lanes, :], r.normed[...]).astype(BF16)
    r.total[rows_at(base + 384, 128)] = mm(r.grad_place_t[lanes, :], r.table[...]).astype(BF16)


def project_places(r):
    r.place[...] = mm(r.table[...], r.w_rel[...]).astype(BF16)


def project_memory(rows, r):
    unit, unused = normalize(r.memory[rows].astype(F32))
    low = (unit * r.vec("gain_one") + r.vec("shift_one")).astype(BF16)
    r.normed[rows] = low
    r.key[rows] = mm(low, r.w_key[...]).astype(BF16)
    r.value[rows] = mm(low, r.w_value[...]).astype(BF16)


def project_segments(n, seg, r):
    rows, keys, unused = query_block(n, seg)
    places = slice(keys - HALF, keys)
    unit, unused = normalize(r.pooled[rows])
    low = (unit * r.vec("gain_one") + r.vec("shift_one")).astype(BF16)
    r.normed[places] = low
    query = mm(low, r.w_query[...])
    scale = 0.125
    r.query_u[rows] = (query + r.vec("bias_u")).astype(BF16) * jnp.asarray(scale, BF16)
    r.query_v[rows] = (query + r.vec("bias_v")).astype(BF16) * jnp.asarray(scale, BF16)
    r.key[places] = mm(low, r.w_key[...]).astype(BF16)
    r.value[places] = mm(low, r.w_value[...]).astype(BF16)


def feed_forward_in(n, r):
    rows = slice(n * HALF, (n + 1) * HALF)
    residual = r.pooled[rows] + mm(r.mixed[rows], r.w_out[...])
    r.residual[rows] = residual
    unit, unused = normalize(residual)
    r.normed_two[rows] = (unit * r.vec("gain_two") + r.vec("shift_two")).astype(BF16)

    for m in range(r.w_up.shape[1] // 512):
        cols = slice(m * 512, (m + 1) * 512)
        inner = mm(r.normed_two[rows], r.w_up[:, cols]) + r.bias_up[0:1, cols]
        gate, slope = gelu_parts(inner)
        r.hidden[rows, cols] = (inner * gate).astype(BF16)
        r.slope[rows, cols] = slope.astype(BF16)


def feed_forward_out(n, r):
    rows = slice(n * HALF, (n + 1) * HALF)
    branch = mm(r.hidden[rows], r.w_down[...]) + r.vec("bias_down")
    r.out_rows[rows] = (r.residual[rows] + branch).astype(BF16)


def feed_forward_back(n, r):
    cols = slice(n * 512, (n + 1) * 512)
    r.total[rows_at(BASES[n], 512)] = mm(r.grad_down_t[...], r.hidden[:, cols]).astype(BF16)
    grad_hidden = mm_nt(r.grad_down[...], r.w_down[cols, :])
    low = (grad_hidden * r.slope[:, cols].astype(F32)).astype(BF16)
    r.grad_inner[:, cols] = low
    r.small[7 + n : 8 + n, :] = jnp.sum(low.astype(F32), axis=0, keepdims=True)
    r.total[rows_at(BASES[n] + 512, 512)] = mm(r.normed_two_t[...], low).astype(BF16)


def middle_back(r, base):
    grad_normed = mm_nt(r.grad_inner[...], r.w_up[...])
    unit, inv = normalize(r.residual[...])
    r.small[4:5, :] = jnp.sum(grad_normed * unit, axis=0, keepdims=True)
    r.small[5:6, :] = jnp.sum(grad_normed, axis=0, keepdims=True)
    grad = r.grad_output[...] + norm_back(grad_normed, unit, inv, r.vec("gain_two"))
    r.grad_residual[...] = grad
    low = grad.astype(BF16)
    mixed = r.mixed[...]
    r.total[rows_at(base, 512)] = mm(mixed.astype(F32).T.astype(BF16), low).astype(BF16)
    grad_mixed = (mm_nt(low, r.w_out[...]) * r.scale[...]).astype(BF16)
    r.grad_mixed_t[...] = grad_mixed.astype(F32).T.astype(BF16)
    flip_low = flip_matrix()
    r.grad_mixed[...] = flip(flip_low, grad_mixed)
    r.mixed_flip[...] = flip(flip_low, mixed)
    r.query_u_t[...] = flip(flip_low, r.query_u[...]).astype(F32).T.astype(BF16)
    r.query_v_t[...] = flip(flip_low, r.query_v[...]).astype(F32).T.astype(BF16)


def first_back(seg, r):
    grad_key = r.grad_key_t[...].astype(F32).T.astype(BF16)
    grad_value = r.grad_value_t[...].astype(F32).T.astype(BF16)
    grad_normed = mm_nt(r.grad_query[...], r.w_query[...])
    grad_normed += mm_nt(grad_key[seg:], r.w_key[...])
    grad_normed += mm_nt(grad_value[seg:], r.w_value[...])
    grad_mem = mm_nt(grad_key[:seg], r.w_key[...]) + mm_nt(grad_value[:seg], r.w_value[...])
    unit, inv = normalize(r.pooled[...])
    unit_mem, unused = normalize(r.memory[...].astype(F32))
    r.small[2:3, :] = jnp.sum(grad_normed * unit + grad_mem * unit_mem, axis=0, keepdims=True)
    r.small[3:4, :] = jnp.sum(grad_normed + grad_mem, axis=0, keepdims=True)
    return r.grad_residual[...] + norm_back(grad_normed, unit, inv, r.vec("gain_one"))


QUIET = 384
MOST = 16
BACK_PARTS = 6
BACK_EARLY = BACK_PARTS * HALF // QUIET
KEPT_DURING = (18, 9, 14)


def sine_table(count, width):
    freqs = np.exp(np.arange(width // 2) * (-2.0 * math.log(10000.0) / width))
    angles = np.arange(count)[::-1, None] * freqs[None, :]
    return np.concatenate([np.sin(angles), np.cos(angles)], axis=1).astype(jnp.bfloat16)


def span_columns(lengths, low):
    seg = lengths.shape[1]
    lens = lengths.astype(F32).astype(BF16)
    row, col = ramp((seg - low, seg), 0) + low, ramp((seg - low, seg), 1)
    upto = jnp.where(col <= row, 1.0, 0.0).astype(BF16)
    same = jnp.where(col == row, 1.0, 0.0).astype(BF16)
    return mm_nt(upto, lens), mm_nt(same, lens)


def column(value, n):
    return jnp.sum(jnp.where(ramp(value.shape, 1) == n, value, 0.0), axis=1, keepdims=True)


WEIGHTS = ("w_query", "w_key", "w_value", "w_rel", "w_out", "w_up", "w_down")


def layer_scratch(seg, width, hidden, shapes):
    def low(*shape):
        return pltpu.VMEM(shape, BF16)

    def full(*shape):
        return pltpu.VMEM(shape, F32)

    return dict(
        table=low(2 * seg, width),
        w_query=low(width, width),
        w_key=low(width, width),
        w_value=low(width, width),
        w_rel=low(width, width),
        w_out=low(width, width),
        w_up=low(width, hidden),
        w_down=low(hidden, width),
        memory=low(seg, width),
        pooled=full(seg, width),
        normed=low(2 * seg, width),
        key=low(2 * seg, width),
        value=low(2 * seg, width),
        place=low(2 * seg, width),
        query_u=low(seg, width),
        query_v=low(seg, width),
        mixed=low(seg, width),
        probs=low(8, seg, 2 * seg),
        scale=full(seg, width),
        residual=full(seg, width),
        normed_two=low(seg, width),
        normed_two_t=low(width, seg),
        hidden=low(seg, hidden),
        slope=low(seg, hidden),
        grad_inner=low(seg, hidden),
        grad_output=full(seg, width),
        grad_down=low(seg, width),
        grad_down_t=low(width, seg),
        low_rows=low(seg, width),
        out_rows=low(seg, width),
        chars_quiet=low(QUIET, width),
        chars_parts=low(7, seg - QUIET, width),
        grads_quiet=low(QUIET, width),
        grads_parts=low(7, seg - QUIET, width),
        total=low(BASES[-1], width),
        land=low(LANDS[1], width),
        bias_up=full(1, hidden),
        vectors=full(16, width),
        lengths=pltpu.VMEM((4, seg), jnp.int32),
        **{f"raw_{name}": low(*shape) for name, shape in shapes.items()},
        small_load=pltpu.SemaphoreType.DMA((len(VECTORS) + 1,)),
        small=full(16, width),
        small_sum=full(5, 16, width),
        small_land=full(5, 16, width),
        load_sem=pltpu.SemaphoreType.DMA((len(WEIGHTS) + 1,)),
        stage_sem=pltpu.SemaphoreType.DMA((2, 4)),
        memory_send=pltpu.SemaphoreType.DMA((4,)),
        memory_recv=pltpu.SemaphoreType.DMA((4,)),
        quiet_send=pltpu.SemaphoreType.DMA((2, 4, 2)),
        quiet_recv=pltpu.SemaphoreType.DMA((2, 2)),
        parts_send=pltpu.SemaphoreType.DMA((2, 3)),
        parts_recv=pltpu.SemaphoreType.DMA((2, 3)),
        kept_send=pltpu.SemaphoreType.DMA((6,)),
        kept_recv=pltpu.SemaphoreType.DMA((4,)),
        back_send=pltpu.SemaphoreType.DMA((2, 5)),
        back_recv=pltpu.SemaphoreType.DMA((2, 2, 4)),
        sum_send=pltpu.SemaphoreType.DMA((SENDS[1],)),
        sum_recv=pltpu.SemaphoreType.DMA((RECVS[1],)),
        small_send=pltpu.SemaphoreType.DMA((5,)),
        small_recv=pltpu.SemaphoreType.DMA((5,)),
        small_sem=pltpu.SemaphoreType.DMA,
        store_sem=pltpu.SemaphoreType.DMA((len(PIECES),)),
    )


def chip_spans(places, loud):
    half = 2 * places
    most = -(-(loud - half // MOST) // 16) * 16
    least = (half - QUIET) // MOST // 16 * 16
    return (0, most), (least, loud - least)


class Rows:
    def __init__(self, r, place, way, source, stage, quiet, parts):
        self.r, self.p, self.way = r, place, way
        self.source, self.stage, self.quiet, self.parts = source, stage, quiet, parts
        self.spans = [pl.ds(*span) for span in chip_spans(source.shape[1], parts.shape[1])]

    def load(self, n):
        cols = pl.ds(pl.multiple_of(n * 512, 512), 512)
        return pltpu.make_async_copy(self.source.at[n], self.stage.at[:, cols], self.r.stage_sem.at[self.way, n])

    def quiet_copy(self, to, part):
        r = self.r
        span = pl.ds(0, HALF) if part == 0 else pl.ds(HALF, QUIET - HALF)
        src, dst = self.source.at[to, span], self.quiet.at[span]
        if to == 0:
            return pltpu.make_async_copy(src, dst, r.quiet_send.at[self.way, 0, part])
        return remote(src, dst, r.quiet_send.at[self.way, to, part], r.quiet_recv.at[self.way, part], (self.p.s, to))

    def start_quiet(self):
        @pl.when(self.p.b == 0)
        def _():
            for part in range(2):
                for to in (2, 3, 1, 0):
                    self.quiet_copy(to, part).start()

    def wait_quiet(self, part):
        @pl.when(self.p.b == 0)
        def _():
            self.quiet_copy(0, part).wait()

        @pl.when(self.p.b != 0)
        def _():
            self.quiet_copy(1, part).wait_recv()

    def on_chip(self, act):
        for chip in range(2):
            pl.when(self.p.x == chip)(functools.partial(act, chip))

    def parts_copy(self, n, chip=None):
        src, dst, to = ((3, 1, self.p.core()), (4, 5, self.p.core()), (6, 2, self.p.across()))[n]
        span = pl.ds(0, self.parts.shape[1]) if chip is None else self.spans[chip]
        return remote(
            self.parts.at[src, span],
            self.parts.at[dst, span],
            self.r.parts_send.at[self.way, n],
            self.r.parts_recv.at[self.way, n],
            to,
        )

    def clear(self):
        self.parts[2] = jnp.zeros(self.parts.shape[1:], BF16)

    def part(self, to, ends, lens):
        self.load(to).wait()
        cols = pl.ds(pl.multiple_of(to * 512, 512), 512)
        chosen = pool_matrix(column(ends, to), column(lens, to), self.p.b * 512, 512)
        return mm(chosen, self.stage[:, cols])

    def start_parts(self, ends, lens):
        b, sibling, away = self.p.b, self.p.core()[1], self.p.across()[1]
        self.parts[4] = self.part(away + sibling - b, ends, lens).astype(BF16)
        self.parts_copy(1).start()
        self.parts[3] = self.part(sibling, ends, lens).astype(BF16)
        self.parts_copy(0).start()
        self.parts[6] = self.part(away, ends, lens).astype(BF16)
        self.parts[0] = self.part(b, ends, lens).astype(BF16)

    def join_parts(self):
        self.parts_copy(1).wait_recv()
        self.parts[6] = (self.parts[6].astype(F32) + self.parts[5].astype(F32)).astype(BF16)
        self.on_chip(lambda chip: self.parts_copy(2, chip).start())

    def wait_parts(self):
        self.parts_copy(0).wait_recv()
        self.on_chip(lambda chip: self.parts_copy(2, 1 - chip).wait_recv())
        return sum(self.parts[n].astype(F32) for n in range(3))

    def wait_sent(self):
        for n in range(2):
            self.parts_copy(n).wait_send()
        self.on_chip(lambda chip: self.parts_copy(2, chip).wait_send())

        @pl.when(self.p.b == 0)
        def _():
            for part in range(2):
                for to in (1, 2, 3):
                    self.quiet_copy(to, part).wait_send()

    def back(self, rows, quiet_out, loud_out):
        self.rows, self.quiet_out, self.loud_out = rows, quiet_out, loud_out
        return self

    def loud_rows(self, chip):
        start, size = chip_spans(self.source.shape[1], self.parts.shape[1])[chip]
        return self.rows.at[pl.ds(QUIET + start, size)]

    def quiet_rows(self):
        return self.rows.at[pl.ds(0, QUIET)]

    def loud_copy(self, n, slot, chip):
        r, p, way = self.r, self.p, self.way
        dst = self.loud_out.at[slot, self.spans[chip]]
        to = p.across() if n == 1 else p.core()
        return remote(
            dst if n == 2 else self.loud_rows(chip), dst, r.back_send.at[way, n], r.back_recv.at[way, 0, slot], to
        )

    def quiet_back(self, slot, start=0, size=QUIET):
        r, way = self.r, self.way
        span = pl.ds(start, size)
        return remote(
            self.rows.at[span],
            self.quiet_out.at[slot, span],
            r.back_send.at[way, 3],
            r.back_recv.at[way, 1, slot],
            (self.p.s, 0),
        )

    def own_quiet(self):
        return pltpu.make_async_copy(self.quiet_rows(), self.quiet_out.at[0], self.r.back_send.at[self.way, 3])

    def own_loud(self, chip):
        dst = self.loud_out.at[self.p.b, self.spans[chip]]
        return pltpu.make_async_copy(self.loud_rows(chip), dst, self.r.back_send.at[self.way, 4])

    def start_back(self):
        def start(chip):
            self.loud_copy(1, self.p.b, 1 - chip).start()
            self.loud_copy(0, self.p.b, chip).start()
            self.own_loud(chip).start()

        self.on_chip(start)
        pl.when(self.p.b == 0)(self.own_quiet().start)

    def start_quiet_back(self, n):
        size = QUIET // BACK_PARTS
        pl.when(self.p.b != 0)(self.quiet_back(self.p.b, n * size, size).start)

    def pass_on(self):
        away = self.p.across()[1]

        def pass_on(chip):
            self.loud_copy(1, away, chip).wait_recv()
            self.loud_copy(2, away, chip).start()

        self.on_chip(pass_on)

    def wait_back(self):
        p = self.p
        sibling, away = p.core()[1], p.across()[1]

        def wait(chip):
            self.loud_copy(0, p.b, chip).wait_send()
            self.loud_copy(1, p.b, 1 - chip).wait_send()
            self.loud_copy(2, away, chip).wait_send()
            self.own_loud(chip).wait()
            self.loud_copy(0, sibling, chip).wait_recv()
            self.loud_copy(2, away + sibling - p.b, chip).wait_recv()

        self.on_chip(wait)
        pl.when(p.b != 0)(self.quiet_back(p.b).wait_send)

        @pl.when(p.b == 0)
        def _():
            self.own_quiet().wait()
            for n in (1, 2, 3):
                self.quiet_back(n).wait_recv()


class Kept:
    def __init__(self, r, place, chars, kept):
        self.r, self.p, self.chars, self.kept = r, place, chars, kept
        self.count = kept.shape[1]

    def rows(self, to):
        return self.r.low_rows.at[pl.ds(to * self.count, self.count)]

    def late(self, to, slot):
        r = self.r
        return remote(self.rows(to), self.kept.at[slot], r.kept_send.at[4 + to - 2], r.kept_recv.at[slot], (self.p.s, to))

    def late_own(self, to):
        return pltpu.make_async_copy(self.rows(to), self.kept.at[to], self.r.kept_send.at[4 + to - 2])

    def early(self, slot):
        r = self.r
        src = self.chars.at[slot, pl.ds(self.count, self.count)]
        return remote(src, self.kept.at[slot], r.kept_send.at[slot], r.kept_recv.at[slot], (self.p.s, 1))

    def early_own(self, slot):
        src = self.chars.at[slot, pl.ds(0, self.count)]
        return pltpu.make_async_copy(src, self.kept.at[slot], self.r.kept_recv.at[slot])

    def start_late(self, to):
        pl.when(self.p.b != to)(self.late(to, self.p.b).start)
        pl.when(self.p.b == to)(self.late_own(to).start)

    def start_early(self):
        @pl.when(self.p.b == 0)
        def _():
            for slot in range(4):
                self.early_own(slot).start()
                self.early(slot).start()

    def wait(self):
        b = self.p.b

        @pl.when(b == 0)
        def _():
            for slot in range(4):
                self.early_own(slot).wait()
                self.early(slot).wait_send()

        @pl.when(b == 1)
        def _():
            for slot in range(4):
                self.early(slot).wait_recv()

        for to in (2, 3):
            pl.when(b != to)(self.late(to, b).wait_send)

            @pl.when(b == to)
            def _():
                self.late_own(to).wait()
                for slot in range(4):
                    if slot != to:
                        self.late(to, slot).wait_recv()


class Small:
    def __init__(self, r, place):
        self.r, self.p = r, place

    def source(self, step):
        return self.r.small if step == 0 else self.r.small_sum.at[step - 1]

    def copy(self, step):
        r, p = self.r, self.p
        to = p.core() if step == 0 else p.pair(AXES[step - 1])
        return remote(self.source(step), r.small_land.at[step], r.small_send.at[step], r.small_recv.at[step], to)

    def start(self, step):
        self.copy(step).start()

    def finish(self, step):
        self.copy(step).wait()
        self.r.small_sum[step] = self.source(step)[...] + self.r.small_land[step]


def layer_kernel(names, chars, lengths, memory, grad_out, *rest):
    count = len(VECTORS) + 1 + len(WEIGHTS)
    vectors, table, weights = rest[: len(VECTORS)], rest[len(VECTORS)], rest[len(VECTORS) + 1 : count]
    kept, out_quiet, out_loud, grad_quiet, grad_loud, total_out, small_out = rest[count : count + 7]
    r = types.SimpleNamespace(**dict(zip(names, rest[count + 7 :])))
    p = Place()
    seg, width = r.pooled.shape
    r.grad_residual, r.grad_mixed, r.grad_rows = r.grad_output, r.grad_down, r.normed_two
    for n, name in enumerate(("mixed_flip", "query_u_t", "query_v_t", "grad_mixed_t")):
        setattr(r, name, r.slope.at[:, n * width : (n + 1) * width])
    r.grad_key_t, r.grad_value_t = r.hidden.at[:, : 2 * seg], r.hidden.at[:, 2 * seg :]
    r.grad_place_t, r.grad_query = r.grad_inner.at[:, : 2 * seg], r.grad_inner.at[:, 2 * seg : 3 * seg]
    loads = [
        pltpu.make_async_copy(src, dst, r.load_sem.at[n])
        for n, (src, dst) in enumerate(
            zip((*weights, table), [getattr(r, name) for name in WEIGHTS] + [r.table])
        )
    ]
    chars_rows = Rows(r, p, 0, chars, r.hidden, r.chars_quiet, r.chars_parts).back(r.out_rows, out_quiet, out_loud)
    grads_rows = Rows(r, p, 1, grad_out, r.grad_inner, r.grads_quiet, r.grads_parts).back(
        r.grad_rows, grad_quiet, grad_loud
    )
    raw = [getattr(r, f"raw_{name}") for name in VECTORS]
    small_loads = [
        pltpu.make_async_copy(src, dst, r.small_load.at[n])
        for n, (src, dst) in enumerate(zip((*vectors, lengths), (*raw, r.lengths)))
    ]
    small_loads[-1].start()
    for n in range(4):
        chars_rows.load(n).start()
    for copy in small_loads[:-1]:
        copy.start()
    for n in range(4):
        grads_rows.load(n).start()
    for copy in loads:
        copy.start()
    r.vec = lambda name: r.vectors[VECTORS.index(name) : VECTORS.index(name) + 1, :]

    chars_rows.clear()
    grads_rows.clear()
    barrier = pltpu.get_barrier_semaphore()
    others = [p.group(1), p.group(2), p.group(3), *(to for to, unused, other in p.peers("xy")[1][1:]), p.line(1), p.line(2), p.line(3)]
    for other in others:
        pl.semaphore_signal(barrier, inc=1, device_id=other, device_id_type=MESH)
    pl.semaphore_wait(barrier, len(others))

    rows = memory.shape[1]

    def memory_copy(k, slot):
        to = (p.b + k) % 4
        return remote(
            memory.at[to], r.memory.at[rows_at(slot * rows, rows)], r.memory_send.at[k], r.memory_recv.at[slot], p.group(k)
        )

    own_memory = pltpu.make_async_copy(memory.at[p.b], r.memory.at[rows_at(p.b * rows, rows)], r.memory_send.at[0])
    for k in (2, 3, 1):
        memory_copy(k, p.b).start()
    own_memory.start()
    chars_rows.start_quiet()
    small_loads[-1].wait()
    ends, lens = span_columns(r.lengths[...], QUIET)
    chars_rows.start_parts(ends, lens)
    for copy in loads:
        copy.wait()
    for copy in small_loads[:-1]:
        copy.wait()
    for n, name in enumerate(VECTORS):
        value = raw[n][...].astype(F32)
        if name == "bias_up":
            r.bias_up[...] = value.reshape(1, -1)
        elif value.ndim == 2:
            r.vectors[n : n + 1, :] = jnp.concatenate([value[h : h + 1, :] for h in range(value.shape[0])], axis=1)
        else:
            r.vectors[n : n + 1, :] = value.reshape(1, -1)
    project_places(r)
    waits = (1 - p.x) * p.c
    pl.when(waits == 0)(chars_rows.join_parts)
    grads_rows.start_quiet()
    grads_rows.start_parts(ends, lens)
    own_memory.wait()
    memory_copy(1, p.core()[1]).wait_recv()
    project_memory(rows_at(p.x * 2 * rows, 2 * rows), r)
    for slot in (2 * (1 - p.x), 2 * (1 - p.x) + 1):
        memory_copy(1, slot).wait_recv()
    project_memory(rows_at((1 - p.x) * 2 * rows, 2 * rows), r)
    own_lens = column(lens, p.b)

    def forward(block):
        project_segments(block, seg, r)
        attend(block, seg, r)
        if block == 0:
            pl.when(waits == 1)(chars_rows.join_parts)
        feed_forward_in(block, r)

    chars_rows.wait_quiet(0)
    r.pooled[0:HALF] = chars_rows.quiet[0:HALF].astype(F32)
    forward(0)
    grads_rows.join_parts()
    feed_forward_out(0, r)
    for part in range(BACK_EARLY):
        chars_rows.start_quiet_back(part)
    chars_rows.wait_quiet(1)
    r.pooled[HALF:QUIET] = chars_rows.quiet[HALF:QUIET].astype(F32)
    r.pooled[QUIET:seg] = chars_rows.wait_parts() / own_lens
    r.low_rows[...] = r.pooled[...].astype(BF16)

    forward(1)
    grads_rows.wait_quiet(0)
    grads_rows.wait_quiet(1)
    r.grad_output[0:QUIET] = grads_rows.quiet[...].astype(F32)
    r.grad_output[QUIET:seg] = grads_rows.wait_parts()
    low = r.grad_output[...].astype(BF16)
    r.grad_down[...] = low
    r.grad_down_t[...] = low.astype(F32).T.astype(BF16)
    r.normed_two_t[...] = r.normed_two[...].astype(F32).T.astype(BF16)
    r.small[...] = jnp.zeros(r.small.shape, F32)
    r.small[6:7, :] = jnp.sum(low.astype(F32), axis=0, keepdims=True)

    sums = Sum(p, r.total, r.land, total_out, r.sum_send, r.sum_recv, r.store_sem)

    rows_kept = Kept(r, p, chars, kept)

    def take(n):
        if n == KEPT_DURING[0]:
            rows_kept.start_early()
        for to in (2, 3):
            if n == KEPT_DURING[to - 1]:
                rows_kept.start_late(to)
        for part, at in enumerate(BACK_DURING):
            if at == n:
                chars_rows.start_quiet_back(BACK_EARLY + part)
        for k, step in DURING[n]:
            sums.step(k, step)

    def between(pair, unit):
        for n in range(4):
            at = n * 5 + 6 + unit
            if DURING[at] or at in BACK_DURING or at in KEPT_DURING:
                pl.when(pair == n)(functools.partial(take, at))

    for n in range(4):
        feed_forward_back(n, r)
        take(n)
    feed_forward_out(1, r)
    chars_rows.start_back()
    take(4)
    middle_back(r, BASES[4])
    take(5)

    def back(n, carry):
        attend_back_pair(n, seg, r, functools.partial(between, n))
        pair_weights(n, seg, r, BASES[5] + n * PIECES[5][0])
        between(n, 4)
        return carry

    lax.fori_loop(0, 4, back, 0)
    grad_pooled = first_back(seg, r)
    r.grad_rows[0:QUIET] = grad_pooled[:QUIET].astype(BF16)
    r.grad_rows[QUIET:seg] = (grad_pooled[QUIET:] / own_lens).astype(BF16)
    grads_rows.start_back()
    small = Small(r, p)
    small_store = pltpu.make_async_copy(r.small_sum.at[4], small_out, r.small_sem)
    small.start(0)
    take(26)
    every = len(AFTER) // 12
    for n, (k, step) in enumerate(AFTER):
        for part, at in enumerate(BACK_AFTER):
            if at == n:
                grads_rows.start_quiet_back(part)
        if n % every == every - 1 and n // every < 10:
            at = n // every
            if at % 2 == 1:
                small.finish(at // 2)
                if at // 2 < 4:
                    small.start(at // 2 + 1)
                else:
                    small_store.start()
            if at == 4:
                chars_rows.pass_on()
            if at == 8:
                grads_rows.pass_on()
        sums.step(k, step)
    for k in (1, 2, 3):
        memory_copy(k, p.b).wait_send()
    rows_kept.wait()
    chars_rows.wait_sent()
    grads_rows.wait_sent()
    chars_rows.wait_back()
    grads_rows.wait_back()
    small_store.wait()


def spread_kernel(
    lengths, chars, grad_out, rows, out_quiet, out_loud, grad_quiet, grad_loud, wide, flat, pairs, small,
    out_chars, grad_chars, kept, w_query, w_key, w_value, w_rel, w_out, w_up, w_down, bias_u, bias_v, *vectors,
):
    n = pl.program_id(0)
    b = lax.axis_index("blk")
    places = chars.shape[1]
    seg = lengths.shape[1]
    lens = lengths[...].astype(F32).astype(BF16)
    row, col = ramp((seg - QUIET, seg), 0) + QUIET, ramp((seg - QUIET, seg), 1)
    upto = jnp.where(col <= row, 1.0, 0.0).astype(BF16)
    same = jnp.where(col == row, 1.0, 0.0).astype(BF16)
    pick = ramp((lengths.shape[0], seg - QUIET), 0) == n
    end = jnp.sum(jnp.where(pick, mm_nt(lens, upto), 0.0), axis=0, keepdims=True)
    length = jnp.sum(jnp.where(pick, mm_nt(lens, same), 0.0), axis=0, keepdims=True)
    place = (ramp((places, seg - QUIET), 0) + b * places).astype(F32)
    chosen = jnp.where((place < end) & (place >= end - length), 1.0, 0.0).astype(BF16)
    first = b == 0
    spans = chip_spans(places, seg - QUIET)
    here = ramp((seg - QUIET, 1), 0)
    inside = [(here >= start) & (here < start + size) for start, size in spans]
    there = jnp.where(b < 2, inside[0].astype(F32), inside[1].astype(F32)) > 0
    kept[...] = rows[...]
    for source, quiet, loud, out in (
        (chars, out_quiet, out_loud, out_chars),
        (grad_out, grad_quiet, grad_loud, grad_chars),
    ):
        spread = mm(chosen, jnp.where(there, loud[0].astype(F32), 0.0).astype(BF16))
        whole = source[0].astype(F32) + spread
        out[0, QUIET:places] = whole[QUIET:].astype(out.dtype)
        out[0, 0:QUIET] = (whole[:QUIET] + jnp.where(first, quiet[0].astype(F32), 0.0)).astype(out.dtype)
    w_down[...] = wide[0:512].astype(F32).T
    w_up[...] = wide[512:1024].astype(F32)
    w_out[...] = flat[...].astype(F32)
    for m, out in enumerate((w_query, w_key, w_value, w_rel)):
        out[...] = pairs[m * 128 : (m + 1) * 128].astype(F32).T
    for m, out in enumerate((bias_u, bias_v)):
        out[...] = jnp.concatenate([small[m : m + 1, h * 64 : (h + 1) * 64] for h in range(8)], axis=0)
    for m, out in enumerate(vectors[:4]):
        out[...] = small[2 + m : 3 + m, :]
    vectors[4][...] = jnp.concatenate([small[m : m + 1, :] for m in range(7, 11)], axis=1)
    vectors[5][...] = small[6:7, :]


def shards_whole(
    chars, seg_lengths, memory, grad_out, w_query, w_key, w_value, w_rel, w_out, w_up, w_down,
    bias_u, bias_v, gain_one, shift_one, gain_two, shift_two, bias_up, bias_down,
):
    count, places, width = chars.shape
    seg, hidden = seg_lengths.shape[1], w_up.shape[1]
    rows = memory.shape[1]
    table = jnp.asarray(sine_table(2 * seg, width))
    vectors = (bias_u, bias_v, gain_one, shift_one, gain_two, shift_two, bias_up, bias_down)
    scratch = layer_scratch(seg, width, hidden, {name: v.shape for name, v in zip(VECTORS, vectors)})
    anywhere, near = pl.BlockSpec(memory_space=pl.ANY), pl.BlockSpec(memory_space=pltpu.VMEM)
    loud = seg - QUIET
    kept, out_quiet, out_loud, grad_quiet, grad_loud, total, small = pl.pallas_call(
        functools.partial(layer_kernel, tuple(scratch)),
        out_shape=[
            jax.ShapeDtypeStruct((count, rows, width), BF16),
            jax.ShapeDtypeStruct((count, QUIET, width), BF16),
            jax.ShapeDtypeStruct((count, loud, width), BF16),
            jax.ShapeDtypeStruct((count, QUIET, width), BF16),
            jax.ShapeDtypeStruct((count, loud, width), BF16),
            jax.ShapeDtypeStruct((BASES[-1], width), BF16),
            jax.ShapeDtypeStruct((16, width), F32),
        ],
        in_specs=[anywhere] * (12 + len(VECTORS)),
        out_specs=[anywhere] * 7,
        scratch_shapes=list(scratch.values()),
        compiler_params=pltpu.CompilerParams(
            collective_id=0, has_side_effects=True, vmem_limit_bytes=VMEM_BYTES
        ),
        name="layer",
    )(
        chars, seg_lengths, memory, grad_out,
        *vectors, table,
        w_query, w_key, w_value, w_rel, w_out, w_up, w_down,
    )

    def block(shape, index):
        return pl.BlockSpec(shape, index)

    def each(*shape):
        return block((1, *shape), lambda n: (n, 0, 0))

    def whole(*shape):
        return block(shape, lambda n: (0, 0))

    vector = [(1, width)] * 4 + [(1, hidden), (1, width)]
    outs = pl.pallas_call(
        spread_kernel,
        grid=(count,),
        out_shape=[
            jax.ShapeDtypeStruct(chars.shape, BF16),
            jax.ShapeDtypeStruct(chars.shape, F32),
            jax.ShapeDtypeStruct(memory.shape, BF16),
            *[jax.ShapeDtypeStruct((width, width), F32)] * 5,
            jax.ShapeDtypeStruct((width, hidden), F32),
            jax.ShapeDtypeStruct((hidden, width), F32),
            *[jax.ShapeDtypeStruct(bias_u.shape, F32)] * 2,
            *[jax.ShapeDtypeStruct(shape, F32) for shape in vector],
        ],
        in_specs=[
            whole(*seg_lengths.shape),
            each(places, width),
            each(places, width),
            each(rows, width),
            each(QUIET, width),
            each(loud, width),
            each(QUIET, width),
            each(loud, width),
            block((1024, width), lambda n: (n, 0)),
            block((128, width), lambda n: (BASES[4] // 128 + n, 0)),
            block((512, width), lambda n: (BASES[5] // 512 + n, 0)),
            whole(16, width),
        ],
        out_specs=[
            each(places, width),
            each(places, width),
            each(rows, width),
            *[block((width, 128), lambda n: (0, n))] * 4,
            block((128, width), lambda n: (n, 0)),
            block((width, 512), lambda n: (0, n)),
            block((512, width), lambda n: (n, 0)),
            *[whole(*bias_u.shape)] * 2,
            *[whole(*shape) for shape in vector],
        ],
        compiler_params=pltpu.CompilerParams(vmem_limit_bytes=VMEM_BYTES),
        name="spread",
    )(seg_lengths, chars, grad_out, kept, out_quiet, out_loud, grad_quiet, grad_loud, total, total, total, small)
    return (*outs[:12], *[v.reshape(-1) for v in outs[12:]])


VMEM_BYTES = 64 * 2**20 - 2**16


def fits_whole(mesh):
    return dict(mesh.shape) == {"seq": 8, "blk": 4}


def layer_norm(value, gain, shift):
    center = value - jnp.mean(value, axis=-1, keepdims=True)
    spread = jnp.mean(center * center, axis=-1, keepdims=True)
    return center * lax.rsqrt(spread + 1e-05) * gain + shift


def angle_tables(places, feature_width):
    freqs = jnp.exp(
        jnp.arange(feature_width // 2, dtype=jnp.float32)
        * (-2.0 * math.log(10000.0) / feature_width)
    )
    angles = places[:, None] * freqs[None, :]
    return (jnp.sin(angles), jnp.cos(angles))


def smooth_gate(value):
    return jax.nn.gelu(value, approximate=False)


def segment_ids(seg_end, char_places):
    return jnp.sum((seg_end[:, None, :] <= char_places[None, :, None]).astype(jnp.int32), axis=2)


def shards(
    chars,
    seg_lengths,
    memory,
    grad_out,
    w_query,
    w_key,
    w_value,
    w_rel,
    w_out,
    w_up,
    w_down,
    bias_u,
    bias_v,
    gain_one,
    shift_one,
    gain_two,
    shift_two,
    bias_up,
    bias_down,
):
    blk_index = lax.axis_index("blk")
    seq_local, char_rows, feature_width = chars.shape
    seg_rows = memory.shape[1]
    seg_count = seg_lengths.shape[1]
    head_count, head_dim = bias_u.shape
    half_width = feature_width // 2
    score_scale = head_dim ** (-0.5)
    seg_start = blk_index * seg_rows
    gain_one_f = gain_one.astype(jnp.float32)
    shift_one_f = shift_one.astype(jnp.float32)
    gain_two_f = gain_two.astype(jnp.float32)
    shift_two_f = shift_two.astype(jnp.float32)
    seg_end = jnp.cumsum(seg_lengths, axis=1)
    char_places = blk_index * char_rows + jnp.arange(char_rows, dtype=jnp.int32)
    segment = segment_ids(seg_end, char_places)
    own_lengths = lax.dynamic_slice_in_dim(seg_lengths, seg_start, seg_rows, 1).astype(jnp.float32)
    chars_f = chars.astype(jnp.float32)
    grad_f = grad_out.astype(jnp.float32)

    def full_table(values, ids):
        return jax.ops.segment_sum(values, ids, num_segments=seg_count)

    part_sums = jax.vmap(full_table)(chars_f, segment)
    pooled_sum = lax.psum_scatter(part_sums, "blk", scatter_dimension=1, tiled=True)
    pooled = pooled_sum / own_lengths[:, :, None]
    normed = layer_norm(pooled, gain_one_f, shift_one_f)
    normed_low = normed.astype(jnp.bfloat16)
    memory_f = memory.astype(jnp.float32)
    mem_low = layer_norm(memory_f, gain_one_f, shift_one_f).astype(jnp.bfloat16)
    query_rows = jnp.einsum("sid,de->sie", normed_low, w_query, preferred_element_type=jnp.float32)
    key_local = jnp.stack(
        [
            jnp.einsum("sid,de->sie", mem_low, w_key, preferred_element_type=jnp.float32),
            jnp.einsum("sid,de->sie", normed_low, w_key, preferred_element_type=jnp.float32),
        ],
        axis=1,
    ).astype(jnp.bfloat16)
    value_local = jnp.stack(
        [
            jnp.einsum("sid,de->sie", mem_low, w_value, preferred_element_type=jnp.float32),
            jnp.einsum("sid,de->sie", normed_low, w_value, preferred_element_type=jnp.float32),
        ],
        axis=1,
    ).astype(jnp.bfloat16)
    key_all, value_all = (
        lax.all_gather(key_local, "blk", axis=2, tiled=True),
        lax.all_gather(value_local, "blk", axis=2, tiled=True),
    )
    key_heads = key_all.reshape(seq_local, 2 * seg_count, head_count, head_dim)
    value_heads = value_all.reshape(seq_local, 2 * seg_count, head_count, head_dim)
    query_u = (
        (query_rows + bias_u.astype(jnp.float32).reshape(-1))
        .astype(jnp.bfloat16)
        .reshape(seq_local, seg_rows, head_count, head_dim)
    )
    query_v = (
        (query_rows + bias_v.astype(jnp.float32).reshape(-1))
        .astype(jnp.bfloat16)
        .reshape(seq_local, seg_rows, head_count, head_dim)
    )
    w_rel_heads = w_rel.reshape(feature_width, head_count, head_dim)
    rel_coeff = jnp.einsum(
        "sihe,fhe->sihf", query_v, w_rel_heads, preferred_element_type=jnp.float32
    )
    sin_all, cos_all = angle_tables(jnp.arange(2 * seg_count).astype(jnp.float32), feature_width)
    key_pos = jnp.concatenate([cos_all, sin_all], axis=-1).astype(jnp.bfloat16)
    query_index = seg_count + seg_start + jnp.arange(seg_rows, dtype=jnp.int32)
    sin_q, cos_q = angle_tables(query_index.astype(jnp.float32), feature_width)
    sin_query = sin_q[None, :, None, :]
    cos_query = cos_q[None, :, None, :]
    coeff_sin = rel_coeff[..., :half_width]
    coeff_cos = rel_coeff[..., half_width:]
    query_pos = jnp.concatenate(
        [
            coeff_sin * sin_query + coeff_cos * cos_query,
            coeff_cos * sin_query - coeff_sin * cos_query,
        ],
        axis=-1,
    ).astype(jnp.bfloat16)
    allowed = jnp.arange(2 * seg_count, dtype=jnp.int32)[None, :] <= query_index[:, None]

    def score_block():
        raw_scores = (
            jnp.einsum("sihe,sjhe->shij", query_u, key_heads, preferred_element_type=jnp.float32)
            + jnp.einsum("sihf,jf->shij", query_pos, key_pos, preferred_element_type=jnp.float32)
        ) * score_scale
        return jnp.where(allowed[None, None], raw_scores, -1e30)

    scores = score_block()
    row_top = jnp.max(scores, axis=-1, keepdims=True)
    expo = jnp.exp(scores - row_top)
    row_total = jnp.sum(expo, axis=-1, keepdims=True)
    log_total = row_top + jnp.log(row_total)
    att_probs = (expo / row_total).astype(jnp.bfloat16)
    att_mixed = jnp.einsum(
        "shij,sjhe->sihe", att_probs, value_heads, preferred_element_type=jnp.float32
    )
    mixed_low = att_mixed.reshape(seq_local, seg_rows, feature_width).astype(jnp.bfloat16)
    residual = pooled + jnp.einsum(
        "sid,de->sie", mixed_low, w_out, preferred_element_type=jnp.float32
    )
    normed_two = layer_norm(residual, gain_two_f, shift_two_f)
    two_low = normed_two.astype(jnp.bfloat16)
    ffn_inner = jnp.einsum(
        "sid,df->sif", two_low, w_up, preferred_element_type=jnp.float32
    ) + bias_up.astype(jnp.float32)
    hidden_low = smooth_gate(ffn_inner).astype(jnp.bfloat16)
    branch_out = jnp.einsum(
        "sif,fd->sid", hidden_low, w_down, preferred_element_type=jnp.float32
    ) + bias_down.astype(jnp.float32)
    out_low = (residual + branch_out).astype(jnp.bfloat16)
    rows_all = lax.all_gather(out_low, "blk", axis=1, tiled=True)
    picked = jnp.take_along_axis(rows_all, segment[:, :, None], axis=1)
    out_chars = (chars_f + picked.astype(jnp.float32)).astype(jnp.bfloat16)
    new_memory = pooled.astype(jnp.bfloat16)
    grad_table = jax.vmap(full_table)(grad_f, segment)
    grad_output = lax.psum_scatter(grad_table, "blk", scatter_dimension=1, tiled=True)
    grad_down_low = grad_output.astype(jnp.bfloat16)
    grad_bias_down = jnp.sum(grad_down_low.astype(jnp.float32), axis=(0, 1))
    grad_w_down = jnp.einsum(
        "sif,sid->fd", hidden_low, grad_down_low, preferred_element_type=jnp.float32
    )
    grad_hidden = jnp.einsum(
        "sid,fd->sif", grad_down_low, w_down, preferred_element_type=jnp.float32
    )
    unused_value, gate_back = jax.vjp(smooth_gate, ffn_inner)
    grad_inner = gate_back(grad_hidden)[0].astype(jnp.bfloat16)
    grad_bias_up = jnp.sum(grad_inner.astype(jnp.float32), axis=(0, 1))
    grad_w_up = jnp.einsum("sid,sif->df", two_low, grad_inner, preferred_element_type=jnp.float32)
    grad_normed_two = jnp.einsum(
        "sif,df->sid", grad_inner, w_up, preferred_element_type=jnp.float32
    )
    unused_norm, norm_two_back = jax.vjp(layer_norm, residual, gain_two_f, shift_two_f)
    grad_resid_norm, grad_gain_two, grad_shift_two = norm_two_back(grad_normed_two)
    grad_residual = grad_output + grad_resid_norm
    grad_att_low = grad_residual.astype(jnp.bfloat16)
    grad_w_out = jnp.einsum(
        "sid,sie->de", mixed_low, grad_att_low, preferred_element_type=jnp.float32
    )
    grad_mixed = jnp.einsum("sie,de->sid", grad_att_low, w_out, preferred_element_type=jnp.float32)
    grad_mixed = grad_mixed.astype(jnp.bfloat16).reshape(seq_local, seg_rows, head_count, head_dim)
    scores_again = score_block()
    probs_full = jnp.exp(scores_again - log_total)
    probs_low = probs_full.astype(jnp.bfloat16)
    grad_probs = jnp.einsum(
        "sihe,sjhe->shij", grad_mixed, value_heads, preferred_element_type=jnp.float32
    )
    grad_values = jnp.einsum(
        "shij,sihe->sjhe", probs_low, grad_mixed, preferred_element_type=jnp.float32
    )
    prob_delta = jnp.sum(probs_full * grad_probs, axis=-1, keepdims=True)
    grad_scores = (probs_full * (grad_probs - prob_delta)).astype(jnp.bfloat16)
    grad_query_u = (
        jnp.einsum("shij,sjhe->sihe", grad_scores, key_heads, preferred_element_type=jnp.float32)
        * score_scale
    )
    grad_keys = (
        jnp.einsum("shij,sihe->sjhe", grad_scores, query_u, preferred_element_type=jnp.float32)
        * score_scale
    )
    grad_query_pos = (
        jnp.einsum("shij,jf->sihf", grad_scores, key_pos, preferred_element_type=jnp.float32)
        * score_scale
    )
    grad_first = grad_query_pos[..., :half_width]
    grad_second = grad_query_pos[..., half_width:]
    grad_coeff = jnp.concatenate(
        [
            grad_first * sin_query - grad_second * cos_query,
            grad_first * cos_query + grad_second * sin_query,
        ],
        axis=-1,
    ).astype(jnp.bfloat16)
    grad_w_rel = jnp.einsum(
        "sihf,sihe->fhe", grad_coeff, query_v, preferred_element_type=jnp.float32
    ).reshape(feature_width, feature_width)
    grad_query_v = jnp.einsum(
        "sihf,fhe->sihe", grad_coeff, w_rel_heads, preferred_element_type=jnp.float32
    )
    grad_bias_u = jnp.sum(grad_query_u, axis=(0, 1))
    grad_bias_v = jnp.sum(grad_query_v, axis=(0, 1))
    grad_query = (
        (grad_query_u + grad_query_v)
        .reshape(seq_local, seg_rows, feature_width)
        .astype(jnp.bfloat16)
    )
    grad_w_query = jnp.einsum(
        "sid,sie->de", normed_low, grad_query, preferred_element_type=jnp.float32
    )
    grad_normed = jnp.einsum("sie,de->sid", grad_query, w_query, preferred_element_type=jnp.float32)
    key_share, value_share = (
        lax.psum_scatter(
            grad_keys.reshape(seq_local, 2, seg_count, feature_width),
            "blk",
            scatter_dimension=2,
            tiled=True,
        ),
        lax.psum_scatter(
            grad_values.reshape(seq_local, 2, seg_count, feature_width),
            "blk",
            scatter_dimension=2,
            tiled=True,
        ),
    )
    key_low = key_share.astype(jnp.bfloat16)
    value_low = value_share.astype(jnp.bfloat16)
    grad_w_key = jnp.einsum(
        "sid,sie->de", mem_low, key_low[:, 0], preferred_element_type=jnp.float32
    ) + jnp.einsum("sid,sie->de", normed_low, key_low[:, 1], preferred_element_type=jnp.float32)
    grad_w_value = jnp.einsum(
        "sid,sie->de", mem_low, value_low[:, 0], preferred_element_type=jnp.float32
    ) + jnp.einsum("sid,sie->de", normed_low, value_low[:, 1], preferred_element_type=jnp.float32)
    grad_normed = grad_normed + jnp.einsum(
        "sie,de->sid", key_low[:, 1], w_key, preferred_element_type=jnp.float32
    )
    grad_normed = grad_normed + jnp.einsum(
        "sie,de->sid", value_low[:, 1], w_value, preferred_element_type=jnp.float32
    )
    grad_mem_normed = jnp.einsum(
        "sie,de->sid", key_low[:, 0], w_key, preferred_element_type=jnp.float32
    ) + jnp.einsum("sie,de->sid", value_low[:, 0], w_value, preferred_element_type=jnp.float32)
    unused_one, norm_one_back = jax.vjp(layer_norm, pooled, gain_one_f, shift_one_f)
    grad_pooled_norm, grad_gain_one, grad_shift_one = norm_one_back(grad_normed)
    unused_mem, norm_mem_back = jax.vjp(layer_norm, memory_f, gain_one_f, shift_one_f)
    unused_grad, grad_gain_mem, grad_shift_mem = norm_mem_back(grad_mem_normed)
    grad_gain_one = grad_gain_one + grad_gain_mem
    grad_shift_one = grad_shift_one + grad_shift_mem
    grad_pooled = grad_residual + grad_pooled_norm
    grad_sum = grad_pooled / own_lengths[:, :, None]
    grad_sum_all = lax.all_gather(grad_sum, "blk", axis=1, tiled=True)
    grad_chars = grad_f + jnp.take_along_axis(grad_sum_all, segment[:, :, None], axis=1)
    (
        grad_w_query,
        grad_w_key,
        grad_w_value,
        grad_w_rel,
        grad_w_out,
        grad_w_up,
        grad_w_down,
        grad_bias_u,
        grad_bias_v,
        grad_gain_one,
        grad_shift_one,
        grad_gain_two,
        grad_shift_two,
        grad_bias_up,
        grad_bias_down,
    ) = lax.psum(
        (
            grad_w_query,
            grad_w_key,
            grad_w_value,
            grad_w_rel,
            grad_w_out,
            grad_w_up,
            grad_w_down,
            grad_bias_u,
            grad_bias_v,
            grad_gain_one,
            grad_shift_one,
            grad_gain_two,
            grad_shift_two,
            grad_bias_up,
            grad_bias_down,
        ),
        ("seq", "blk"),
    )
    return (
        out_chars,
        grad_chars,
        new_memory,
        grad_w_query,
        grad_w_key,
        grad_w_value,
        grad_w_rel,
        grad_w_out,
        grad_w_up,
        grad_w_down,
        grad_bias_u,
        grad_bias_v,
        grad_gain_one,
        grad_shift_one,
        grad_gain_two,
        grad_shift_two,
        grad_bias_up,
        grad_bias_down,
    )


def solution(mesh):
    placed = (
        P("seq", "blk", None),
        P("seq", None),
        P("seq", "blk", None),
        P("seq", "blk", None),
        P(),
        P(),
        P(),
        P(),
        P(),
        P(),
        P(),
        P(),
        P(),
        P(),
        P(),
        P(),
        P(),
        P(),
        P(),
    )
    return jax.shard_map(
        shards_whole if fits_whole(mesh) else shards,
        mesh=mesh,
        in_specs=placed,
        out_specs=(
            P("seq", "blk", None),
            P("seq", "blk", None),
            P("seq", "blk", None),
            P(),
            P(),
            P(),
            P(),
            P(),
            P(),
            P(),
            P(),
            P(),
            P(),
            P(),
            P(),
            P(),
            P(),
            P(),
        ),
        check_vma=False,
    )
```

```python
import functools
import math
import types

import jax
import jax.numpy as jnp
import numpy as np
from jax import lax
from jax.experimental import pallas as pl
from jax.experimental.pallas import tpu as pltpu
from jax.sharding import PartitionSpec as P

F32, BF16 = jnp.float32, jnp.bfloat16
NT = (((1,), (1,)), ((), ()))


def mm(a, b):
    return jnp.dot(a, b, preferred_element_type=F32)


def mm_nt(a, b):
    return lax.dot_general(a, b, NT, preferred_element_type=F32)


def normalize(value):
    center = value - jnp.mean(value, axis=-1, keepdims=True)
    inv = lax.rsqrt(jnp.mean(center * center, axis=-1, keepdims=True) + 1e-05)
    return center * inv, inv


def norm_back(grad, unit, inv, gain):
    scaled = grad * gain
    along = jnp.mean(scaled * unit, axis=-1, keepdims=True)
    return inv * (scaled - jnp.mean(scaled, axis=-1, keepdims=True) - unit * along)


def gelu_parts(value):
    gate = 0.5 + 0.5 * lax.erf(value * 0.7071067811865476)
    return gate, gate + value * jnp.exp(-0.5 * value * value) * 0.3989422804014327


def ramp(shape, dim):
    return lax.broadcasted_iota(jnp.int32, shape, dim)


MESH = pl.DeviceIdType.MESH
HALF = 256
FACTOR = dict(x=2, y=2, near=2, far=2, z=4, xy=4)
AXES = ("x", "y", "near", "far")
PIECES = tuple((1024, f"tile{n}") for n in range(4)) + ((512, "middle"),) + tuple((512, f"pair{n}") for n in range(4))
BASES = tuple(sum(rows for rows, unused in PIECES[:n]) for n in range(len(PIECES) + 1))
VECTORS = ("bias_u", "bias_v", "gain_one", "shift_one", "gain_two", "shift_two", "bias_up", "bias_down")
ORDERS = (
    (("y", "x", "z"), ("x", "y", "z")),
    (("x", "y", "z"), ("y", "x", "z")),
    (("near", "y", "x", "far"), ("far", "x", "near", "y")),
    (("y", "x", "near", "far"), ("near", "y", "x", "far")),
    (("near", "far", "xy"), ("far", "near", "xy")),
    (("y", "x", "near", "far"), ("y", "x", "near", "far")),
    (("y", "x", "z"), ("x", "y", "z")),
    (("x", "y", "z"), ("x", "y", "z")),
    (("y", "x", "z"), ("y", "x", "z")),
)
DURING = (
    ((0, 0),), ((1, 0),), ((2, 0),), ((3, 0),), ((0, 1),), ((2, 1), (1, 1), (4, 0)), ((3, 1),), (), (),
    ((4, 1),), ((0, 2), (5, 0)), (), (), ((1, 2),), ((5, 1),), ((6, 0),), ((2, 2),), ((0, 3),), (),
    ((6, 1), (3, 2)), ((1, 3), (7, 0)), (), ((5, 2), (4, 2)), ((2, 3), (7, 1)), (), ((0, 4), (6, 2), (8, 0)),
    ((5, 3), (3, 3)),
)
AFTER = (
    (2, 4), (1, 4), (8, 1), (4, 3), (7, 2), (6, 3), (5, 4), (3, 4), (0, 5), (2, 5), (8, 2), (1, 5), (7, 3),
    (4, 4), (6, 4), (5, 5), (0, 6), (8, 3), (3, 5), (2, 6), (1, 6), (4, 5), (7, 4), (6, 5), (5, 6), (0, 7),
    (2, 7), (8, 4), (3, 6), (0, 8), (1, 7), (5, 7), (4, 6), (6, 6), (2, 8), (7, 5), (3, 7), (1, 8), (8, 5),
    (5, 8), (6, 7), (7, 6), (4, 7), (6, 8), (3, 8), (4, 8), (8, 6), (5, 9), (2, 9), (5, 10), (7, 7), (3, 9),
    (2, 10), (7, 8), (8, 7), (3, 10), (8, 8),
)
BACK_DURING = (8, 13)
BACK_AFTER = (0, 37, 43, 46, 51, 51)


class Place:
    def __init__(self):
        self.s = lax.axis_index("seq")
        self.b = lax.axis_index("blk")
        self.z, self.y = self.s // 2, self.s % 2
        self.x, self.c = self.b // 2, self.b % 2
        self.bit = dict(x=self.x, y=self.y, near=self.z % 2, far=self.z // 2)

    def group(self, k):
        return (self.s, (self.b + k) % 4)

    def core(self):
        return (self.s, self.b + 1 - 2 * self.c)

    def across(self):
        return (self.s, self.b + 2 - 4 * self.x)

    def move(self, axis):
        reach = dict(x=(0, 2), y=(1, 0), near=(2, 0), far=(4, 0))[axis]
        turn = 1 - 2 * self.bit[axis]
        return reach[0] * turn, reach[1] * turn

    def peers(self, axis):
        if axis == "z":
            return self.z, [(self.line(j), (self.z + j) % 4, (self.z + 4 - j) % 4) for j in (1, 2, 3)]
        if axis == "xy":
            out = []
            for across, along in ((1, 0), (0, 1), (1, 1)):
                x, y = self.x + across * (1 - 2 * self.x), self.y + along * (1 - 2 * self.y)
                device = (self.s + along * (1 - 2 * self.y), self.b + across * 2 * (1 - 2 * self.x))
                out.append((device, x + 2 * y, x + 2 * y))
            return self.x + 2 * self.y, out
        bit = self.bit[axis]
        return bit, [(self.pair(axis), 1 - bit, 1 - bit)]

    def stage(self, zero, one):
        if zero == one:
            return self.peers(zero)

        def pick(a, b):
            return a * (1 - self.c) + b * self.c

        (own_zero, peers_zero), (own_one, peers_one) = self.peers(zero), self.peers(one)
        peers = [
            ((pick(d[0], e[0]), pick(d[1], e[1])), pick(i, j), pick(f, g))
            for (d, i, f), (e, j, g) in zip(peers_zero, peers_one)
        ]
        return pick(own_zero, own_one), peers

    def line(self, j):
        return (((self.z + j) % 4) * 2 + self.y, self.b)

    def pair(self, axis):
        away = self.move(axis)
        return (self.s + away[0], self.b + away[1])


def rows_at(start, size):
    return pl.ds(pl.multiple_of(start, 16), size)


def remote(src, dst, send, recv, to):
    return pltpu.make_async_remote_copy(src, dst, send, recv, device_id=to, device_id_type=MESH)


def piece_rows(k):
    rows = [PIECES[k][0] // 2]
    for axis in ORDERS[k][0]:
        rows.append(rows[-1] // FACTOR[axis])
    return rows


def piece_lands(k):
    rows = piece_rows(k)
    return [rows[0]] + [(FACTOR[axis] - 1) * rows[n + 1] for n, axis in enumerate(ORDERS[k][0])]


def piece_peers(k):
    stages = [FACTOR[axis] - 1 for axis in ORDERS[k][0]]
    return [1, *stages, *stages[::-1], 1]


def starts(counts):
    out, end = [], 0
    for piece in counts:
        out.append([])
        for count in piece:
            out[-1].append(end)
            end += count
    return out, end


LANDS = starts([piece_lands(k) for k in range(len(PIECES))])
SENDS = starts([[max(piece_peers(k))] for k in range(len(PIECES))])
RECVS = starts([piece_peers(k) for k in range(len(PIECES))])


class Sum:
    def __init__(self, place, total, land, out, send, recv, store):
        self.p, self.g, self.land, self.out = place, total, land, out
        self.send, self.recv, self.store = send, recv, store
        known = {}
        self.stages = []
        for orders in ORDERS:
            for axes in zip(*orders):
                if axes not in known:
                    known[axes] = place.stage(*axes)
            self.stages.append([known[axes] for axes in zip(*orders)])

    def offset(self, k, n):
        rows = piece_rows(k)
        start = BASES[k] + self.p.c * rows[0]
        for m in range(n):
            start = start + self.stages[k][m][0] * rows[m + 1]
        return start

    def lands(self, k, n, start, size):
        return self.land.at[rows_at(LANDS[0][k][n] + start, size)]

    def copies(self, step, k, landing=False):
        p, rows = self.p, piece_rows(k)
        count = len(rows) - 1

        def copy(src, dst, to, j=0):
            return remote(src, dst, self.send.at[SENDS[0][k][0] + j], self.recv.at[RECVS[0][k][step] + j], to)

        if step == 0:
            src = self.g.at[rows_at(BASES[k] + (1 - p.c) * rows[0], rows[0])]
            return [copy(src, self.lands(k, 0, 0, rows[0]), p.core())]
        if step == 2 * count + 1:
            span = BASES[k] + (1 - p.c if landing else p.c) * rows[0]
            return [copy(self.lands(k, 0, 0, rows[0]), self.out.at[rows_at(span, rows[0])], p.core())]
        n = step - 1 if step <= count else 2 * count - step
        size = rows[n + 1]
        own, peers = self.stages[k][n]
        if step <= count:
            start = self.offset(k, n)
            return [
                copy(self.g.at[rows_at(start + at * size, size)], self.lands(k, n + 1, j * size, size), to, j)
                for j, (to, at, unused) in enumerate(peers)
            ]
        src = self.lands(k, n, own * size, size) if n == count - 1 else self.lands(k, n + 1, 0, size)
        return [
            copy(src, self.lands(k, n, (back if landing else own) * size, size), to, j)
            for j, (to, unused, back) in enumerate(peers)
        ]

    def own(self, k):
        rows = piece_rows(k)[0]
        span = rows_at(BASES[k] + self.p.c * rows, rows)
        return pltpu.make_async_copy(self.lands(k, 0, 0, rows), self.out.at[span], self.store.at[k])

    def added(self, k, n, start, size):
        mine = self.g[rows_at(self.offset(k, n) + start, size)]
        if n == 0 or len(self.stages[k][n - 1][1]) == 1:
            return mine + self.lands(k, n, start, size)[...]
        whole = piece_rows(k)[n]
        mine = mine.astype(F32)
        for j in range(len(self.stages[k][n - 1][1])):
            mine = mine + self.lands(k, n, j * whole + start, size)[...].astype(F32)
        return mine.astype(BF16)

    def step(self, k, step):
        rows = piece_rows(k)
        count = len(rows) - 1
        if step > 0:
            for copy in self.copies(step - 1, k):
                copy.wait_send()
            for copy in self.copies(step - 1, k, landing=True):
                copy.wait_recv()
        if 1 <= step <= count:
            n, size = step - 1, rows[step]
            own, peers = self.stages[k][n]
            copies = self.copies(step, k)
            for index, copy in zip([at for unused, at, other in peers] + [own], copies + [None]):
                part = self.added(k, n, index * size, size)
                self.g[rows_at(self.offset(k, n) + index * size, size)] = part
                if copy is not None:
                    copy.start()
        elif step <= 2 * count + 1:
            if step == count + 1:
                size = rows[count]
                self.lands(k, count - 1, self.stages[k][count - 1][0] * size, size)[...] = self.added(k, count, 0, size)
            for copy in self.copies(step, k):
                copy.start()
        if count + 2 <= step <= 2 * count:
            n = 2 * count - step
            size = rows[n + 1]
            self.lands(k, n, self.stages[k][n][0] * size, size)[...] = self.lands(k, n + 1, 0, size)[...]
        if step == 2 * count + 1:
            self.own(k).start()
        if step == 2 * count + 2:
            self.own(k).wait()


def pair_lanes(p, start=0, size=128):
    if isinstance(p, int):
        return slice(p * 128 + start, p * 128 + start + size)
    return pl.ds(pl.multiple_of(p * 128 + start, size), size)


def lane_mask(par):
    lane = ramp((1, 128), 1)
    return jnp.where((lane >= 64) == bool(par), 1.0, 0.0).astype(BF16)


def flip_matrix():
    return jnp.where(ramp((HALF, HALF), 0) + ramp((HALF, HALF), 1) == HALF - 1, 1.0, 0.0).astype(BF16)


def flip(flip_low, value):
    return jnp.concatenate(
        [mm(flip_low, value[r : r + HALF]) for r in range(0, value.shape[0], HALF)], axis=0
    ).astype(value.dtype)


def pool_matrix(end, length, first_place, places):
    place = (ramp((end.shape[0], places), 1) + first_place).astype(F32)
    return jnp.where((place < end) & (place >= end - length), 1.0, 0.0).astype(BF16)


def query_block(n, seg):
    keys = seg + HALF * (n + 1)
    return slice(n * HALF, (n + 1) * HALF), keys, 2 * seg - keys


def attend(n, seg, r):
    seen = ramp((HALF, HALF), 1) <= ramp((HALF, HALF), 0)
    lane = ramp((HALF, 128), 1)
    rows, keys, skip = query_block(n, seg)

    def products(head):
        lanes, keep = pair_lanes(head // 2), lane_mask(head % 2)
        near = mm_nt(r.query_u[rows, lanes] * keep, r.key[0:keys, lanes])
        return near, mm_nt(r.query_v[rows, lanes] * keep, r.place[skip : 2 * seg, lanes])

    ahead = products(0)
    for p in range(4):
        mixed, scale = [], []
        for head in (2 * p, 2 * p + 1):
            near, far = ahead
            ahead = products(head + 1) if head < 7 else None
            scores = near + pltpu.roll(far, keys - (HALF - 1), 1, stride=1, stride_axis=0)
            scores = jnp.concatenate(
                [scores[:, : keys - HALF], jnp.where(seen, scores[:, keys - HALF :], -1e30)], axis=1
            )
            expo = jnp.exp(scores - jnp.max(scores, axis=1, keepdims=True))
            probs = expo.astype(BF16)
            r.probs[head, rows, 0:keys] = probs
            mixed.append(mm(probs, r.value[0:keys, pair_lanes(p)]))
            scale.append(1.0 / jnp.sum(expo, axis=1, keepdims=True))
        scale = jnp.where(lane >= 64, scale[1], scale[0])
        r.scale[rows, pair_lanes(p)] = scale
        r.mixed[rows, pair_lanes(p)] = (jnp.where(lane >= 64, mixed[1], mixed[0]) * scale).astype(BF16)


def attend_back_pair(p, seg, r, between):
    lanes = pair_lanes(p)
    flip_low = flip_matrix()
    scale = 0.125
    lane = ramp((HALF, 128), 1)
    sums = [None] * 6
    bias = []
    for n in range(seg // HALF):
        rows, keys, skip = query_block(n, seg)
        key, value, place = r.key[0:keys, lanes], r.value[0:keys, lanes], r.place[skip : 2 * seg, lanes]
        grad_u, grad_v = [], []
        for par in range(2):
            keep = lane_mask(par)
            feats = pair_lanes(p, par * 64, 64)
            probs = r.probs[2 * p + par, rows, 0:keys]
            turned = mm(flip_low, probs)
            grad_mixed = r.grad_mixed[rows, lanes] * keep
            delta = jnp.sum(grad_mixed.astype(F32) * r.mixed_flip[rows, lanes].astype(F32), axis=1, keepdims=True)
            grad_scores = turned * (mm_nt(grad_mixed, value) - delta)
            near = grad_scores.astype(BF16)
            far = pltpu.roll(grad_scores, 0, 1, stride=1, stride_axis=0).astype(BF16)
            grad_u.append(mm(near, key) * scale)
            grad_v.append(mm(far, place) * scale)
            now = (
                mm(r.query_u_t[feats, rows], near),
                mm(r.grad_mixed_t[feats, rows], probs),
                mm(r.query_v_t[feats, rows], far),
            )
            for m in range(3):
                slot = par * 3 + m
                if n == 0:
                    sums[slot] = now[m]
                else:
                    old, new = sums[slot], now[m]
                    cut = old.shape[1]
                    if m < 2:
                        sums[slot] = jnp.concatenate([new[:, :cut] + old, new[:, cut:]], axis=1)
                    else:
                        sums[slot] = jnp.concatenate([new[:, :-cut], new[:, -cut:] + old], axis=1)
            between(n * 2 + par)
        grad_u = jnp.where(lane >= 64, grad_u[1], grad_u[0])
        grad_v = jnp.where(lane >= 64, grad_v[1], grad_v[0])
        bias.append((jnp.sum(grad_u, axis=0, keepdims=True), jnp.sum(grad_v, axis=0, keepdims=True)))
        r.grad_query[rows, lanes] = mm(flip_low, (grad_u + grad_v).astype(BF16)).astype(BF16)
    r.small[0:1, lanes] = sum(b[0] for b in bias)
    r.small[1:2, lanes] = sum(b[1] for b in bias)
    for par in range(2):
        feats = pair_lanes(p, par * 64, 64)
        for m, out in enumerate((r.grad_key_t, r.grad_value_t, r.grad_place_t)):
            out[feats, :] = sums[par * 3 + m].astype(BF16)


def pair_weights(p, seg, r, base):
    lanes = pair_lanes(p)
    grad_query_t = r.grad_query[:, lanes].astype(F32).T.astype(BF16)
    r.total[rows_at(base, 128)] = mm(grad_query_t, r.normed[seg : 2 * seg]).astype(BF16)
    r.total[rows_at(base + 128, 128)] = mm(r.grad_key_t[lanes, :], r.normed[...]).astype(BF16)
    r.total[rows_at(base + 256, 128)] = mm(r.grad_value_t[lanes, :], r.normed[...]).astype(BF16)
    r.total[rows_at(base + 384, 128)] = mm(r.grad_place_t[lanes, :], r.table[...]).astype(BF16)


def project_places(r):
    r.place[...] = mm(r.table[...], r.w_rel[...]).astype(BF16)


def project_memory(rows, r):
    unit, unused = normalize(r.memory[rows].astype(F32))
    low = (unit * r.vec("gain_one") + r.vec("shift_one")).astype(BF16)
    r.normed[rows] = low
    r.key[rows] = mm(low, r.w_key[...]).astype(BF16)
    r.value[rows] = mm(low, r.w_value[...]).astype(BF16)


def project_segments(n, seg, r):
    rows, keys, unused = query_block(n, seg)
    places = slice(keys - HALF, keys)
    unit, unused = normalize(r.pooled[rows])
    low = (unit * r.vec("gain_one") + r.vec("shift_one")).astype(BF16)
    r.normed[places] = low
    query = mm(low, r.w_query[...])
    scale = 0.125
    r.query_u[rows] = (query + r.vec("bias_u")).astype(BF16) * jnp.asarray(scale, BF16)
    r.query_v[rows] = (query + r.vec("bias_v")).astype(BF16) * jnp.asarray(scale, BF16)
    r.key[places] = mm(low, r.w_key[...]).astype(BF16)
    r.value[places] = mm(low, r.w_value[...]).astype(BF16)


def feed_forward_in(n, r):
    rows = slice(n * HALF, (n + 1) * HALF)
    residual = r.pooled[rows] + mm(r.mixed[rows], r.w_out[...])
    r.residual[rows] = residual
    unit, unused = normalize(residual)
    r.normed_two[rows] = (unit * r.vec("gain_two") + r.vec("shift_two")).astype(BF16)

    for m in range(r.w_up.shape[1] // 512):
        cols = slice(m * 512, (m + 1) * 512)
        inner = mm(r.normed_two[rows], r.w_up[:, cols]) + r.bias_up[0:1, cols]
        gate, slope = gelu_parts(inner)
        r.hidden[rows, cols] = (inner * gate).astype(BF16)
        r.slope[rows, cols] = slope.astype(BF16)


def feed_forward_out(n, r):
    rows = slice(n * HALF, (n + 1) * HALF)
    branch = mm(r.hidden[rows], r.w_down[...]) + r.vec("bias_down")
    r.out_rows[rows] = (r.residual[rows] + branch).astype(BF16)


def feed_forward_back(n, r):
    cols = slice(n * 512, (n + 1) * 512)
    r.total[rows_at(BASES[n], 512)] = mm(r.grad_down_t[...], r.hidden[:, cols]).astype(BF16)
    grad_hidden = mm_nt(r.grad_down[...], r.w_down[cols, :])
    low = (grad_hidden * r.slope[:, cols].astype(F32)).astype(BF16)
    r.grad_inner[:, cols] = low
    r.small[7 + n : 8 + n, :] = jnp.sum(low.astype(F32), axis=0, keepdims=True)
    r.total[rows_at(BASES[n] + 512, 512)] = mm(r.normed_two_t[...], low).astype(BF16)


def middle_back(r, base):
    grad_normed = mm_nt(r.grad_inner[...], r.w_up[...])
    unit, inv = normalize(r.residual[...])
    r.small[4:5, :] = jnp.sum(grad_normed * unit, axis=0, keepdims=True)
    r.small[5:6, :] = jnp.sum(grad_normed, axis=0, keepdims=True)
    grad = r.grad_output[...] + norm_back(grad_normed, unit, inv, r.vec("gain_two"))
    r.grad_residual[...] = grad
    low = grad.astype(BF16)
    mixed = r.mixed[...]
    r.total[rows_at(base, 512)] = mm(mixed.astype(F32).T.astype(BF16), low).astype(BF16)
    grad_mixed = (mm_nt(low, r.w_out[...]) * r.scale[...]).astype(BF16)
    r.grad_mixed_t[...] = grad_mixed.astype(F32).T.astype(BF16)
    flip_low = flip_matrix()
    r.grad_mixed[...] = flip(flip_low, grad_mixed)
    r.mixed_flip[...] = flip(flip_low, mixed)
    r.query_u_t[...] = flip(flip_low, r.query_u[...]).astype(F32).T.astype(BF16)
    r.query_v_t[...] = flip(flip_low, r.query_v[...]).astype(F32).T.astype(BF16)


def first_back(seg, r):
    grad_key = r.grad_key_t[...].astype(F32).T.astype(BF16)
    grad_value = r.grad_value_t[...].astype(F32).T.astype(BF16)
    grad_normed = mm_nt(r.grad_query[...], r.w_query[...])
    grad_normed += mm_nt(grad_key[seg:], r.w_key[...])
    grad_normed += mm_nt(grad_value[seg:], r.w_value[...])
    grad_mem = mm_nt(grad_key[:seg], r.w_key[...]) + mm_nt(grad_value[:seg], r.w_value[...])
    unit, inv = normalize(r.pooled[...])
    unit_mem, unused = normalize(r.memory[...].astype(F32))
    r.small[2:3, :] = jnp.sum(grad_normed * unit + grad_mem * unit_mem, axis=0, keepdims=True)
    r.small[3:4, :] = jnp.sum(grad_normed + grad_mem, axis=0, keepdims=True)
    return r.grad_residual[...] + norm_back(grad_normed, unit, inv, r.vec("gain_one"))


QUIET = 384
MOST = 16
BACK_PARTS = 6
BACK_EARLY = BACK_PARTS * HALF // QUIET
KEPT_DURING = (18, 9, 14)


def sine_table(count, width):
    freqs = np.exp(np.arange(width // 2) * (-2.0 * math.log(10000.0) / width))
    angles = np.arange(count)[::-1, None] * freqs[None, :]
    return np.concatenate([np.sin(angles), np.cos(angles)], axis=1).astype(jnp.bfloat16)


def span_columns(lengths, low):
    seg = lengths.shape[1]
    lens = lengths.astype(F32).astype(BF16)
    row, col = ramp((seg - low, seg), 0) + low, ramp((seg - low, seg), 1)
    upto = jnp.where(col <= row, 1.0, 0.0).astype(BF16)
    same = jnp.where(col == row, 1.0, 0.0).astype(BF16)
    return mm_nt(upto, lens), mm_nt(same, lens)


def column(value, n):
    return jnp.sum(jnp.where(ramp(value.shape, 1) == n, value, 0.0), axis=1, keepdims=True)


WEIGHTS = ("w_query", "w_key", "w_value", "w_rel", "w_out", "w_up", "w_down")


def layer_scratch(seg, width, hidden, shapes):
    def low(*shape):
        return pltpu.VMEM(shape, BF16)

    def full(*shape):
        return pltpu.VMEM(shape, F32)

    return dict(
        table=low(2 * seg, width),
        w_query=low(width, width),
        w_key=low(width, width),
        w_value=low(width, width),
        w_rel=low(width, width),
        w_out=low(width, width),
        w_up=low(width, hidden),
        w_down=low(hidden, width),
        memory=low(seg, width),
        pooled=full(seg, width),
        normed=low(2 * seg, width),
        key=low(2 * seg, width),
        value=low(2 * seg, width),
        place=low(2 * seg, width),
        query_u=low(seg, width),
        query_v=low(seg, width),
        mixed=low(seg, width),
        probs=low(8, seg, 2 * seg),
        scale=full(seg, width),
        residual=full(seg, width),
        normed_two=low(seg, width),
        normed_two_t=low(width, seg),
        hidden=low(seg, hidden),
        slope=low(seg, hidden),
        grad_inner=low(seg, hidden),
        grad_output=full(seg, width),
        grad_down=low(seg, width),
        grad_down_t=low(width, seg),
        low_rows=low(seg, width),
        out_rows=low(seg, width),
        chars_quiet=low(QUIET, width),
        chars_parts=low(7, seg - QUIET, width),
        grads_quiet=low(QUIET, width),
        grads_parts=low(7, seg - QUIET, width),
        total=low(BASES[-1], width),
        land=low(LANDS[1], width),
        bias_up=full(1, hidden),
        vectors=full(16, width),
        lengths=pltpu.VMEM((4, seg), jnp.int32),
        **{f"raw_{name}": low(*shape) for name, shape in shapes.items()},
        small_load=pltpu.SemaphoreType.DMA((len(VECTORS) + 1,)),
        small=full(16, width),
        small_sum=full(5, 16, width),
        small_land=full(5, 16, width),
        load_sem=pltpu.SemaphoreType.DMA((len(WEIGHTS) + 1,)),
        stage_sem=pltpu.SemaphoreType.DMA((2, 4)),
        memory_send=pltpu.SemaphoreType.DMA((4,)),
        memory_recv=pltpu.SemaphoreType.DMA((4,)),
        quiet_send=pltpu.SemaphoreType.DMA((2, 4, 2)),
        quiet_recv=pltpu.SemaphoreType.DMA((2, 2)),
        parts_send=pltpu.SemaphoreType.DMA((2, 3)),
        parts_recv=pltpu.SemaphoreType.DMA((2, 3)),
        kept_send=pltpu.SemaphoreType.DMA((6,)),
        kept_recv=pltpu.SemaphoreType.DMA((4,)),
        back_send=pltpu.SemaphoreType.DMA((2, 5)),
        back_recv=pltpu.SemaphoreType.DMA((2, 2, 4)),
        sum_send=pltpu.SemaphoreType.DMA((SENDS[1],)),
        sum_recv=pltpu.SemaphoreType.DMA((RECVS[1],)),
        small_send=pltpu.SemaphoreType.DMA((5,)),
        small_recv=pltpu.SemaphoreType.DMA((5,)),
        small_sem=pltpu.SemaphoreType.DMA,
        store_sem=pltpu.SemaphoreType.DMA((len(PIECES),)),
    )


def chip_spans(places, loud):
    half = 2 * places
    most = -(-(loud - half // MOST) // 16) * 16
    least = (half - QUIET) // MOST // 16 * 16
    return (0, most), (least, loud - least)


class Rows:
    def __init__(self, r, place, way, source, stage, quiet, parts):
        self.r, self.p, self.way = r, place, way
        self.source, self.stage, self.quiet, self.parts = source, stage, quiet, parts
        self.spans = [pl.ds(*span) for span in chip_spans(source.shape[1], parts.shape[1])]

    def load(self, n):
        cols = pl.ds(pl.multiple_of(n * 512, 512), 512)
        return pltpu.make_async_copy(self.source.at[n], self.stage.at[:, cols], self.r.stage_sem.at[self.way, n])

    def quiet_copy(self, to, part):
        r = self.r
        span = pl.ds(0, HALF) if part == 0 else pl.ds(HALF, QUIET - HALF)
        src, dst = self.source.at[to, span], self.quiet.at[span]
        if to == 0:
            return pltpu.make_async_copy(src, dst, r.quiet_send.at[self.way, 0, part])
        return remote(src, dst, r.quiet_send.at[self.way, to, part], r.quiet_recv.at[self.way, part], (self.p.s, to))

    def start_quiet(self):
        @pl.when(self.p.b == 0)
        def _():
            for part in range(2):
                for to in (2, 3, 1, 0):
                    self.quiet_copy(to, part).start()

    def wait_quiet(self, part):
        @pl.when(self.p.b == 0)
        def _():
            self.quiet_copy(0, part).wait()

        @pl.when(self.p.b != 0)
        def _():
            self.quiet_copy(1, part).wait_recv()

    def on_chip(self, act):
        for chip in range(2):
            pl.when(self.p.x == chip)(functools.partial(act, chip))

    def parts_copy(self, n, chip=None):
        src, dst, to = ((3, 1, self.p.core()), (4, 5, self.p.core()), (6, 2, self.p.across()))[n]
        span = pl.ds(0, self.parts.shape[1]) if chip is None else self.spans[chip]
        return remote(
            self.parts.at[src, span],
            self.parts.at[dst, span],
            self.r.parts_send.at[self.way, n],
            self.r.parts_recv.at[self.way, n],
            to,
        )

    def clear(self):
        self.parts[2] = jnp.zeros(self.parts.shape[1:], BF16)

    def part(self, to, ends, lens):
        self.load(to).wait()
        cols = pl.ds(pl.multiple_of(to * 512, 512), 512)
        chosen = pool_matrix(column(ends, to), column(lens, to), self.p.b * 512, 512)
        return mm(chosen, self.stage[:, cols])

    def start_parts(self, ends, lens):
        b, sibling, away = self.p.b, self.p.core()[1], self.p.across()[1]
        self.parts[4] = self.part(away + sibling - b, ends, lens).astype(BF16)
        self.parts_copy(1).start()
        self.parts[3] = self.part(sibling, ends, lens).astype(BF16)
        self.parts_copy(0).start()
        self.parts[6] = self.part(away, ends, lens).astype(BF16)
        self.parts[0] = self.part(b, ends, lens).astype(BF16)

    def join_parts(self):
        self.parts_copy(1).wait_recv()
        self.parts[6] = (self.parts[6].astype(F32) + self.parts[5].astype(F32)).astype(BF16)
        self.on_chip(lambda chip: self.parts_copy(2, chip).start())

    def wait_parts(self):
        self.parts_copy(0).wait_recv()
        self.on_chip(lambda chip: self.parts_copy(2, 1 - chip).wait_recv())
        return sum(self.parts[n].astype(F32) for n in range(3))

    def wait_sent(self):
        for n in range(2):
            self.parts_copy(n).wait_send()
        self.on_chip(lambda chip: self.parts_copy(2, chip).wait_send())

        @pl.when(self.p.b == 0)
        def _():
            for part in range(2):
                for to in (1, 2, 3):
                    self.quiet_copy(to, part).wait_send()

    def back(self, rows, quiet_out, loud_out):
        self.rows, self.quiet_out, self.loud_out = rows, quiet_out, loud_out
        return self

    def loud_rows(self, chip):
        start, size = chip_spans(self.source.shape[1], self.parts.shape[1])[chip]
        return self.rows.at[pl.ds(QUIET + start, size)]

    def quiet_rows(self):
        return self.rows.at[pl.ds(0, QUIET)]

    def loud_copy(self, n, slot, chip):
        r, p, way = self.r, self.p, self.way
        dst = self.loud_out.at[slot, self.spans[chip]]
        to = p.across() if n == 1 else p.core()
        return remote(
            dst if n == 2 else self.loud_rows(chip), dst, r.back_send.at[way, n], r.back_recv.at[way, 0, slot], to
        )

    def quiet_back(self, slot, start=0, size=QUIET):
        r, way = self.r, self.way
        span = pl.ds(start, size)
        return remote(
            self.rows.at[span],
            self.quiet_out.at[slot, span],
            r.back_send.at[way, 3],
            r.back_recv.at[way, 1, slot],
            (self.p.s, 0),
        )

    def own_quiet(self):
        return pltpu.make_async_copy(self.quiet_rows(), self.quiet_out.at[0], self.r.back_send.at[self.way, 3])

    def own_loud(self, chip):
        dst = self.loud_out.at[self.p.b, self.spans[chip]]
        return pltpu.make_async_copy(self.loud_rows(chip), dst, self.r.back_send.at[self.way, 4])

    def start_back(self):
        def start(chip):
            self.loud_copy(1, self.p.b, 1 - chip).start()
            self.loud_copy(0, self.p.b, chip).start()
            self.own_loud(chip).start()

        self.on_chip(start)
        pl.when(self.p.b == 0)(self.own_quiet().start)

    def start_quiet_back(self, n):
        size = QUIET // BACK_PARTS
        pl.when(self.p.b != 0)(self.quiet_back(self.p.b, n * size, size).start)

    def pass_on(self):
        away = self.p.across()[1]

        def pass_on(chip):
            self.loud_copy(1, away, chip).wait_recv()
            self.loud_copy(2, away, chip).start()

        self.on_chip(pass_on)

    def wait_back(self):
        p = self.p
        sibling, away = p.core()[1], p.across()[1]

        def wait(chip):
            self.loud_copy(0, p.b, chip).wait_send()
            self.loud_copy(1, p.b, 1 - chip).wait_send()
            self.loud_copy(2, away, chip).wait_send()
            self.own_loud(chip).wait()
            self.loud_copy(0, sibling, chip).wait_recv()
            self.loud_copy(2, away + sibling - p.b, chip).wait_recv()

        self.on_chip(wait)
        pl.when(p.b != 0)(self.quiet_back(p.b).wait_send)

        @pl.when(p.b == 0)
        def _():
            self.own_quiet().wait()
            for n in (1, 2, 3):
                self.quiet_back(n).wait_recv()


class Kept:
    def __init__(self, r, place, chars, kept):
        self.r, self.p, self.chars, self.kept = r, place, chars, kept
        self.count = kept.shape[1]

    def rows(self, to):
        return self.r.low_rows.at[pl.ds(to * self.count, self.count)]

    def late(self, to, slot):
        r = self.r
        return remote(self.rows(to), self.kept.at[slot], r.kept_send.at[4 + to - 2], r.kept_recv.at[slot], (self.p.s, to))

    def late_own(self, to):
        return pltpu.make_async_copy(self.rows(to), self.kept.at[to], self.r.kept_send.at[4 + to - 2])

    def early(self, slot):
        r = self.r
        src = self.chars.at[slot, pl.ds(self.count, self.count)]
        return remote(src, self.kept.at[slot], r.kept_send.at[slot], r.kept_recv.at[slot], (self.p.s, 1))

    def early_own(self, slot):
        src = self.chars.at[slot, pl.ds(0, self.count)]
        return pltpu.make_async_copy(src, self.kept.at[slot], self.r.kept_recv.at[slot])

    def start_late(self, to):
        pl.when(self.p.b != to)(self.late(to, self.p.b).start)
        pl.when(self.p.b == to)(self.late_own(to).start)

    def start_early(self):
        @pl.when(self.p.b == 0)
        def _():
            for slot in range(4):
                self.early_own(slot).start()
                self.early(slot).start()

    def wait(self):
        b = self.p.b

        @pl.when(b == 0)
        def _():
            for slot in range(4):
                self.early_own(slot).wait()
                self.early(slot).wait_send()

        @pl.when(b == 1)
        def _():
            for slot in range(4):
                self.early(slot).wait_recv()

        for to in (2, 3):
            pl.when(b != to)(self.late(to, b).wait_send)

            @pl.when(b == to)
            def _():
                self.late_own(to).wait()
                for slot in range(4):
                    if slot != to:
                        self.late(to, slot).wait_recv()


class Small:
    def __init__(self, r, place):
        self.r, self.p = r, place

    def source(self, step):
        return self.r.small if step == 0 else self.r.small_sum.at[step - 1]

    def copy(self, step):
        r, p = self.r, self.p
        to = p.core() if step == 0 else p.pair(AXES[step - 1])
        return remote(self.source(step), r.small_land.at[step], r.small_send.at[step], r.small_recv.at[step], to)

    def start(self, step):
        self.copy(step).start()

    def finish(self, step):
        self.copy(step).wait()
        self.r.small_sum[step] = self.source(step)[...] + self.r.small_land[step]


def layer_kernel(names, chars, lengths, memory, grad_out, *rest):
    count = len(VECTORS) + 1 + len(WEIGHTS)
    vectors, table, weights = rest[: len(VECTORS)], rest[len(VECTORS)], rest[len(VECTORS) + 1 : count]
    kept, out_quiet, out_loud, grad_quiet, grad_loud, total_out, small_out = rest[count : count + 7]
    r = types.SimpleNamespace(**dict(zip(names, rest[count + 7 :])))
    p = Place()
    seg, width = r.pooled.shape
    r.grad_residual, r.grad_mixed, r.grad_rows = r.grad_output, r.grad_down, r.normed_two
    for n, name in enumerate(("mixed_flip", "query_u_t", "query_v_t", "grad_mixed_t")):
        setattr(r, name, r.slope.at[:, n * width : (n + 1) * width])
    r.grad_key_t, r.grad_value_t = r.hidden.at[:, : 2 * seg], r.hidden.at[:, 2 * seg :]
    r.grad_place_t, r.grad_query = r.grad_inner.at[:, : 2 * seg], r.grad_inner.at[:, 2 * seg : 3 * seg]
    loads = [
        pltpu.make_async_copy(src, dst, r.load_sem.at[n])
        for n, (src, dst) in enumerate(
            zip((*weights, table), [getattr(r, name) for name in WEIGHTS] + [r.table])
        )
    ]
    chars_rows = Rows(r, p, 0, chars, r.hidden, r.chars_quiet, r.chars_parts).back(r.out_rows, out_quiet, out_loud)
    grads_rows = Rows(r, p, 1, grad_out, r.grad_inner, r.grads_quiet, r.grads_parts).back(
        r.grad_rows, grad_quiet, grad_loud
    )
    raw = [getattr(r, f"raw_{name}") for name in VECTORS]
    small_loads = [
        pltpu.make_async_copy(src, dst, r.small_load.at[n])
        for n, (src, dst) in enumerate(zip((*vectors, lengths), (*raw, r.lengths)))
    ]
    small_loads[-1].start()
    for n in range(4):
        chars_rows.load(n).start()
    for copy in small_loads[:-1]:
        copy.start()
    for n in range(4):
        grads_rows.load(n).start()
    for copy in loads:
        copy.start()
    r.vec = lambda name: r.vectors[VECTORS.index(name) : VECTORS.index(name) + 1, :]

    chars_rows.clear()
    grads_rows.clear()
    barrier = pltpu.get_barrier_semaphore()
    others = [p.group(1), p.group(2), p.group(3), *(to for to, unused, other in p.peers("xy")[1][1:]), p.line(1), p.line(2), p.line(3)]
    for other in others:
        pl.semaphore_signal(barrier, inc=1, device_id=other, device_id_type=MESH)
    pl.semaphore_wait(barrier, len(others))

    rows = memory.shape[1]

    def memory_copy(k, slot):
        to = (p.b + k) % 4
        return remote(
            memory.at[to], r.memory.at[rows_at(slot * rows, rows)], r.memory_send.at[k], r.memory_recv.at[slot], p.group(k)
        )

    own_memory = pltpu.make_async_copy(memory.at[p.b], r.memory.at[rows_at(p.b * rows, rows)], r.memory_send.at[0])
    for k in (2, 3, 1):
        memory_copy(k, p.b).start()
    own_memory.start()
    chars_rows.start_quiet()
    small_loads[-1].wait()
    ends, lens = span_columns(r.lengths[...], QUIET)
    chars_rows.start_parts(ends, lens)
    for copy in loads:
        copy.wait()
    for copy in small_loads[:-1]:
        copy.wait()
    for n, name in enumerate(VECTORS):
        value = raw[n][...].astype(F32)
        if name == "bias_up":
            r.bias_up[...] = value.reshape(1, -1)
        elif value.ndim == 2:
            r.vectors[n : n + 1, :] = jnp.concatenate([value[h : h + 1, :] for h in range(value.shape[0])], axis=1)
        else:
            r.vectors[n : n + 1, :] = value.reshape(1, -1)
    project_places(r)
    waits = (1 - p.x) * p.c
    pl.when(waits == 0)(chars_rows.join_parts)
    grads_rows.start_quiet()
    grads_rows.start_parts(ends, lens)
    own_memory.wait()
    memory_copy(1, p.core()[1]).wait_recv()
    project_memory(rows_at(p.x * 2 * rows, 2 * rows), r)
    for slot in (2 * (1 - p.x), 2 * (1 - p.x) + 1):
        memory_copy(1, slot).wait_recv()
    project_memory(rows_at((1 - p.x) * 2 * rows, 2 * rows), r)
    own_lens = column(lens, p.b)

    def forward(block):
        project_segments(block, seg, r)
        attend(block, seg, r)
        if block == 0:
            pl.when(waits == 1)(chars_rows.join_parts)
        feed_forward_in(block, r)

    chars_rows.wait_quiet(0)
    r.pooled[0:HALF] = chars_rows.quiet[0:HALF].astype(F32)
    forward(0)
    grads_rows.join_parts()
    feed_forward_out(0, r)
    for part in range(BACK_EARLY):
        chars_rows.start_quiet_back(part)
    chars_rows.wait_quiet(1)
    r.pooled[HALF:QUIET] = chars_rows.quiet[HALF:QUIET].astype(F32)
    r.pooled[QUIET:seg] = chars_rows.wait_parts() / own_lens
    r.low_rows[...] = r.pooled[...].astype(BF16)

    forward(1)
    grads_rows.wait_quiet(0)
    grads_rows.wait_quiet(1)
    r.grad_output[0:QUIET] = grads_rows.quiet[...].astype(F32)
    r.grad_output[QUIET:seg] = grads_rows.wait_parts()
    low = r.grad_output[...].astype(BF16)
    r.grad_down[...] = low
    r.grad_down_t[...] = low.astype(F32).T.astype(BF16)
    r.normed_two_t[...] = r.normed_two[...].astype(F32).T.astype(BF16)
    r.small[...] = jnp.zeros(r.small.shape, F32)
    r.small[6:7, :] = jnp.sum(low.astype(F32), axis=0, keepdims=True)

    sums = Sum(p, r.total, r.land, total_out, r.sum_send, r.sum_recv, r.store_sem)

    rows_kept = Kept(r, p, chars, kept)

    def take(n):
        if n == KEPT_DURING[0]:
            rows_kept.start_early()
        for to in (2, 3):
            if n == KEPT_DURING[to - 1]:
                rows_kept.start_late(to)
        for part, at in enumerate(BACK_DURING):
            if at == n:
                chars_rows.start_quiet_back(BACK_EARLY + part)
        for k, step in DURING[n]:
            sums.step(k, step)

    def between(pair, unit):
        for n in range(4):
            at = n * 5 + 6 + unit
            if DURING[at] or at in BACK_DURING or at in KEPT_DURING:
                pl.when(pair == n)(functools.partial(take, at))

    for n in range(4):
        feed_forward_back(n, r)
        take(n)
    feed_forward_out(1, r)
    chars_rows.start_back()
    take(4)
    middle_back(r, BASES[4])
    take(5)

    def back(n, carry):
        attend_back_pair(n, seg, r, functools.partial(between, n))
        pair_weights(n, seg, r, BASES[5] + n * PIECES[5][0])
        between(n, 4)
        return carry

    lax.fori_loop(0, 4, back, 0)
    grad_pooled = first_back(seg, r)
    r.grad_rows[0:QUIET] = grad_pooled[:QUIET].astype(BF16)
    r.grad_rows[QUIET:seg] = (grad_pooled[QUIET:] / own_lens).astype(BF16)
    grads_rows.start_back()
    small = Small(r, p)
    small_store = pltpu.make_async_copy(r.small_sum.at[4], small_out, r.small_sem)
    small.start(0)
    take(26)
    every = len(AFTER) // 12
    for n, (k, step) in enumerate(AFTER):
        for part, at in enumerate(BACK_AFTER):
            if at == n:
                grads_rows.start_quiet_back(part)
        if n % every == every - 1 and n // every < 10:
            at = n // every
            if at % 2 == 1:
                small.finish(at // 2)
                if at // 2 < 4:
                    small.start(at // 2 + 1)
                else:
                    small_store.start()
            if at == 4:
                chars_rows.pass_on()
            if at == 8:
                grads_rows.pass_on()
        sums.step(k, step)
    for k in (1, 2, 3):
        memory_copy(k, p.b).wait_send()
    rows_kept.wait()
    chars_rows.wait_sent()
    grads_rows.wait_sent()
    chars_rows.wait_back()
    grads_rows.wait_back()
    small_store.wait()


def spread_kernel(
    lengths, chars, grad_out, rows, out_quiet, out_loud, grad_quiet, grad_loud, wide, flat, pairs, small,
    out_chars, grad_chars, kept, w_query, w_key, w_value, w_rel, w_out, w_up, w_down, bias_u, bias_v, *vectors,
):
    n = pl.program_id(0)
    b = lax.axis_index("blk")
    places = chars.shape[1]
    seg = lengths.shape[1]
    lens = lengths[...].astype(F32).astype(BF16)
    row, col = ramp((seg - QUIET, seg), 0) + QUIET, ramp((seg - QUIET, seg), 1)
    upto = jnp.where(col <= row, 1.0, 0.0).astype(BF16)
    same = jnp.where(col == row, 1.0, 0.0).astype(BF16)
    pick = ramp((lengths.shape[0], seg - QUIET), 0) == n
    end = jnp.sum(jnp.where(pick, mm_nt(lens, upto), 0.0), axis=0, keepdims=True)
    length = jnp.sum(jnp.where(pick, mm_nt(lens, same), 0.0), axis=0, keepdims=True)
    place = (ramp((places, seg - QUIET), 0) + b * places).astype(F32)
    chosen = jnp.where((place < end) & (place >= end - length), 1.0, 0.0).astype(BF16)
    first = b == 0
    spans = chip_spans(places, seg - QUIET)
    here = ramp((seg - QUIET, 1), 0)
    inside = [(here >= start) & (here < start + size) for start, size in spans]
    there = jnp.where(b < 2, inside[0].astype(F32), inside[1].astype(F32)) > 0
    kept[...] = rows[...]
    for source, quiet, loud, out in (
        (chars, out_quiet, out_loud, out_chars),
        (grad_out, grad_quiet, grad_loud, grad_chars),
    ):
        spread = mm(chosen, jnp.where(there, loud[0].astype(F32), 0.0).astype(BF16))
        whole = source[0].astype(F32) + spread
        out[0, QUIET:places] = whole[QUIET:].astype(out.dtype)
        out[0, 0:QUIET] = (whole[:QUIET] + jnp.where(first, quiet[0].astype(F32), 0.0)).astype(out.dtype)
    w_down[...] = wide[0:512].astype(F32).T
    w_up[...] = wide[512:1024].astype(F32)
    w_out[...] = flat[...].astype(F32)
    for m, out in enumerate((w_query, w_key, w_value, w_rel)):
        out[...] = pairs[m * 128 : (m + 1) * 128].astype(F32).T
    for m, out in enumerate((bias_u, bias_v)):
        out[...] = jnp.concatenate([small[m : m + 1, h * 64 : (h + 1) * 64] for h in range(8)], axis=0)
    for m, out in enumerate(vectors[:4]):
        out[...] = small[2 + m : 3 + m, :]
    vectors[4][...] = jnp.concatenate([small[m : m + 1, :] for m in range(7, 11)], axis=1)
    vectors[5][...] = small[6:7, :]


def shards_whole(
    chars, seg_lengths, memory, grad_out, w_query, w_key, w_value, w_rel, w_out, w_up, w_down,
    bias_u, bias_v, gain_one, shift_one, gain_two, shift_two, bias_up, bias_down,
):
    count, places, width = chars.shape
    seg, hidden = seg_lengths.shape[1], w_up.shape[1]
    rows = memory.shape[1]
    table = jnp.asarray(sine_table(2 * seg, width))
    vectors = (bias_u, bias_v, gain_one, shift_one, gain_two, shift_two, bias_up, bias_down)
    scratch = layer_scratch(seg, width, hidden, {name: v.shape for name, v in zip(VECTORS, vectors)})
    anywhere, near = pl.BlockSpec(memory_space=pl.ANY), pl.BlockSpec(memory_space=pltpu.VMEM)
    loud = seg - QUIET
    kept, out_quiet, out_loud, grad_quiet, grad_loud, total, small = pl.pallas_call(
        functools.partial(layer_kernel, tuple(scratch)),
        out_shape=[
            jax.ShapeDtypeStruct((count, rows, width), BF16),
            jax.ShapeDtypeStruct((count, QUIET, width), BF16),
            jax.ShapeDtypeStruct((count, loud, width), BF16),
            jax.ShapeDtypeStruct((count, QUIET, width), BF16),
            jax.ShapeDtypeStruct((count, loud, width), BF16),
            jax.ShapeDtypeStruct((BASES[-1], width), BF16),
            jax.ShapeDtypeStruct((16, width), F32),
        ],
        in_specs=[anywhere] * (12 + len(VECTORS)),
        out_specs=[anywhere] * 7,
        scratch_shapes=list(scratch.values()),
        compiler_params=pltpu.CompilerParams(
            collective_id=0, has_side_effects=True, vmem_limit_bytes=VMEM_BYTES
        ),
        name="layer",
    )(
        chars, seg_lengths, memory, grad_out,
        *vectors, table,
        w_query, w_key, w_value, w_rel, w_out, w_up, w_down,
    )

    def block(shape, index):
        return pl.BlockSpec(shape, index)

    def each(*shape):
        return block((1, *shape), lambda n: (n, 0, 0))

    def whole(*shape):
        return block(shape, lambda n: (0, 0))

    vector = [(1, width)] * 4 + [(1, hidden), (1, width)]
    outs = pl.pallas_call(
        spread_kernel,
        grid=(count,),
        out_shape=[
            jax.ShapeDtypeStruct(chars.shape, BF16),
            jax.ShapeDtypeStruct(chars.shape, F32),
            jax.ShapeDtypeStruct(memory.shape, BF16),
            *[jax.ShapeDtypeStruct((width, width), F32)] * 5,
            jax.ShapeDtypeStruct((width, hidden), F32),
            jax.ShapeDtypeStruct((hidden, width), F32),
            *[jax.ShapeDtypeStruct(bias_u.shape, F32)] * 2,
            *[jax.ShapeDtypeStruct(shape, F32) for shape in vector],
        ],
        in_specs=[
            whole(*seg_lengths.shape),
            each(places, width),
            each(places, width),
            each(rows, width),
            each(QUIET, width),
            each(loud, width),
            each(QUIET, width),
            each(loud, width),
            block((1024, width), lambda n: (n, 0)),
            block((128, width), lambda n: (BASES[4] // 128 + n, 0)),
            block((512, width), lambda n: (BASES[5] // 512 + n, 0)),
            whole(16, width),
        ],
        out_specs=[
            each(places, width),
            each(places, width),
            each(rows, width),
            *[block((width, 128), lambda n: (0, n))] * 4,
            block((128, width), lambda n: (n, 0)),
            block((width, 512), lambda n: (0, n)),
            block((512, width), lambda n: (n, 0)),
            *[whole(*bias_u.shape)] * 2,
            *[whole(*shape) for shape in vector],
        ],
        compiler_params=pltpu.CompilerParams(vmem_limit_bytes=VMEM_BYTES),
        name="spread",
    )(seg_lengths, chars, grad_out, kept, out_quiet, out_loud, grad_quiet, grad_loud, total, total, total, small)
    return (*outs[:12], *[v.reshape(-1) for v in outs[12:]])


VMEM_BYTES = 64 * 2**20 - 2**16


def fits_whole(mesh):
    return dict(mesh.shape) == {"seq": 8, "blk": 4}


def layer_norm(value, gain, shift):
    center = value - jnp.mean(value, axis=-1, keepdims=True)
    spread = jnp.mean(center * center, axis=-1, keepdims=True)
    return center * lax.rsqrt(spread + 1e-05) * gain + shift


def angle_tables(places, feature_width):
    freqs = jnp.exp(
        jnp.arange(feature_width // 2, dtype=jnp.float32)
        * (-2.0 * math.log(10000.0) / feature_width)
    )
    angles = places[:, None] * freqs[None, :]
    return (jnp.sin(angles), jnp.cos(angles))


def smooth_gate(value):
    return jax.nn.gelu(value, approximate=False)


def segment_ids(seg_end, char_places):
    return jnp.sum((seg_end[:, None, :] <= char_places[None, :, None]).astype(jnp.int32), axis=2)


def shards(
    chars,
    seg_lengths,
    memory,
    grad_out,
    w_query,
    w_key,
    w_value,
    w_rel,
    w_out,
    w_up,
    w_down,
    bias_u,
    bias_v,
    gain_one,
    shift_one,
    gain_two,
    shift_two,
    bias_up,
    bias_down,
):
    blk_index = lax.axis_index("blk")
    seq_local, char_rows, feature_width = chars.shape
    seg_rows = memory.shape[1]
    seg_count = seg_lengths.shape[1]
    head_count, head_dim = bias_u.shape
    half_width = feature_width // 2
    score_scale = head_dim ** (-0.5)
    seg_start = blk_index * seg_rows
    gain_one_f = gain_one.astype(jnp.float32)
    shift_one_f = shift_one.astype(jnp.float32)
    gain_two_f = gain_two.astype(jnp.float32)
    shift_two_f = shift_two.astype(jnp.float32)
    seg_end = jnp.cumsum(seg_lengths, axis=1)
    char_places = blk_index * char_rows + jnp.arange(char_rows, dtype=jnp.int32)
    segment = segment_ids(seg_end, char_places)
    own_lengths = lax.dynamic_slice_in_dim(seg_lengths, seg_start, seg_rows, 1).astype(jnp.float32)
    chars_f = chars.astype(jnp.float32)
    grad_f = grad_out.astype(jnp.float32)

    def full_table(values, ids):
        return jax.ops.segment_sum(values, ids, num_segments=seg_count)

    part_sums = jax.vmap(full_table)(chars_f, segment)
    pooled_sum = lax.psum_scatter(part_sums, "blk", scatter_dimension=1, tiled=True)
    pooled = pooled_sum / own_lengths[:, :, None]
    normed = layer_norm(pooled, gain_one_f, shift_one_f)
    normed_low = normed.astype(jnp.bfloat16)
    memory_f = memory.astype(jnp.float32)
    mem_low = layer_norm(memory_f, gain_one_f, shift_one_f).astype(jnp.bfloat16)
    query_rows = jnp.einsum("sid,de->sie", normed_low, w_query, preferred_element_type=jnp.float32)
    key_local = jnp.stack(
        [
            jnp.einsum("sid,de->sie", mem_low, w_key, preferred_element_type=jnp.float32),
            jnp.einsum("sid,de->sie", normed_low, w_key, preferred_element_type=jnp.float32),
        ],
        axis=1,
    ).astype(jnp.bfloat16)
    value_local = jnp.stack(
        [
            jnp.einsum("sid,de->sie", mem_low, w_value, preferred_element_type=jnp.float32),
            jnp.einsum("sid,de->sie", normed_low, w_value, preferred_element_type=jnp.float32),
        ],
        axis=1,
    ).astype(jnp.bfloat16)
    key_all, value_all = (
        lax.all_gather(key_local, "blk", axis=2, tiled=True),
        lax.all_gather(value_local, "blk", axis=2, tiled=True),
    )
    key_heads = key_all.reshape(seq_local, 2 * seg_count, head_count, head_dim)
    value_heads = value_all.reshape(seq_local, 2 * seg_count, head_count, head_dim)
    query_u = (
        (query_rows + bias_u.astype(jnp.float32).reshape(-1))
        .astype(jnp.bfloat16)
        .reshape(seq_local, seg_rows, head_count, head_dim)
    )
    query_v = (
        (query_rows + bias_v.astype(jnp.float32).reshape(-1))
        .astype(jnp.bfloat16)
        .reshape(seq_local, seg_rows, head_count, head_dim)
    )
    w_rel_heads = w_rel.reshape(feature_width, head_count, head_dim)
    rel_coeff = jnp.einsum(
        "sihe,fhe->sihf", query_v, w_rel_heads, preferred_element_type=jnp.float32
    )
    sin_all, cos_all = angle_tables(jnp.arange(2 * seg_count).astype(jnp.float32), feature_width)
    key_pos = jnp.concatenate([cos_all, sin_all], axis=-1).astype(jnp.bfloat16)
    query_index = seg_count + seg_start + jnp.arange(seg_rows, dtype=jnp.int32)
    sin_q, cos_q = angle_tables(query_index.astype(jnp.float32), feature_width)
    sin_query = sin_q[None, :, None, :]
    cos_query = cos_q[None, :, None, :]
    coeff_sin = rel_coeff[..., :half_width]
    coeff_cos = rel_coeff[..., half_width:]
    query_pos = jnp.concatenate(
        [
            coeff_sin * sin_query + coeff_cos * cos_query,
            coeff_cos * sin_query - coeff_sin * cos_query,
        ],
        axis=-1,
    ).astype(jnp.bfloat16)
    allowed = jnp.arange(2 * seg_count, dtype=jnp.int32)[None, :] <= query_index[:, None]

    def score_block():
        raw_scores = (
            jnp.einsum("sihe,sjhe->shij", query_u, key_heads, preferred_element_type=jnp.float32)
            + jnp.einsum("sihf,jf->shij", query_pos, key_pos, preferred_element_type=jnp.float32)
        ) * score_scale
        return jnp.where(allowed[None, None], raw_scores, -1e30)

    scores = score_block()
    row_top = jnp.max(scores, axis=-1, keepdims=True)
    expo = jnp.exp(scores - row_top)
    row_total = jnp.sum(expo, axis=-1, keepdims=True)
    log_total = row_top + jnp.log(row_total)
    att_probs = (expo / row_total).astype(jnp.bfloat16)
    att_mixed = jnp.einsum(
        "shij,sjhe->sihe", att_probs, value_heads, preferred_element_type=jnp.float32
    )
    mixed_low = att_mixed.reshape(seq_local, seg_rows, feature_width).astype(jnp.bfloat16)
    residual = pooled + jnp.einsum(
        "sid,de->sie", mixed_low, w_out, preferred_element_type=jnp.float32
    )
    normed_two = layer_norm(residual, gain_two_f, shift_two_f)
    two_low = normed_two.astype(jnp.bfloat16)
    ffn_inner = jnp.einsum(
        "sid,df->sif", two_low, w_up, preferred_element_type=jnp.float32
    ) + bias_up.astype(jnp.float32)
    hidden_low = smooth_gate(ffn_inner).astype(jnp.bfloat16)
    branch_out = jnp.einsum(
        "sif,fd->sid", hidden_low, w_down, preferred_element_type=jnp.float32
    ) + bias_down.astype(jnp.float32)
    out_low = (residual + branch_out).astype(jnp.bfloat16)
    rows_all = lax.all_gather(out_low, "blk", axis=1, tiled=True)
    picked = jnp.take_along_axis(rows_all, segment[:, :, None], axis=1)
    out_chars = (chars_f + picked.astype(jnp.float32)).astype(jnp.bfloat16)
    new_memory = pooled.astype(jnp.bfloat16)
    grad_table = jax.vmap(full_table)(grad_f, segment)
    grad_output = lax.psum_scatter(grad_table, "blk", scatter_dimension=1, tiled=True)
    grad_down_low = grad_output.astype(jnp.bfloat16)
    grad_bias_down = jnp.sum(grad_down_low.astype(jnp.float32), axis=(0, 1))
    grad_w_down = jnp.einsum(
        "sif,sid->fd", hidden_low, grad_down_low, preferred_element_type=jnp.float32
    )
    grad_hidden = jnp.einsum(
        "sid,fd->sif", grad_down_low, w_down, preferred_element_type=jnp.float32
    )
    unused_value, gate_back = jax.vjp(smooth_gate, ffn_inner)
    grad_inner = gate_back(grad_hidden)[0].astype(jnp.bfloat16)
    grad_bias_up = jnp.sum(grad_inner.astype(jnp.float32), axis=(0, 1))
    grad_w_up = jnp.einsum("sid,sif->df", two_low, grad_inner, preferred_element_type=jnp.float32)
    grad_normed_two = jnp.einsum(
        "sif,df->sid", grad_inner, w_up, preferred_element_type=jnp.float32
    )
    unused_norm, norm_two_back = jax.vjp(layer_norm, residual, gain_two_f, shift_two_f)
    grad_resid_norm, grad_gain_two, grad_shift_two = norm_two_back(grad_normed_two)
    grad_residual = grad_output + grad_resid_norm
    grad_att_low = grad_residual.astype(jnp.bfloat16)
    grad_w_out = jnp.einsum(
        "sid,sie->de", mixed_low, grad_att_low, preferred_element_type=jnp.float32
    )
    grad_mixed = jnp.einsum("sie,de->sid", grad_att_low, w_out, preferred_element_type=jnp.float32)
    grad_mixed = grad_mixed.astype(jnp.bfloat16).reshape(seq_local, seg_rows, head_count, head_dim)
    scores_again = score_block()
    probs_full = jnp.exp(scores_again - log_total)
    probs_low = probs_full.astype(jnp.bfloat16)
    grad_probs = jnp.einsum(
        "sihe,sjhe->shij", grad_mixed, value_heads, preferred_element_type=jnp.float32
    )
    grad_values = jnp.einsum(
        "shij,sihe->sjhe", probs_low, grad_mixed, preferred_element_type=jnp.float32
    )
    prob_delta = jnp.sum(probs_full * grad_probs, axis=-1, keepdims=True)
    grad_scores = (probs_full * (grad_probs - prob_delta)).astype(jnp.bfloat16)
    grad_query_u = (
        jnp.einsum("shij,sjhe->sihe", grad_scores, key_heads, preferred_element_type=jnp.float32)
        * score_scale
    )
    grad_keys = (
        jnp.einsum("shij,sihe->sjhe", grad_scores, query_u, preferred_element_type=jnp.float32)
        * score_scale
    )
    grad_query_pos = (
        jnp.einsum("shij,jf->sihf", grad_scores, key_pos, preferred_element_type=jnp.float32)
        * score_scale
    )
    grad_first = grad_query_pos[..., :half_width]
    grad_second = grad_query_pos[..., half_width:]
    grad_coeff = jnp.concatenate(
        [
            grad_first * sin_query - grad_second * cos_query,
            grad_first * cos_query + grad_second * sin_query,
        ],
        axis=-1,
    ).astype(jnp.bfloat16)
    grad_w_rel = jnp.einsum(
        "sihf,sihe->fhe", grad_coeff, query_v, preferred_element_type=jnp.float32
    ).reshape(feature_width, feature_width)
    grad_query_v = jnp.einsum(
        "sihf,fhe->sihe", grad_coeff, w_rel_heads, preferred_element_type=jnp.float32
    )
    grad_bias_u = jnp.sum(grad_query_u, axis=(0, 1))
    grad_bias_v = jnp.sum(grad_query_v, axis=(0, 1))
    grad_query = (
        (grad_query_u + grad_query_v)
        .reshape(seq_local, seg_rows, feature_width)
        .astype(jnp.bfloat16)
    )
    grad_w_query = jnp.einsum(
        "sid,sie->de", normed_low, grad_query, preferred_element_type=jnp.float32
    )
    grad_normed = jnp.einsum("sie,de->sid", grad_query, w_query, preferred_element_type=jnp.float32)
    key_share, value_share = (
        lax.psum_scatter(
            grad_keys.reshape(seq_local, 2, seg_count, feature_width),
            "blk",
            scatter_dimension=2,
            tiled=True,
        ),
        lax.psum_scatter(
            grad_values.reshape(seq_local, 2, seg_count, feature_width),
            "blk",
            scatter_dimension=2,
            tiled=True,
        ),
    )
    key_low = key_share.astype(jnp.bfloat16)
    value_low = value_share.astype(jnp.bfloat16)
    grad_w_key = jnp.einsum(
        "sid,sie->de", mem_low, key_low[:, 0], preferred_element_type=jnp.float32
    ) + jnp.einsum("sid,sie->de", normed_low, key_low[:, 1], preferred_element_type=jnp.float32)
    grad_w_value = jnp.einsum(
        "sid,sie->de", mem_low, value_low[:, 0], preferred_element_type=jnp.float32
    ) + jnp.einsum("sid,sie->de", normed_low, value_low[:, 1], preferred_element_type=jnp.float32)
    grad_normed = grad_normed + jnp.einsum(
        "sie,de->sid", key_low[:, 1], w_key, preferred_element_type=jnp.float32
    )
    grad_normed = grad_normed + jnp.einsum(
        "sie,de->sid", value_low[:, 1], w_value, preferred_element_type=jnp.float32
    )
    grad_mem_normed = jnp.einsum(
        "sie,de->sid", key_low[:, 0], w_key, preferred_element_type=jnp.float32
    ) + jnp.einsum("sie,de->sid", value_low[:, 0], w_value, preferred_element_type=jnp.float32)
    unused_one, norm_one_back = jax.vjp(layer_norm, pooled, gain_one_f, shift_one_f)
    grad_pooled_norm, grad_gain_one, grad_shift_one = norm_one_back(grad_normed)
    unused_mem, norm_mem_back = jax.vjp(layer_norm, memory_f, gain_one_f, shift_one_f)
    unused_grad, grad_gain_mem, grad_shift_mem = norm_mem_back(grad_mem_normed)
    grad_gain_one = grad_gain_one + grad_gain_mem
    grad_shift_one = grad_shift_one + grad_shift_mem
    grad_pooled = grad_residual + grad_pooled_norm
    grad_sum = grad_pooled / own_lengths[:, :, None]
    grad_sum_all = lax.all_gather(grad_sum, "blk", axis=1, tiled=True)
    grad_chars = grad_f + jnp.take_along_axis(grad_sum_all, segment[:, :, None], axis=1)
    (
        grad_w_query,
        grad_w_key,
        grad_w_value,
        grad_w_rel,
        grad_w_out,
        grad_w_up,
        grad_w_down,
        grad_bias_u,
        grad_bias_v,
        grad_gain_one,
        grad_shift_one,
        grad_gain_two,
        grad_shift_two,
        grad_bias_up,
        grad_bias_down,
    ) = lax.psum(
        (
            grad_w_query,
            grad_w_key,
            grad_w_value,
            grad_w_rel,
            grad_w_out,
            grad_w_up,
            grad_w_down,
            grad_bias_u,
            grad_bias_v,
            grad_gain_one,
            grad_shift_one,
            grad_gain_two,
            grad_shift_two,
            grad_bias_up,
            grad_bias_down,
        ),
        ("seq", "blk"),
    )
    return (
        out_chars,
        grad_chars,
        new_memory,
        grad_w_query,
        grad_w_key,
        grad_w_value,
        grad_w_rel,
        grad_w_out,
        grad_w_up,
        grad_w_down,
        grad_bias_u,
        grad_bias_v,
        grad_gain_one,
        grad_shift_one,
        grad_gain_two,
        grad_shift_two,
        grad_bias_up,
        grad_bias_down,
    )


def solution(mesh):
    placed = (
        P("seq", "blk", None),
        P("seq", None),
        P("seq", "blk", None),
        P("seq", "blk", None),
        P(),
        P(),
        P(),
        P(),
        P(),
        P(),
        P(),
        P(),
        P(),
        P(),
        P(),
        P(),
        P(),
        P(),
        P(),
    )
    return jax.shard_map(
        shards_whole if fits_whole(mesh) else shards,
        mesh=mesh,
        in_specs=placed,
        out_specs=(
            P("seq", "blk", None),
            P("seq", "blk", None),
            P("seq", "blk", None),
            P(),
            P(),
            P(),
            P(),
            P(),
            P(),
            P(),
            P(),
            P(),
            P(),
            P(),
            P(),
            P(),
            P(),
            P(),
        ),
        check_vma=False,
    )
```

```python
import functools
import math
import types

import jax
import jax.numpy as jnp
import numpy as np
from jax import lax
from jax.experimental import pallas as pl
from jax.experimental.pallas import tpu as pltpu
from jax.sharding import PartitionSpec as P

F32, BF16 = jnp.float32, jnp.bfloat16
NT = (((1,), (1,)), ((), ()))


def mm(a, b):
    return jnp.dot(a, b, preferred_element_type=F32)


def mm_nt(a, b):
    return lax.dot_general(a, b, NT, preferred_element_type=F32)


def normalize(value):
    center = value - jnp.mean(value, axis=-1, keepdims=True)
    inv = lax.rsqrt(jnp.mean(center * center, axis=-1, keepdims=True) + 1e-05)
    return center * inv, inv


def norm_back(grad, unit, inv, gain):
    scaled = grad * gain
    along = jnp.mean(scaled * unit, axis=-1, keepdims=True)
    return inv * (scaled - jnp.mean(scaled, axis=-1, keepdims=True) - unit * along)


def gelu_parts(value):
    gate = 0.5 + 0.5 * lax.erf(value * 0.7071067811865476)
    return gate, gate + value * jnp.exp(-0.5 * value * value) * 0.3989422804014327


def ramp(shape, dim):
    return lax.broadcasted_iota(jnp.int32, shape, dim)


MESH = pl.DeviceIdType.MESH
HALF = 256
FACTOR = dict(x=2, y=2, near=2, far=2, z=4, xy=4)
AXES = ("x", "y", "near", "far")
PIECES = tuple((1024, f"tile{n}") for n in range(4)) + ((512, "middle"),) + tuple((512, f"pair{n}") for n in range(4))
BASES = tuple(sum(rows for rows, unused in PIECES[:n]) for n in range(len(PIECES) + 1))
VECTORS = ("bias_u", "bias_v", "gain_one", "shift_one", "gain_two", "shift_two", "bias_up", "bias_down")
ORDERS = (
    (("y", "x", "z"), ("x", "y", "z")),
    (("x", "y", "z"), ("y", "x", "z")),
    (("near", "y", "x", "far"), ("far", "x", "near", "y")),
    (("y", "x", "near", "far"), ("near", "y", "x", "far")),
    (("near", "far", "xy"), ("far", "near", "xy")),
    (("y", "x", "near", "far"), ("y", "x", "near", "far")),
    (("y", "x", "z"), ("x", "y", "z")),
    (("x", "y", "z"), ("x", "y", "z")),
    (("y", "x", "z"), ("y", "x", "z")),
)
DURING = (
    ((0, 0),), ((1, 0),), ((2, 0),), ((3, 0),), ((0, 1),), ((2, 1), (1, 1), (4, 0)), ((3, 1),), (), (),
    ((4, 1),), ((0, 2), (5, 0)), (), (), ((1, 2),), ((5, 1),), ((6, 0),), ((2, 2),), ((0, 3),), (),
    ((6, 1), (3, 2)), ((1, 3), (7, 0)), (), ((5, 2), (4, 2)), ((2, 3), (7, 1)), (), ((0, 4), (6, 2), (8, 0)),
    ((5, 3), (3, 3)),
)
AFTER = (
    (2, 4), (1, 4), (8, 1), (4, 3), (7, 2), (6, 3), (5, 4), (3, 4), (0, 5), (2, 5), (8, 2), (1, 5), (7, 3),
    (4, 4), (6, 4), (5, 5), (0, 6), (8, 3), (3, 5), (2, 6), (1, 6), (4, 5), (7, 4), (6, 5), (5, 6), (0, 7),
    (2, 7), (8, 4), (3, 6), (0, 8), (1, 7), (5, 7), (4, 6), (6, 6), (2, 8), (7, 5), (3, 7), (1, 8), (8, 5),
    (5, 8), (6, 7), (7, 6), (4, 7), (6, 8), (3, 8), (4, 8), (8, 6), (5, 9), (2, 9), (5, 10), (7, 7), (3, 9),
    (2, 10), (7, 8), (8, 7), (3, 10), (8, 8),
)
BACK_DURING = (8, 13)
BACK_AFTER = (0, 37, 43, 46, 51, 51)


class Place:
    def __init__(self):
        self.s = lax.axis_index("seq")
        self.b = lax.axis_index("blk")
        self.z, self.y = self.s // 2, self.s % 2
        self.x, self.c = self.b // 2, self.b % 2
        self.bit = dict(x=self.x, y=self.y, near=self.z % 2, far=self.z // 2)

    def group(self, k):
        return (self.s, (self.b + k) % 4)

    def core(self):
        return (self.s, self.b + 1 - 2 * self.c)

    def across(self):
        return (self.s, self.b + 2 - 4 * self.x)

    def move(self, axis):
        reach = dict(x=(0, 2), y=(1, 0), near=(2, 0), far=(4, 0))[axis]
        turn = 1 - 2 * self.bit[axis]
        return reach[0] * turn, reach[1] * turn

    def peers(self, axis):
        if axis == "z":
            return self.z, [(self.line(j), (self.z + j) % 4, (self.z + 4 - j) % 4) for j in (1, 2, 3)]
        if axis == "xy":
            out = []
            for across, along in ((1, 0), (0, 1), (1, 1)):
                x, y = self.x + across * (1 - 2 * self.x), self.y + along * (1 - 2 * self.y)
                device = (self.s + along * (1 - 2 * self.y), self.b + across * 2 * (1 - 2 * self.x))
                out.append((device, x + 2 * y, x + 2 * y))
            return self.x + 2 * self.y, out
        bit = self.bit[axis]
        return bit, [(self.pair(axis), 1 - bit, 1 - bit)]

    def stage(self, zero, one):
        if zero == one:
            return self.peers(zero)

        def pick(a, b):
            return a * (1 - self.c) + b * self.c

        (own_zero, peers_zero), (own_one, peers_one) = self.peers(zero), self.peers(one)
        peers = [
            ((pick(d[0], e[0]), pick(d[1], e[1])), pick(i, j), pick(f, g))
            for (d, i, f), (e, j, g) in zip(peers_zero, peers_one)
        ]
        return pick(own_zero, own_one), peers

    def line(self, j):
        return (((self.z + j) % 4) * 2 + self.y, self.b)

    def pair(self, axis):
        away = self.move(axis)
        return (self.s + away[0], self.b + away[1])


def rows_at(start, size):
    return pl.ds(pl.multiple_of(start, 16), size)


def remote(src, dst, send, recv, to):
    return pltpu.make_async_remote_copy(src, dst, send, recv, device_id=to, device_id_type=MESH)


def piece_rows(k):
    rows = [PIECES[k][0] // 2]
    for axis in ORDERS[k][0]:
        rows.append(rows[-1] // FACTOR[axis])
    return rows


def piece_lands(k):
    rows = piece_rows(k)
    return [rows[0]] + [(FACTOR[axis] - 1) * rows[n + 1] for n, axis in enumerate(ORDERS[k][0])]


def piece_peers(k):
    stages = [FACTOR[axis] - 1 for axis in ORDERS[k][0]]
    return [1, *stages, *stages[::-1], 1]


def starts(counts):
    out, end = [], 0
    for piece in counts:
        out.append([])
        for count in piece:
            out[-1].append(end)
            end += count
    return out, end


LANDS = starts([piece_lands(k) for k in range(len(PIECES))])
SENDS = starts([[max(piece_peers(k))] for k in range(len(PIECES))])
RECVS = starts([piece_peers(k) for k in range(len(PIECES))])


class Sum:
    def __init__(self, place, total, land, out, send, recv, store):
        self.p, self.g, self.land, self.out = place, total, land, out
        self.send, self.recv, self.store = send, recv, store
        known = {}
        self.stages = []
        for orders in ORDERS:
            for axes in zip(*orders):
                if axes not in known:
                    known[axes] = place.stage(*axes)
            self.stages.append([known[axes] for axes in zip(*orders)])

    def offset(self, k, n):
        rows = piece_rows(k)
        start = BASES[k] + self.p.c * rows[0]
        for m in range(n):
            start = start + self.stages[k][m][0] * rows[m + 1]
        return start

    def lands(self, k, n, start, size):
        return self.land.at[rows_at(LANDS[0][k][n] + start, size)]

    def copies(self, step, k, landing=False):
        p, rows = self.p, piece_rows(k)
        count = len(rows) - 1

        def copy(src, dst, to, j=0):
            return remote(src, dst, self.send.at[SENDS[0][k][0] + j], self.recv.at[RECVS[0][k][step] + j], to)

        if step == 0:
            src = self.g.at[rows_at(BASES[k] + (1 - p.c) * rows[0], rows[0])]
            return [copy(src, self.lands(k, 0, 0, rows[0]), p.core())]
        if step == 2 * count + 1:
            span = BASES[k] + (1 - p.c if landing else p.c) * rows[0]
            return [copy(self.lands(k, 0, 0, rows[0]), self.out.at[rows_at(span, rows[0])], p.core())]
        n = step - 1 if step <= count else 2 * count - step
        size = rows[n + 1]
        own, peers = self.stages[k][n]
        if step <= count:
            start = self.offset(k, n)
            return [
                copy(self.g.at[rows_at(start + at * size, size)], self.lands(k, n + 1, j * size, size), to, j)
                for j, (to, at, unused) in enumerate(peers)
            ]
        src = self.lands(k, n, own * size, size) if n == count - 1 else self.lands(k, n + 1, 0, size)
        return [
            copy(src, self.lands(k, n, (back if landing else own) * size, size), to, j)
            for j, (to, unused, back) in enumerate(peers)
        ]

    def own(self, k):
        rows = piece_rows(k)[0]
        span = rows_at(BASES[k] + self.p.c * rows, rows)
        return pltpu.make_async_copy(self.lands(k, 0, 0, rows), self.out.at[span], self.store.at[k])

    def added(self, k, n, start, size):
        mine = self.g[rows_at(self.offset(k, n) + start, size)]
        if n == 0 or len(self.stages[k][n - 1][1]) == 1:
            return mine + self.lands(k, n, start, size)[...]
        whole = piece_rows(k)[n]
        mine = mine.astype(F32)
        for j in range(len(self.stages[k][n - 1][1])):
            mine = mine + self.lands(k, n, j * whole + start, size)[...].astype(F32)
        return mine.astype(BF16)

    def step(self, k, step):
        rows = piece_rows(k)
        count = len(rows) - 1
        if step > 0:
            for copy in self.copies(step - 1, k):
                copy.wait_send()
            for copy in self.copies(step - 1, k, landing=True):
                copy.wait_recv()
        if 1 <= step <= count:
            n, size = step - 1, rows[step]
            own, peers = self.stages[k][n]
            copies = self.copies(step, k)
            for index, copy in zip([at for unused, at, other in peers] + [own], copies + [None]):
                part = self.added(k, n, index * size, size)
                self.g[rows_at(self.offset(k, n) + index * size, size)] = part
                if copy is not None:
                    copy.start()
        elif step <= 2 * count + 1:
            if step == count + 1:
                size = rows[count]
                self.lands(k, count - 1, self.stages[k][count - 1][0] * size, size)[...] = self.added(k, count, 0, size)
            for copy in self.copies(step, k):
                copy.start()
        if count + 2 <= step <= 2 * count:
            n = 2 * count - step
            size = rows[n + 1]
            self.lands(k, n, self.stages[k][n][0] * size, size)[...] = self.lands(k, n + 1, 0, size)[...]
        if step == 2 * count + 1:
            self.own(k).start()
        if step == 2 * count + 2:
            self.own(k).wait()


def pair_lanes(p, start=0, size=128):
    if isinstance(p, int):
        return slice(p * 128 + start, p * 128 + start + size)
    return pl.ds(pl.multiple_of(p * 128 + start, size), size)


def lane_mask(par):
    lane = ramp((1, 128), 1)
    return jnp.where((lane >= 64) == bool(par), 1.0, 0.0).astype(BF16)


def flip_matrix():
    return jnp.where(ramp((HALF, HALF), 0) + ramp((HALF, HALF), 1) == HALF - 1, 1.0, 0.0).astype(BF16)


def flip(flip_low, value):
    return jnp.concatenate(
        [mm(flip_low, value[r : r + HALF]) for r in range(0, value.shape[0], HALF)], axis=0
    ).astype(value.dtype)


def pool_matrix(end, length, first_place, places):
    place = (ramp((end.shape[0], places), 1) + first_place).astype(F32)
    return jnp.where((place < end) & (place >= end - length), 1.0, 0.0).astype(BF16)


def query_block(n, seg):
    keys = seg + HALF * (n + 1)
    return slice(n * HALF, (n + 1) * HALF), keys, 2 * seg - keys


def attend(n, seg, r):
    seen = ramp((HALF, HALF), 1) <= ramp((HALF, HALF), 0)
    lane = ramp((HALF, 128), 1)
    rows, keys, skip = query_block(n, seg)

    def products(head):
        lanes, keep = pair_lanes(head // 2), lane_mask(head % 2)
        near = mm_nt(r.query_u[rows, lanes] * keep, r.key[0:keys, lanes])
        return near, mm_nt(r.query_v[rows, lanes] * keep, r.place[skip : 2 * seg, lanes])

    ahead = products(0)
    for p in range(4):
        mixed, scale = [], []
        for head in (2 * p, 2 * p + 1):
            near, far = ahead
            ahead = products(head + 1) if head < 7 else None
            scores = near + pltpu.roll(far, keys - (HALF - 1), 1, stride=1, stride_axis=0)
            scores = jnp.concatenate(
                [scores[:, : keys - HALF], jnp.where(seen, scores[:, keys - HALF :], -1e30)], axis=1
            )
            expo = jnp.exp(scores - jnp.max(scores, axis=1, keepdims=True))
            probs = expo.astype(BF16)
            r.probs[head, rows, 0:keys] = probs
            mixed.append(mm(probs, r.value[0:keys, pair_lanes(p)]))
            scale.append(1.0 / jnp.sum(expo, axis=1, keepdims=True))
        scale = jnp.where(lane >= 64, scale[1], scale[0])
        r.scale[rows, pair_lanes(p)] = scale
        r.mixed[rows, pair_lanes(p)] = (jnp.where(lane >= 64, mixed[1], mixed[0]) * scale).astype(BF16)


def attend_back_pair(p, seg, r, between):
    lanes = pair_lanes(p)
    flip_low = flip_matrix()
    scale = 0.125
    lane = ramp((HALF, 128), 1)
    sums = [None] * 6
    bias = []
    for n in range(seg // HALF):
        rows, keys, skip = query_block(n, seg)
        key, value, place = r.key[0:keys, lanes], r.value[0:keys, lanes], r.place[skip : 2 * seg, lanes]
        grad_u, grad_v = [], []
        for par in range(2):
            keep = lane_mask(par)
            feats = pair_lanes(p, par * 64, 64)
            probs = r.probs[2 * p + par, rows, 0:keys]
            turned = mm(flip_low, probs)
            grad_mixed = r.grad_mixed[rows, lanes] * keep
            delta = jnp.sum(grad_mixed.astype(F32) * r.mixed_flip[rows, lanes].astype(F32), axis=1, keepdims=True)
            grad_scores = turned * (mm_nt(grad_mixed, value) - delta)
            near = grad_scores.astype(BF16)
            far = pltpu.roll(grad_scores, 0, 1, stride=1, stride_axis=0).astype(BF16)
            grad_u.append(mm(near, key) * scale)
            grad_v.append(mm(far, place) * scale)
            now = (
                mm(r.query_u_t[feats, rows], near),
                mm(r.grad_mixed_t[feats, rows], probs),
                mm(r.query_v_t[feats, rows], far),
            )
            for m in range(3):
                slot = par * 3 + m
                if n == 0:
                    sums[slot] = now[m]
                else:
                    old, new = sums[slot], now[m]
                    cut = old.shape[1]
                    if m < 2:
                        sums[slot] = jnp.concatenate([new[:, :cut] + old, new[:, cut:]], axis=1)
                    else:
                        sums[slot] = jnp.concatenate([new[:, :-cut], new[:, -cut:] + old], axis=1)
            between(n * 2 + par)
        grad_u = jnp.where(lane >= 64, grad_u[1], grad_u[0])
        grad_v = jnp.where(lane >= 64, grad_v[1], grad_v[0])
        bias.append((jnp.sum(grad_u, axis=0, keepdims=True), jnp.sum(grad_v, axis=0, keepdims=True)))
        r.grad_query[rows, lanes] = mm(flip_low, (grad_u + grad_v).astype(BF16)).astype(BF16)
    r.small[0:1, lanes] = sum(b[0] for b in bias)
    r.small[1:2, lanes] = sum(b[1] for b in bias)
    for par in range(2):
        feats = pair_lanes(p, par * 64, 64)
        for m, out in enumerate((r.grad_key_t, r.grad_value_t, r.grad_place_t)):
            out[feats, :] = sums[par * 3 + m].astype(BF16)


def pair_weights(p, seg, r, base):
    lanes = pair_lanes(p)
    grad_query_t = r.grad_query[:, lanes].astype(F32).T.astype(BF16)
    r.total[rows_at(base, 128)] = mm(grad_query_t, r.normed[seg : 2 * seg]).astype(BF16)
    r.total[rows_at(base + 128, 128)] = mm(r.grad_key_t[lanes, :], r.normed[...]).astype(BF16)
    r.total[rows_at(base + 256, 128)] = mm(r.grad_value_t[lanes, :], r.normed[...]).astype(BF16)
    r.total[rows_at(base + 384, 128)] = mm(r.grad_place_t[lanes, :], r.table[...]).astype(BF16)


def project_places(r):
    r.place[...] = mm(r.table[...], r.w_rel[...]).astype(BF16)


def project_memory(rows, r):
    unit, unused = normalize(r.memory[rows].astype(F32))
    low = (unit * r.vec("gain_one") + r.vec("shift_one")).astype(BF16)
    r.normed[rows] = low
    r.key[rows] = mm(low, r.w_key[...]).astype(BF16)
    r.value[rows] = mm(low, r.w_value[...]).astype(BF16)


def project_segments(n, seg, r):
    rows, keys, unused = query_block(n, seg)
    places = slice(keys - HALF, keys)
    unit, unused = normalize(r.pooled[rows])
    low = (unit * r.vec("gain_one") + r.vec("shift_one")).astype(BF16)
    r.normed[places] = low
    query = mm(low, r.w_query[...])
    scale = 0.125
    r.query_u[rows] = (query + r.vec("bias_u")).astype(BF16) * jnp.asarray(scale, BF16)
    r.query_v[rows] = (query + r.vec("bias_v")).astype(BF16) * jnp.asarray(scale, BF16)
    r.key[places] = mm(low, r.w_key[...]).astype(BF16)
    r.value[places] = mm(low, r.w_value[...]).astype(BF16)


def feed_forward_in(n, r):
    rows = slice(n * HALF, (n + 1) * HALF)
    residual = r.pooled[rows] + mm(r.mixed[rows], r.w_out[...])
    r.residual[rows] = residual
    unit, unused = normalize(residual)
    r.normed_two[rows] = (unit * r.vec("gain_two") + r.vec("shift_two")).astype(BF16)

    for m in range(r.w_up.shape[1] // 512):
        cols = slice(m * 512, (m + 1) * 512)
        inner = mm(r.normed_two[rows], r.w_up[:, cols]) + r.bias_up[0:1, cols]
        gate, slope = gelu_parts(inner)
        r.hidden[rows, cols] = (inner * gate).astype(BF16)
        r.slope[rows, cols] = slope.astype(BF16)


def feed_forward_out(n, r):
    rows = slice(n * HALF, (n + 1) * HALF)
    branch = mm(r.hidden[rows], r.w_down[...]) + r.vec("bias_down")
    r.out_rows[rows] = (r.residual[rows] + branch).astype(BF16)


def feed_forward_back(n, r):
    cols = slice(n * 512, (n + 1) * 512)
    r.total[rows_at(BASES[n], 512)] = mm(r.grad_down_t[...], r.hidden[:, cols]).astype(BF16)
    grad_hidden = mm_nt(r.grad_down[...], r.w_down[cols, :])
    low = (grad_hidden * r.slope[:, cols].astype(F32)).astype(BF16)
    r.grad_inner[:, cols] = low
    r.small[7 + n : 8 + n, :] = jnp.sum(low.astype(F32), axis=0, keepdims=True)
    r.total[rows_at(BASES[n] + 512, 512)] = mm(r.normed_two_t[...], low).astype(BF16)


def middle_back(r, base):
    grad_normed = mm_nt(r.grad_inner[...], r.w_up[...])
    unit, inv = normalize(r.residual[...])
    r.small[4:5, :] = jnp.sum(grad_normed * unit, axis=0, keepdims=True)
    r.small[5:6, :] = jnp.sum(grad_normed, axis=0, keepdims=True)
    grad = r.grad_output[...] + norm_back(grad_normed, unit, inv, r.vec("gain_two"))
    r.grad_residual[...] = grad
    low = grad.astype(BF16)
    mixed = r.mixed[...]
    r.total[rows_at(base, 512)] = mm(mixed.astype(F32).T.astype(BF16), low).astype(BF16)
    grad_mixed = (mm_nt(low, r.w_out[...]) * r.scale[...]).astype(BF16)
    r.grad_mixed_t[...] = grad_mixed.astype(F32).T.astype(BF16)
    flip_low = flip_matrix()
    r.grad_mixed[...] = flip(flip_low, grad_mixed)
    r.mixed_flip[...] = flip(flip_low, mixed)
    r.query_u_t[...] = flip(flip_low, r.query_u[...]).astype(F32).T.astype(BF16)
    r.query_v_t[...] = flip(flip_low, r.query_v[...]).astype(F32).T.astype(BF16)


def first_back(seg, r):
    grad_key = r.grad_key_t[...].astype(F32).T.astype(BF16)
    grad_value = r.grad_value_t[...].astype(F32).T.astype(BF16)
    grad_normed = mm_nt(r.grad_query[...], r.w_query[...])
    grad_normed += mm_nt(grad_key[seg:], r.w_key[...])
    grad_normed += mm_nt(grad_value[seg:], r.w_value[...])
    grad_mem = mm_nt(grad_key[:seg], r.w_key[...]) + mm_nt(grad_value[:seg], r.w_value[...])
    unit, inv = normalize(r.pooled[...])
    unit_mem, unused = normalize(r.memory[...].astype(F32))
    r.small[2:3, :] = jnp.sum(grad_normed * unit + grad_mem * unit_mem, axis=0, keepdims=True)
    r.small[3:4, :] = jnp.sum(grad_normed + grad_mem, axis=0, keepdims=True)
    return r.grad_residual[...] + norm_back(grad_normed, unit, inv, r.vec("gain_one"))


QUIET = 384
MOST = 16
BACK_PARTS = 6
BACK_EARLY = BACK_PARTS * HALF // QUIET
KEPT_DURING = (18, 9, 14)


def sine_table(count, width):
    freqs = np.exp(np.arange(width // 2) * (-2.0 * math.log(10000.0) / width))
    angles = np.arange(count)[::-1, None] * freqs[None, :]
    return np.concatenate([np.sin(angles), np.cos(angles)], axis=1).astype(jnp.bfloat16)


def span_columns(lengths, low):
    seg = lengths.shape[1]
    lens = lengths.astype(F32).astype(BF16)
    row, col = ramp((seg - low, seg), 0) + low, ramp((seg - low, seg), 1)
    upto = jnp.where(col <= row, 1.0, 0.0).astype(BF16)
    same = jnp.where(col == row, 1.0, 0.0).astype(BF16)
    return mm_nt(upto, lens), mm_nt(same, lens)


def column(value, n):
    return jnp.sum(jnp.where(ramp(value.shape, 1) == n, value, 0.0), axis=1, keepdims=True)


WEIGHTS = ("w_query", "w_key", "w_value", "w_rel", "w_out", "w_up", "w_down")


def layer_scratch(seg, width, hidden, shapes):
    def low(*shape):
        return pltpu.VMEM(shape, BF16)

    def full(*shape):
        return pltpu.VMEM(shape, F32)

    return dict(
        table=low(2 * seg, width),
        w_query=low(width, width),
        w_key=low(width, width),
        w_value=low(width, width),
        w_rel=low(width, width),
        w_out=low(width, width),
        w_up=low(width, hidden),
        w_down=low(hidden, width),
        memory=low(seg, width),
        pooled=full(seg, width),
        normed=low(2 * seg, width),
        key=low(2 * seg, width),
        value=low(2 * seg, width),
        place=low(2 * seg, width),
        query_u=low(seg, width),
        query_v=low(seg, width),
        mixed=low(seg, width),
        probs=low(8, seg, 2 * seg),
        scale=full(seg, width),
        residual=full(seg, width),
        normed_two=low(seg, width),
        normed_two_t=low(width, seg),
        hidden=low(seg, hidden),
        slope=low(seg, hidden),
        grad_inner=low(seg, hidden),
        grad_output=full(seg, width),
        grad_down=low(seg, width),
        grad_down_t=low(width, seg),
        low_rows=low(seg, width),
        out_rows=low(seg, width),
        chars_quiet=low(QUIET, width),
        chars_parts=low(7, seg - QUIET, width),
        grads_quiet=low(QUIET, width),
        grads_parts=low(7, seg - QUIET, width),
        total=low(BASES[-1], width),
        land=low(LANDS[1], width),
        bias_up=full(1, hidden),
        vectors=full(16, width),
        lengths=pltpu.VMEM((4, seg), jnp.int32),
        **{f"raw_{name}": low(*shape) for name, shape in shapes.items()},
        small=full(16, width),
        small_sum=full(5, 16, width),
        small_land=full(5, 16, width),
        local_sem=pltpu.SemaphoreType.DMA((max(8 + len(WEIGHTS) + 1 + len(VECTORS) + 1, SENDS[1]),)),
        memory_send=pltpu.SemaphoreType.DMA((4,)),
        memory_recv=pltpu.SemaphoreType.DMA((4,)),
        quiet_send=pltpu.SemaphoreType.DMA((2, 4, 2)),
        quiet_recv=pltpu.SemaphoreType.DMA((2, 2)),
        parts_send=pltpu.SemaphoreType.DMA((2, 3)),
        parts_recv=pltpu.SemaphoreType.DMA((2, 3)),
        kept_send=pltpu.SemaphoreType.DMA((6,)),
        kept_recv=pltpu.SemaphoreType.DMA((4,)),
        back_send=pltpu.SemaphoreType.DMA((2, 5)),
        back_recv=pltpu.SemaphoreType.DMA((2, 2, 4)),
        sum_recv=pltpu.SemaphoreType.DMA((RECVS[1],)),
        small_send=pltpu.SemaphoreType.DMA((5,)),
        small_recv=pltpu.SemaphoreType.DMA((5,)),
        small_sem=pltpu.SemaphoreType.DMA,
        store_sem=pltpu.SemaphoreType.DMA((len(PIECES),)),
    )


def chip_spans(places, loud):
    half = 2 * places
    most = -(-(loud - half // MOST) // 16) * 16
    least = (half - QUIET) // MOST // 16 * 16
    return (0, most), (least, loud - least)


class Rows:
    def __init__(self, r, place, way, source, stage, quiet, parts):
        self.r, self.p, self.way = r, place, way
        self.source, self.stage, self.quiet, self.parts = source, stage, quiet, parts
        self.spans = [pl.ds(*span) for span in chip_spans(source.shape[1], parts.shape[1])]

    def load(self, n):
        cols = pl.ds(pl.multiple_of(n * 512, 512), 512)
        return pltpu.make_async_copy(self.source.at[n], self.stage.at[:, cols], self.r.local_sem.at[self.way * 4 + n])

    def quiet_copy(self, to, part):
        r = self.r
        span = pl.ds(0, HALF) if part == 0 else pl.ds(HALF, QUIET - HALF)
        src, dst = self.source.at[to, span], self.quiet.at[span]
        if to == 0:
            return pltpu.make_async_copy(src, dst, r.quiet_send.at[self.way, 0, part])
        return remote(src, dst, r.quiet_send.at[self.way, to, part], r.quiet_recv.at[self.way, part], (self.p.s, to))

    def start_quiet(self):
        @pl.when(self.p.b == 0)
        def _():
            for part in range(2):
                for to in (2, 3, 1, 0):
                    self.quiet_copy(to, part).start()

    def wait_quiet(self, part):
        @pl.when(self.p.b == 0)
        def _():
            self.quiet_copy(0, part).wait()

        @pl.when(self.p.b != 0)
        def _():
            self.quiet_copy(1, part).wait_recv()

    def on_chip(self, act):
        for chip in range(2):
            pl.when(self.p.x == chip)(functools.partial(act, chip))

    def parts_copy(self, n, chip=None):
        src, dst, to = ((3, 1, self.p.core()), (4, 5, self.p.core()), (6, 2, self.p.across()))[n]
        span = pl.ds(0, self.parts.shape[1]) if chip is None else self.spans[chip]
        return remote(
            self.parts.at[src, span],
            self.parts.at[dst, span],
            self.r.parts_send.at[self.way, n],
            self.r.parts_recv.at[self.way, n],
            to,
        )

    def clear(self):
        self.parts[2] = jnp.zeros(self.parts.shape[1:], BF16)

    def part(self, to, ends, lens):
        self.load(to).wait()
        cols = pl.ds(pl.multiple_of(to * 512, 512), 512)
        chosen = pool_matrix(column(ends, to), column(lens, to), self.p.b * 512, 512)
        return mm(chosen, self.stage[:, cols])

    def start_parts(self, ends, lens):
        b, sibling, away = self.p.b, self.p.core()[1], self.p.across()[1]
        self.parts[4] = self.part(away + sibling - b, ends, lens).astype(BF16)
        self.parts_copy(1).start()
        self.parts[3] = self.part(sibling, ends, lens).astype(BF16)
        self.parts_copy(0).start()
        self.parts[6] = self.part(away, ends, lens).astype(BF16)
        self.parts[0] = self.part(b, ends, lens).astype(BF16)

    def join_parts(self):
        self.parts_copy(1).wait_recv()
        self.parts[6] = (self.parts[6].astype(F32) + self.parts[5].astype(F32)).astype(BF16)
        self.on_chip(lambda chip: self.parts_copy(2, chip).start())

    def wait_parts(self):
        self.parts_copy(0).wait_recv()
        self.on_chip(lambda chip: self.parts_copy(2, 1 - chip).wait_recv())
        return sum(self.parts[n].astype(F32) for n in range(3))

    def wait_sent(self):
        for n in range(2):
            self.parts_copy(n).wait_send()
        self.on_chip(lambda chip: self.parts_copy(2, chip).wait_send())

        @pl.when(self.p.b == 0)
        def _():
            for part in range(2):
                for to in (1, 2, 3):
                    self.quiet_copy(to, part).wait_send()

    def back(self, rows, quiet_out, loud_out):
        self.rows, self.quiet_out, self.loud_out = rows, quiet_out, loud_out
        return self

    def loud_rows(self, chip):
        start, size = chip_spans(self.source.shape[1], self.parts.shape[1])[chip]
        return self.rows.at[pl.ds(QUIET + start, size)]

    def quiet_rows(self):
        return self.rows.at[pl.ds(0, QUIET)]

    def loud_copy(self, n, slot, chip):
        r, p, way = self.r, self.p, self.way
        dst = self.loud_out.at[slot, self.spans[chip]]
        to = p.across() if n == 1 else p.core()
        return remote(
            dst if n == 2 else self.loud_rows(chip), dst, r.back_send.at[way, n], r.back_recv.at[way, 0, slot], to
        )

    def quiet_back(self, slot, start=0, size=QUIET):
        r, way = self.r, self.way
        span = pl.ds(start, size)
        return remote(
            self.rows.at[span],
            self.quiet_out.at[slot, span],
            r.back_send.at[way, 3],
            r.back_recv.at[way, 1, slot],
            (self.p.s, 0),
        )

    def own_quiet(self):
        return pltpu.make_async_copy(self.quiet_rows(), self.quiet_out.at[0], self.r.back_send.at[self.way, 3])

    def own_loud(self, chip):
        dst = self.loud_out.at[self.p.b, self.spans[chip]]
        return pltpu.make_async_copy(self.loud_rows(chip), dst, self.r.back_send.at[self.way, 4])

    def start_back(self):
        def start(chip):
            self.loud_copy(1, self.p.b, 1 - chip).start()
            self.loud_copy(0, self.p.b, chip).start()
            self.own_loud(chip).start()

        self.on_chip(start)
        pl.when(self.p.b == 0)(self.own_quiet().start)

    def start_quiet_back(self, n):
        size = QUIET // BACK_PARTS
        pl.when(self.p.b != 0)(self.quiet_back(self.p.b, n * size, size).start)

    def pass_on(self):
        away = self.p.across()[1]

        def pass_on(chip):
            self.loud_copy(1, away, chip).wait_recv()
            self.loud_copy(2, away, chip).start()

        self.on_chip(pass_on)

    def wait_back(self):
        p = self.p
        sibling, away = p.core()[1], p.across()[1]

        def wait(chip):
            self.loud_copy(0, p.b, chip).wait_send()
            self.loud_copy(1, p.b, 1 - chip).wait_send()
            self.loud_copy(2, away, chip).wait_send()
            self.own_loud(chip).wait()
            self.loud_copy(0, sibling, chip).wait_recv()
            self.loud_copy(2, away + sibling - p.b, chip).wait_recv()

        self.on_chip(wait)
        pl.when(p.b != 0)(self.quiet_back(p.b).wait_send)

        @pl.when(p.b == 0)
        def _():
            self.own_quiet().wait()
            for n in (1, 2, 3):
                self.quiet_back(n).wait_recv()


class Kept:
    def __init__(self, r, place, chars, kept):
        self.r, self.p, self.chars, self.kept = r, place, chars, kept
        self.count = kept.shape[1]

    def rows(self, to):
        return self.r.low_rows.at[pl.ds(to * self.count, self.count)]

    def late(self, to, slot):
        r = self.r
        return remote(self.rows(to), self.kept.at[slot], r.kept_send.at[4 + to - 2], r.kept_recv.at[slot], (self.p.s, to))

    def late_own(self, to):
        return pltpu.make_async_copy(self.rows(to), self.kept.at[to], self.r.kept_send.at[4 + to - 2])

    def early(self, slot):
        r = self.r
        src = self.chars.at[slot, pl.ds(self.count, self.count)]
        return remote(src, self.kept.at[slot], r.kept_send.at[slot], r.kept_recv.at[slot], (self.p.s, 1))

    def early_own(self, slot):
        src = self.chars.at[slot, pl.ds(0, self.count)]
        return pltpu.make_async_copy(src, self.kept.at[slot], self.r.kept_recv.at[slot])

    def start_late(self, to):
        pl.when(self.p.b != to)(self.late(to, self.p.b).start)
        pl.when(self.p.b == to)(self.late_own(to).start)

    def start_early(self):
        @pl.when(self.p.b == 0)
        def _():
            for slot in range(4):
                self.early_own(slot).start()
                self.early(slot).start()

    def wait(self):
        b = self.p.b

        @pl.when(b == 0)
        def _():
            for slot in range(4):
                self.early_own(slot).wait()
                self.early(slot).wait_send()

        @pl.when(b == 1)
        def _():
            for slot in range(4):
                self.early(slot).wait_recv()

        for to in (2, 3):
            pl.when(b != to)(self.late(to, b).wait_send)

            @pl.when(b == to)
            def _():
                self.late_own(to).wait()
                for slot in range(4):
                    if slot != to:
                        self.late(to, slot).wait_recv()


class Small:
    def __init__(self, r, place):
        self.r, self.p = r, place

    def source(self, step):
        return self.r.small if step == 0 else self.r.small_sum.at[step - 1]

    def copy(self, step):
        r, p = self.r, self.p
        to = p.core() if step == 0 else p.pair(AXES[step - 1])
        return remote(self.source(step), r.small_land.at[step], r.small_send.at[step], r.small_recv.at[step], to)

    def start(self, step):
        self.copy(step).start()

    def finish(self, step):
        self.copy(step).wait()
        self.r.small_sum[step] = self.source(step)[...] + self.r.small_land[step]


def layer_kernel(names, chars, lengths, memory, grad_out, *rest):
    count = len(VECTORS) + 1 + len(WEIGHTS)
    vectors, table, weights = rest[: len(VECTORS)], rest[len(VECTORS)], rest[len(VECTORS) + 1 : count]
    kept, out_quiet, out_loud, grad_quiet, grad_loud, total_out, small_out = rest[count : count + 7]
    r = types.SimpleNamespace(**dict(zip(names, rest[count + 7 :])))
    p = Place()
    seg, width = r.pooled.shape
    r.grad_residual, r.grad_mixed, r.grad_rows = r.grad_output, r.grad_down, r.normed_two
    for n, name in enumerate(("mixed_flip", "query_u_t", "query_v_t", "grad_mixed_t")):
        setattr(r, name, r.slope.at[:, n * width : (n + 1) * width])
    r.grad_key_t, r.grad_value_t = r.hidden.at[:, : 2 * seg], r.hidden.at[:, 2 * seg :]
    r.grad_place_t, r.grad_query = r.grad_inner.at[:, : 2 * seg], r.grad_inner.at[:, 2 * seg : 3 * seg]
    loads = [
        pltpu.make_async_copy(src, dst, r.local_sem.at[8 + n])
        for n, (src, dst) in enumerate(
            zip((*weights, table), [getattr(r, name) for name in WEIGHTS] + [r.table])
        )
    ]
    chars_rows = Rows(r, p, 0, chars, r.hidden, r.chars_quiet, r.chars_parts).back(r.out_rows, out_quiet, out_loud)
    grads_rows = Rows(r, p, 1, grad_out, r.grad_inner, r.grads_quiet, r.grads_parts).back(
        r.grad_rows, grad_quiet, grad_loud
    )
    raw = [getattr(r, f"raw_{name}") for name in VECTORS]
    small_loads = [
        pltpu.make_async_copy(src, dst, r.local_sem.at[8 + len(WEIGHTS) + 1 + n])
        for n, (src, dst) in enumerate(zip((*vectors, lengths), (*raw, r.lengths)))
    ]
    small_loads[-1].start()
    for n in range(4):
        chars_rows.load(n).start()
    for copy in small_loads[:-1]:
        copy.start()
    for n in range(4):
        grads_rows.load(n).start()
    for copy in loads:
        copy.start()
    r.vec = lambda name: r.vectors[VECTORS.index(name) : VECTORS.index(name) + 1, :]

    chars_rows.clear()
    grads_rows.clear()
    barrier = pltpu.get_barrier_semaphore()
    others = [p.group(1), p.group(2), p.group(3), *(to for to, unused, other in p.peers("xy")[1][1:]), p.line(1), p.line(2), p.line(3)]
    for other in others:
        pl.semaphore_signal(barrier, inc=1, device_id=other, device_id_type=MESH)
    pl.semaphore_wait(barrier, len(others))

    rows = memory.shape[1]

    def memory_copy(k, slot):
        to = (p.b + k) % 4
        return remote(
            memory.at[to], r.memory.at[rows_at(slot * rows, rows)], r.memory_send.at[k], r.memory_recv.at[slot], p.group(k)
        )

    own_memory = pltpu.make_async_copy(memory.at[p.b], r.memory.at[rows_at(p.b * rows, rows)], r.memory_send.at[0])
    for k in (2, 3, 1):
        memory_copy(k, p.b).start()
    own_memory.start()
    chars_rows.start_quiet()
    small_loads[-1].wait()
    ends, lens = span_columns(r.lengths[...], QUIET)
    chars_rows.start_parts(ends, lens)
    for copy in loads:
        copy.wait()
    for copy in small_loads[:-1]:
        copy.wait()
    for n, name in enumerate(VECTORS):
        value = raw[n][...].astype(F32)
        if name == "bias_up":
            r.bias_up[...] = value.reshape(1, -1)
        elif value.ndim == 2:
            r.vectors[n : n + 1, :] = jnp.concatenate([value[h : h + 1, :] for h in range(value.shape[0])], axis=1)
        else:
            r.vectors[n : n + 1, :] = value.reshape(1, -1)
    project_places(r)
    waits = (1 - p.x) * p.c
    pl.when(waits == 0)(chars_rows.join_parts)
    grads_rows.start_quiet()
    grads_rows.start_parts(ends, lens)
    own_memory.wait()
    memory_copy(1, p.core()[1]).wait_recv()
    project_memory(rows_at(p.x * 2 * rows, 2 * rows), r)
    for slot in (2 * (1 - p.x), 2 * (1 - p.x) + 1):
        memory_copy(1, slot).wait_recv()
    project_memory(rows_at((1 - p.x) * 2 * rows, 2 * rows), r)
    own_lens = column(lens, p.b)

    def forward(block):
        project_segments(block, seg, r)
        attend(block, seg, r)
        if block == 0:
            pl.when(waits == 1)(chars_rows.join_parts)
        feed_forward_in(block, r)

    chars_rows.wait_quiet(0)
    r.pooled[0:HALF] = chars_rows.quiet[0:HALF].astype(F32)
    forward(0)
    grads_rows.join_parts()
    feed_forward_out(0, r)
    for part in range(BACK_EARLY):
        chars_rows.start_quiet_back(part)
    chars_rows.wait_quiet(1)
    r.pooled[HALF:QUIET] = chars_rows.quiet[HALF:QUIET].astype(F32)
    r.pooled[QUIET:seg] = chars_rows.wait_parts() / own_lens
    r.low_rows[...] = r.pooled[...].astype(BF16)

    forward(1)
    grads_rows.wait_quiet(0)
    grads_rows.wait_quiet(1)
    r.grad_output[0:QUIET] = grads_rows.quiet[...].astype(F32)
    r.grad_output[QUIET:seg] = grads_rows.wait_parts()
    low = r.grad_output[...].astype(BF16)
    r.grad_down[...] = low
    r.grad_down_t[...] = low.astype(F32).T.astype(BF16)
    r.normed_two_t[...] = r.normed_two[...].astype(F32).T.astype(BF16)
    r.small[...] = jnp.zeros(r.small.shape, F32)
    r.small[6:7, :] = jnp.sum(low.astype(F32), axis=0, keepdims=True)

    sums = Sum(p, r.total, r.land, total_out, r.local_sem, r.sum_recv, r.store_sem)

    rows_kept = Kept(r, p, chars, kept)

    def take(n):
        if n == KEPT_DURING[0]:
            rows_kept.start_early()
        for to in (2, 3):
            if n == KEPT_DURING[to - 1]:
                rows_kept.start_late(to)
        for part, at in enumerate(BACK_DURING):
            if at == n:
                chars_rows.start_quiet_back(BACK_EARLY + part)
        for k, step in DURING[n]:
            sums.step(k, step)

    def between(pair, unit):
        for n in range(4):
            at = n * 5 + 6 + unit
            if DURING[at] or at in BACK_DURING or at in KEPT_DURING:
                pl.when(pair == n)(functools.partial(take, at))

    for n in range(4):
        feed_forward_back(n, r)
        take(n)
    feed_forward_out(1, r)
    chars_rows.start_back()
    take(4)
    middle_back(r, BASES[4])
    take(5)

    def back(n, carry):
        attend_back_pair(n, seg, r, functools.partial(between, n))
        pair_weights(n, seg, r, BASES[5] + n * PIECES[5][0])
        between(n, 4)
        return carry

    lax.fori_loop(0, 4, back, 0)
    grad_pooled = first_back(seg, r)
    r.grad_rows[0:QUIET] = grad_pooled[:QUIET].astype(BF16)
    r.grad_rows[QUIET:seg] = (grad_pooled[QUIET:] / own_lens).astype(BF16)
    grads_rows.start_back()
    small = Small(r, p)
    small_store = pltpu.make_async_copy(r.small_sum.at[4], small_out, r.small_sem)
    small.start(0)
    take(26)
    every = len(AFTER) // 12
    for n, (k, step) in enumerate(AFTER):
        for part, at in enumerate(BACK_AFTER):
            if at == n:
                grads_rows.start_quiet_back(part)
        if n % every == every - 1 and n // every < 10:
            at = n // every
            if at % 2 == 1:
                small.finish(at // 2)
                if at // 2 < 4:
                    small.start(at // 2 + 1)
                else:
                    small_store.start()
            if at == 4:
                chars_rows.pass_on()
            if at == 8:
                grads_rows.pass_on()
        sums.step(k, step)
    for k in (1, 2, 3):
        memory_copy(k, p.b).wait_send()
    rows_kept.wait()
    chars_rows.wait_sent()
    grads_rows.wait_sent()
    chars_rows.wait_back()
    grads_rows.wait_back()
    small_store.wait()


def spread_kernel(
    lengths, chars, grad_out, rows, out_quiet, out_loud, grad_quiet, grad_loud, wide, flat, pairs, small,
    out_chars, grad_chars, kept, w_query, w_key, w_value, w_rel, w_out, w_up, w_down, bias_u, bias_v, *vectors,
):
    n = pl.program_id(0)
    b = lax.axis_index("blk")
    places = chars.shape[1]
    seg = lengths.shape[1]
    lens = lengths[...].astype(F32).astype(BF16)
    row, col = ramp((seg - QUIET, seg), 0) + QUIET, ramp((seg - QUIET, seg), 1)
    upto = jnp.where(col <= row, 1.0, 0.0).astype(BF16)
    same = jnp.where(col == row, 1.0, 0.0).astype(BF16)
    pick = ramp((lengths.shape[0], seg - QUIET), 0) == n
    end = jnp.sum(jnp.where(pick, mm_nt(lens, upto), 0.0), axis=0, keepdims=True)
    length = jnp.sum(jnp.where(pick, mm_nt(lens, same), 0.0), axis=0, keepdims=True)
    place = (ramp((places, seg - QUIET), 0) + b * places).astype(F32)
    chosen = jnp.where((place < end) & (place >= end - length), 1.0, 0.0).astype(BF16)
    first = b == 0
    spans = chip_spans(places, seg - QUIET)
    here = ramp((seg - QUIET, 1), 0)
    inside = [(here >= start) & (here < start + size) for start, size in spans]
    there = jnp.where(b < 2, inside[0].astype(F32), inside[1].astype(F32)) > 0
    kept[...] = rows[...]
    for source, quiet, loud, out in (
        (chars, out_quiet, out_loud, out_chars),
        (grad_out, grad_quiet, grad_loud, grad_chars),
    ):
        spread = mm(chosen, jnp.where(there, loud[0].astype(F32), 0.0).astype(BF16))
        whole = source[0].astype(F32) + spread
        out[0, QUIET:places] = whole[QUIET:].astype(out.dtype)
        out[0, 0:QUIET] = (whole[:QUIET] + jnp.where(first, quiet[0].astype(F32), 0.0)).astype(out.dtype)
    w_down[...] = wide[0:512].astype(F32).T
    w_up[...] = wide[512:1024].astype(F32)
    w_out[...] = flat[...].astype(F32)
    for m, out in enumerate((w_query, w_key, w_value, w_rel)):
        out[...] = pairs[m * 128 : (m + 1) * 128].astype(F32).T
    for m, out in enumerate((bias_u, bias_v)):
        out[...] = jnp.concatenate([small[m : m + 1, h * 64 : (h + 1) * 64] for h in range(8)], axis=0)
    for m, out in enumerate(vectors[:4]):
        out[...] = small[2 + m : 3 + m, :]
    vectors[4][...] = jnp.concatenate([small[m : m + 1, :] for m in range(7, 11)], axis=1)
    vectors[5][...] = small[6:7, :]


def shards_whole(
    chars, seg_lengths, memory, grad_out, w_query, w_key, w_value, w_rel, w_out, w_up, w_down,
    bias_u, bias_v, gain_one, shift_one, gain_two, shift_two, bias_up, bias_down,
):
    count, places, width = chars.shape
    seg, hidden = seg_lengths.shape[1], w_up.shape[1]
    rows = memory.shape[1]
    table = jnp.asarray(sine_table(2 * seg, width))
    vectors = (bias_u, bias_v, gain_one, shift_one, gain_two, shift_two, bias_up, bias_down)
    scratch = layer_scratch(seg, width, hidden, {name: v.shape for name, v in zip(VECTORS, vectors)})
    anywhere, near = pl.BlockSpec(memory_space=pl.ANY), pl.BlockSpec(memory_space=pltpu.VMEM)
    loud = seg - QUIET
    kept, out_quiet, out_loud, grad_quiet, grad_loud, total, small = pl.pallas_call(
        functools.partial(layer_kernel, tuple(scratch)),
        out_shape=[
            jax.ShapeDtypeStruct((count, rows, width), BF16),
            jax.ShapeDtypeStruct((count, QUIET, width), BF16),
            jax.ShapeDtypeStruct((count, loud, width), BF16),
            jax.ShapeDtypeStruct((count, QUIET, width), BF16),
            jax.ShapeDtypeStruct((count, loud, width), BF16),
            jax.ShapeDtypeStruct((BASES[-1], width), BF16),
            jax.ShapeDtypeStruct((16, width), F32),
        ],
        in_specs=[anywhere] * (12 + len(VECTORS)),
        out_specs=[anywhere] * 7,
        scratch_shapes=list(scratch.values()),
        compiler_params=pltpu.CompilerParams(
            collective_id=0, has_side_effects=True, vmem_limit_bytes=VMEM_BYTES
        ),
        name="layer",
    )(
        chars, seg_lengths, memory, grad_out,
        *vectors, table,
        w_query, w_key, w_value, w_rel, w_out, w_up, w_down,
    )

    def block(shape, index):
        return pl.BlockSpec(shape, index)

    def each(*shape):
        return block((1, *shape), lambda n: (n, 0, 0))

    def whole(*shape):
        return block(shape, lambda n: (0, 0))

    vector = [(1, width)] * 4 + [(1, hidden), (1, width)]
    outs = pl.pallas_call(
        spread_kernel,
        grid=(count,),
        out_shape=[
            jax.ShapeDtypeStruct(chars.shape, BF16),
            jax.ShapeDtypeStruct(chars.shape, F32),
            jax.ShapeDtypeStruct(memory.shape, BF16),
            *[jax.ShapeDtypeStruct((width, width), F32)] * 5,
            jax.ShapeDtypeStruct((width, hidden), F32),
            jax.ShapeDtypeStruct((hidden, width), F32),
            *[jax.ShapeDtypeStruct(bias_u.shape, F32)] * 2,
            *[jax.ShapeDtypeStruct(shape, F32) for shape in vector],
        ],
        in_specs=[
            whole(*seg_lengths.shape),
            each(places, width),
            each(places, width),
            each(rows, width),
            each(QUIET, width),
            each(loud, width),
            each(QUIET, width),
            each(loud, width),
            block((1024, width), lambda n: (n, 0)),
            block((128, width), lambda n: (BASES[4] // 128 + n, 0)),
            block((512, width), lambda n: (BASES[5] // 512 + n, 0)),
            whole(16, width),
        ],
        out_specs=[
            each(places, width),
            each(places, width),
            each(rows, width),
            *[block((width, 128), lambda n: (0, n))] * 4,
            block((128, width), lambda n: (n, 0)),
            block((width, 512), lambda n: (0, n)),
            block((512, width), lambda n: (n, 0)),
            *[whole(*bias_u.shape)] * 2,
            *[whole(*shape) for shape in vector],
        ],
        compiler_params=pltpu.CompilerParams(vmem_limit_bytes=VMEM_BYTES),
        name="spread",
    )(seg_lengths, chars, grad_out, kept, out_quiet, out_loud, grad_quiet, grad_loud, total, total, total, small)
    return (*outs[:12], *[v.reshape(-1) for v in outs[12:]])


VMEM_BYTES = 64 * 2**20 - 2**16


def fits_whole(mesh):
    return dict(mesh.shape) == {"seq": 8, "blk": 4}


def layer_norm(value, gain, shift):
    center = value - jnp.mean(value, axis=-1, keepdims=True)
    spread = jnp.mean(center * center, axis=-1, keepdims=True)
    return center * lax.rsqrt(spread + 1e-05) * gain + shift


def angle_tables(places, feature_width):
    freqs = jnp.exp(
        jnp.arange(feature_width // 2, dtype=jnp.float32)
        * (-2.0 * math.log(10000.0) / feature_width)
    )
    angles = places[:, None] * freqs[None, :]
    return (jnp.sin(angles), jnp.cos(angles))


def smooth_gate(value):
    return jax.nn.gelu(value, approximate=False)


def segment_ids(seg_end, char_places):
    return jnp.sum((seg_end[:, None, :] <= char_places[None, :, None]).astype(jnp.int32), axis=2)


def shards(
    chars,
    seg_lengths,
    memory,
    grad_out,
    w_query,
    w_key,
    w_value,
    w_rel,
    w_out,
    w_up,
    w_down,
    bias_u,
    bias_v,
    gain_one,
    shift_one,
    gain_two,
    shift_two,
    bias_up,
    bias_down,
):
    blk_index = lax.axis_index("blk")
    seq_local, char_rows, feature_width = chars.shape
    seg_rows = memory.shape[1]
    seg_count = seg_lengths.shape[1]
    head_count, head_dim = bias_u.shape
    half_width = feature_width // 2
    score_scale = head_dim ** (-0.5)
    seg_start = blk_index * seg_rows
    gain_one_f = gain_one.astype(jnp.float32)
    shift_one_f = shift_one.astype(jnp.float32)
    gain_two_f = gain_two.astype(jnp.float32)
    shift_two_f = shift_two.astype(jnp.float32)
    seg_end = jnp.cumsum(seg_lengths, axis=1)
    char_places = blk_index * char_rows + jnp.arange(char_rows, dtype=jnp.int32)
    segment = segment_ids(seg_end, char_places)
    own_lengths = lax.dynamic_slice_in_dim(seg_lengths, seg_start, seg_rows, 1).astype(jnp.float32)
    chars_f = chars.astype(jnp.float32)
    grad_f = grad_out.astype(jnp.float32)

    def full_table(values, ids):
        return jax.ops.segment_sum(values, ids, num_segments=seg_count)

    part_sums = jax.vmap(full_table)(chars_f, segment)
    pooled_sum = lax.psum_scatter(part_sums, "blk", scatter_dimension=1, tiled=True)
    pooled = pooled_sum / own_lengths[:, :, None]
    normed = layer_norm(pooled, gain_one_f, shift_one_f)
    normed_low = normed.astype(jnp.bfloat16)
    memory_f = memory.astype(jnp.float32)
    mem_low = layer_norm(memory_f, gain_one_f, shift_one_f).astype(jnp.bfloat16)
    query_rows = jnp.einsum("sid,de->sie", normed_low, w_query, preferred_element_type=jnp.float32)
    key_local = jnp.stack(
        [
            jnp.einsum("sid,de->sie", mem_low, w_key, preferred_element_type=jnp.float32),
            jnp.einsum("sid,de->sie", normed_low, w_key, preferred_element_type=jnp.float32),
        ],
        axis=1,
    ).astype(jnp.bfloat16)
    value_local = jnp.stack(
        [
            jnp.einsum("sid,de->sie", mem_low, w_value, preferred_element_type=jnp.float32),
            jnp.einsum("sid,de->sie", normed_low, w_value, preferred_element_type=jnp.float32),
        ],
        axis=1,
    ).astype(jnp.bfloat16)
    key_all, value_all = (
        lax.all_gather(key_local, "blk", axis=2, tiled=True),
        lax.all_gather(value_local, "blk", axis=2, tiled=True),
    )
    key_heads = key_all.reshape(seq_local, 2 * seg_count, head_count, head_dim)
    value_heads = value_all.reshape(seq_local, 2 * seg_count, head_count, head_dim)
    query_u = (
        (query_rows + bias_u.astype(jnp.float32).reshape(-1))
        .astype(jnp.bfloat16)
        .reshape(seq_local, seg_rows, head_count, head_dim)
    )
    query_v = (
        (query_rows + bias_v.astype(jnp.float32).reshape(-1))
        .astype(jnp.bfloat16)
        .reshape(seq_local, seg_rows, head_count, head_dim)
    )
    w_rel_heads = w_rel.reshape(feature_width, head_count, head_dim)
    rel_coeff = jnp.einsum(
        "sihe,fhe->sihf", query_v, w_rel_heads, preferred_element_type=jnp.float32
    )
    sin_all, cos_all = angle_tables(jnp.arange(2 * seg_count).astype(jnp.float32), feature_width)
    key_pos = jnp.concatenate([cos_all, sin_all], axis=-1).astype(jnp.bfloat16)
    query_index = seg_count + seg_start + jnp.arange(seg_rows, dtype=jnp.int32)
    sin_q, cos_q = angle_tables(query_index.astype(jnp.float32), feature_width)
    sin_query = sin_q[None, :, None, :]
    cos_query = cos_q[None, :, None, :]
    coeff_sin = rel_coeff[..., :half_width]
    coeff_cos = rel_coeff[..., half_width:]
    query_pos = jnp.concatenate(
        [
            coeff_sin * sin_query + coeff_cos * cos_query,
            coeff_cos * sin_query - coeff_sin * cos_query,
        ],
        axis=-1,
    ).astype(jnp.bfloat16)
    allowed = jnp.arange(2 * seg_count, dtype=jnp.int32)[None, :] <= query_index[:, None]

    def score_block():
        raw_scores = (
            jnp.einsum("sihe,sjhe->shij", query_u, key_heads, preferred_element_type=jnp.float32)
            + jnp.einsum("sihf,jf->shij", query_pos, key_pos, preferred_element_type=jnp.float32)
        ) * score_scale
        return jnp.where(allowed[None, None], raw_scores, -1e30)

    scores = score_block()
    row_top = jnp.max(scores, axis=-1, keepdims=True)
    expo = jnp.exp(scores - row_top)
    row_total = jnp.sum(expo, axis=-1, keepdims=True)
    log_total = row_top + jnp.log(row_total)
    att_probs = (expo / row_total).astype(jnp.bfloat16)
    att_mixed = jnp.einsum(
        "shij,sjhe->sihe", att_probs, value_heads, preferred_element_type=jnp.float32
    )
    mixed_low = att_mixed.reshape(seq_local, seg_rows, feature_width).astype(jnp.bfloat16)
    residual = pooled + jnp.einsum(
        "sid,de->sie", mixed_low, w_out, preferred_element_type=jnp.float32
    )
    normed_two = layer_norm(residual, gain_two_f, shift_two_f)
    two_low = normed_two.astype(jnp.bfloat16)
    ffn_inner = jnp.einsum(
        "sid,df->sif", two_low, w_up, preferred_element_type=jnp.float32
    ) + bias_up.astype(jnp.float32)
    hidden_low = smooth_gate(ffn_inner).astype(jnp.bfloat16)
    branch_out = jnp.einsum(
        "sif,fd->sid", hidden_low, w_down, preferred_element_type=jnp.float32
    ) + bias_down.astype(jnp.float32)
    out_low = (residual + branch_out).astype(jnp.bfloat16)
    rows_all = lax.all_gather(out_low, "blk", axis=1, tiled=True)
    picked = jnp.take_along_axis(rows_all, segment[:, :, None], axis=1)
    out_chars = (chars_f + picked.astype(jnp.float32)).astype(jnp.bfloat16)
    new_memory = pooled.astype(jnp.bfloat16)
    grad_table = jax.vmap(full_table)(grad_f, segment)
    grad_output = lax.psum_scatter(grad_table, "blk", scatter_dimension=1, tiled=True)
    grad_down_low = grad_output.astype(jnp.bfloat16)
    grad_bias_down = jnp.sum(grad_down_low.astype(jnp.float32), axis=(0, 1))
    grad_w_down = jnp.einsum(
        "sif,sid->fd", hidden_low, grad_down_low, preferred_element_type=jnp.float32
    )
    grad_hidden = jnp.einsum(
        "sid,fd->sif", grad_down_low, w_down, preferred_element_type=jnp.float32
    )
    unused_value, gate_back = jax.vjp(smooth_gate, ffn_inner)
    grad_inner = gate_back(grad_hidden)[0].astype(jnp.bfloat16)
    grad_bias_up = jnp.sum(grad_inner.astype(jnp.float32), axis=(0, 1))
    grad_w_up = jnp.einsum("sid,sif->df", two_low, grad_inner, preferred_element_type=jnp.float32)
    grad_normed_two = jnp.einsum(
        "sif,df->sid", grad_inner, w_up, preferred_element_type=jnp.float32
    )
    unused_norm, norm_two_back = jax.vjp(layer_norm, residual, gain_two_f, shift_two_f)
    grad_resid_norm, grad_gain_two, grad_shift_two = norm_two_back(grad_normed_two)
    grad_residual = grad_output + grad_resid_norm
    grad_att_low = grad_residual.astype(jnp.bfloat16)
    grad_w_out = jnp.einsum(
        "sid,sie->de", mixed_low, grad_att_low, preferred_element_type=jnp.float32
    )
    grad_mixed = jnp.einsum("sie,de->sid", grad_att_low, w_out, preferred_element_type=jnp.float32)
    grad_mixed = grad_mixed.astype(jnp.bfloat16).reshape(seq_local, seg_rows, head_count, head_dim)
    scores_again = score_block()
    probs_full = jnp.exp(scores_again - log_total)
    probs_low = probs_full.astype(jnp.bfloat16)
    grad_probs = jnp.einsum(
        "sihe,sjhe->shij", grad_mixed, value_heads, preferred_element_type=jnp.float32
    )
    grad_values = jnp.einsum(
        "shij,sihe->sjhe", probs_low, grad_mixed, preferred_element_type=jnp.float32
    )
    prob_delta = jnp.sum(probs_full * grad_probs, axis=-1, keepdims=True)
    grad_scores = (probs_full * (grad_probs - prob_delta)).astype(jnp.bfloat16)
    grad_query_u = (
        jnp.einsum("shij,sjhe->sihe", grad_scores, key_heads, preferred_element_type=jnp.float32)
        * score_scale
    )
    grad_keys = (
        jnp.einsum("shij,sihe->sjhe", grad_scores, query_u, preferred_element_type=jnp.float32)
        * score_scale
    )
    grad_query_pos = (
        jnp.einsum("shij,jf->sihf", grad_scores, key_pos, preferred_element_type=jnp.float32)
        * score_scale
    )
    grad_first = grad_query_pos[..., :half_width]
    grad_second = grad_query_pos[..., half_width:]
    grad_coeff = jnp.concatenate(
        [
            grad_first * sin_query - grad_second * cos_query,
            grad_first * cos_query + grad_second * sin_query,
        ],
        axis=-1,
    ).astype(jnp.bfloat16)
    grad_w_rel = jnp.einsum(
        "sihf,sihe->fhe", grad_coeff, query_v, preferred_element_type=jnp.float32
    ).reshape(feature_width, feature_width)
    grad_query_v = jnp.einsum(
        "sihf,fhe->sihe", grad_coeff, w_rel_heads, preferred_element_type=jnp.float32
    )
    grad_bias_u = jnp.sum(grad_query_u, axis=(0, 1))
    grad_bias_v = jnp.sum(grad_query_v, axis=(0, 1))
    grad_query = (
        (grad_query_u + grad_query_v)
        .reshape(seq_local, seg_rows, feature_width)
        .astype(jnp.bfloat16)
    )
    grad_w_query = jnp.einsum(
        "sid,sie->de", normed_low, grad_query, preferred_element_type=jnp.float32
    )
    grad_normed = jnp.einsum("sie,de->sid", grad_query, w_query, preferred_element_type=jnp.float32)
    key_share, value_share = (
        lax.psum_scatter(
            grad_keys.reshape(seq_local, 2, seg_count, feature_width),
            "blk",
            scatter_dimension=2,
            tiled=True,
        ),
        lax.psum_scatter(
            grad_values.reshape(seq_local, 2, seg_count, feature_width),
            "blk",
            scatter_dimension=2,
            tiled=True,
        ),
    )
    key_low = key_share.astype(jnp.bfloat16)
    value_low = value_share.astype(jnp.bfloat16)
    grad_w_key = jnp.einsum(
        "sid,sie->de", mem_low, key_low[:, 0], preferred_element_type=jnp.float32
    ) + jnp.einsum("sid,sie->de", normed_low, key_low[:, 1], preferred_element_type=jnp.float32)
    grad_w_value = jnp.einsum(
        "sid,sie->de", mem_low, value_low[:, 0], preferred_element_type=jnp.float32
    ) + jnp.einsum("sid,sie->de", normed_low, value_low[:, 1], preferred_element_type=jnp.float32)
    grad_normed = grad_normed + jnp.einsum(
        "sie,de->sid", key_low[:, 1], w_key, preferred_element_type=jnp.float32
    )
    grad_normed = grad_normed + jnp.einsum(
        "sie,de->sid", value_low[:, 1], w_value, preferred_element_type=jnp.float32
    )
    grad_mem_normed = jnp.einsum(
        "sie,de->sid", key_low[:, 0], w_key, preferred_element_type=jnp.float32
    ) + jnp.einsum("sie,de->sid", value_low[:, 0], w_value, preferred_element_type=jnp.float32)
    unused_one, norm_one_back = jax.vjp(layer_norm, pooled, gain_one_f, shift_one_f)
    grad_pooled_norm, grad_gain_one, grad_shift_one = norm_one_back(grad_normed)
    unused_mem, norm_mem_back = jax.vjp(layer_norm, memory_f, gain_one_f, shift_one_f)
    unused_grad, grad_gain_mem, grad_shift_mem = norm_mem_back(grad_mem_normed)
    grad_gain_one = grad_gain_one + grad_gain_mem
    grad_shift_one = grad_shift_one + grad_shift_mem
    grad_pooled = grad_residual + grad_pooled_norm
    grad_sum = grad_pooled / own_lengths[:, :, None]
    grad_sum_all = lax.all_gather(grad_sum, "blk", axis=1, tiled=True)
    grad_chars = grad_f + jnp.take_along_axis(grad_sum_all, segment[:, :, None], axis=1)
    (
        grad_w_query,
        grad_w_key,
        grad_w_value,
        grad_w_rel,
        grad_w_out,
        grad_w_up,
        grad_w_down,
        grad_bias_u,
        grad_bias_v,
        grad_gain_one,
        grad_shift_one,
        grad_gain_two,
        grad_shift_two,
        grad_bias_up,
        grad_bias_down,
    ) = lax.psum(
        (
            grad_w_query,
            grad_w_key,
            grad_w_value,
            grad_w_rel,
            grad_w_out,
            grad_w_up,
            grad_w_down,
            grad_bias_u,
            grad_bias_v,
            grad_gain_one,
            grad_shift_one,
            grad_gain_two,
            grad_shift_two,
            grad_bias_up,
            grad_bias_down,
        ),
        ("seq", "blk"),
    )
    return (
        out_chars,
        grad_chars,
        new_memory,
        grad_w_query,
        grad_w_key,
        grad_w_value,
        grad_w_rel,
        grad_w_out,
        grad_w_up,
        grad_w_down,
        grad_bias_u,
        grad_bias_v,
        grad_gain_one,
        grad_shift_one,
        grad_gain_two,
        grad_shift_two,
        grad_bias_up,
        grad_bias_down,
    )


def solution(mesh):
    placed = (
        P("seq", "blk", None),
        P("seq", None),
        P("seq", "blk", None),
        P("seq", "blk", None),
        P(),
        P(),
        P(),
        P(),
        P(),
        P(),
        P(),
        P(),
        P(),
        P(),
        P(),
        P(),
        P(),
        P(),
        P(),
    )
    return jax.shard_map(
        shards_whole if fits_whole(mesh) else shards,
        mesh=mesh,
        in_specs=placed,
        out_specs=(
            P("seq", "blk", None),
            P("seq", "blk", None),
            P("seq", "blk", None),
            P(),
            P(),
            P(),
            P(),
            P(),
            P(),
            P(),
            P(),
            P(),
            P(),
            P(),
            P(),
            P(),
            P(),
            P(),
        ),
        check_vma=False,
    )
```
